128 devices in a mesh: dp: 4 (over x_hi, core), wide: 32 (over y, x_lo, z).
Axes of the slice: x: 4 (x_hi: 2, x_lo: 2; x = x_hi * 2 + x_lo), y: 4, z: 4, core: 2. Of those that a mesh axis runs over, the one named last changes fastest.
Arguments:
- hidden: bfloat16 [16384, 768], P(('dp', 'wide')), may hold values from -6 to 6
- cotangent: bfloat16 [16384, 768], P(('dp', 'wide')), may hold values from -6 to 6
- routes: int32 [16384, 1], P(('dp', 'wide')), may hold values from 0 to 31
- seg_lengths: int32 [4, 16], P('dp'), may hold values from 1 to 2048, 4096 in all within a row
- gain_mix: float32 [768], replicated, may hold values from 0.5 to 1.5
- in_x: bfloat16 [768, 1536], P(None, 'wide'), may hold values from -0.21875 to 0.21875
- in_z: bfloat16 [768, 1536], P(None, 'wide'), may hold values from -0.21875 to 0.21875
- conv_w: float32 [4, 1536], P(None, 'wide'), may hold values from -3 to 3
- conv_b: float32 [1536], P('wide'), may hold values from -3 to 3
- x_proj: bfloat16 [1536, 80], P('wide'), may hold values from -0.15625 to 0.15625
- dt_proj: bfloat16 [48, 1536], P(None, 'wide'), may hold values from -0.875 to 0.875
- dt_bias: float32 [1536], P('wide'), may hold values from -6.2 to -2
- a_log: float32 [16, 1536], P(None, 'wide'), may hold values from -2.5 to 2.77
- skip_d: float32 [1536], P('wide'), may hold values from 0.5 to 1.5
- out_proj: bfloat16 [1536, 768], P('wide'), may hold values from -0.15625 to 0.15625
- gain_moe: float32 [768], replicated, may hold values from 0.5 to 1.5
- router: bfloat16 [768, 32], replicated, may hold values from -0.109375 to 0.109375
- w_gate: bfloat16 [32, 768, 3072], P('wide', None, 'dp'), may hold values from -0.21875 to 0.21875
- w_up: bfloat16 [32, 768, 3072], P('wide', None, 'dp'), may hold values from -0.21875 to 0.21875
- w_down: bfloat16 [32, 3072, 768], P('wide', 'dp'), may hold values from -6 to 6
Outputs:
- output: bfloat16 [16384, 768], P(('dp', 'wide'))
- grad_hidden: float32 [16384, 768], P(('dp', 'wide'))
- grad_gain_mix: float32 [768], replicated
- grad_in_x: float32 [768, 1536], P(None, 'wide')
- grad_in_z: float32 [768, 1536], P(None, 'wide')
- grad_conv_w: float32 [4, 1536], P(None, 'wide')
- grad_conv_b: float32 [1536], P('wide')
- grad_x_proj: float32 [1536, 80], P('wide')
- grad_dt_proj: float32 [48, 1536], P(None, 'wide')
- grad_dt_bias: float32 [1536], P('wide')
- grad_a_log: float32 [16, 1536], P(None, 'wide')
- grad_skip_d: float32 [1536], P('wide')
- grad_out_proj: float32 [1536, 768], P('wide')
- grad_gain_moe: float32 [768], replicated
- grad_router: float32 [768, 32], replicated
- grad_w_gate: float32 [32, 768, 3072], P('wide', None, 'dp')
- grad_w_up: float32 [32, 768, 3072], P('wide', None, 'dp')
- grad_w_down: float32 [32, 3072, 768], P('wide', 'dp')
The draws below stay inside these ranges and needn't reach their ends.
Inputs may be any that keep to these rules, and one draw needn't show every extreme that they name: `seg_lengths`: each row lists in order the lengths of its segments, which fill its 4096 positions; the last entry is the padding at the row's end; the largest entry of every row is 2048.
All inputs are finite; a program needn't handle non-finite values.
Results may differ from the reference program's by a relative error of at most 0.028.
Values may be sent and summed in bfloat16 or wider, within the bound.
No kernel may reach another device: no remote copies, remote signals or barrier semaphores. Data moves between devices by JAX's collectives and lax.ppermute only.
A program may use at most 128 MiB of HBM per device.

```python
import math
import jax
import jax.numpy as jnp
import numpy as np
from jax import lax

D = 768
DI = 1536
NST = 16
R = 48
KC = 4
FF = 3072
TOK_DEV = 128
NSEG = 16
SCAN_BLOCK = 512
SEQ = 4096
TOKENS = 16384
EXPERTS = 32
CAP = 5
N_DP = 4


def lasting_channels(key, portion):
    return jax.random.bernoulli(key, portion, (DI,)).astype(jnp.float32)


def draw_a_log(key, part):
    lasting = lasting_channels(key, 0.5)
    key = jax.random.fold_in(key, 3)
    slow_key, fast_key = jax.random.split(key)
    slow_values = jax.random.uniform(slow_key, (NST, DI), jnp.float32, -2.5, -1.6)
    fast_values = jax.random.uniform(fast_key, (NST, DI), jnp.float32, 0.0, 2.77)
    return jnp.where(lasting[None, :] > 0.5, slow_values, fast_values)


def draw_dt_bias(key, part):
    lasting = lasting_channels(key, 0.5)
    key = jax.random.fold_in(key, 7)
    slow_key, fast_key = jax.random.split(key)
    slow_values = jax.random.uniform(slow_key, (DI,), jnp.float32, -6.2, -5.5)
    fast_values = jax.random.uniform(fast_key, (DI,), jnp.float32, -4.5, -2.0)
    return jnp.where(lasting > 0.5, slow_values, fast_values)


def block_levels(rng, shape, cuts, smallest, high):
    level = 1.0
    for dim, blocks in cuts:
        draws = jax.random.uniform(jax.random.fold_in(jax.random.fold_in(rng, 6), dim), (blocks,), jnp.float32, smallest / len(cuts), high / len(cuts))
        level = level * jnp.repeat(jnp.exp(draws), shape[dim] // blocks).reshape((-1,) + (1,) * (len(shape) - 1 - dim))
    return level


def picks_of(stream_key, rows, amount, top, lift):
    ranking = jax.random.permutation(jax.random.fold_in(stream_key, 1), amount)
    pull = ranking
    for power in range(3):
        pull = pull * pull // amount
    pull = pull * lift // amount
    tickets = jax.random.randint(jax.random.fold_in(stream_key, 2), (rows, amount), 0, 4096) + pull
    sure = jax.random.permutation(jax.random.fold_in(stream_key, 3), rows)[jnp.arange(amount) % rows]
    tickets = jnp.where(jnp.arange(rows)[:, None] == sure[None, :], 1 << 14, tickets)
    priority = tickets * amount + jnp.arange(amount)
    return lax.top_k(priority.astype(jnp.int32), top)[1].astype(jnp.int32)


def split_up(count, total, limit, slope):
    portions = [(1 << 20) // math.isqrt(standing ** slope) + 1 for standing in range(2, count + 1)]
    rest, holding = total - limit - (count - 1), [1] * (count - 1)
    while rest > 0:
        movable = [i for i in range(count - 1) if holding[i] < limit]
        mass, remaining = sum([portions[i] for i in movable]), rest
        for i in movable:
            extra = min(limit - holding[i], max(1, remaining * portions[i] // mass), rest)
            holding[i] = holding[i] + extra
            rest = rest - extra
    return np.array([limit] + holding)


def uneven_parts(key, amount, total, most, lean):
    if amount == 2:
        one = jax.random.randint(key, (), max(1, total - most), min(most, total - 1) + 1)
        return jnp.stack([one, total - one])
    sizes = jnp.asarray(split_up(amount, total, most, lean), jnp.int32)
    couples = (amount - 1) // 2
    giver, receiver = sizes[1:1 + 2 * couples:2], sizes[2:2 + 2 * couples:2]
    room = jnp.minimum(giver - 1, most - receiver)
    moved = jax.random.randint(jax.random.fold_in(key, 1), (couples,), 0, 1 << 20) % (room + 1)
    sizes = sizes.at[1:1 + 2 * couples:2].set(giver - moved).at[2:2 + 2 * couples:2].set(receiver + moved)
    return sizes[jax.random.permutation(jax.random.fold_in(key, 2), amount)]


def scatter_about(stream_key, shape, deviation, reach, cuts=(), held_as=jnp.bfloat16):
    values = jax.random.normal(stream_key, shape, jnp.float32) * deviation
    if len(cuts) > 0:
        values = block_levels(stream_key, shape, cuts, -0.22, 0.18) * values
    return jnp.clip(values, min=-reach, max=reach).astype(held_as)


def setup_inputs(seed: int = 0) -> dict:
    key_list = jax.random.split(jax.random.key(seed), 21)
    hidden = scatter_about(key_list[0], (TOKENS, D), 1.0, 6.0, ((0, 128),))
    cotangent = scatter_about(key_list[1], (TOKENS, D), 1.0, 6.0, ((0, 128),))
    routes = picks_of(key_list[2], TOKENS, EXPERTS, 1, 256)
    seg_lengths = jax.vmap(lambda own: uneven_parts(own, NSEG, SEQ, SEQ // 2, 2))(jax.random.split(key_list[3], N_DP)).reshape((N_DP, NSEG)).astype(jnp.int32)
    gain_mix = jnp.clip(1.0 + 0.1 * jax.random.normal(key_list[4], (D,), jnp.float32), 0.5, 1.5)
    in_x = scatter_about(key_list[5], (D, DI), D ** -0.5, 0.21875, ((1, 32),))
    in_z = scatter_about(key_list[6], (D, DI), D ** -0.5, 0.21875, ((1, 32),))
    conv_w = scatter_about(key_list[7], (KC, DI), 0.5, 3.0, ((1, 32),), jnp.float32)
    conv_b = scatter_about(key_list[8], (DI,), 0.5, 3.0, ((0, 32),), jnp.float32)
    x_proj = scatter_about(key_list[9], (DI, R + 2 * NST), DI ** -0.5, 0.15625, ((0, 32),))
    dt_proj = scatter_about(key_list[10], (R, DI), R ** -0.5, 0.875, ((1, 32),))
    dt_bias = draw_dt_bias(jax.random.fold_in(key_list[20], 71), 0)
    a_log = draw_a_log(jax.random.fold_in(key_list[20], 71), 0)
    skip_d = jnp.clip(0.5 + 1.0 * jax.random.uniform(key_list[13], (DI,), jnp.float32) ** block_levels(key_list[13], (DI,), ((0, 32),), -0.2, 0.2), 0.5, 1.5)
    out_proj = scatter_about(key_list[14], (DI, D), DI ** -0.5, 0.15625, ((0, 32),))
    gain_moe = jnp.clip(1.0 + 0.1 * jax.random.normal(key_list[15], (D,), jnp.float32), 0.5, 1.5)
    router = scatter_about(key_list[16], (D, EXPERTS), (4 * D) ** -0.5, 0.109375)
    w_gate = scatter_about(key_list[17], (EXPERTS, D, FF), D ** -0.5, 0.21875, ((0, 32), (2, 4)))
    w_up = scatter_about(key_list[18], (EXPERTS, D, FF), D ** -0.5, 0.21875, ((0, 32), (2, 4)))
    w_down = scatter_about(key_list[19], (EXPERTS, FF, D), (max(FF // (2 * EXPERTS * EXPERTS), 1)) ** -0.5, 6.0, ((0, 32), (1, 4)))
    return dict(hidden=hidden, cotangent=cotangent, routes=routes, seg_lengths=seg_lengths, gain_mix=gain_mix, in_x=in_x, in_z=in_z, conv_w=conv_w, conv_b=conv_b, x_proj=x_proj, dt_proj=dt_proj, dt_bias=dt_bias, a_log=a_log, skip_d=skip_d, out_proj=out_proj, gain_moe=gain_moe, router=router, w_gate=w_gate, w_up=w_up, w_down=w_down)


epsilon = 1e-05
highest = lax.Precision.HIGHEST

@jax.custom_vjp
def low(v):
    return lax.optimization_barrier(v.astype(jnp.bfloat16)).astype(jnp.float32)

@jax.custom_vjp
def low_back(v):
    return v

def low_keep(v):
    return (low(v), None)

def low_pass(kept, grad):
    return (grad,)

def back_keep(v):
    return (v, None)

def back_low(kept, grad):
    return (low(grad),)
low.defvjp(low_keep, low_pass)
low_back.defvjp(back_keep, back_low)

def product(left, right):
    return jnp.dot(left, right, precision=highest, preferred_element_type=jnp.float32)

def rms_norm(values, gain):
    scale = lax.rsqrt(lax.optimization_barrier(jnp.mean(values * values, axis=-1, keepdims=True)) + epsilon)
    return values * scale * gain

def row_layout(lengths):
    lengths = lengths.astype(jnp.int32)
    ends = jnp.cumsum(lengths).astype(jnp.int32)
    starts = (ends - lengths).astype(jnp.int32)
    position = jnp.arange(SEQ, dtype=jnp.int32)
    segment = lax.optimization_barrier(jnp.sum((position[:, None] >= ends[None, :-1]).astype(jnp.int32), axis=1)).astype(jnp.int32)
    reset = jnp.any(position[:, None] == starts[None, :], axis=1)
    live = position < starts[-1]
    return (segment, reset, live)

def conv_rows(inner, segment, conv_w, conv_b):
    length = inner.shape[0]
    total = conv_b[None, :] + conv_w[KC - 1][None, :] * inner
    for back in range(1, KC):
        shifted = jnp.pad(inner, ((back, 0), (0, 0)))[:length]
        earlier = jnp.pad(segment, (back, 0), constant_values=-1)[:length]
        same = (earlier == segment).astype(jnp.float32)
        total = total + conv_w[KC - 1 - back][None, :] * shifted * same[:, None]
    return total

def linear_step(earlier, later):
    return (earlier[0] * later[0], later[0] * earlier[1] + later[1])

def selective_scan(inputs, steps, b_coef, c_coef, rates, keep):
    blocks = inputs.shape[0] // SCAN_BLOCK
    width = inputs.shape[1]

    def block(state, pieces):
        in_blk, step_blk, b_blk, c_blk, keep_blk = pieces
        decay = jnp.exp(step_blk[:, None, :] * rates[None]) * keep_blk[:, None, None]
        drive = step_blk[:, None, :] * b_blk[:, :, None] * in_blk[:, None, :]
        acc_decay, acc_drive = lax.associative_scan(linear_step, (decay, drive), axis=0)
        states = acc_decay * state[None] + acc_drive
        return (states[-1], lax.optimization_barrier(jnp.sum(states * c_blk[:, :, None], axis=1)))
    pieces = (inputs.reshape(blocks, SCAN_BLOCK, width), steps.reshape(blocks, SCAN_BLOCK, width), b_coef.reshape(blocks, SCAN_BLOCK, NST), c_coef.reshape(blocks, SCAN_BLOCK, NST), keep.reshape(blocks, SCAN_BLOCK))
    _, outputs = lax.scan(jax.checkpoint(block), jnp.zeros((NST, width), jnp.float32), pieces)
    return outputs.reshape(-1, width)

def routing(route, live):
    blocks = route.shape[0] // TOK_DEV
    chosen = route[:, None] == jnp.arange(EXPERTS, dtype=jnp.int32)[None, :]
    taken = (chosen & live[:, None]).astype(jnp.int32)
    counts = jnp.cumsum(taken.reshape(blocks, TOK_DEV, EXPERTS), axis=1).astype(jnp.int32).reshape(-1, EXPERTS)
    rank = lax.optimization_barrier(jnp.sum((counts - 1) * taken, axis=1)).astype(jnp.int32)
    kept = live & (rank < CAP)
    block_id = (jnp.arange(route.shape[0], dtype=jnp.int32) // TOK_DEV).astype(jnp.int32)
    slot = jnp.where(kept, (route * blocks + block_id) * CAP + rank, EXPERTS * blocks * CAP).astype(jnp.int32)
    return (slot, kept, chosen.astype(jnp.float32))

def expert(pieces):
    rows_in, gate_weight, up_weight, down_weight = pieces
    gate_in = low_back(product(rows_in, gate_weight))
    up_in = low_back(product(rows_in, up_weight))
    hidden_act = low(jax.nn.silu(gate_in) * up_in)
    return low_back(low(product(hidden_act, down_weight)))

def reference(hidden, cotangent, routes, seg_lengths, gain_mix, in_x, in_z, conv_w, conv_b, x_proj, dt_proj, dt_bias, a_log, skip_d, out_proj, gain_moe, router, w_gate, w_up, w_down):
    segment, reset, live = jax.vmap(row_layout)(seg_lengths)
    live_all = live.reshape(-1)
    slot, kept, chosen = routing(routes[:, 0].astype(jnp.int32), live_all)
    kept_f = kept.astype(jnp.float32)
    blocks = TOKENS // TOK_DEV
    slots = EXPERTS * blocks * CAP

    def forward(first, gain_mix, in_x, in_z, conv_w, conv_b, x_proj, dt_proj, dt_bias, a_log, skip_d, out_proj, gain_moe, router, w_gate, w_up, w_down):
        rates = -jnp.exp(a_log)

        def row(pieces):
            row_in, row_segment, row_reset, row_live = pieces
            normed = low(rms_norm(row_in, gain_mix))
            inner = low_back(product(normed, in_x))
            gate_z = low_back(product(normed, in_z))
            conv_act = jax.nn.silu(conv_rows(inner, row_segment, conv_w, conv_b))
            act_low = low(conv_act)
            small = low_back(product(act_low, x_proj))
            step_low = low(small[:, :R])
            b_coef = small[:, R:R + NST]
            c_coef = small[:, R + NST:]
            steps = jax.nn.softplus(low_back(product(step_low, dt_proj)) + dt_bias)
            keep = 1.0 - row_reset.astype(jnp.float32)
            scanned = selective_scan(conv_act, steps, b_coef, c_coef, rates, keep) + skip_d * conv_act
            gated = low(scanned * jax.nn.silu(gate_z) * row_live.astype(jnp.float32)[:, None])
            return low_back(product(gated, out_proj))
        mixed = lax.map(jax.checkpoint(row), (first.reshape(N_DP, SEQ, D), segment, reset, live)).reshape(-1, D)
        middle = first + mixed
        normed_two = low(rms_norm(middle, gain_moe))
        logits = low_back(product(normed_two, router))
        chances = jax.nn.softmax(logits, axis=-1)
        gate = lax.optimization_barrier(jnp.sum(chances * chosen, axis=1))
        outgoing = low_back(normed_two)
        buffer = jnp.zeros((slots + 1, D), jnp.float32).at[slot].add(outgoing)
        expert_in = buffer[:slots].reshape(EXPERTS, blocks * CAP, D)
        expert_out = lax.map(jax.checkpoint(expert), (expert_in, w_gate, w_up, w_down))
        back = jnp.concatenate([expert_out.reshape(slots, D), jnp.zeros((1, D), jnp.float32)], axis=0)[slot]
        return middle + (gate * kept_f)[:, None] * back
    floats = (hidden, gain_mix, in_x, in_z, conv_w, conv_b, x_proj, dt_proj, dt_bias, a_log, skip_d, out_proj, gain_moe, router, w_gate, w_up, w_down)
    floats = tuple((item.astype(jnp.float32) for item in floats))
    result, pullback = jax.vjp(forward, *floats)
    grads = pullback(cotangent.astype(jnp.float32))
    return (result.astype(jnp.bfloat16), grads[0], grads[1], grads[2], grads[3], grads[4], grads[5], grads[6], grads[7], grads[8], grads[9], grads[10], grads[11], grads[12], grads[13], grads[14], grads[15], grads[16])
```

```python
from functools import partial

import jax
import jax.numpy as jnp
from jax import lax
from jax.experimental import pallas as pl
from jax.experimental.pallas import tpu as pltpu
from jax.sharding import PartitionSpec as P

f32 = jnp.float32
bf16 = jnp.bfloat16
KC = 4
SUB = 8
CAP = 5
STOP = 1e6
epsilon = 1e-05
VMEM_LIMIT = 56 * 1024 * 1024


def dot_nn(left, right):
    return lax.dot_general(left, right, (((1,), (0,)), ((), ())), preferred_element_type=f32)


def dot_nt(left, right):
    return lax.dot_general(left, right, (((1,), (1,)), ((), ())), preferred_element_type=f32)


def dot_tn(left, right):
    return lax.dot_general(left, right, (((0,), (0,)), ((), ())), preferred_element_type=f32)


def call(kernel, out_shapes, scratch, args, smem=0):
    specs = [pl.BlockSpec(memory_space=pltpu.SMEM)] * smem
    specs = specs + [pl.BlockSpec(memory_space=pltpu.VMEM)] * (len(args) - smem)
    return pl.pallas_call(
        kernel,
        out_shape=out_shapes,
        in_specs=specs,
        out_specs=[pl.BlockSpec(memory_space=pltpu.VMEM)] * len(out_shapes),
        scratch_shapes=scratch,
        compiler_params=pltpu.CompilerParams(vmem_limit_bytes=VMEM_LIMIT),
    )(*args)


def shape(dims, dtype=f32):
    return jax.ShapeDtypeStruct(dims, dtype)


def group_of(di):
    return 256 if di % 256 == 0 else 128


def sublane_iota(width):
    return lax.broadcasted_iota(jnp.int32, (SUB, width), 0)


def from_before(block, first):
    row = sublane_iota(block.shape[1])
    return jnp.where(row == 0, jnp.broadcast_to(first, block.shape), pltpu.roll(block, 1, 0))


def from_after(block, last):
    row = sublane_iota(block.shape[1])
    return jnp.where(
        row == SUB - 1, jnp.broadcast_to(last, block.shape), pltpu.roll(block, SUB - 1, 0)
    )


def spread_columns(small, first, count, out):
    steps = small.shape[0] // SUB
    for j in range(steps):
        block = small[j * SUB : (j + 1) * SUB, :]
        for n in range(count):
            out[j * count + n] = jnp.broadcast_to(block[:, first + n : first + n + 1], (SUB, 128))


def prefix_states(decay, state):
    row = sublane_iota(state.shape[1])
    for shift in (1, 2, 4):
        inside = row >= shift
        state = state + decay * jnp.where(inside, pltpu.roll(state, shift, 0), 0.0)
        decay = decay * jnp.where(inside, pltpu.roll(decay, shift, 0), 1.0)
    return state


def suffix_states(decay, state):
    row = sublane_iota(state.shape[1])
    for shift in (1, 2, 4):
        inside = row < SUB - shift
        state = state + decay * jnp.where(inside, pltpu.roll(state, SUB - shift, 0), 0.0)
        decay = decay * jnp.where(inside, pltpu.roll(decay, SUB - shift, 0), 1.0)
    return state


def prefix_sum(values):
    row = sublane_iota(values.shape[1])
    for shift in (1, 2, 4):
        values = values + jnp.where(row >= shift, pltpu.roll(values, shift, 0), 0.0)
    return values


def suffix_sum(values):
    row = sublane_iota(values.shape[1])
    for shift in (1, 2, 4):
        values = values + jnp.where(row < SUB - shift, pltpu.roll(values, SUB - shift, 0), 0.0)
    return values


def one_hot(dims, offset):
    row = lax.broadcasted_iota(jnp.int32, dims, 0)
    column = lax.broadcasted_iota(jnp.int32, dims, 1)
    return (row + offset == column).astype(bf16)


def pack_front_kernel(
    core, in_x, x_proj, dt_proj, conv_w, conv_b, dt_bias, skip_d, a_log, out, *, places
):
    width, model = in_x.shape
    half = model // 2
    here = core[0]
    mine = in_x[:, pl.ds(pl.multiple_of(here * half, 128), half)]
    narrow = x_proj.shape[1]
    steps = dot_nn(x_proj[...], one_hot((narrow, 128), 0)) + dot_tn(
        dt_proj[...], one_hot((dt_proj.shape[0], 128), 128 - dt_proj.shape[0])
    )
    values = jnp.concatenate(
        [
            conv_w[...],
            conv_b[...].reshape(1, width),
            dt_bias[...].reshape(1, width),
            skip_d[...].reshape(1, width),
            jnp.zeros((1, width), f32),
            a_log[...],
        ],
        axis=0,
    )
    top = values.astype(bf16)
    left = values - top.astype(f32)
    mid = left.astype(bf16)
    low = (left - mid.astype(f32)).astype(bf16)
    count = values.shape[0]
    extra = dot_tn(top, one_hot((count, 128), 0))
    extra = extra + dot_tn(mid, one_hot((count, 128), count))
    extra = extra + dot_tn(low, one_hot((count, 128), 2 * count))
    rest = jnp.where(here == 0, steps, extra).astype(bf16)
    for place in range(places):
        out[place * width : (place + 1) * width, :half] = mine
        out[place * width : (place + 1) * width, half:] = rest


def pack_gate_kernel(core, in_z, out_proj, out):
    half = in_z.shape[1] // 2
    start = pl.multiple_of(core[0] * half, 128)
    out[:, :half] = in_z[:, pl.ds(start, half)]
    out[:, half:] = out_proj[:, pl.ds(start, half)]


def prepare_kernel(
    base, lengths, hidden, cot, route, gain, nrm_o, tail_o, hid_o, cot_o, route_o, aux_o, auxn_o
):
    rows = hidden.shape[0]
    steps_in = rows // SUB
    row = lax.broadcasted_iota(jnp.int32, (rows, rows), 0)
    column = lax.broadcasted_iota(jnp.int32, (rows, rows), 1)
    in_order = (row % SUB) * steps_in + row // SUB == column
    order = in_order.astype(bf16)
    hid = dot_nn(order, hidden[...])
    hid_o[...] = hid.astype(bf16)
    cot_o[...] = dot_nn(order, cot[...]).astype(bf16)
    ours = jnp.where(in_order, jnp.broadcast_to(route[...], (rows, rows)), 0)
    route_o[...] = jnp.sum(ours, axis=1, keepdims=True)
    scale = lax.rsqrt(jnp.mean(hid * hid, axis=1, keepdims=True) + epsilon)
    normed = (hid * scale * gain[...].reshape(1, -1)).astype(bf16)
    nrm_o[...] = normed
    tail_row = lax.broadcasted_iota(jnp.int32, (16, rows), 0)
    tail_column = lax.broadcasted_iota(jnp.int32, (16, rows), 1)
    picked = (tail_column == rows - 1 - (KC - 2 - tail_row) * SUB) & (tail_row < KC - 1)
    tail_o[...] = dot_nn(picked.astype(bf16), normed).astype(bf16)

    def layout(position, lane):
        back = position - (lane + 1)
        segment = jnp.zeros_like(position)
        segment_back = jnp.zeros_like(position)
        reset = position == 0
        end = jnp.int32(0)
        for j in range(lengths.shape[1] - 1):
            end = end + lengths[0, j]
            segment = segment + (position >= end).astype(jnp.int32)
            segment_back = segment_back + (back >= end).astype(jnp.int32)
            reset = reset | (position == end)
        same = (back >= 0) & (segment == segment_back)
        live = position < end
        picked = jnp.where(lane == KC - 1, live.astype(f32), reset.astype(f32))
        return jnp.where(lane < KC - 1, same.astype(f32), picked)

    at = lax.broadcasted_iota(jnp.int32, (rows, 128), 0)
    lane = lax.broadcasted_iota(jnp.int32, (rows, 128), 1)
    aux_o[...] = layout(base[0] + (at % SUB) * steps_in + at // SUB, lane)
    later = lax.broadcasted_iota(jnp.int32, (SUB, 128), 0)
    lane = lax.broadcasted_iota(jnp.int32, (SUB, 128), 1)
    auxn_o[...] = layout(base[0] + rows + later, lane)


def front_kernel(
    core, nrm_in, halo_in, wm, wo, aux, ext_o, pre_o, steps_o, sig_o, small_o, x_o, tpre_o, tsuf_o,
    state_o, par_o, xd_o, bw_s, sd_s, q_s, nrm_s, sum_s, *, rank, count
):
    rows, di = pre_o.shape
    half = wo.shape[1] - 128
    steps_in = rows // SUB
    gs = group_of(di)
    low = core[0] == 0
    nrm_s[0, :rows] = jnp.where(low, nrm_in[:, :half], nrm_in[:, half:])
    nrm_s[1, :rows] = jnp.where(low, nrm_in[:, half:], nrm_in[:, :half])
    nrm_s[0, rows:] = jnp.where(low, halo_in[:, :half], halo_in[:, half:])
    nrm_s[1, rows:] = jnp.where(low, halo_in[:, half:], halo_in[:, :half])
    small_o[...] = jnp.zeros_like(small_o)
    par = par_o
    total_rows = par_o.shape[0]

    def unpack(g, _):
        lanes = pl.ds(pl.multiple_of(g * 128, 128), 128)
        mine = wm[lanes, half:]
        other = wo[lanes, half:]
        xd_o[lanes, :] = jnp.where(low, mine, other)
        turned = jnp.where(low, other, mine).astype(f32).T
        par_o[:, lanes] = (
            turned[:total_rows, :]
            + turned[total_rows : 2 * total_rows, :]
            + turned[2 * total_rows : 3 * total_rows, :]
        )
        return 0

    lax.fori_loop(0, di // 128, unpack, 0)

    def project(g, _):
        lanes = pl.ds(pl.multiple_of(g * gs, gs), gs)
        inner = dot_nt(nrm_s[0], wm[lanes, :half]) + dot_nt(nrm_s[1], wo[lanes, :half])
        for back in range(1, KC):
            block = inner[rows - back * SUB : rows - (back - 1) * SUB, :]
            halo = inner[rows + KC - 1 - back : rows + KC - back, :]
            ext_o[(KC - 1 - back) * SUB : (KC - back) * SUB, lanes] = from_before(block, halo)
        ext_o[(KC - 1) * SUB :, lanes] = inner[:rows, :]
        total = par[KC : KC + 1, lanes] + par[KC - 1 : KC, lanes] * inner[:rows, :]
        for back in range(1, KC):
            shifted = ext_o[(KC - 1 - back) * SUB : (KC - 1 - back) * SUB + rows, lanes]
            total = total + par[KC - 1 - back : KC - back, lanes] * shifted * aux[:, back - 1 : back]
        pre_o[:, lanes] = total
        act = total * jax.nn.sigmoid(total)
        q_s[:, lanes] = act
        small_o[...] += dot_nn(act.astype(bf16), xd_o[lanes, :])
        return 0

    lax.fori_loop(0, di // gs, project, 0)
    small = small_o[...]
    lane = lax.broadcasted_iota(jnp.int32, small.shape, 1)
    step_low = jnp.where(lane >= 128 - rank, pltpu.roll(small, 128 - rank, 1), 0.0).astype(bf16)
    spread_columns(small, rank, count, bw_s)

    def stepping(g, _):
        lanes = pl.ds(pl.multiple_of(g * gs, gs), gs)
        step_pre = dot_nt(step_low, xd_o[lanes, :]) + par[KC + 1 : KC + 2, lanes]
        small_exp = jnp.exp(-jnp.abs(step_pre))
        steps = jnp.maximum(step_pre, 0.0) + jnp.log1p(small_exp)
        steps_o[:, lanes] = steps
        sig_o[:, lanes] = jax.nn.sigmoid(step_pre)
        q_s[:, lanes] = q_s[:, lanes] * steps
        sd_s[:, lanes] = jnp.where(aux[:, 4:5] > 0.5, STOP, steps)
        return 0

    lax.fori_loop(0, di // gs, stepping, 0)

    def chunk(g, _):
        lanes = pl.ds(pl.multiple_of(g * 128, 128), 128)
        rates = [
            jnp.broadcast_to(-jnp.exp(par[8 + n : 9 + n, lanes]), (SUB, 128)) for n in range(count)
        ]

        def step(j, carry):
            states, total = carry
            at = pl.ds(pl.multiple_of(j * SUB, SUB), SUB)
            sd = sd_s[at, lanes]
            q = q_s[at, lanes]
            states = tuple(
                jnp.exp(sd * rates[n]) * states[n] + q * bw_s[j * count + n] for n in range(count)
            )
            return (states, total + sd)

        zero = jnp.zeros((SUB, 128), f32)
        states, total = lax.fori_loop(0, steps_in, step, ((zero,) * count, zero), unroll=4)
        row = sublane_iota(128)
        ahead = prefix_sum(total)
        behind = suffix_sum(total)
        tpre_o[:, lanes] = jnp.where(row == 0, 0.0, pltpu.roll(ahead, 1, 0))
        tsuf_o[:, lanes] = jnp.where(row == SUB - 1, 0.0, pltpu.roll(behind, SUB - 1, 0))
        last = []
        for n in range(count):
            joined = prefix_states(jnp.exp(rates[n] * total), states[n])
            x_o[n, :, lanes] = jnp.where(row == 0, 0.0, pltpu.roll(joined, 1, 0))
            last.append(joined[SUB - 1 : SUB, :])
        sum_s[pl.ds(g, 1), :] = ahead[SUB - 1 : SUB, :]
        to_copies(state_o, jnp.concatenate(last, axis=0).astype(bf16), lanes)
        return 0

    sum_s[...] = jnp.zeros_like(sum_s)
    lax.fori_loop(0, di // 128, chunk, 0)
    sums = sum_s[...]
    top = sums.astype(bf16)
    left = (sums - top.astype(f32)).astype(bf16)
    to_copies(state_o, top, slice(di, di + 128))
    to_copies(state_o, left, slice(di + 128, di + 256))


def to_copies(out, values, lanes):
    count = values.shape[0]
    for place in range(out.shape[0] // count):
        out[place * count : (place + 1) * count, lanes] = values


def negative_rates(par, out):
    out[...] = -jnp.exp(par[8:, :])


def carry_step(decay_sums, arrived, rate_s, state_s):
    for g in range(state_s.shape[1] // 128):
        lanes = slice(g * 128, (g + 1) * 128)
        decay = jnp.exp(rate_s[:, lanes] * decay_sums[g : g + 1, :])
        state_s[:, lanes] = decay * state_s[:, lanes] + arrived[:, lanes].astype(f32)


def middle_kernel(
    core, place, nrm, zm, zo, par, aux, pre, steps, small, x_in, tpre, arrived, hid, cot, route,
    gain, router, gate_z_o, scan_o, send_o, middle_o, ntwo_o, chance_o, meta_o, hot_o,
    entry_o, sums_o, turned_o, bw_s, cw_s, nrm_s, rate_s, *, rank, count, experts, stride, capacity,
    shift
):
    rows, di = pre.shape
    half = zm.shape[1] // 2
    steps_in = rows // SUB
    gs = group_of(di)
    low = core[0] == 0
    nrm_s[0] = jnp.where(low, nrm[:, :half], nrm[:, half:])
    nrm_s[1] = jnp.where(low, nrm[:, half:], nrm[:, :half])

    def project(g, _):
        lanes = pl.ds(pl.multiple_of(g * gs, gs), gs)
        gate_z_o[:, lanes] = dot_nt(nrm_s[0], zm[lanes, :half]) + dot_nt(
            nrm_s[1], zo[lanes, :half]
        )
        return 0

    lax.fori_loop(0, di // gs, project, 0)
    spread_columns(small[...], rank, count, bw_s)
    spread_columns(small[...], rank + count, count, cw_s)
    negative_rates(par, rate_s)
    for there in range(sums_o.shape[0] // count):
        block = slice(there * count, (there + 1) * count)
        sums_o[block, :] = arrived[block, di : di + 128].astype(f32) + arrived[
            block, di + 128 : di + 256
        ].astype(f32)
    entry_o[...] = jnp.zeros_like(entry_o)

    def before_here(there, _):
        block = pl.ds(pl.multiple_of(there * count, count), count)
        carry_step(sums_o[block, :], arrived[block, :di], rate_s, entry_o)
        return 0

    lax.fori_loop(0, place[0], before_here, 0)

    def scan(g, _):
        lanes = pl.ds(pl.multiple_of(g * 128, 128), 128)
        rates = [jnp.broadcast_to(rate_s[n : n + 1, lanes], (SUB, 128)) for n in range(count)]
        before = tpre[:, lanes]
        first = tuple(
            x_in[n, :, lanes] + jnp.exp(rates[n] * before) * entry_o[n : n + 1, lanes]
            for n in range(count)
        )
        skip = par[KC + 2 : KC + 3, lanes]

        def step(j, states):
            at = pl.ds(pl.multiple_of(j * SUB, SUB), SUB)
            step = steps[at, lanes]
            sd = jnp.where(aux[at, 4:5] > 0.5, STOP, step)
            pre_here = pre[at, lanes]
            act = pre_here * jax.nn.sigmoid(pre_here)
            q = step * act
            total = skip * act
            fresh = []
            for n in range(count):
                state = jnp.exp(sd * rates[n]) * states[n] + q * bw_s[j * count + n]
                total = total + state * cw_s[j * count + n]
                fresh.append(state)
            scan_o[at, lanes] = total
            return tuple(fresh)

        lax.fori_loop(0, steps_in, step, first, unroll=4)
        return 0

    lax.fori_loop(0, di // 128, scan, 0)

    def gating(g, carry):
        mine, other = carry
        lanes = pl.ds(pl.multiple_of(g * gs, gs), gs)
        z = gate_z_o[:, lanes]
        gated_wide = scan_o[:, lanes] * (z * jax.nn.sigmoid(z)) * aux[:, 3:4]
        gated = gated_wide.astype(bf16)
        turned_o[lanes, :] = gated_wide.T.astype(bf16)
        return (
            mine + dot_nn(gated, zm[lanes, half:]),
            other + dot_nn(gated, zo[lanes, half:]),
        )

    zero = jnp.zeros((rows, half), f32)
    mine, other = lax.fori_loop(0, di // gs, gating, (zero, zero))
    mixed = jnp.concatenate([jnp.where(low, mine, other), jnp.where(low, other, mine)], axis=1)
    middle = hid[...].astype(f32) + mixed
    middle_o[...] = middle
    scale = lax.rsqrt(jnp.mean(middle * middle, axis=1, keepdims=True) + epsilon)
    ntwo = (middle * scale * gain[...].reshape(1, -1)).astype(bf16)
    ntwo_o[...] = ntwo
    logits = dot_nt(ntwo, router[...])
    top = jnp.max(logits, axis=1, keepdims=True)
    raised = jnp.exp(logits - top)
    chances = raised / jnp.sum(raised, axis=1, keepdims=True)
    chance_o[...] = chances
    lane = lax.broadcasted_iota(jnp.int32, (rows, experts), 1)
    chosen = route[...] == lane
    chosen_f = chosen.astype(f32)
    gate = jnp.sum(chances * chosen_f, axis=1, keepdims=True)
    taken = chosen_f * aux[:, 3:4]
    here = lax.broadcasted_iota(jnp.int32, (rows, rows), 0)
    there = lax.broadcasted_iota(jnp.int32, (rows, rows), 1)
    own_id = (here & (SUB - 1)) * steps_in + (here >> shift)
    other_id = (there & (SUB - 1)) * steps_in + (there >> shift)
    earlier = (other_id < own_id).astype(bf16)
    ranks = jnp.sum(dot_nn(earlier, taken.astype(bf16)) * chosen_f, axis=1, keepdims=True)
    kept = aux[:, 3:4] * (ranks < capacity).astype(f32)
    slot = route[...] * stride + ranks.astype(jnp.int32)
    place = lax.broadcasted_iota(jnp.int32, (rows, experts * stride), 1)
    kept_on = kept > 0.5
    hot_x = ((slot == place) & kept_on).astype(bf16)
    hot_g = ((slot + capacity == place) & kept_on).astype(bf16)
    hot_o[0] = hot_x
    hot_o[1] = hot_g
    weight = gate * kept
    up = (cot[...].astype(f32) * weight).astype(bf16)
    send_o[...] = (dot_tn(hot_x, ntwo) + dot_tn(hot_g, up)).astype(bf16)
    lane8 = lax.broadcasted_iota(jnp.int32, (rows, 8), 1)
    meta_o[...] = jnp.where(
        lane8 == 0, gate, jnp.where(lane8 == 1, kept, jnp.where(lane8 == 2, scale, 0.0))
    )


def back_kernel(
    core, back, zm, zo, par, aux, pre, steps, small, gate_z, scanned, hot, ntwo, middle, meta,
    chances, route, cot, gain, router, gated_t, out_o, mixlow_o, mgrad_o, sg_o, comb_o, zlow_o,
    skip_o, gain_o, y_o, state_o, cw_s, mix_s, *, rank, count, experts, width, span
):
    rows, di = pre.shape
    half = zm.shape[1] // 2
    steps_in = rows // SUB
    gs = group_of(di)
    rows_back = back[...]
    combined = dot_nn(hot[0], rows_back)
    dispatch = dot_nn(hot[1], rows_back)
    gate = meta[:, 0:1]
    kept = meta[:, 1:2]
    scale = meta[:, 2:3]
    mid = middle[...]
    up = cot[...].astype(f32)
    result = (mid + gate * kept * combined).astype(bf16)
    out_o[...] = dot_tn(token_order(rows), result).astype(bf16)
    gate_total = kept * jnp.sum(up * combined, axis=1, keepdims=True)
    lane = lax.broadcasted_iota(jnp.int32, (rows, experts), 1)
    chosen_f = (route[...] == lane).astype(f32)
    logit_grad = (gate * (chosen_f - chances[...]) * gate_total).astype(bf16)
    ngrad = dot_nn(logit_grad, router[...]) + dispatch
    router_rows = dot_tn(logit_grad, ntwo[...])
    gain_o[...] = jnp.sum(ngrad * mid * scale, axis=0, keepdims=True)
    model = mid.shape[1]
    for expert in range(experts):
        row = router_rows[expert : expert + 1, :]
        rows_here = [row[:, k * 128 : (k + 1) * 128] for k in range(model // 128)]
        rows_here.append(jnp.zeros((16 - model // 128, 128), f32))
        comb_o[expert * span + 2 * width : (expert + 1) * span, :] = jnp.concatenate(
            rows_here, axis=0
        ).astype(bf16)
    for there in range(experts):
        comb_o[there * span + width : there * span + 2 * width, :] = gated_t[
            there * width : (there + 1) * width, :
        ]
    scaled = gain[...].reshape(1, -1) * ngrad
    cube = scale * scale * scale
    mgrad = up + scale * scaled - mid * cube * jnp.mean(mid * scaled, axis=1, keepdims=True)
    mgrad_o[...] = mgrad
    low = core[0] == 0
    mixlow = mgrad.astype(bf16)
    mixlow_o[...] = mixlow
    mix_s[0] = jnp.where(low, mixlow[:, :half], mixlow[:, half:])
    mix_s[1] = jnp.where(low, mixlow[:, half:], mixlow[:, :half])
    pieces = width // 16

    def gating(g, _):
        lanes = pl.ds(pl.multiple_of(g * gs, gs), gs)
        ggrad = dot_nt(mix_s[0], zm[lanes, half:]) + dot_nt(mix_s[1], zo[lanes, half:])
        z = gate_z[:, lanes]
        sig = jax.nn.sigmoid(z)
        live = aux[:, 3:4]
        sgrad = ggrad * (z * sig) * live
        sg_o[:, lanes] = sgrad
        zgrad = ggrad * scanned[:, lanes] * live * sig * (1.0 + z * (1.0 - sig))
        zlow_o[:, lanes] = zgrad.astype(bf16)
        turned = zgrad.T.astype(bf16)
        for i in range(gs // 16):
            piece = g * (gs // 16) + i
            to = pl.multiple_of(piece // pieces * span + piece % pieces * 16, 16)
            comb_o[pl.ds(to, 16), :] = turned[i * 16 : (i + 1) * 16, :]
        pre_here = pre[:, lanes]
        act = pre_here * jax.nn.sigmoid(pre_here)
        skip_o[:, lanes] = jnp.sum(sgrad * act, axis=0, keepdims=True)
        return 0

    lax.fori_loop(0, di // gs, gating, 0)
    spread_columns(small[...], rank + count, count, cw_s)

    def chunk(g, _):
        lanes = pl.ds(pl.multiple_of(g * 128, 128), 128)
        rates = [
            jnp.broadcast_to(-jnp.exp(par[8 + n : 9 + n, lanes]), (SUB, 128)) for n in range(count)
        ]

        def step(i, carry):
            grads, total = carry
            j = steps_in - 1 - i
            at = pl.ds(pl.multiple_of(j * SUB, SUB), SUB)
            sd = jnp.where(aux[at, 4:5] > 0.5, STOP, steps[at, lanes])
            sgrad = sg_o[at, lanes]
            grads = tuple(
                jnp.exp(sd * rates[n]) * (grads[n] + sgrad * cw_s[j * count + n])
                for n in range(count)
            )
            return (grads, total + sd)

        zero = jnp.zeros((SUB, 128), f32)
        grads, total = lax.fori_loop(0, steps_in, step, ((zero,) * count, zero), unroll=4)
        row = sublane_iota(128)
        last = []
        for n in range(count):
            joined = suffix_states(jnp.exp(rates[n] * total), grads[n])
            y_o[n, :, lanes] = jnp.where(row == SUB - 1, 0.0, pltpu.roll(joined, SUB - 1, 0))
            last.append(joined[0:1, :])
        to_copies(state_o, jnp.concatenate(last, axis=0).astype(bf16), lanes)
        return 0

    lax.fori_loop(0, di // 128, chunk, 0)


def scan_kernel(
    place, xd, par, aux, pre, steps, sig_step, small, x_in, tpre, entry, y_in, tsuf, arrived, sums,
    sgrad, cgrad_o, xd_o, spar_o, bw_s, cw_s, bacc_s, cacc_s, st_s, dk_s, sgr_s, asc_s, plow_s,
    rate_s, after_s, *, rank, count
):
    rows, di = pre.shape
    negative_rates(par, rate_s)
    after_s[...] = jnp.zeros_like(after_s)
    places = sums.shape[0] // count

    def after_here(i, _):
        block = pl.ds(pl.multiple_of((places - 1 - i) * count, count), count)
        carry_step(sums[block, :], arrived[block, :], rate_s, after_s)
        return 0

    lax.fori_loop(0, places - 1 - place[0], after_here, 0)
    steps_in = rows // SUB
    gs = group_of(di)
    spread_columns(small[...], rank, count, bw_s)
    spread_columns(small[...], rank + count, count, cw_s)
    bacc_s[...] = jnp.zeros_like(bacc_s)
    cacc_s[...] = jnp.zeros_like(cacc_s)
    spar_o[...] = jnp.zeros_like(spar_o)

    def scan(g, _):
        lanes = pl.ds(pl.multiple_of(g * 128, 128), 128)
        rates = [
            jnp.broadcast_to(-jnp.exp(par[8 + n : 9 + n, lanes]), (SUB, 128)) for n in range(count)
        ]
        before = tpre[:, lanes]
        behind = tsuf[:, lanes]
        first = tuple(
            x_in[n, :, lanes] + jnp.exp(rates[n] * before) * entry[n : n + 1, lanes]
            for n in range(count)
        )

        def forward(j, states):
            at = pl.ds(pl.multiple_of(j * SUB, SUB), SUB)
            step = steps[at, lanes]
            sd = jnp.where(aux[at, 4:5] > 0.5, STOP, step)
            pre_here = pre[at, lanes]
            q = step * (pre_here * jax.nn.sigmoid(pre_here))
            fresh = []
            for n in range(count):
                decay = jnp.exp(sd * rates[n])
                dk_s[j * count + n] = decay
                st_s[j * count + n] = states[n]
                fresh.append(decay * states[n] + q * bw_s[j * count + n])
            return tuple(fresh)

        last = lax.fori_loop(0, steps_in, forward, first, unroll=4)
        for n in range(count):
            st_s[steps_in * count + n] = last[n]
        zero = jnp.zeros((SUB, 128), f32)
        arriving = tuple(
            y_in[n, :, lanes] + jnp.exp(rates[n] * behind) * after_s[n : n + 1, lanes]
            for n in range(count)
        )

        def backward(i, carry):
            grads, rate_grads = carry
            j = steps_in - 1 - i
            at = pl.ds(pl.multiple_of(j * SUB, SUB), SUB)
            step = steps[at, lanes]
            pre_here = pre[at, lanes]
            act = pre_here * jax.nn.sigmoid(pre_here)
            q = step * act
            sg = sgrad[at, lanes]
            onto = zero
            along = zero
            fresh = []
            fresh_rates = []
            for n in range(count):
                k = j * count + n
                lam = grads[n] + sg * cw_s[k]
                cacc_s[k] += sg * st_s[k + count]
                bacc_s[k] += lam * q
                onto = onto + lam * bw_s[k]
                carried = lam * dk_s[k]
                logs = carried * st_s[k]
                along = along + logs * rates[n]
                fresh.append(carried)
                fresh_rates.append(rate_grads[n] + logs * step)
            sgr_s[at, lanes] = along + act * onto
            asc_s[at, lanes] = step * onto
            return (tuple(fresh), tuple(fresh_rates))

        _, rate_grads = lax.fori_loop(0, steps_in, backward, (arriving, (zero,) * count), unroll=2)
        for n in range(count):
            spar_o[8 + n : 9 + n, lanes] = jnp.sum(
                rate_grads[n] * rates[n], axis=0, keepdims=True
            )
        return 0

    lax.fori_loop(0, di // 128, scan, 0)

    lane8 = lax.broadcasted_iota(jnp.int32, (SUB, 128), 1)
    blocks = []
    for j in range(steps_in):
        block = jnp.zeros((SUB, 128), f32)
        for n in range(count):
            k = j * count + n
            block = jnp.where(
                lane8 == rank + n, jnp.sum(bacc_s[k], axis=1, keepdims=True), block
            )
            block = jnp.where(
                lane8 == rank + count + n, jnp.sum(cacc_s[k], axis=1, keepdims=True), block
            )
        blocks.append(block)
    coef_grad = jnp.concatenate(blocks, axis=0)
    lane = lax.broadcasted_iota(jnp.int32, (rows, 128), 1)
    step_low = jnp.where(
        lane >= 128 - rank, pltpu.roll(small[...], 128 - rank, 1), 0.0
    ).astype(bf16)

    def steps_back(g, total):
        lanes = pl.ds(pl.multiple_of(g * gs, gs), gs)
        pre_grad = sgr_s[:, lanes] * sig_step[:, lanes]
        spar_o[KC + 1 : KC + 2, lanes] = jnp.sum(pre_grad, axis=0, keepdims=True)
        pre_low = pre_grad.astype(bf16)
        plow_s[:, lanes] = pre_low
        return total + dot_nn(pre_low, xd[lanes, :])

    rank_grad = lax.fori_loop(0, di // gs, steps_back, jnp.zeros((rows, 128), f32))
    small_low = jnp.where(lane < rank, pltpu.roll(rank_grad, rank, 1), coef_grad).astype(bf16)

    def act_back(g, _):
        lanes = pl.ds(pl.multiple_of(g * gs, gs), gs)
        pre_here = pre[:, lanes]
        sig = jax.nn.sigmoid(pre_here)
        act_low = (pre_here * sig).astype(bf16)
        total = (
            sgrad[:, lanes] * par[KC + 2 : KC + 3, lanes]
            + asc_s[:, lanes]
            + dot_nt(small_low, xd[lanes, :])
        )
        cgrad_o[:, lanes] = total * sig * (1.0 + pre_here * (1.0 - sig))
        xd_o[lanes, :] = (dot_tn(act_low, small_low) + dot_tn(plow_s[:, lanes], step_low)).astype(bf16)
        return 0

    lax.fori_loop(0, di // gs, act_back, 0)


def last_kernel(
    core, cgrad, halo, auxn, aux, ext, par, wm, wo, zm, zo, zlow, spar, skip, xd, hid, mgrad, gain,
    gain_two, comb, pay_o, first_o, *, width, span
):
    rows, di = cgrad.shape
    half = wo.shape[1] - 128
    gs = 128

    def conv(g, carry):
        mine, other = carry
        lanes = pl.ds(pl.multiple_of(g * gs, gs), gs)
        cg = cgrad[:, lanes]
        grad = par[KC - 1 : KC, lanes] * cg
        parts = [jnp.sum(cg * ext[(KC - 1) * SUB :, lanes], axis=0, keepdims=True)]
        for ahead in range(1, KC):
            masked = cg * aux[:, ahead - 1 : ahead]
            shifted = ext[(KC - 1 - ahead) * SUB : (KC - 1 - ahead) * SUB + rows, lanes]
            parts.append(jnp.sum(masked * shifted, axis=0, keepdims=True))
            pieces = [masked[ahead * SUB :, :]]
            for i in range(ahead):
                far = halo[i : i + 1, lanes] * auxn[i : i + 1, ahead - 1 : ahead]
                pieces.append(from_after(masked[i * SUB : (i + 1) * SUB, :], far))
            grad = grad + par[KC - 1 - ahead : KC - ahead, lanes] * jnp.concatenate(pieces, axis=0)
        grad_low = grad.astype(bf16)
        pay_o[lanes, 0:128] = grad.T.astype(bf16)
        pay_o[lanes, 128:256] = xd[lanes, :]
        own = jnp.concatenate(
            parts[::-1]
            + [jnp.sum(cg, axis=0, keepdims=True), spar[KC + 1 : KC + 2, lanes], skip[:, lanes]]
            + [jnp.zeros((1, gs), f32), spar[8:, lanes], jnp.zeros((128 - spar.shape[0], gs), f32)],
            axis=0,
        )
        pay_o[lanes, 256:384] = own.T.astype(bf16)
        z = zlow[:, lanes]
        return (
            mine + dot_nn(grad_low, wm[lanes, :half]) + dot_nn(z, zm[lanes, :half]),
            other + dot_nn(grad_low, wo[lanes, :half]) + dot_nn(z, zo[lanes, :half]),
        )

    zero = jnp.zeros((rows, half), f32)
    mine, other = lax.fori_loop(0, di // gs, conv, (zero, zero))
    low = core[0] == 0
    ngrad = jnp.concatenate([jnp.where(low, mine, other), jnp.where(low, other, mine)], axis=1)
    first = hid[...].astype(f32)
    scale = lax.rsqrt(jnp.mean(first * first, axis=1, keepdims=True) + epsilon)
    gains = jnp.sum(ngrad * first * scale, axis=0, keepdims=True)
    model = first.shape[1]
    each = model // width
    row = lax.broadcasted_iota(jnp.int32, (width, model), 0)
    column = lax.broadcasted_iota(jnp.int32, (width, model), 1)
    here = column // each == row
    extra = jnp.zeros((width, 128), f32)
    router_sum = jnp.zeros((16, 128), f32)
    for place in range(di // width):
        router_sum += comb[place * span + 2 * width : (place + 1) * span, :].astype(f32)
    router_row = jnp.concatenate(
        [router_sum[k : k + 1, :] for k in range(model // 128)], axis=1
    )
    router_top = router_row.astype(bf16).astype(f32)
    rows_sent = (gains, gain_two[...], router_top, router_row - router_top)
    for k, values in enumerate(rows_sent):
        spread = jnp.where(here, values, 0.0).astype(bf16)
        at = lax.broadcasted_iota(jnp.int32, (model, 128), 0)
        to = lax.broadcasted_iota(jnp.int32, (model, 128), 1)
        placed = (at % each + spar.shape[0] + k * each == to).astype(bf16)
        extra = extra + dot_nn(spread, placed)
    extra = extra.astype(bf16)
    for place in range(di // width):
        pay_o[place * width : (place + 1) * width, 256:384] += extra
    scaled = gain[...].reshape(1, -1) * ngrad
    cube = scale * scale * scale
    grad = (
        mgrad[...] + scale * scaled - first * cube * jnp.mean(first * scaled, axis=1, keepdims=True)
    )
    order = token_order(first.shape[0])
    top = grad.astype(bf16)
    left = grad - top.astype(f32)
    mid = left.astype(bf16)
    low_part = (left - mid.astype(f32)).astype(bf16)
    first_o[...] = dot_tn(order, top) + dot_tn(order, mid) + dot_tn(order, low_part)


def grads_kernel(got, comb, nrm_all, mix_all, out_o, left_s, *, places_order, base):
    places, width, _ = got.shape
    model = nrm_all.shape[1]
    each = model // width
    rest = jnp.zeros((width, 256), f32)
    routers = [jnp.zeros((width, 128), f32) for _ in range(places * each // 128)]
    lane = lax.broadcasted_iota(jnp.int32, (width, 128), 1)
    for place in range(places):
        at = places_order[place]
        tokens = slice(at * 128, (at + 1) * 128)
        left_s[:width, tokens] = got[place, :, :128]
        left_s[width : 3 * width, tokens] = comb[place, : 2 * width, :]
        there = got[place, :, 128:].astype(f32)
        rest = rest + there
        k = place * each // 128
        inside = place * each % 128
        mine = (lane >= inside) & (lane < inside + each)
        for part in range(2):
            turn = (inside - base - part * each) % 128
            routers[k] = routers[k] + jnp.where(mine, pltpu.roll(there[:, 128:], turn, 1), 0.0)
    out_o[: 2 * width, :model] = dot_nn(left_s[: 2 * width, :], nrm_all[...]).astype(bf16)
    out_o[2 * width : 3 * width, :model] = dot_nn(left_s[2 * width :, :], mix_all[...]).astype(bf16)
    out_o[3 * width :, :256] = rest.astype(bf16)
    out_o[3 * width :, 256:] = jnp.concatenate(routers, axis=1).astype(bf16)


def final_kernel(
    ours, theirs, x_o, z_o, out_o, conv_o, bias_o, xp_o, dt_o, db_o, al_o, skip_o, router_o, one_o,
    two_o, mine_s, other_s, *, rank, count, experts
):
    width = out_o.shape[0]
    model = router_o.shape[1]
    each = model // width
    x_o[...] = ours[:width, :model].astype(f32) + theirs[:width, :model].astype(f32)
    middle = slice(width, 2 * width)
    z_o[...] = ours[middle, :model].astype(f32) + theirs[middle, :model].astype(f32)
    last = slice(2 * width, 3 * width)
    out_o[...] = ours[last, :model].astype(f32) + theirs[last, :model].astype(f32)
    rest = slice(3 * width, 4 * width)
    xd = ours[rest, :128].astype(f32) + theirs[rest, :128].astype(f32)
    xp_o[...] = xd[:, : rank + 2 * count]
    gap = jnp.zeros((128 - width, 128), f32)
    turned = jnp.concatenate([xd, gap], axis=0).T
    dt_o[...] = turned[128 - rank :, :width]
    vectors = jnp.zeros((128, 128), f32)
    for part, held in ((ours, mine_s), (theirs, other_s)):
        block = jnp.concatenate([part[rest, 128:256].astype(f32), gap], axis=0).T
        vectors = vectors + block
        for k in range(experts * each // 128):
            lanes = slice(256 + k * 128, 384 + k * 128)
            piece = jnp.concatenate([part[rest, lanes].astype(f32), gap], axis=0)
            held[k * 128 : (k + 1) * 128, :] = piece.T
        held[experts * each :, :] = jnp.zeros_like(held[experts * each :, :])
        held[experts * each : (experts + 2) * each, :] = block[8 + count : 8 + count + 2 * each, :]
    conv_o[...] = vectors[:KC, :width]
    bias_o[...] = vectors[KC : KC + 1, :width].reshape(width)
    db_o[...] = vectors[KC + 1 : KC + 2, :width].reshape(width)
    skip_o[...] = vectors[KC + 2 : KC + 3, :width].reshape(width)
    al_o[...] = vectors[8 : 8 + count, :width]
    row = lax.broadcasted_iota(jnp.int32, (128, model), 0)
    column = lax.broadcasted_iota(jnp.int32, (128, model), 1)
    total = jnp.zeros((experts + 8, model), f32)
    for at in range(each):
        to = (row * each + at == column).astype(bf16)
        picked = pl.ds(at, experts + 8, stride=each)
        total = total + dot_nn(mine_s[picked, :].astype(bf16), to)
        total = total + dot_nn(other_s[picked, :].astype(bf16), to)
    router_o[...] = total[:experts, :]
    one_o[...] = total[experts : experts + 1, :].reshape(model)
    two_o[...] = total[experts + 1 : experts + 2, :].reshape(model)


def token_order(rows):
    steps_in = rows // SUB
    row = lax.broadcasted_iota(jnp.int32, (rows, rows), 0)
    column = lax.broadcasted_iota(jnp.int32, (rows, rows), 1)
    return ((row % SUB) * steps_in + row // SUB == column).astype(bf16)


def exchange(values):
    return lax.all_to_all(values, "wide", split_axis=0, concat_axis=0, tiled=True)


def gather_pairs(values, place):
    partner = lax.ppermute(values, "wide", [(i, i ^ 4) for i in range(32)])
    first = (place // 4) % 2 == 0
    both = jnp.concatenate(
        [jnp.where(first, values, partner), jnp.where(first, partner, values)], axis=0
    )
    groups = [[(y * 2 + x) * 4 + z for y in range(4) for z in range(4)] for x in range(2)]
    return lax.all_gather(both, "wide", axis=0, tiled=True, axis_index_groups=groups)


def other_core(values):
    return lax.ppermute(values, "dp", [(0, 1), (1, 0), (2, 3), (3, 2)])


def other_side(values):
    return lax.ppermute(values, "dp", [(0, 2), (2, 0), (1, 3), (3, 1)])


def body(
    hidden, cotangent, routes, seg_lengths, gain_mix, in_x, in_z, conv_w, conv_b, x_proj, dt_proj,
    dt_bias, a_log, skip_d, out_proj, gain_moe, router, w_gate, w_up, w_down,
):
    rows, model = hidden.shape
    places = lax.axis_size("wide")
    place = lax.axis_index("wide")
    core = (lax.axis_index("dp") % 2).astype(jnp.int32).reshape(1)
    place_arr = place.astype(jnp.int32).reshape(1)
    width = in_x.shape[1]
    di = width * places
    count = a_log.shape[0]
    rank = dt_proj.shape[0]
    experts = router.shape[1]
    capacity = max(CAP * rows // (4 * places), 2)
    stride = -(-2 * capacity // 16) * 16
    half = model // 2
    steps_in = rows // SUB
    shift = SUB.bit_length() - 1
    span = 2 * width + 16

    pay_one = call(
        partial(pack_front_kernel, places=places),
        [shape((di, half + 128), bf16)],
        [],
        (core, in_x.T, x_proj, dt_proj, conv_w, conv_b, dt_bias, skip_d, a_log),
        smem=1,
    )[0]
    pay_one, in_z, out_proj, hidden, cotangent, routes, seg_lengths = lax.optimization_barrier(
        (pay_one, in_z, out_proj, hidden, cotangent, routes, seg_lengths)
    )
    wm = exchange(pay_one.reshape(places, width, half + 128)).reshape(di, half + 128)
    wo = other_core(wm)
    gate_share = call(
        pack_gate_kernel, [shape((width, model), bf16)], [], (core, in_z.T, out_proj), smem=1
    )[0]
    zm = gather_pairs(gate_share, place)
    nrm, tail, hid, cot, route, aux, auxn = call(
        prepare_kernel,
        [
            shape((rows, model), bf16),
            shape((16, model), bf16),
            shape((rows, model), bf16),
            shape((rows, model), bf16),
            shape((rows, 1), jnp.int32),
            shape((rows, 128)),
            shape((SUB, 128)),
        ],
        [],
        (place_arr * rows, seg_lengths, hidden, cotangent, routes.T, gain_mix),
        smem=2,
    )
    halo = lax.ppermute(tail, "wide", [(i, i + 1) for i in range(places - 1)])
    ext, pre, steps, sig_step, small, x_in, tpre, tsuf, states, par, xd_weight = call(
        partial(front_kernel, rank=rank, count=count),
        [
            shape((rows + (KC - 1) * SUB, di)),
            shape((rows, di)),
            shape((rows, di)),
            shape((rows, di)),
            shape((rows, 128)),
            shape((count, SUB, di)),
            shape((SUB, di)),
            shape((SUB, di)),
            shape((places * count, di + 256), bf16),
            shape((8 + count, di)),
            shape((di, 128), bf16),
        ],
        [
            pltpu.VMEM((steps_in * count, SUB, 128), f32),
            pltpu.VMEM((rows, di), f32),
            pltpu.VMEM((rows, di), f32),
            pltpu.VMEM((2, rows + 16, half), bf16),
            pltpu.VMEM((16, 128), f32),
        ],
        (core, nrm, halo, wm, wo, aux),
        smem=1,
    )

    zm, states = lax.optimization_barrier((zm, states))
    zm = zm.reshape(4, 4, 2, width, model).swapaxes(1, 2).reshape(di, model)
    zo = other_core(zm)
    states = exchange(states.reshape(places, count, di + 256)).reshape(places * count, di + 256)

    gate_z, scanned, send, middle, ntwo, chances, meta, hot, entry, sums, gated_t = call(
        partial(
            middle_kernel,
            rank=rank,
            count=count,
            experts=experts,
            stride=stride,
            capacity=capacity,
            shift=shift,
        ),
        [
            shape((rows, di)),
            shape((rows, di)),
            shape((experts * stride, model), bf16),
            shape((rows, model)),
            shape((rows, model), bf16),
            shape((rows, experts)),
            shape((rows, 8)),
            shape((2, rows, experts * stride), bf16),
            shape((count, di)),
            shape((places * count, 128)),
            shape((di, rows), bf16),
        ],
        [
            pltpu.VMEM((steps_in * count, SUB, 128), f32),
            pltpu.VMEM((steps_in * count, SUB, 128), f32),
            pltpu.VMEM((2, rows, half), bf16),
            pltpu.VMEM((count, di), f32),
        ],
        (
            core, place_arr, nrm, zm, zo, par, aux, pre, steps, small, x_in, tpre, states, hid,
            cot, route, gain_moe, router.T,
        ),
        smem=2,
    )

    arrived = exchange(send)
    arrived, nrm_late = lax.optimization_barrier((arrived, nrm))
    normed_all = gather_pairs(nrm_late, place)
    slots = places * capacity
    at = jnp.arange(2 * slots, dtype=jnp.int32)
    source = (at % slots) // capacity * stride + at % capacity + (at // slots) * capacity
    pick = (source[:, None] == jnp.arange(experts * stride, dtype=jnp.int32)[None, :]).astype(bf16)
    mine = dot_nn(pick, arrived).astype(bf16)
    side = other_side(mine)
    pair = jnp.stack([mine, side], axis=0)
    cross = other_core(pair)
    both = jnp.concatenate([pair, cross], axis=0)
    expert_in = both[:, :slots].reshape(4 * slots, model)
    grad_rows = both[:, slots:].reshape(4 * slots, model)
    gate_in = dot_nn(expert_in, w_gate[0])
    up_in = dot_nn(expert_in, w_up[0])
    hidden_act = (jax.nn.silu(gate_in) * up_in).astype(bf16)
    act_grad = dot_nt(grad_rows, w_down[0])
    sig_gate = jax.nn.sigmoid(gate_in)
    gate_grad = (act_grad * up_in * sig_gate * (1.0 + gate_in * (1.0 - sig_gate))).astype(bf16)
    up_grad = (act_grad * gate_in * sig_gate).astype(bf16)
    y_part = dot_nn(hidden_act, w_down[0]).reshape(4, slots, model)
    dx_part = (dot_nt(gate_grad, w_gate[0]) + dot_nt(up_grad, w_up[0])).reshape(4, slots, model)
    parts = jnp.concatenate([y_part, dx_part], axis=1)
    from_core = other_core(parts[2:].astype(bf16))
    summed = parts[:2] + from_core.astype(f32)
    from_side = other_side(summed[1].astype(bf16))
    total = (summed[0] + from_side.astype(f32)).astype(bf16)
    back = exchange(dot_tn(pick, total).astype(bf16))
    grad_w_down = dot_tn(hidden_act, grad_rows)[None]
    grad_w_gate = dot_tn(expert_in, gate_grad)[None]
    grad_w_up = dot_tn(expert_in, up_grad)[None]
    back, grad_w_down, grad_w_gate, grad_w_up = lax.optimization_barrier(
        (back, grad_w_down, grad_w_gate, grad_w_up)
    )

    out, mixlow, mgrad, sgrad, comb, zlow, skip_part, gain_two, y_in, adjoints = call(
        partial(back_kernel, rank=rank, count=count, experts=experts, width=width, span=span),
        [
            shape((rows, model), bf16),
            shape((rows, model), bf16),
            shape((rows, model)),
            shape((rows, di)),
            shape((places * span, 128), bf16),
            shape((rows, di), bf16),
            shape((1, di)),
            shape((1, model)),
            shape((count, SUB, di)),
            shape((places * count, di), bf16),
        ],
        [
            pltpu.VMEM((steps_in * count, SUB, 128), f32),
            pltpu.VMEM((2, rows, half), bf16),
        ],
        (
            core, back, zm, zo, par, aux, pre, steps, small, gate_z, scanned, hot, ntwo, middle,
            meta, chances, route, cot, gain_moe, router.T, gated_t,
        ),
        smem=1,
    )
    adjoints = exchange(adjoints.reshape(places, count, di)).reshape(places * count, di)
    comb, adjoints, mixlow = lax.optimization_barrier((comb, adjoints, mixlow))
    mix_all = gather_pairs(mixlow, place)
    comb_got = exchange(comb.reshape(places, span, 128))

    cgrad, xd, spar = call(
        partial(scan_kernel, rank=rank, count=count),
        [shape((rows, di)), shape((di, 128), bf16), shape((8 + count, di))],
        [pltpu.VMEM((steps_in * count, SUB, 128), f32)] * 4
        + [pltpu.VMEM(((steps_in + 1) * count, SUB, 128), f32)]
        + [pltpu.VMEM((steps_in * count, SUB, 128), f32)]
        + [pltpu.VMEM((rows, di), f32)] * 2
        + [pltpu.VMEM((rows, di), bf16)]
        + [pltpu.VMEM((count, di), f32)] * 2,
        (
            place_arr, xd_weight, par, aux, pre, steps, sig_step, small, x_in, tpre, entry, y_in,
            tsuf, adjoints, sums, sgrad,
        ),
        smem=1,
    )
    lead = jnp.concatenate(
        [cgrad[i * SUB : i * SUB + 1] for i in range(KC - 1)] + [jnp.zeros((5, di), f32)], axis=0
    )
    lead_next = lax.ppermute(lead, "wide", [(i + 1, i) for i in range(places - 1)])
    pay, first_grad = call(
        partial(last_kernel, width=width, span=span),
        [shape((di, 384), bf16), shape((rows, model))],
        [],
        (
            core, cgrad, lead_next, auxn, aux, ext, par, wm, wo, zm, zo, zlow, spar, skip_part,
            xd, hid, mgrad, gain_mix, gain_two, comb_got.reshape(places * span, 128),
        ),
        smem=1,
    )
    got_pay = exchange(pay.reshape(places, width, 384))
    per_place = model // width
    mats = call(
        partial(
            grads_kernel,
            places_order=[(p // 8 * 4 + p % 4) * 2 + p // 4 % 2 for p in range(places)],
            base=8 + count + 2 * per_place,
        ),
        [shape((4 * width, 256 + places * per_place), bf16)],
        [pltpu.VMEM((3 * width, places * rows), bf16)],
        (got_pay, comb_got, normed_all, mix_all),
    )[0]
    mats = (mats.astype(f32) + other_core(mats).astype(f32)).astype(bf16)
    grad_x, grad_z, grad_out, grad_conv, grad_bias, grad_xp, grad_dt, grad_db, grad_al, grad_sk, grad_router, gain_one, gain_two = call(
        partial(final_kernel, rank=rank, count=count, experts=experts),
        [
            shape((width, model)),
            shape((width, model)),
            shape((width, model)),
            shape((KC, width)),
            shape((width,)),
            shape((width, rank + 2 * count)),
            shape((rank, width)),
            shape((width,)),
            shape((count, width)),
            shape((width,)),
            shape((experts, model)),
            shape((model,)),
            shape((model,)),
        ],
        [pltpu.VMEM(((experts + 8) * per_place, 128), f32)] * 2,
        (mats, other_side(mats)),
    )
    return (
        out,
        first_grad,
        gain_one,
        grad_x.T,
        grad_z.T,
        grad_conv,
        grad_bias,
        grad_xp,
        grad_dt,
        grad_db,
        grad_al,
        grad_sk,
        grad_out,
        gain_two,
        grad_router.T,
        grad_w_gate,
        grad_w_up,
        grad_w_down,
    )


def solution(mesh):
    rows = P(("dp", "wide"), None)
    expert_columns = P("wide", None, "dp")
    expert_rows = P("wide", "dp", None)
    placed = (
        rows, rows, rows, P("dp", None), P(), P(None, "wide"), P(None, "wide"), P(None, "wide"),
        P("wide"), P("wide", None), P(None, "wide"), P("wide"), P(None, "wide"), P("wide"),
        P("wide", None), P(), P(), expert_columns, expert_columns, expert_rows,
    )
    given = (
        rows, rows, P(), P(None, "wide"), P(None, "wide"), P(None, "wide"), P("wide"),
        P("wide", None), P(None, "wide"), P("wide"), P(None, "wide"), P("wide"), P("wide", None),
        P(), P(), expert_columns, expert_columns, expert_rows,
    )
    return jax.shard_map(body, mesh=mesh, in_specs=placed, out_specs=given, check_vma=False)
```

```python
from functools import partial

import jax
import jax.numpy as jnp
from jax import lax
from jax.experimental import pallas as pl
from jax.experimental.pallas import tpu as pltpu
from jax.sharding import PartitionSpec as P

f32 = jnp.float32
bf16 = jnp.bfloat16
KC = 4
SUB = 8
CAP = 5
STOP = 1e6
epsilon = 1e-05
VMEM_LIMIT = 56 * 1024 * 1024


def dot_nn(left, right):
    return lax.dot_general(left, right, (((1,), (0,)), ((), ())), preferred_element_type=f32)


def dot_nt(left, right):
    return lax.dot_general(left, right, (((1,), (1,)), ((), ())), preferred_element_type=f32)


def dot_tn(left, right):
    return lax.dot_general(left, right, (((0,), (0,)), ((), ())), preferred_element_type=f32)


class Moves:
    def __init__(self):
        self.arriving = {}
        self.leaving = {}
        self.started = []

    def need(self, *refs):
        for ref in refs:
            copy = self.arriving.pop(id(ref), None)
            if copy is not None:
                copy.wait()

    def done(self, *refs):
        for ref in refs:
            copy = self.leaving.pop(id(ref), None)
            if copy is not None:
                copy.start()
                self.started.append(copy)


def call(kernel, out_shapes, scratch, args, smem=0, late=(), early=()):
    vmem = pl.BlockSpec(memory_space=pltpu.VMEM)
    hbm = pl.BlockSpec(memory_space=pl.ANY)
    specs = [pl.BlockSpec(memory_space=pltpu.SMEM)] * smem
    specs += [hbm if i in late else vmem for i in range(smem, len(args))]
    buffers = [pltpu.VMEM(args[i].shape, args[i].dtype) for i in late]
    buffers += [pltpu.VMEM(out_shapes[i].shape, out_shapes[i].dtype) for i in early]
    moving = len(buffers)
    extra = buffers + [pltpu.SemaphoreType.DMA((moving,))] if moving else []

    def staged(*refs):
        refs = list(refs)
        own = refs[len(refs) - moving - 1 : -1]
        semaphores = refs[-1]
        refs = refs[: len(refs) - moving - 1]
        moves = Moves()
        for k, i in enumerate(late):
            copy = pltpu.make_async_copy(refs[i], own[k], semaphores.at[k])
            copy.start()
            refs[i] = own[k]
            moves.arriving[id(own[k])] = copy
        for k, i in enumerate(early, len(late)):
            at = len(args) + i
            moves.leaving[id(own[k])] = pltpu.make_async_copy(own[k], refs[at], semaphores.at[k])
            refs[at] = own[k]
        kernel(moves, *refs)
        moves.need(*own)
        moves.done(*own)
        for copy in moves.started:
            copy.wait()

    return pl.pallas_call(
        staged if moving else kernel,
        out_shape=out_shapes,
        in_specs=specs,
        out_specs=[hbm if i in early else vmem for i in range(len(out_shapes))],
        scratch_shapes=list(scratch) + extra,
        compiler_params=pltpu.CompilerParams(vmem_limit_bytes=VMEM_LIMIT),
    )(*args)


def shape(dims, dtype=f32):
    return jax.ShapeDtypeStruct(dims, dtype)


def group_of(di):
    return 256 if di % 256 == 0 else 128


def sublane_iota(width):
    return lax.broadcasted_iota(jnp.int32, (SUB, width), 0)


def from_before(block, first):
    row = sublane_iota(block.shape[1])
    return jnp.where(row == 0, jnp.broadcast_to(first, block.shape), pltpu.roll(block, 1, 0))


def from_after(block, last):
    row = sublane_iota(block.shape[1])
    return jnp.where(
        row == SUB - 1, jnp.broadcast_to(last, block.shape), pltpu.roll(block, SUB - 1, 0)
    )


def spread_columns(small, first, count, out):
    steps = small.shape[0] // SUB
    for j in range(steps):
        block = small[j * SUB : (j + 1) * SUB, :]
        for n in range(count):
            out[j * count + n] = jnp.broadcast_to(block[:, first + n : first + n + 1], (SUB, 128))


def prefix_states(decay, state):
    row = sublane_iota(state.shape[1])
    for shift in (1, 2, 4):
        inside = row >= shift
        state = state + decay * jnp.where(inside, pltpu.roll(state, shift, 0), 0.0)
        decay = decay * jnp.where(inside, pltpu.roll(decay, shift, 0), 1.0)
    return state


def suffix_states(decay, state):
    row = sublane_iota(state.shape[1])
    for shift in (1, 2, 4):
        inside = row < SUB - shift
        state = state + decay * jnp.where(inside, pltpu.roll(state, SUB - shift, 0), 0.0)
        decay = decay * jnp.where(inside, pltpu.roll(decay, SUB - shift, 0), 1.0)
    return state


def prefix_sum(values):
    row = sublane_iota(values.shape[1])
    for shift in (1, 2, 4):
        values = values + jnp.where(row >= shift, pltpu.roll(values, shift, 0), 0.0)
    return values


def suffix_sum(values):
    row = sublane_iota(values.shape[1])
    for shift in (1, 2, 4):
        values = values + jnp.where(row < SUB - shift, pltpu.roll(values, SUB - shift, 0), 0.0)
    return values


def one_hot(dims, offset):
    row = lax.broadcasted_iota(jnp.int32, dims, 0)
    column = lax.broadcasted_iota(jnp.int32, dims, 1)
    return (row + offset == column).astype(bf16)


def pack_kernel(
    core, in_x, x_proj, dt_proj, conv_w, conv_b, dt_bias, skip_d, a_log, in_z, out_proj, out, gate_o,
    *, places
):
    width, model = in_x.shape
    half = model // 2
    here = core[0]
    start = pl.multiple_of(here * half, 128)
    mine = in_x[:, pl.ds(start, half)]
    gate_o[:, :half] = in_z[:, pl.ds(start, half)]
    gate_o[:, half:] = out_proj[:, pl.ds(start, half)]
    narrow = x_proj.shape[1]
    steps = dot_nn(x_proj[...], one_hot((narrow, 128), 0)) + dot_tn(
        dt_proj[...], one_hot((dt_proj.shape[0], 128), 128 - dt_proj.shape[0])
    )
    values = jnp.concatenate(
        [
            conv_w[...],
            conv_b[...].reshape(1, width),
            dt_bias[...].reshape(1, width),
            skip_d[...].reshape(1, width),
            jnp.zeros((1, width), f32),
            a_log[...],
        ],
        axis=0,
    )
    top = values.astype(bf16)
    left = values - top.astype(f32)
    mid = left.astype(bf16)
    low = (left - mid.astype(f32)).astype(bf16)
    count = values.shape[0]
    extra = dot_tn(top, one_hot((count, 128), 0))
    extra = extra + dot_tn(mid, one_hot((count, 128), count))
    extra = extra + dot_tn(low, one_hot((count, 128), 2 * count))
    rest = jnp.where(here == 0, steps, extra).astype(bf16)
    for place in range(places):
        out[place * width : (place + 1) * width, :half] = mine
        out[place * width : (place + 1) * width, half:] = rest


def prepare_kernel(
    base, lengths, hidden, cot, route, gain, nrm_o, tail_o, hid_o, cot_o, route_o, aux_o
):
    rows = hidden.shape[0]
    steps_in = rows // SUB
    row = lax.broadcasted_iota(jnp.int32, (rows, rows), 0)
    column = lax.broadcasted_iota(jnp.int32, (rows, rows), 1)
    in_order = (row % SUB) * steps_in + row // SUB == column
    order = in_order.astype(bf16)
    hid = dot_nn(order, hidden[...])
    hid_o[...] = hid.astype(bf16)
    cot_o[...] = dot_nn(order, cot[...]).astype(bf16)
    ours = jnp.where(in_order, jnp.broadcast_to(route[...], (rows, rows)), 0)
    route_o[...] = jnp.sum(ours, axis=1, keepdims=True)
    scale = lax.rsqrt(jnp.mean(hid * hid, axis=1, keepdims=True) + epsilon)
    normed = (hid * scale * gain[...].reshape(1, -1)).astype(bf16)
    nrm_o[...] = normed
    tail_row = lax.broadcasted_iota(jnp.int32, (16, rows), 0)
    tail_column = lax.broadcasted_iota(jnp.int32, (16, rows), 1)
    picked = (tail_column == rows - 1 - (KC - 2 - tail_row) * SUB) & (tail_row < KC - 1)
    tail = dot_nn(picked.astype(bf16), normed)
    tail_row = tail_row - SUB
    picked = (tail_column == rows - 1 - (KC - 2 - tail_row) * SUB) & (tail_row < KC - 1)
    picked = picked & (tail_row >= 0)
    tail_o[...] = (tail + dot_nn(picked.astype(bf16), hid.astype(bf16))).astype(bf16)

    def layout(position, lane):
        back = position - (lane + 1)
        segment = jnp.zeros_like(position)
        segment_back = jnp.zeros_like(position)
        reset = position == 0
        end = jnp.int32(0)
        for j in range(lengths.shape[1] - 1):
            end = end + lengths[0, j]
            segment = segment + (position >= end).astype(jnp.int32)
            segment_back = segment_back + (back >= end).astype(jnp.int32)
            reset = reset | (position == end)
        same = (back >= 0) & (segment == segment_back)
        live = position < end
        picked = jnp.where(lane == KC - 1, live.astype(f32), reset.astype(f32))
        return jnp.where(lane < KC - 1, same.astype(f32), picked)

    at = lax.broadcasted_iota(jnp.int32, (rows, 128), 0)
    lane = lax.broadcasted_iota(jnp.int32, (rows, 128), 1)
    aux_o[...] = layout(base[0] + (at % SUB) * steps_in + at // SUB, lane)


def front_kernel(
    moves, core, nrm_in, halo_in, wm, wo, aux, ext_o, pre_o, steps_o, sig_o, small_o, x_o, tpre_o, tsuf_o,
    state_o, par_o, xd_o, sd_s, q_s, bw_s, nrm_s, sum_s, *, rank, count
):
    rows, di = pre_o.shape
    half = wo.shape[1] - 128
    steps_in = rows // SUB
    gs = group_of(di)
    low = core[0] == 0
    nrm_s[0, :rows] = jnp.where(low, nrm_in[:, :half], nrm_in[:, half:])
    nrm_s[1, :rows] = jnp.where(low, nrm_in[:, half:], nrm_in[:, :half])
    nrm_s[0, rows:] = jnp.where(low, halo_in[:, :half], halo_in[:, half:])
    nrm_s[1, rows:] = jnp.where(low, halo_in[:, half:], halo_in[:, :half])
    small_o[...] = jnp.zeros_like(small_o)
    moves.need(wm, wo)
    par = par_o
    total_rows = par_o.shape[0]

    def unpack(g, _):
        lanes = pl.ds(pl.multiple_of(g * 128, 128), 128)
        mine = wm[lanes, half:]
        other = wo[lanes, half:]
        xd_o[lanes, :] = jnp.where(low, mine, other)
        turned = jnp.where(low, other, mine).astype(f32).T
        par_o[:, lanes] = (
            turned[:total_rows, :]
            + turned[total_rows : 2 * total_rows, :]
            + turned[2 * total_rows : 3 * total_rows, :]
        )
        return 0

    lax.fori_loop(0, di // 128, unpack, 0)

    def project(g, _):
        lanes = pl.ds(pl.multiple_of(g * gs, gs), gs)
        inner = dot_nt(nrm_s[0], wm[lanes, :half]) + dot_nt(nrm_s[1], wo[lanes, :half])
        for back in range(1, KC):
            block = inner[rows - back * SUB : rows - (back - 1) * SUB, :]
            halo = inner[rows + KC - 1 - back : rows + KC - back, :]
            ext_o[(KC - 1 - back) * SUB : (KC - back) * SUB, lanes] = from_before(block, halo)
        ext_o[(KC - 1) * SUB :, lanes] = inner[:rows, :]
        total = par[KC : KC + 1, lanes] + par[KC - 1 : KC, lanes] * inner[:rows, :]
        for back in range(1, KC):
            shifted = ext_o[(KC - 1 - back) * SUB : (KC - 1 - back) * SUB + rows, lanes]
            total = total + par[KC - 1 - back : KC - back, lanes] * shifted * aux[:, back - 1 : back]
        pre_o[:, lanes] = total
        act = total * jax.nn.sigmoid(total)
        q_s[:, lanes] = act
        small_o[...] += dot_nn(act.astype(bf16), xd_o[lanes, :])
        return 0

    lax.fori_loop(0, di // gs, project, 0)
    moves.done(ext_o, pre_o, par_o, xd_o)
    small = small_o[...]
    lane = lax.broadcasted_iota(jnp.int32, small.shape, 1)
    step_low = jnp.where(lane >= 128 - rank, pltpu.roll(small, 128 - rank, 1), 0.0).astype(bf16)
    spread_columns(small, rank, count, bw_s)

    def stepping(g, _):
        lanes = pl.ds(pl.multiple_of(g * gs, gs), gs)
        step_pre = dot_nt(step_low, xd_o[lanes, :]) + par[KC + 1 : KC + 2, lanes]
        small_exp = jnp.exp(-jnp.abs(step_pre))
        steps = jnp.maximum(step_pre, 0.0) + jnp.log1p(small_exp)
        steps_o[:, lanes] = steps
        sig_o[:, lanes] = jax.nn.sigmoid(step_pre)
        q_s[:, lanes] = q_s[:, lanes] * steps
        sd_s[:, lanes] = jnp.where(aux[:, 4:5] > 0.5, STOP, steps)
        return 0

    lax.fori_loop(0, di // gs, stepping, 0)
    moves.done(steps_o, sig_o, sd_s, q_s)

    def chunk(g, _):
        lanes = pl.ds(pl.multiple_of(g * 128, 128), 128)
        rates = [
            jnp.broadcast_to(-jnp.exp(par[8 + n : 9 + n, lanes]), (SUB, 128)) for n in range(count)
        ]

        def step(j, carry):
            states, total = carry
            at = pl.ds(pl.multiple_of(j * SUB, SUB), SUB)
            sd = sd_s[at, lanes]
            q = q_s[at, lanes]
            states = tuple(
                jnp.exp(sd * rates[n]) * states[n] + q * bw_s[j * count + n] for n in range(count)
            )
            return (states, total + sd)

        zero = jnp.zeros((SUB, 128), f32)
        states, total = lax.fori_loop(0, steps_in, step, ((zero,) * count, zero), unroll=4)
        row = sublane_iota(128)
        ahead = prefix_sum(total)
        behind = suffix_sum(total)
        tpre_o[:, lanes] = jnp.where(row == 0, 0.0, pltpu.roll(ahead, 1, 0))
        tsuf_o[:, lanes] = jnp.where(row == SUB - 1, 0.0, pltpu.roll(behind, SUB - 1, 0))
        last = []
        for n in range(count):
            joined = prefix_states(jnp.exp(rates[n] * total), states[n])
            x_o[n, :, lanes] = jnp.where(row == 0, 0.0, pltpu.roll(joined, 1, 0))
            last.append(joined[SUB - 1 : SUB, :])
        sum_s[pl.ds(g, 1), :] = ahead[SUB - 1 : SUB, :]
        to_copies(state_o, jnp.concatenate(last, axis=0).astype(bf16), lanes)
        return 0

    sum_s[...] = jnp.zeros_like(sum_s)
    lax.fori_loop(0, di // 128, chunk, 0)
    sums = sum_s[...]
    top = sums.astype(bf16)
    left = (sums - top.astype(f32)).astype(bf16)
    to_copies(state_o, top, slice(di, di + 128))
    to_copies(state_o, left, slice(di + 128, di + 256))


def to_copies(out, values, lanes):
    count = values.shape[0]
    for place in range(out.shape[0] // count):
        out[place * count : (place + 1) * count, lanes] = values


def negative_rates(par, out):
    out[...] = -jnp.exp(par[8:, :])


def carry_step(decay_sums, arrived, rate_s, state_s):
    for g in range(state_s.shape[1] // 128):
        lanes = slice(g * 128, (g + 1) * 128)
        decay = jnp.exp(rate_s[:, lanes] * decay_sums[g : g + 1, :])
        state_s[:, lanes] = decay * state_s[:, lanes] + arrived[:, lanes].astype(f32)


def gate_kernel(core, nrm, zm, zo, gate_z_o, nrm_s):
    rows, di = gate_z_o.shape
    half = zm.shape[1]
    gs = group_of(di)
    low = core[0] == 0
    nrm_s[0] = jnp.where(low, nrm[:, :half], nrm[:, half:])
    nrm_s[1] = jnp.where(low, nrm[:, half:], nrm[:, :half])

    def project(g, _):
        lanes = pl.ds(pl.multiple_of(g * gs, gs), gs)
        gate_z_o[:, lanes] = dot_nt(nrm_s[0], zm[lanes, :]) + dot_nt(nrm_s[1], zo[lanes, :])
        return 0

    lax.fori_loop(0, di // gs, project, 0)


def middle_kernel(
    moves, core, place, om, oo, par, aux, pre, sd, q, x_in, small, arrived, tpre, hid, cot, route,
    gain, router, gate_z, scan_o, send_o, middle_o, ntwo_o, chance_o, meta_o, hot_o,
    entry_o, sums_o, bw_s, cw_s, rate_s, *, rank, count, experts, stride, capacity, shift
):
    rows, di = pre.shape
    half = om.shape[1]
    steps_in = rows // SUB
    gs = group_of(di)
    low = core[0] == 0
    spread_columns(small[...], rank, count, bw_s)
    spread_columns(small[...], rank + count, count, cw_s)
    negative_rates(par, rate_s)
    moves.need(arrived)
    for there in range(sums_o.shape[0] // count):
        block = slice(there * count, (there + 1) * count)
        sums_o[block, :] = arrived[block, di : di + 128].astype(f32) + arrived[
            block, di + 128 : di + 256
        ].astype(f32)
    entry_o[...] = jnp.zeros_like(entry_o)

    def before_here(there, _):
        block = pl.ds(pl.multiple_of(there * count, count), count)
        carry_step(sums_o[block, :], arrived[block, :di], rate_s, entry_o)
        return 0

    lax.fori_loop(0, place[0], before_here, 0)
    moves.done(sums_o, entry_o)
    moves.need(x_in, sd, q)

    def scan(g, _):
        lanes = pl.ds(pl.multiple_of(g * 128, 128), 128)
        rates = [jnp.broadcast_to(rate_s[n : n + 1, lanes], (SUB, 128)) for n in range(count)]
        before = tpre[:, lanes]
        first = tuple(
            x_in[n, :, lanes] + jnp.exp(rates[n] * before) * entry_o[n : n + 1, lanes]
            for n in range(count)
        )
        def step(j, states):
            at = pl.ds(pl.multiple_of(j * SUB, SUB), SUB)
            sd_here = sd[at, lanes]
            q_here = q[at, lanes]
            total = jnp.zeros((SUB, 128), f32)
            fresh = []
            for n in range(count):
                state = jnp.exp(sd_here * rates[n]) * states[n] + q_here * bw_s[j * count + n]
                total = total + state * cw_s[j * count + n]
                fresh.append(state)
            scan_o[at, lanes] = total
            return tuple(fresh)

        lax.fori_loop(0, steps_in, step, first, unroll=4)
        return 0

    lax.fori_loop(0, di // 128, scan, 0)

    def gating(g, carry):
        mine, other = carry
        lanes = pl.ds(pl.multiple_of(g * gs, gs), gs)
        z = gate_z[:, lanes]
        pre_here = pre[:, lanes]
        scanned = scan_o[:, lanes] + par[KC + 2 : KC + 3, lanes] * (
            pre_here * jax.nn.sigmoid(pre_here)
        )
        scan_o[:, lanes] = scanned
        gated = (scanned * (z * jax.nn.sigmoid(z)) * aux[:, 3:4]).astype(bf16)
        return (mine + dot_nn(gated, om[lanes, :]), other + dot_nn(gated, oo[lanes, :]))

    zero = jnp.zeros((rows, half), f32)
    moves.need(pre, gate_z, om, oo)
    mine, other = lax.fori_loop(0, di // gs, gating, (zero, zero))
    moves.done(scan_o)
    mixed = jnp.concatenate([jnp.where(low, mine, other), jnp.where(low, other, mine)], axis=1)
    middle = hid[...].astype(f32) + mixed
    middle_o[...] = middle
    scale = lax.rsqrt(jnp.mean(middle * middle, axis=1, keepdims=True) + epsilon)
    ntwo = (middle * scale * gain[...].reshape(1, -1)).astype(bf16)
    ntwo_o[...] = ntwo
    logits = dot_nt(ntwo, router[...])
    top = jnp.max(logits, axis=1, keepdims=True)
    raised = jnp.exp(logits - top)
    chances = raised / jnp.sum(raised, axis=1, keepdims=True)
    chance_o[...] = chances
    lane = lax.broadcasted_iota(jnp.int32, (rows, experts), 1)
    chosen = route[...] == lane
    chosen_f = chosen.astype(f32)
    gate = jnp.sum(chances * chosen_f, axis=1, keepdims=True)
    taken = chosen_f * aux[:, 3:4]
    here = lax.broadcasted_iota(jnp.int32, (rows, rows), 0)
    there = lax.broadcasted_iota(jnp.int32, (rows, rows), 1)
    own_id = (here & (SUB - 1)) * steps_in + (here >> shift)
    other_id = (there & (SUB - 1)) * steps_in + (there >> shift)
    earlier = (other_id < own_id).astype(bf16)
    ranks = jnp.sum(dot_nn(earlier, taken.astype(bf16)) * chosen_f, axis=1, keepdims=True)
    kept = aux[:, 3:4] * (ranks < capacity).astype(f32)
    slot = route[...] * stride + ranks.astype(jnp.int32)
    place = lax.broadcasted_iota(jnp.int32, (rows, experts * stride), 1)
    kept_on = kept > 0.5
    hot_x = ((slot == place) & kept_on).astype(bf16)
    hot_g = ((slot + capacity == place) & kept_on).astype(bf16)
    hot_o[0] = hot_x
    hot_o[1] = hot_g
    weight = gate * kept
    up = (cot[...].astype(f32) * weight).astype(bf16)
    send_o[...] = (dot_tn(hot_x, ntwo) + dot_tn(hot_g, up)).astype(bf16)
    lane8 = lax.broadcasted_iota(jnp.int32, (rows, 8), 1)
    meta_o[...] = jnp.where(
        lane8 == 0, gate, jnp.where(lane8 == 1, kept, jnp.where(lane8 == 2, scale, 0.0))
    )


def back_kernel(
    moves, core, back, om, oo, par, aux, sd, small, gate_z, hot, middle, meta, chances, route, cot, gain,
    router, combined_o, logit_o, mixlow_o, mgrad_o, ggrad_o, sg_o, gain_o, y_o, state_o, cw_s, mix_s,
    rate_s, *, rank, count, experts
):
    rows, di = sd.shape
    half = om.shape[1]
    steps_in = rows // SUB
    gs = group_of(di)
    negative_rates(par, rate_s)
    rows_back = back[...]
    combined = dot_nn(hot[0], rows_back)
    dispatch = dot_nn(hot[1], rows_back)
    combined_o[...] = combined
    gate = meta[:, 0:1]
    kept = meta[:, 1:2]
    scale = meta[:, 2:3]
    mid = middle[...]
    up = cot[...].astype(f32)
    gate_total = kept * jnp.sum(up * combined, axis=1, keepdims=True)
    lane = lax.broadcasted_iota(jnp.int32, (rows, experts), 1)
    chosen_f = (route[...] == lane).astype(f32)
    logit_grad = (gate * (chosen_f - chances[...]) * gate_total).astype(bf16)
    logit_o[...] = logit_grad
    ngrad = dot_nn(logit_grad, router[...]) + dispatch
    gain_o[...] = jnp.sum(ngrad * mid * scale, axis=0, keepdims=True)
    scaled = gain[...].reshape(1, -1) * ngrad
    cube = scale * scale * scale
    mgrad = up + scale * scaled - mid * cube * jnp.mean(mid * scaled, axis=1, keepdims=True)
    mgrad_o[...] = mgrad
    low = core[0] == 0
    mixlow = mgrad.astype(bf16)
    mixlow_o[...] = mixlow
    mix_s[0] = jnp.where(low, mixlow[:, :half], mixlow[:, half:])
    mix_s[1] = jnp.where(low, mixlow[:, half:], mixlow[:, :half])
    moves.done(mixlow_o, mgrad_o, combined_o)
    moves.need(om, oo, gate_z)

    def gating(g, _):
        lanes = pl.ds(pl.multiple_of(g * gs, gs), gs)
        ggrad = dot_nt(mix_s[0], om[lanes, :]) + dot_nt(mix_s[1], oo[lanes, :])
        ggrad = ggrad * aux[:, 3:4]
        ggrad_o[:, lanes] = ggrad
        z = gate_z[:, lanes]
        sg_o[:, lanes] = ggrad * (z * jax.nn.sigmoid(z))
        return 0

    lax.fori_loop(0, di // gs, gating, 0)
    moves.done(ggrad_o, sg_o)
    spread_columns(small[...], rank + count, count, cw_s)
    moves.need(sd)

    def chunk(g, _):
        lanes = pl.ds(pl.multiple_of(g * 128, 128), 128)
        rates = [jnp.broadcast_to(rate_s[n : n + 1, lanes], (SUB, 128)) for n in range(count)]

        def step(i, carry):
            grads, total = carry
            j = steps_in - 1 - i
            at = pl.ds(pl.multiple_of(j * SUB, SUB), SUB)
            sd_here = sd[at, lanes]
            sgrad = sg_o[at, lanes]
            grads = tuple(
                jnp.exp(sd_here * rates[n]) * (grads[n] + sgrad * cw_s[j * count + n])
                for n in range(count)
            )
            return (grads, total + sd_here)

        zero = jnp.zeros((SUB, 128), f32)
        grads, total = lax.fori_loop(0, steps_in, step, ((zero,) * count, zero), unroll=4)
        row = sublane_iota(128)
        last = []
        for n in range(count):
            joined = suffix_states(jnp.exp(rates[n] * total), grads[n])
            y_o[n, :, lanes] = jnp.where(row == SUB - 1, 0.0, pltpu.roll(joined, SUB - 1, 0))
            last.append(joined[0:1, :])
        to_copies(state_o, jnp.concatenate(last, axis=0).astype(bf16), lanes)
        return 0

    lax.fori_loop(0, di // 128, chunk, 0)


def aside_kernel(
    core, side, zm, zo, aux, pre, gate_z, scanned, ggrad, combined, logit_grad, ntwo, middle, meta,
    out_o, comb_o, skip_o, ngrad_o, *, experts, width, span
):
    rows, di = pre.shape
    half = zm.shape[1]
    gs = group_of(di)
    pieces = width // 16
    result = (middle[...] + meta[:, 0:1] * meta[:, 1:2] * combined[...]).astype(bf16)
    out_o[...] = dot_tn(token_order(rows), result).astype(bf16)
    router_rows = dot_tn(logit_grad[...], ntwo[...])
    model = router_rows.shape[1]
    for expert in range(experts):
        row = router_rows[expert : expert + 1, :]
        rows_here = [row[:, k * 128 : (k + 1) * 128] for k in range(model // 128)]
        rows_here.append(jnp.zeros((16 - model // 128, 128), f32))
        comb_o[expert * span + 3 * width : (expert + 1) * span, :] = jnp.concatenate(
            rows_here, axis=0
        ).astype(bf16)

    def gating(g, carry):
        mine, other = carry
        lanes = pl.ds(pl.multiple_of(g * gs, gs), gs)
        grad = ggrad[:, lanes]
        z = gate_z[:, lanes]
        sig = jax.nn.sigmoid(z)
        here = scanned[:, lanes]
        zgrad = grad * here * sig * (1.0 + z * (1.0 - sig))
        z_low = zgrad.astype(bf16)
        z_turned = zgrad.T.astype(bf16)
        gated_turned = (here * (z * sig) * aux[:, 3:4]).T.astype(bf16)
        for i in range(gs // 16):
            piece = g * (gs // 16) + i
            to = pl.multiple_of(piece // pieces * span + piece % pieces * 16, 16)
            comb_o[pl.ds(to, 16), :] = z_turned[i * 16 : (i + 1) * 16, :]
            owner = piece // pieces
            holder = owner // 8 * 8 + side[0] * 4 + owner % 4
            to = holder * span + (1 + owner // 4 % 2) * width + piece % pieces * 16
            comb_o[pl.ds(pl.multiple_of(to, 16), 16), :] = gated_turned[i * 16 : (i + 1) * 16, :]
        pre_here = pre[:, lanes]
        act = pre_here * jax.nn.sigmoid(pre_here)
        skip_o[:, lanes] = jnp.sum(grad * (z * sig) * act, axis=0, keepdims=True)
        return (mine + dot_nn(z_low, zm[lanes, :]), other + dot_nn(z_low, zo[lanes, :]))

    zero = jnp.zeros((rows, half), f32)
    mine, other = lax.fori_loop(0, di // gs, gating, (zero, zero))
    ngrad_o[0] = mine
    ngrad_o[1] = other


def scan_kernel(
    moves, place, xd, par, sd, q, pre, steps, sig_step, small, x_in, tpre, entry, y_in, tsuf, arrived, sums,
    sgrad, cgrad_o, xd_o, spar_o, bw_s, cw_s, bacc_s, cacc_s, st_s, dk_s, sgr_s, asc_s, plow_s,
    rate_s, after_s, *, rank, count
):
    rows, di = pre.shape
    negative_rates(par, rate_s)
    after_s[...] = jnp.zeros_like(after_s)
    places = sums.shape[0] // count
    spread_columns(small[...], rank, count, bw_s)
    spread_columns(small[...], rank + count, count, cw_s)
    bacc_s[...] = jnp.zeros_like(bacc_s)
    cacc_s[...] = jnp.zeros_like(cacc_s)
    spar_o[...] = jnp.zeros_like(spar_o)
    moves.need(arrived, sums)

    def after_here(i, _):
        block = pl.ds(pl.multiple_of((places - 1 - i) * count, count), count)
        carry_step(sums[block, :], arrived[block, :], rate_s, after_s)
        return 0

    lax.fori_loop(0, places - 1 - place[0], after_here, 0)
    steps_in = rows // SUB
    gs = group_of(di)
    moves.need(x_in, sd, q, sgrad, y_in)

    def scan(g, _):
        lanes = pl.ds(pl.multiple_of(g * 128, 128), 128)
        rates = [
            jnp.broadcast_to(-jnp.exp(par[8 + n : 9 + n, lanes]), (SUB, 128)) for n in range(count)
        ]
        before = tpre[:, lanes]
        behind = tsuf[:, lanes]
        first = tuple(
            x_in[n, :, lanes] + jnp.exp(rates[n] * before) * entry[n : n + 1, lanes]
            for n in range(count)
        )

        def forward(j, states):
            at = pl.ds(pl.multiple_of(j * SUB, SUB), SUB)
            sd_here = sd[at, lanes]
            q_here = q[at, lanes]
            fresh = []
            for n in range(count):
                decay = jnp.exp(sd_here * rates[n])
                dk_s[j * count + n] = decay
                st_s[j * count + n] = states[n]
                fresh.append(decay * states[n] + q_here * bw_s[j * count + n])
            return tuple(fresh)

        last = lax.fori_loop(0, steps_in, forward, first, unroll=4)
        for n in range(count):
            st_s[steps_in * count + n] = last[n]
        zero = jnp.zeros((SUB, 128), f32)
        arriving = tuple(
            y_in[n, :, lanes] + jnp.exp(rates[n] * behind) * after_s[n : n + 1, lanes]
            for n in range(count)
        )

        def backward(i, carry):
            grads, rate_grads = carry
            j = steps_in - 1 - i
            at = pl.ds(pl.multiple_of(j * SUB, SUB), SUB)
            sd_here = sd[at, lanes]
            q_here = q[at, lanes]
            sg = sgrad[at, lanes]
            onto = zero
            along = zero
            fresh = []
            fresh_rates = []
            for n in range(count):
                k = j * count + n
                lam = grads[n] + sg * cw_s[k]
                cacc_s[k] += sg * st_s[k + count]
                bacc_s[k] += lam * q_here
                onto = onto + lam * bw_s[k]
                carried = lam * dk_s[k]
                logs = carried * st_s[k]
                along = along + logs * rates[n]
                fresh.append(carried)
                fresh_rates.append(rate_grads[n] + logs * sd_here)
            sgr_s[at, lanes] = along
            asc_s[at, lanes] = onto
            return (tuple(fresh), tuple(fresh_rates))

        _, rate_grads = lax.fori_loop(0, steps_in, backward, (arriving, (zero,) * count), unroll=2)
        for n in range(count):
            spar_o[8 + n : 9 + n, lanes] = jnp.sum(
                rate_grads[n] * rates[n], axis=0, keepdims=True
            )
        return 0

    lax.fori_loop(0, di // 128, scan, 0)

    moves.need(pre, sig_step, xd, steps)
    lane8 = lax.broadcasted_iota(jnp.int32, (SUB, 128), 1)
    blocks = []
    for j in range(steps_in):
        block = jnp.zeros((SUB, 128), f32)
        for n in range(count):
            k = j * count + n
            block = jnp.where(
                lane8 == rank + n, jnp.sum(bacc_s[k], axis=1, keepdims=True), block
            )
            block = jnp.where(
                lane8 == rank + count + n, jnp.sum(cacc_s[k], axis=1, keepdims=True), block
            )
        blocks.append(block)
    coef_grad = jnp.concatenate(blocks, axis=0)
    lane = lax.broadcasted_iota(jnp.int32, (rows, 128), 1)
    step_low = jnp.where(
        lane >= 128 - rank, pltpu.roll(small[...], 128 - rank, 1), 0.0
    ).astype(bf16)

    def steps_back(g, total):
        lanes = pl.ds(pl.multiple_of(g * gs, gs), gs)
        pre_here = pre[:, lanes]
        act = pre_here * jax.nn.sigmoid(pre_here)
        pre_grad = (sgr_s[:, lanes] + act * asc_s[:, lanes]) * sig_step[:, lanes]
        spar_o[KC + 1 : KC + 2, lanes] = jnp.sum(pre_grad, axis=0, keepdims=True)
        pre_low = pre_grad.astype(bf16)
        plow_s[:, lanes] = pre_low
        return total + dot_nn(pre_low, xd[lanes, :])

    rank_grad = lax.fori_loop(0, di // gs, steps_back, jnp.zeros((rows, 128), f32))
    small_low = jnp.where(lane < rank, pltpu.roll(rank_grad, rank, 1), coef_grad).astype(bf16)

    def act_back(g, _):
        lanes = pl.ds(pl.multiple_of(g * gs, gs), gs)
        pre_here = pre[:, lanes]
        sig = jax.nn.sigmoid(pre_here)
        act_low = (pre_here * sig).astype(bf16)
        total = (
            sgrad[:, lanes] * par[KC + 2 : KC + 3, lanes]
            + steps[:, lanes] * asc_s[:, lanes]
            + dot_nt(small_low, xd[lanes, :])
        )
        cgrad_o[:, lanes] = total * sig * (1.0 + pre_here * (1.0 - sig))
        xd_o[lanes, :] = (dot_tn(act_low, small_low) + dot_tn(plow_s[:, lanes], step_low)).astype(bf16)
        return 0

    lax.fori_loop(0, di // gs, act_back, 0)


def last_kernel(
    moves, core, cgrad, halo, aux, ext, par, wm, wo, ngrad_z, spar, skip, xd, hid, gain_two, comb,
    pay_o, ngrad_o, extra_o, low_s, far_s, *, width, span
):
    rows, di = cgrad.shape
    half = wo.shape[1] - 128
    gs = 128
    ahead_lane = spar.shape[0] + 4 * (hid.shape[1] // width)
    moves.need(xd)

    def conv(g, _):
        lanes = pl.ds(pl.multiple_of(g * gs, gs), gs)
        cg = cgrad[:, lanes]
        grad = par[KC - 1 : KC, lanes] * cg
        parts = [jnp.sum(cg * ext[(KC - 1) * SUB :, lanes], axis=0, keepdims=True)]
        zero = jnp.zeros((1, gs), f32)
        behind = [zero] * (KC - 1)
        for ahead in range(1, KC):
            tap = par[KC - 1 - ahead : KC - ahead, lanes]
            masked = cg * aux[:, ahead - 1 : ahead]
            shifted = ext[(KC - 1 - ahead) * SUB : (KC - 1 - ahead) * SUB + rows, lanes]
            parts.append(jnp.sum(masked * shifted, axis=0, keepdims=True))
            pieces = [masked[ahead * SUB :, :]]
            for i in range(ahead):
                pieces.append(from_after(masked[i * SUB : (i + 1) * SUB, :], zero))
                k = KC - 1 - ahead + i
                behind[k] = behind[k] + tap * masked[i * SUB : i * SUB + 1, :]
            grad = grad + tap * jnp.concatenate(pieces, axis=0)
        low_s[:, lanes] = grad.astype(bf16)
        pay_o[lanes, 0:128] = grad.T.astype(bf16)
        pay_o[lanes, 128:256] = xd[lanes, :]
        extra = jnp.concatenate(behind + [jnp.zeros((SUB - KC + 1, gs), f32)], axis=0)
        far_s[:SUB, lanes] = extra.astype(bf16)
        own = jnp.concatenate(
            parts[::-1]
            + [jnp.sum(cg, axis=0, keepdims=True), spar[KC + 1 : KC + 2, lanes], skip[:, lanes]]
            + [zero, spar[8:, lanes], jnp.zeros((ahead_lane - spar.shape[0], gs), f32), extra]
            + [jnp.zeros((128 - ahead_lane - SUB, gs), f32)],
            axis=0,
        )
        pay_o[lanes, 256:384] = own.T.astype(bf16)
        return 0

    lax.fori_loop(0, di // gs, conv, 0)
    far_s[SUB:, :] = jnp.zeros_like(far_s[SUB:, :])
    moves.need(wm, wo, ngrad_z, comb, hid)
    low = core[0] == 0

    def onto_inputs(values):
        mine = dot_nn(values, wm[:, :half])
        other = dot_nn(values, wo[:, :half])
        return mine, other

    def joined(mine, other):
        return jnp.concatenate([jnp.where(low, mine, other), jnp.where(low, other, mine)], axis=1)

    mine, other = onto_inputs(low_s[...])
    ngrad = joined(mine + ngrad_z[0], other + ngrad_z[1])
    ngrad_o[...] = ngrad
    far = joined(*onto_inputs(far_s[...]))[:SUB, :]
    extra_o[...] = far
    first = hid[...].astype(f32)
    scale = lax.rsqrt(jnp.mean(first * first, axis=1, keepdims=True) + epsilon)
    gains = jnp.sum(ngrad * first * scale, axis=0, keepdims=True)
    first = halo[SUB:, :].astype(f32)
    scale = lax.rsqrt(jnp.mean(first * first, axis=1, keepdims=True) + epsilon)
    gains = gains + jnp.sum(far * first * scale, axis=0, keepdims=True)
    model = first.shape[1]
    each = model // width
    row = lax.broadcasted_iota(jnp.int32, (width, model), 0)
    column = lax.broadcasted_iota(jnp.int32, (width, model), 1)
    here = column // each == row
    extra = jnp.zeros((width, 128), f32)
    router_sum = jnp.zeros((16, 128), f32)
    for place in range(di // width):
        router_sum += comb[place * span + 3 * width : (place + 1) * span, :].astype(f32)
    router_row = jnp.concatenate([router_sum[k : k + 1, :] for k in range(model // 128)], axis=1)
    router_top = router_row.astype(bf16).astype(f32)
    rows_sent = (gains, gain_two[...], router_top, router_row - router_top)
    for k, values in enumerate(rows_sent):
        spread = jnp.where(here, values, 0.0).astype(bf16)
        at = lax.broadcasted_iota(jnp.int32, (model, 128), 0)
        to = lax.broadcasted_iota(jnp.int32, (model, 128), 1)
        placed = (at % each + spar.shape[0] + k * each == to).astype(bf16)
        extra = extra + dot_nn(spread, placed)
    extra = extra.astype(bf16)
    for place in range(di // width):
        pay_o[place * width : (place + 1) * width, 256:384] += extra


def hidden_kernel(ngrad_in, beyond, hid, mgrad, gain, first_o):
    first = hid[...].astype(f32)
    rows = first.shape[0]
    ngrad = ngrad_in[...]
    row = lax.broadcasted_iota(jnp.int32, first.shape, 0)
    for i in range(KC - 1):
        at = rows - 1 - (KC - 2 - i) * SUB
        ngrad = ngrad + jnp.where(row == at, beyond[i : i + 1, :], 0.0)
    scale = lax.rsqrt(jnp.mean(first * first, axis=1, keepdims=True) + epsilon)
    scaled = gain[...].reshape(1, -1) * ngrad
    cube = scale * scale * scale
    grad = (
        mgrad[...] + scale * scaled - first * cube * jnp.mean(first * scaled, axis=1, keepdims=True)
    )
    order = token_order(rows)
    top = grad.astype(bf16)
    left = grad - top.astype(f32)
    mid = left.astype(bf16)
    low_part = (left - mid.astype(f32)).astype(bf16)
    first_o[...] = dot_tn(order, top) + dot_tn(order, mid) + dot_tn(order, low_part)


def ready_kernel(
    moves, side, comb, nrm_all, mix_half, z_o, mine_o, theirs_o, z_s, gated_s, *, places_order
):
    places = comb.shape[0]
    width = z_o.shape[0]
    for place in range(places):
        at = places_order[place]
        z_s[:, at * 128 : (at + 1) * 128] = comb[place, :width, :]
    for k in range(places // 2):
        place = k // 4 * 8 + side[0] * 4 + k % 4
        gated_s[:, k * 128 : (k + 1) * 128] = comb[place, width : 3 * width, :]
    moves.need(mix_half)
    grads = dot_nn(gated_s[...], mix_half[...]).astype(bf16)
    first = side[0] == 0
    mine_o[...] = jnp.where(first, grads[:width, :], grads[width:, :])
    theirs_o[...] = jnp.where(first, grads[width:, :], grads[:width, :])
    moves.need(nrm_all)
    z_o[...] = dot_nn(z_s[...], nrm_all[...]).astype(bf16)


def grads_kernel(moves, got, nrm_all, out_o, left_s, *, places_order, base):
    places, width, _ = got.shape
    model = nrm_all.shape[1]
    each = model // width
    rest = jnp.zeros((width, 256), f32)
    routers = [jnp.zeros((width, 128), f32) for _ in range(places * each // 128)]
    lane = lax.broadcasted_iota(jnp.int32, (width, 128), 1)
    row = lax.broadcasted_iota(jnp.int32, (128, 128), 0)
    column = lax.broadcasted_iota(jnp.int32, (128, 128), 1)
    after = row - (base + 2 * each)
    late = column == 127 - (KC - 2 - after) * SUB
    placed = (late & (after >= 0) & (after < KC - 1)).astype(bf16)
    for place in range(places):
        at = places_order[place]
        inner = got[place, :, :128]
        if place + 1 < places:
            beyond = dot_nn(got[place + 1, :, 256:384], placed)
            inner = (inner.astype(f32) + beyond).astype(bf16)
        left_s[:, at * 128 : (at + 1) * 128] = inner
        there = got[place, :, 128:].astype(f32)
        rest = rest + there
        k = place * each // 128
        inside = place * each % 128
        mine = (lane >= inside) & (lane < inside + each)
        for part in range(2):
            turn = (inside - base - part * each) % 128
            routers[k] = routers[k] + jnp.where(mine, pltpu.roll(there[:, 128:], turn, 1), 0.0)
    out_o[width:, :256] = rest.astype(bf16)
    out_o[width:, 256:] = jnp.concatenate(routers, axis=1).astype(bf16)
    moves.need(nrm_all)
    out_o[:width, :model] = dot_nn(left_s[...], nrm_all[...]).astype(bf16)


def token_order(rows):
    steps_in = rows // SUB
    row = lax.broadcasted_iota(jnp.int32, (rows, rows), 0)
    column = lax.broadcasted_iota(jnp.int32, (rows, rows), 1)
    return ((row % SUB) * steps_in + row // SUB == column).astype(bf16)


def final_kernel(
    ours, theirs, ours_two, theirs_two, x_o, z_o, out_o, conv_o, bias_o, xp_o, dt_o, db_o, al_o, skip_o, router_o, one_o,
    two_o, mine_s, other_s, *, rank, count, experts
):
    width = out_o.shape[0]
    model = router_o.shape[1]
    each = model // width
    x_o[...] = ours[:width, :model].astype(f32) + theirs[:width, :model].astype(f32)
    z_o[...] = ours_two[:width, :].astype(f32) + theirs_two[:width, :].astype(f32)
    out_o[...] = ours_two[width:, :].astype(f32) + theirs_two[width:, :].astype(f32)
    rest = slice(width, 2 * width)
    xd = ours[rest, :128].astype(f32) + theirs[rest, :128].astype(f32)
    xp_o[...] = xd[:, : rank + 2 * count]
    gap = jnp.zeros((128 - width, 128), f32)
    turned = jnp.concatenate([xd, gap], axis=0).T
    dt_o[...] = turned[128 - rank :, :width]
    vectors = jnp.zeros((128, 128), f32)
    for part, held in ((ours, mine_s), (theirs, other_s)):
        block = jnp.concatenate([part[rest, 128:256].astype(f32), gap], axis=0).T
        vectors = vectors + block
        for k in range(experts * each // 128):
            lanes = slice(256 + k * 128, 384 + k * 128)
            piece = jnp.concatenate([part[rest, lanes].astype(f32), gap], axis=0)
            held[k * 128 : (k + 1) * 128, :] = piece.T
        held[experts * each :, :] = jnp.zeros_like(held[experts * each :, :])
        held[experts * each : (experts + 2) * each, :] = block[8 + count : 8 + count + 2 * each, :]
    conv_o[...] = vectors[:KC, :width]
    bias_o[...] = vectors[KC : KC + 1, :width].reshape(width)
    db_o[...] = vectors[KC + 1 : KC + 2, :width].reshape(width)
    skip_o[...] = vectors[KC + 2 : KC + 3, :width].reshape(width)
    al_o[...] = vectors[8 : 8 + count, :width]
    row = lax.broadcasted_iota(jnp.int32, (128, model), 0)
    column = lax.broadcasted_iota(jnp.int32, (128, model), 1)
    total = jnp.zeros((experts + 8, model), f32)
    for at in range(each):
        to = (row * each + at == column).astype(bf16)
        picked = pl.ds(at, experts + 8, stride=each)
        total = total + dot_nn(mine_s[picked, :].astype(bf16), to)
        total = total + dot_nn(other_s[picked, :].astype(bf16), to)
    router_o[...] = total[:experts, :]
    one_o[...] = total[experts : experts + 1, :].reshape(model)
    two_o[...] = total[experts + 1 : experts + 2, :].reshape(model)


def token_order(rows):
    steps_in = rows // SUB
    row = lax.broadcasted_iota(jnp.int32, (rows, rows), 0)
    column = lax.broadcasted_iota(jnp.int32, (rows, rows), 1)
    return ((row % SUB) * steps_in + row // SUB == column).astype(bf16)


def exchange(values):
    return lax.all_to_all(values, "wide", split_axis=0, concat_axis=0, tiled=True)


def pair_up(values, place):
    partner = lax.ppermute(values, "wide", [(i, i ^ 4) for i in range(32)])
    first = (place // 4) % 2 == 0
    return jnp.concatenate(
        [jnp.where(first, values, partner), jnp.where(first, partner, values)], axis=0
    )


def gather_pairs(both):
    groups = [[(y * 2 + x) * 4 + z for y in range(4) for z in range(4)] for x in range(2)]
    return lax.all_gather(both, "wide", axis=0, tiled=True, axis_index_groups=groups)


def other_core(values):
    return lax.ppermute(values, "dp", [(0, 1), (1, 0), (2, 3), (3, 2)])


def other_side(values):
    return lax.ppermute(values, "dp", [(0, 2), (2, 0), (1, 3), (3, 1)])


def body(
    hidden, cotangent, routes, seg_lengths, gain_mix, in_x, in_z, conv_w, conv_b, x_proj, dt_proj,
    dt_bias, a_log, skip_d, out_proj, gain_moe, router, w_gate, w_up, w_down,
):
    rows, model = hidden.shape
    places = lax.axis_size("wide")
    place = lax.axis_index("wide")
    core = (lax.axis_index("dp") % 2).astype(jnp.int32).reshape(1)
    place_arr = place.astype(jnp.int32).reshape(1)
    width = in_x.shape[1]
    di = width * places
    count = a_log.shape[0]
    rank = dt_proj.shape[0]
    experts = router.shape[1]
    capacity = max(CAP * rows // (4 * places), 2)
    stride = -(-2 * capacity // 16) * 16
    half = model // 2
    steps_in = rows // SUB
    shift = SUB.bit_length() - 1
    span = 3 * width + 16
    side = (place // 4 % 2).astype(jnp.int32).reshape(1)

    pay_one, gate_share = call(
        partial(pack_kernel, places=places),
        [shape((di, half + 128), bf16), shape((width, model), bf16)],
        [],
        (
            core, in_x.T, x_proj, dt_proj, conv_w, conv_b, dt_bias, skip_d, a_log, in_z.T, out_proj,
        ),
        smem=1,
    )
    pay_one, hidden, cotangent, routes, seg_lengths = lax.optimization_barrier(
        (pay_one, hidden, cotangent, routes, seg_lengths)
    )
    wm = exchange(pay_one.reshape(places, width, half + 128)).reshape(di, half + 128)
    zm = gather_pairs(pair_up(gate_share, place))
    nrm, tail, hid, cot, route, aux = call(
        prepare_kernel,
        [
            shape((rows, model), bf16),
            shape((16, model), bf16),
            shape((rows, model), bf16),
            shape((rows, model), bf16),
            shape((rows, 1), jnp.int32),
            shape((rows, 128)),
        ],
        [],
        (place_arr * rows, seg_lengths, hidden, cotangent, routes.T, gain_mix),
        smem=2,
    )
    halo = lax.ppermute(tail, "wide", [(i, i + 1) for i in range(places - 1)])
    nrm_pair = pair_up(nrm, place)
    wm, halo = lax.optimization_barrier((wm, halo))
    wo = other_core(wm)
    ext, pre, steps, sig_step, small, x_in, tpre, tsuf, states, par, xd_weight, sd, q = call(
        partial(front_kernel, rank=rank, count=count),
        [
            shape((rows + (KC - 1) * SUB, di)),
            shape((rows, di)),
            shape((rows, di)),
            shape((rows, di)),
            shape((rows, 128)),
            shape((count, SUB, di)),
            shape((SUB, di)),
            shape((SUB, di)),
            shape((places * count, di + 256), bf16),
            shape((8 + count, di)),
            shape((di, 128), bf16),
            shape((rows, di)),
            shape((rows, di)),
        ],
        [
            pltpu.VMEM((steps_in * count, SUB, 128), f32),
            pltpu.VMEM((2, rows + 16, half), bf16),
            pltpu.VMEM((16, 128), f32),
        ],
        (core, nrm, halo, wm, wo, aux),
        smem=1,
        late=(3, 4),
        early=(0, 1, 2, 3, 9, 10, 11, 12),
    )

    zm, nrm_pair, _ = lax.optimization_barrier((zm, nrm_pair, states))
    zm = zm.reshape(4, 4, 2, width, model).swapaxes(1, 2).reshape(di, model)
    om = zm[:, half:]
    zm = zm[:, :half]
    zo = other_core(zm)
    oo = other_core(om)
    gate_z = call(
        gate_kernel,
        [shape((rows, di))],
        [pltpu.VMEM((2, rows, half), bf16)],
        (core, nrm, zm, zo),
        smem=1,
    )[0]
    states = exchange(states.reshape(places, count, di + 256)).reshape(places * count, di + 256)

    states, gate_z = lax.optimization_barrier((states, gate_z))
    scanned, send, middle, ntwo, chances, meta, hot, entry, sums = call(
        partial(
            middle_kernel,
            rank=rank,
            count=count,
            experts=experts,
            stride=stride,
            capacity=capacity,
            shift=shift,
        ),
        [
            shape((rows, di)),
            shape((experts * stride, model), bf16),
            shape((rows, model)),
            shape((rows, model), bf16),
            shape((rows, experts)),
            shape((rows, 8)),
            shape((2, rows, experts * stride), bf16),
            shape((count, di)),
            shape((places * count, 128)),
        ],
        [
            pltpu.VMEM((steps_in * count, SUB, 128), f32),
            pltpu.VMEM((steps_in * count, SUB, 128), f32),
            pltpu.VMEM((count, di), f32),
        ],
        (
            core, place_arr, om, oo, par, aux, pre, sd, q, x_in, small, states, tpre, hid, cot,
            route, gain_moe, router.T, gate_z,
        ),
        smem=2,
        late=(11, 9, 7, 8, 6, 18, 2, 3),
        early=(7, 8, 0),
    )

    arrived = exchange(send)
    arrived, nrm_pair = lax.optimization_barrier((arrived, nrm_pair))
    normed_all = gather_pairs(nrm_pair)
    slots = places * capacity
    at = jnp.arange(2 * slots, dtype=jnp.int32)
    source = (at % slots) // capacity * stride + at % capacity + (at // slots) * capacity
    pick = (source[:, None] == jnp.arange(experts * stride, dtype=jnp.int32)[None, :]).astype(bf16)
    mine = dot_nn(pick, arrived).astype(bf16)
    pair = jnp.stack([mine, other_side(mine)], axis=0)
    both = jnp.concatenate([pair, other_core(pair)], axis=0)
    expert_in = both[:, :slots].reshape(4 * slots, model)
    grad_rows = both[:, slots:].reshape(4 * slots, model)
    gate_in = dot_nn(expert_in, w_gate[0])
    up_in = dot_nn(expert_in, w_up[0])
    hidden_act = (jax.nn.silu(gate_in) * up_in).astype(bf16)
    act_grad = dot_nt(grad_rows, w_down[0])
    sig_gate = jax.nn.sigmoid(gate_in)
    gate_grad = (act_grad * up_in * sig_gate * (1.0 + gate_in * (1.0 - sig_gate))).astype(bf16)
    up_grad = (act_grad * gate_in * sig_gate).astype(bf16)
    y_part = dot_nn(hidden_act, w_down[0]).reshape(4, slots, model)
    dx_part = (dot_nt(gate_grad, w_gate[0]) + dot_nt(up_grad, w_up[0])).reshape(4, slots, model)
    parts = jnp.concatenate([y_part, dx_part], axis=1)
    summed = parts[:2] + other_core(parts[2:].astype(bf16)).astype(f32)
    total = (summed[0] + other_side(summed[1].astype(bf16)).astype(f32)).astype(bf16)
    back = exchange(dot_tn(pick, total).astype(bf16))
    grad_w_down = dot_tn(hidden_act, grad_rows)[None]
    grad_w_gate = dot_tn(expert_in, gate_grad)[None]
    grad_w_up = dot_tn(expert_in, up_grad)[None]
    back, grad_w_down, grad_w_gate, grad_w_up = lax.optimization_barrier(
        (back, grad_w_down, grad_w_gate, grad_w_up)
    )

    combined, logit_grad, mixlow, mgrad, ggrad, sgrad, gain_two, y_in, adjoints = call(
        partial(back_kernel, rank=rank, count=count, experts=experts),
        [
            shape((rows, model)),
            shape((rows, experts), bf16),
            shape((rows, model), bf16),
            shape((rows, model)),
            shape((rows, di)),
            shape((rows, di)),
            shape((1, model)),
            shape((count, SUB, di)),
            shape((places * count, di), bf16),
        ],
        [
            pltpu.VMEM((steps_in * count, SUB, 128), f32),
            pltpu.VMEM((2, rows, half), bf16),
            pltpu.VMEM((count, di), f32),
        ],
        (
            core, back, om, oo, par, aux, sd, small, gate_z, hot, middle, meta, chances, route,
            cot, gain_moe, router.T,
        ),
        smem=1,
        late=(2, 3, 8, 6),
        early=(2, 3, 0, 4, 5),
    )
    mixlow, normed_all = lax.optimization_barrier((mixlow, normed_all))
    mix_half = gather_pairs(mixlow)
    adjoints = exchange(adjoints.reshape(places, count, di)).reshape(places * count, di)
    out, comb, skip_part, ngrad_z = call(
        partial(aside_kernel, experts=experts, width=width, span=span),
        [
            shape((rows, model), bf16),
            shape((places * span, 128), bf16),
            shape((1, di)),
            shape((2, rows, half)),
        ],
        [],
        (
            core, side, zm, zo, aux, pre, gate_z, scanned, ggrad, combined, logit_grad, ntwo,
            middle, meta,
        ),
        smem=2,
    )
    adjoints, comb = lax.optimization_barrier((adjoints, comb))
    comb_got = exchange(comb.reshape(places, span, 128))

    cgrad, xd, spar = call(
        partial(scan_kernel, rank=rank, count=count),
        [shape((rows, di)), shape((di, 128), bf16), shape((8 + count, di))],
        [pltpu.VMEM((steps_in * count, SUB, 128), f32)] * 4
        + [pltpu.VMEM(((steps_in + 1) * count, SUB, 128), f32)]
        + [pltpu.VMEM((steps_in * count, SUB, 128), f32)]
        + [pltpu.VMEM((rows, di), f32)] * 2
        + [pltpu.VMEM((rows, di), bf16)]
        + [pltpu.VMEM((count, di), f32)] * 2,
        (
            place_arr, xd_weight, par, sd, q, pre, steps, sig_step, small, x_in, tpre, entry, y_in,
            tsuf, adjoints, sums, sgrad,
        ),
        smem=1,
        late=(14, 15, 9, 3, 4, 16, 12, 5, 7, 1, 6),
    )
    pay, ngrad, beyond = call(
        partial(last_kernel, width=width, span=span),
        [shape((di, 384), bf16), shape((rows, model)), shape((SUB, model))],
        [pltpu.VMEM((rows, di), bf16), pltpu.VMEM((16, di), bf16)],
        (
            core, cgrad, halo, aux, ext, par, wm, wo, ngrad_z, spar, skip_part, xd, hid, gain_two,
            comb_got.reshape(places * span, 128),
        ),
        smem=1,
        late=(11, 6, 7, 8, 14, 12),
    )
    got_pay = exchange(pay.reshape(places, width, 384))
    beyond = lax.ppermute(beyond, "wide", [(i + 1, i) for i in range(places - 1)])
    first_grad = call(
        hidden_kernel, [shape((rows, model))], [], (ngrad, beyond, hid, mgrad, gain_mix)
    )[0]
    places_order = [(p // 8 * 4 + p % 4) * 2 + p // 4 % 2 for p in range(places)]
    z_ready, out_ready, out_theirs = call(
        partial(ready_kernel, places_order=places_order),
        [shape((width, model), bf16)] * 3,
        [
            pltpu.VMEM((width, places * rows), bf16),
            pltpu.VMEM((2 * width, places // 2 * rows), bf16),
        ],
        (side, comb_got, normed_all, mix_half),
        smem=1,
        late=(3, 2),
    )
    got_pay, out_theirs = lax.optimization_barrier((got_pay, out_theirs))
    out_other = lax.ppermute(out_theirs, "wide", [(i, i ^ 4) for i in range(places)])
    out_ready = (out_ready.astype(f32) + out_other.astype(f32)).astype(bf16)
    ready = jnp.concatenate([z_ready, out_ready], axis=0)
    ready = (ready.astype(f32) + other_core(ready).astype(f32)).astype(bf16)
    ready_side = other_side(ready)
    per_place = model // width
    mats = call(
        partial(
            grads_kernel, places_order=places_order, base=8 + count + 2 * per_place
        ),
        [shape((2 * width, 256 + places * per_place), bf16)],
        [pltpu.VMEM((width, places * rows), bf16)],
        (got_pay, normed_all),
        late=(1,),
    )[0]
    mats = (mats.astype(f32) + other_core(mats).astype(f32)).astype(bf16)
    grad_x, grad_z, grad_out, grad_conv, grad_bias, grad_xp, grad_dt, grad_db, grad_al, grad_sk, grad_router, gain_one, gain_two = call(
        partial(final_kernel, rank=rank, count=count, experts=experts),
        [
            shape((width, model)),
            shape((width, model)),
            shape((width, model)),
            shape((KC, width)),
            shape((width,)),
            shape((width, rank + 2 * count)),
            shape((rank, width)),
            shape((width,)),
            shape((count, width)),
            shape((width,)),
            shape((experts, model)),
            shape((model,)),
            shape((model,)),
        ],
        [pltpu.VMEM(((experts + 8) * per_place, 128), f32)] * 2,
        (mats, other_side(mats), ready, ready_side),
    )
    return (
        out,
        first_grad,
        gain_one,
        grad_x.T,
        grad_z.T,
        grad_conv,
        grad_bias,
        grad_xp,
        grad_dt,
        grad_db,
        grad_al,
        grad_sk,
        grad_out,
        gain_two,
        grad_router.T,
        grad_w_gate,
        grad_w_up,
        grad_w_down,
    )


def solution(mesh):
    rows = P(("dp", "wide"), None)
    expert_columns = P("wide", None, "dp")
    expert_rows = P("wide", "dp", None)
    placed = (
        rows, rows, rows, P("dp", None), P(), P(None, "wide"), P(None, "wide"), P(None, "wide"),
        P("wide"), P("wide", None), P(None, "wide"), P("wide"), P(None, "wide"), P("wide"),
        P("wide", None), P(), P(), expert_columns, expert_columns, expert_rows,
    )
    given = (
        rows, rows, P(), P(None, "wide"), P(None, "wide"), P(None, "wide"), P("wide"),
        P("wide", None), P(None, "wide"), P("wide"), P(None, "wide"), P("wide"), P("wide", None),
        P(), P(), expert_columns, expert_columns, expert_rows,
    )
    return jax.shard_map(body, mesh=mesh, in_specs=placed, out_specs=given, check_vma=False)
```

```python
from functools import partial

import jax
import jax.numpy as jnp
from jax import lax
from jax.experimental import pallas as pl
from jax.experimental.pallas import tpu as pltpu
from jax.sharding import PartitionSpec as P

f32 = jnp.float32
bf16 = jnp.bfloat16
KC = 4
SUB = 8
CAP = 5
STOP = 1e6
LOG2E = 1.4426950408889634
LN2 = 0.6931471805599453
epsilon = 1e-05
VMEM_LIMIT = 56 * 1024 * 1024


def dot_nn(left, right):
    return lax.dot_general(left, right, (((1,), (0,)), ((), ())), preferred_element_type=f32)


def dot_nt(left, right):
    return lax.dot_general(left, right, (((1,), (1,)), ((), ())), preferred_element_type=f32)


def dot_tn(left, right):
    return lax.dot_general(left, right, (((0,), (0,)), ((), ())), preferred_element_type=f32)


class Moves:
    def __init__(self):
        self.arriving = {}
        self.leaving = {}
        self.started = []

    def need(self, *refs):
        for ref in refs:
            copy = self.arriving.pop(id(ref), None)
            if copy is not None:
                copy.wait()

    def done(self, *refs):
        for ref in refs:
            copy = self.leaving.pop(id(ref), None)
            if copy is not None:
                copy.start()
                self.started.append(copy)


def call(kernel, out_shapes, scratch, args, smem=0, late=(), early=(), lanes=None):
    lanes = lanes or {}
    vmem = pl.BlockSpec(memory_space=pltpu.VMEM)
    hbm = pl.BlockSpec(memory_space=pl.ANY)
    specs = [pl.BlockSpec(memory_space=pltpu.SMEM)] * smem
    specs += [hbm if i in late else vmem for i in range(smem, len(args))]
    buffers = []
    for i in late:
        dims = (args[i].shape[0], lanes[i].size) if i in lanes else args[i].shape
        buffers.append(pltpu.VMEM(dims, args[i].dtype))
    buffers += [pltpu.VMEM(out_shapes[i].shape, out_shapes[i].dtype) for i in early]
    moving = len(buffers)
    extra = buffers + [pltpu.SemaphoreType.DMA((moving,))] if moving else []

    def staged(*refs):
        refs = list(refs)
        own = refs[len(refs) - moving - 1 : -1]
        semaphores = refs[-1]
        refs = refs[: len(refs) - moving - 1]
        moves = Moves()
        for k, i in enumerate(late):
            source = refs[i].at[:, lanes[i]] if i in lanes else refs[i]
            copy = pltpu.make_async_copy(source, own[k], semaphores.at[k])
            copy.start()
            refs[i] = own[k]
            moves.arriving[id(own[k])] = copy
        for k, i in enumerate(early, len(late)):
            at = len(args) + i
            moves.leaving[id(own[k])] = pltpu.make_async_copy(own[k], refs[at], semaphores.at[k])
            refs[at] = own[k]
        kernel(moves, *refs)
        moves.need(*own)
        moves.done(*own)
        for copy in moves.started:
            copy.wait()

    return pl.pallas_call(
        staged if moving else kernel,
        out_shape=out_shapes,
        in_specs=specs,
        out_specs=[hbm if i in early else vmem for i in range(len(out_shapes))],
        scratch_shapes=list(scratch) + extra,
        compiler_params=pltpu.CompilerParams(vmem_limit_bytes=VMEM_LIMIT),
    )(*args)


def shape(dims, dtype=f32):
    return jax.ShapeDtypeStruct(dims, dtype)


def group_of(di):
    return 256 if di % 256 == 0 else 128


def sublane_iota(width):
    return lax.broadcasted_iota(jnp.int32, (SUB, width), 0)


def from_before(block, first):
    row = sublane_iota(block.shape[1])
    return jnp.where(row == 0, jnp.broadcast_to(first, block.shape), pltpu.roll(block, 1, 0))


def from_after(block, last):
    row = sublane_iota(block.shape[1])
    return jnp.where(
        row == SUB - 1, jnp.broadcast_to(last, block.shape), pltpu.roll(block, SUB - 1, 0)
    )


def spread_columns(small, first, count, out):
    steps = small.shape[0] // SUB
    for j in range(steps):
        block = small[j * SUB : (j + 1) * SUB, :]
        for n in range(count):
            out[j * count + n] = jnp.broadcast_to(block[:, first + n : first + n + 1], (SUB, 128))


def prefix_states(decay, state):
    row = sublane_iota(state.shape[1])
    for shift in (1, 2, 4):
        inside = row >= shift
        state = state + decay * jnp.where(inside, pltpu.roll(state, shift, 0), 0.0)
        decay = decay * jnp.where(inside, pltpu.roll(decay, shift, 0), 1.0)
    return state


def suffix_states(decay, state):
    row = sublane_iota(state.shape[1])
    for shift in (1, 2, 4):
        inside = row < SUB - shift
        state = state + decay * jnp.where(inside, pltpu.roll(state, SUB - shift, 0), 0.0)
        decay = decay * jnp.where(inside, pltpu.roll(decay, SUB - shift, 0), 1.0)
    return state


def prefix_sum(values):
    row = sublane_iota(values.shape[1])
    for shift in (1, 2, 4):
        values = values + jnp.where(row >= shift, pltpu.roll(values, shift, 0), 0.0)
    return values


def suffix_sum(values):
    row = sublane_iota(values.shape[1])
    for shift in (1, 2, 4):
        values = values + jnp.where(row < SUB - shift, pltpu.roll(values, SUB - shift, 0), 0.0)
    return values


def one_hot(dims, offset):
    row = lax.broadcasted_iota(jnp.int32, dims, 0)
    column = lax.broadcasted_iota(jnp.int32, dims, 1)
    return (row + offset == column).astype(bf16)


def pack_kernel(
    core, in_x, x_proj, dt_proj, conv_w, conv_b, dt_bias, skip_d, a_log, in_z, out_proj, out, gate_o,
    *, places
):
    width, model = in_x.shape
    half = model // 2
    here = core[0]
    start = pl.multiple_of(here * half, 128)
    mine = in_x[:, pl.ds(start, half)]
    gate_o[:, :half] = in_z[:, pl.ds(start, half)]
    gate_o[:, half:] = out_proj[:, pl.ds(start, half)]
    narrow = x_proj.shape[1]
    steps = dot_nn(x_proj[...], one_hot((narrow, 128), 0)) + dot_tn(
        dt_proj[...], one_hot((dt_proj.shape[0], 128), 128 - dt_proj.shape[0])
    )
    values = jnp.concatenate(
        [
            conv_w[...],
            conv_b[...].reshape(1, width),
            dt_bias[...].reshape(1, width),
            skip_d[...].reshape(1, width),
            jnp.zeros((1, width), f32),
            a_log[...],
        ],
        axis=0,
    )
    top = values.astype(bf16)
    left = values - top.astype(f32)
    mid = left.astype(bf16)
    low = (left - mid.astype(f32)).astype(bf16)
    count = values.shape[0]
    extra = dot_tn(top, one_hot((count, 128), 0))
    extra = extra + dot_tn(mid, one_hot((count, 128), count))
    extra = extra + dot_tn(low, one_hot((count, 128), 2 * count))
    rest = jnp.where(here == 0, steps, extra).astype(bf16)
    for place in range(places):
        out[place * width : (place + 1) * width, :half] = mine
        out[place * width : (place + 1) * width, half:] = rest


def prepare_kernel(
    base, lengths, hidden, cot, route, gain, nrm_o, tail_o, hid_o, cot_o, route_o, aux_o
):
    rows = hidden.shape[0]
    steps_in = rows // SUB
    row = lax.broadcasted_iota(jnp.int32, (rows, rows), 0)
    column = lax.broadcasted_iota(jnp.int32, (rows, rows), 1)
    in_order = (row % SUB) * steps_in + row // SUB == column
    order = in_order.astype(bf16)
    hid = dot_nn(order, hidden[...])
    hid_o[...] = hid.astype(bf16)
    cot_o[...] = dot_nn(order, cot[...]).astype(bf16)
    ours = jnp.where(in_order, jnp.broadcast_to(route[...], (rows, rows)), 0)
    route_o[...] = jnp.sum(ours, axis=1, keepdims=True)
    scale = lax.rsqrt(jnp.mean(hid * hid, axis=1, keepdims=True) + epsilon)
    normed = (hid * scale * gain[...].reshape(1, -1)).astype(bf16)
    nrm_o[...] = normed
    tail_row = lax.broadcasted_iota(jnp.int32, (16, rows), 0)
    tail_column = lax.broadcasted_iota(jnp.int32, (16, rows), 1)
    picked = (tail_column == rows - 1 - (KC - 2 - tail_row) * SUB) & (tail_row < KC - 1)
    tail = dot_nn(picked.astype(bf16), normed)
    tail_row = tail_row - SUB
    picked = (tail_column == rows - 1 - (KC - 2 - tail_row) * SUB) & (tail_row < KC - 1)
    picked = picked & (tail_row >= 0)
    tail_o[...] = (tail + dot_nn(picked.astype(bf16), hid.astype(bf16))).astype(bf16)

    def layout(position, lane):
        back = position - (lane + 1)
        segment = jnp.zeros_like(position)
        segment_back = jnp.zeros_like(position)
        reset = position == 0
        end = jnp.int32(0)
        for j in range(lengths.shape[1] - 1):
            end = end + lengths[0, j]
            segment = segment + (position >= end).astype(jnp.int32)
            segment_back = segment_back + (back >= end).astype(jnp.int32)
            reset = reset | (position == end)
        same = (back >= 0) & (segment == segment_back)
        live = position < end
        picked = jnp.where(lane == KC - 1, live.astype(f32), reset.astype(f32))
        return jnp.where(lane < KC - 1, same.astype(f32), picked)

    at = lax.broadcasted_iota(jnp.int32, (rows, 128), 0)
    lane = lax.broadcasted_iota(jnp.int32, (rows, 128), 1)
    aux_o[...] = layout(base[0] + (at % SUB) * steps_in + at // SUB, lane)


def front_kernel(
    moves, core, nrm_in, halo_in, wm, wo, aux, ext_o, pre_o, steps_o, sig_o, small_o, x_o, tpre_o, tsuf_o,
    state_o, par_o, xd_o, sd_s, q_s, bw_s, nrm_s, sum_s, *, rank, count
):
    rows, di = pre_o.shape
    half = wo.shape[1] - 128
    steps_in = rows // SUB
    gs = group_of(di)
    low = core[0] == 0
    nrm_s[0, :rows] = jnp.where(low, nrm_in[:, :half], nrm_in[:, half:])
    nrm_s[1, :rows] = jnp.where(low, nrm_in[:, half:], nrm_in[:, :half])
    nrm_s[0, rows:] = jnp.where(low, halo_in[:, :half], halo_in[:, half:])
    nrm_s[1, rows:] = jnp.where(low, halo_in[:, half:], halo_in[:, :half])
    small_o[...] = jnp.zeros_like(small_o)
    moves.need(wm, wo)
    par = par_o
    total_rows = par_o.shape[0]

    def unpack(g, _):
        lanes = pl.ds(pl.multiple_of(g * 128, 128), 128)
        mine = wm[lanes, half:]
        other = wo[lanes, half:]
        xd_o[lanes, :] = jnp.where(low, mine, other)
        turned = jnp.where(low, other, mine).astype(f32).T
        par_o[:, lanes] = (
            turned[:total_rows, :]
            + turned[total_rows : 2 * total_rows, :]
            + turned[2 * total_rows : 3 * total_rows, :]
        )
        return 0

    lax.fori_loop(0, di // 128, unpack, 0)

    def project(g, _):
        lanes = pl.ds(pl.multiple_of(g * gs, gs), gs)
        inner = dot_nt(nrm_s[0], wm[lanes, :half]) + dot_nt(nrm_s[1], wo[lanes, :half])
        for back in range(1, KC):
            block = inner[rows - back * SUB : rows - (back - 1) * SUB, :]
            halo = inner[rows + KC - 1 - back : rows + KC - back, :]
            ext_o[(KC - 1 - back) * SUB : (KC - back) * SUB, lanes] = from_before(block, halo)
        ext_o[(KC - 1) * SUB :, lanes] = inner[:rows, :]
        total = par[KC : KC + 1, lanes] + par[KC - 1 : KC, lanes] * inner[:rows, :]
        for back in range(1, KC):
            shifted = ext_o[(KC - 1 - back) * SUB : (KC - 1 - back) * SUB + rows, lanes]
            total = total + par[KC - 1 - back : KC - back, lanes] * shifted * aux[:, back - 1 : back]
        pre_o[:, lanes] = total
        act = total * jax.nn.sigmoid(total)
        q_s[:, lanes] = act
        small_o[...] += dot_nn(act.astype(bf16), xd_o[lanes, :])
        return 0

    lax.fori_loop(0, di // gs, project, 0)
    moves.done(ext_o, pre_o, par_o, xd_o)
    small = small_o[...]
    lane = lax.broadcasted_iota(jnp.int32, small.shape, 1)
    step_low = jnp.where(lane >= 128 - rank, pltpu.roll(small, 128 - rank, 1), 0.0).astype(bf16)
    spread_columns(small, rank, count, bw_s)

    def stepping(g, _):
        lanes = pl.ds(pl.multiple_of(g * gs, gs), gs)
        step_pre = dot_nt(step_low, xd_o[lanes, :]) + par[KC + 1 : KC + 2, lanes]
        small_exp = jnp.exp(-jnp.abs(step_pre))
        steps = jnp.maximum(step_pre, 0.0) + jnp.log1p(small_exp)
        steps_o[:, lanes] = steps
        sig_o[:, lanes] = jax.nn.sigmoid(step_pre)
        q_s[:, lanes] = q_s[:, lanes] * steps
        sd_s[:, lanes] = jnp.where(aux[:, 4:5] > 0.5, STOP, steps)
        return 0

    lax.fori_loop(0, di // gs, stepping, 0)
    moves.done(steps_o, sig_o, sd_s, q_s)

    def chunk(g, _):
        lanes = pl.ds(pl.multiple_of(g * 128, 128), 128)
        rates = [
            jnp.broadcast_to(-LOG2E * jnp.exp(par[8 + n : 9 + n, lanes]), (SUB, 128))
            for n in range(count)
        ]

        def step(j, carry):
            states, total = carry
            at = pl.ds(pl.multiple_of(j * SUB, SUB), SUB)
            sd = sd_s[at, lanes]
            q = q_s[at, lanes]
            states = tuple(
                jnp.exp2(sd * rates[n]) * states[n] + q * bw_s[j * count + n] for n in range(count)
            )
            return (states, total + sd)

        zero = jnp.zeros((SUB, 128), f32)
        states, total = lax.fori_loop(0, steps_in, step, ((zero,) * count, zero), unroll=4)
        row = sublane_iota(128)
        ahead = prefix_sum(total)
        behind = suffix_sum(total)
        tpre_o[:, lanes] = jnp.where(row == 0, 0.0, pltpu.roll(ahead, 1, 0))
        tsuf_o[:, lanes] = jnp.where(row == SUB - 1, 0.0, pltpu.roll(behind, SUB - 1, 0))
        last = []
        for n in range(count):
            joined = prefix_states(jnp.exp2(rates[n] * total), states[n])
            x_o[n, :, lanes] = jnp.where(row == 0, 0.0, pltpu.roll(joined, 1, 0))
            last.append(joined[SUB - 1 : SUB, :])
        sum_s[pl.ds(g, 1), :] = ahead[SUB - 1 : SUB, :]
        to_copies(state_o, jnp.concatenate(last, axis=0).astype(bf16), lanes)
        return 0

    sum_s[...] = jnp.zeros_like(sum_s)
    lax.fori_loop(0, di // 128, chunk, 0)
    sums = sum_s[...]
    top = sums.astype(bf16)
    left = (sums - top.astype(f32)).astype(bf16)
    to_copies(state_o, top, slice(di, di + 128))
    to_copies(state_o, left, slice(di + 128, di + 256))


def to_copies(out, values, lanes):
    count = values.shape[0]
    for place in range(out.shape[0] // count):
        out[place * count : (place + 1) * count, lanes] = values


def negative_rates(par, out):
    out[...] = -LOG2E * jnp.exp(par[8:, :])


def group_kernel(arrived, out, state_s, sum_s, *, di, count, reverse):
    members = arrived.shape[0] // count
    rest = arrived.shape[1] - di - 256
    copies = out.shape[0] // count
    state_s[...] = jnp.zeros_like(state_s)
    total = jnp.zeros((count, 128), f32)
    for place in range(members - 1, -1, -1) if reverse else range(members):
        block = slice(place * count, (place + 1) * count)
        sums = arrived[block, di : di + 128].astype(f32)
        sums = sums + arrived[block, di + 128 : di + 256].astype(f32)
        total = total + sums
        carry_step(sums, arrived[block, :di], sum_s, state_s)
    joined = state_s[...].astype(bf16)
    top = total.astype(bf16)
    left = (total - top.astype(f32)).astype(bf16)
    for copy in range(copies):
        block = slice(copy * count, (copy + 1) * count)
        out[block, :di] = joined
        out[block, di : di + 128] = top
        out[block, di + 128 : di + 256] = left
    if rest:
        extra = jnp.zeros((count, rest), f32)
        for place in range(members):
            extra = extra + arrived[place * count : (place + 1) * count, di + 256 :].astype(f32)
        gap = jnp.zeros((count - 2, rest), f32)
        for copy in range(copies):
            rows = jnp.concatenate([extra[2 * copy : 2 * copy + 2, :], gap], axis=0)
            out[copy * count : (copy + 1) * count, di + 256 :] = rows.astype(bf16)


def forward_group_kernel(arrived, par, out, state_s, rate_s, *, di, count):
    negative_rates(par, rate_s)
    group_kernel(arrived, out, state_s, rate_s, di=di, count=count, reverse=False)


def backward_group_kernel(arrived, par, out, state_s, rate_s, *, di, count):
    negative_rates(par, rate_s)
    group_kernel(arrived, out, state_s, rate_s, di=di, count=count, reverse=True)


def step_sums(arrived, block, di):
    return arrived[block, di : di + 128].astype(f32) + arrived[block, di + 128 : di + 256].astype(
        f32
    )


def carry_step(decay_sums, arrived, rate_s, state_s):
    for g in range(state_s.shape[1] // 128):
        lanes = slice(g * 128, (g + 1) * 128)
        decay = jnp.exp2(rate_s[:, lanes] * decay_sums[g : g + 1, :])
        state_s[:, lanes] = decay * state_s[:, lanes] + arrived[:, lanes].astype(f32)


def gate_kernel(moves, core, nrm, zm, zo, gate_z_o, nrm_s):
    rows, di = gate_z_o.shape
    half = zm.shape[1]
    gs = group_of(di)
    low = core[0] == 0
    nrm_s[0] = jnp.where(low, nrm[:, :half], nrm[:, half:])
    nrm_s[1] = jnp.where(low, nrm[:, half:], nrm[:, :half])
    moves.need(zm, zo)

    def project(g, _):
        lanes = pl.ds(pl.multiple_of(g * gs, gs), gs)
        gate_z_o[:, lanes] = dot_nt(nrm_s[0], zm[lanes, :]) + dot_nt(nrm_s[1], zo[lanes, :])
        return 0

    lax.fori_loop(0, di // gs, project, 0)


def middle_kernel(
    moves, core, place, om, oo, par, aux, pre, sd, q, x_in, small, arrived, near, tpre, hid, cot,
    route, gain, router, gate_z, scan_o, send_o, middle_o, ntwo_o, chance_o, meta_o, hot_o,
    entry_o, bw_s, cw_s, rate_s, *, rank, count, experts, stride, capacity, shift
):
    rows, di = pre.shape
    half = om.shape[1]
    steps_in = rows // SUB
    gs = group_of(di)
    low = core[0] == 0
    spread_columns(small[...], rank, count, bw_s)
    spread_columns(small[...], rank + count, count, cw_s)
    negative_rates(par, rate_s)
    moves.need(arrived, near)
    entry_o[...] = jnp.zeros_like(entry_o)
    members = near.shape[0] // count

    def before_here(there, _):
        block = pl.ds(pl.multiple_of(there * count, count), count)
        carry_step(step_sums(arrived, block, di), arrived[block, :di], rate_s, entry_o)
        return 0

    def just_before(there, _):
        block = pl.ds(pl.multiple_of(there * count, count), count)
        carry_step(step_sums(near, block, di), near[block, :di], rate_s, entry_o)
        return 0

    lax.fori_loop(0, place[0] // members, before_here, 0)
    lax.fori_loop(0, place[0] % members, just_before, 0)
    moves.done(entry_o)
    moves.need(x_in, sd, q)

    def scan(g, _):
        lanes = pl.ds(pl.multiple_of(g * 128, 128), 128)
        rates = [jnp.broadcast_to(rate_s[n : n + 1, lanes], (SUB, 128)) for n in range(count)]
        before = tpre[:, lanes]
        first = tuple(
            x_in[n, :, lanes] + jnp.exp2(rates[n] * before) * entry_o[n : n + 1, lanes]
            for n in range(count)
        )
        def step(j, states):
            at = pl.ds(pl.multiple_of(j * SUB, SUB), SUB)
            sd_here = sd[at, lanes]
            q_here = q[at, lanes]
            total = jnp.zeros((SUB, 128), f32)
            fresh = []
            for n in range(count):
                state = jnp.exp2(sd_here * rates[n]) * states[n] + q_here * bw_s[j * count + n]
                total = total + state * cw_s[j * count + n]
                fresh.append(state)
            scan_o[at, lanes] = total
            return tuple(fresh)

        lax.fori_loop(0, steps_in, step, first, unroll=4)
        return 0

    lax.fori_loop(0, di // 128, scan, 0)

    def gating(g, carry):
        mine, other = carry
        lanes = pl.ds(pl.multiple_of(g * gs, gs), gs)
        z = gate_z[:, lanes]
        pre_here = pre[:, lanes]
        scanned = scan_o[:, lanes] + par[KC + 2 : KC + 3, lanes] * (
            pre_here * jax.nn.sigmoid(pre_here)
        )
        scan_o[:, lanes] = scanned
        gated = (scanned * (z * jax.nn.sigmoid(z)) * aux[:, 3:4]).astype(bf16)
        return (mine + dot_nn(gated, om[lanes, :]), other + dot_nn(gated, oo[lanes, :]))

    zero = jnp.zeros((rows, half), f32)
    moves.need(pre, gate_z, om, oo)
    mine, other = lax.fori_loop(0, di // gs, gating, (zero, zero))
    moves.done(scan_o)
    mixed = jnp.concatenate([jnp.where(low, mine, other), jnp.where(low, other, mine)], axis=1)
    middle = hid[...].astype(f32) + mixed
    middle_o[...] = middle
    scale = lax.rsqrt(jnp.mean(middle * middle, axis=1, keepdims=True) + epsilon)
    ntwo = (middle * scale * gain[...].reshape(1, -1)).astype(bf16)
    ntwo_o[...] = ntwo
    logits = dot_nt(ntwo, router[...])
    top = jnp.max(logits, axis=1, keepdims=True)
    raised = jnp.exp(logits - top)
    chances = raised / jnp.sum(raised, axis=1, keepdims=True)
    chance_o[...] = chances
    lane = lax.broadcasted_iota(jnp.int32, (rows, experts), 1)
    chosen = route[...] == lane
    chosen_f = chosen.astype(f32)
    gate = jnp.sum(chances * chosen_f, axis=1, keepdims=True)
    taken = chosen_f * aux[:, 3:4]
    here = lax.broadcasted_iota(jnp.int32, (rows, rows), 0)
    there = lax.broadcasted_iota(jnp.int32, (rows, rows), 1)
    own_id = (here & (SUB - 1)) * steps_in + (here >> shift)
    other_id = (there & (SUB - 1)) * steps_in + (there >> shift)
    earlier = (other_id < own_id).astype(bf16)
    ranks = jnp.sum(dot_nn(earlier, taken.astype(bf16)) * chosen_f, axis=1, keepdims=True)
    kept = aux[:, 3:4] * (ranks < capacity).astype(f32)
    weight = gate * kept
    up = (cot[...].astype(f32) * weight).astype(bf16)
    values = jnp.concatenate([ntwo, up], axis=0)
    rank_low = ranks.astype(jnp.int32)
    slot = jnp.concatenate([rank_low, rank_low + capacity], axis=0)
    block = route[...] * stride
    block = jnp.concatenate([block, block], axis=0)
    kept_on = jnp.concatenate([kept, kept], axis=0) > 0.5
    place = lax.broadcasted_iota(jnp.int32, (2 * rows, experts * stride), 1)
    wide_hot = ((block + slot == place) & kept_on).astype(bf16)
    at_last = (block + 2 * capacity + slot // 2 == place) & kept_on
    even_hot = (at_last & (slot % 2 == 0)).astype(bf16)
    odd_hot = (at_last & (slot % 2 == 1)).astype(bf16)
    hot_o[0] = wide_hot
    hot_o[1] = even_hot
    hot_o[2] = odd_hot
    third = ntwo.shape[1] // 3
    narrow = values[:, 2 * third :]
    last = jnp.concatenate([dot_tn(even_hot, narrow), dot_tn(odd_hot, narrow)], axis=1)
    packed = (dot_tn(wide_hot, values[:, : 2 * third]) + last).astype(bf16)
    send_o[: experts * stride, :] = packed
    send_o[experts * stride :, :] = packed
    lane8 = lax.broadcasted_iota(jnp.int32, (rows, 8), 1)
    meta_o[...] = jnp.where(
        lane8 == 0, gate, jnp.where(lane8 == 1, kept, jnp.where(lane8 == 2, scale, 0.0))
    )


def back_kernel(
    moves, core, back, om, oo, par, aux, sd, small, gate_z, hot, middle, meta, chances, route, cot, gain,
    router, ntwo, combined_o, mixlow_o, mgrad_o, ggrad_o, sg_o, gain_o, y_o, state_o, cw_s, mix_s,
    rate_s, sum_s, *, rank, count, experts
):
    rows, di = sd.shape
    half = om.shape[1]
    steps_in = rows // SUB
    gs = group_of(di)
    negative_rates(par, rate_s)
    slots = back.shape[0] // 2
    third = back.shape[1] // 2
    rows_back = (back[:slots, :].astype(f32) + back[slots:, :].astype(f32)).astype(bf16)
    last = dot_nn(hot[1], rows_back[:, :third]) + dot_nn(hot[2], rows_back[:, third:])
    both = jnp.concatenate([dot_nn(hot[0], rows_back), last], axis=1)
    combined = both[:rows, :]
    dispatch = both[rows:, :]
    combined_o[...] = combined
    gate = meta[:, 0:1]
    kept = meta[:, 1:2]
    scale = meta[:, 2:3]
    mid = middle[...]
    up = cot[...].astype(f32)
    gate_total = kept * jnp.sum(up * combined, axis=1, keepdims=True)
    lane = lax.broadcasted_iota(jnp.int32, (rows, experts), 1)
    chosen_f = (route[...] == lane).astype(f32)
    logit_grad = (gate * (chosen_f - chances[...]) * gate_total).astype(bf16)
    router_rows = dot_tn(logit_grad, ntwo[...])
    members = state_o.shape[0] // count
    for member in range(members):
        rows_here = []
        for group in range(experts // members):
            row = router_rows[group * members + member : group * members + member + 1, :]
            rows_here += [row[:, :half], row[:, half:]]
        block = slice(member * count, (member + 1) * count)
        state_o[block, di + 256 :] = jnp.concatenate(rows_here, axis=0).astype(bf16)
    ngrad = dot_nn(logit_grad, router[...]) + dispatch
    gain_o[...] = jnp.sum(ngrad * mid * scale, axis=0, keepdims=True)
    scaled = gain[...].reshape(1, -1) * ngrad
    cube = scale * scale * scale
    mgrad = up + scale * scaled - mid * cube * jnp.mean(mid * scaled, axis=1, keepdims=True)
    mgrad_o[...] = mgrad
    low = core[0] == 0
    mixlow = mgrad.astype(bf16)
    mixlow_o[...] = mixlow
    mix_s[0] = jnp.where(low, mixlow[:, :half], mixlow[:, half:])
    mix_s[1] = jnp.where(low, mixlow[:, half:], mixlow[:, :half])
    moves.done(mixlow_o, mgrad_o, combined_o)
    moves.need(om, oo, gate_z)

    def gating(g, _):
        lanes = pl.ds(pl.multiple_of(g * gs, gs), gs)
        ggrad = dot_nt(mix_s[0], om[lanes, :]) + dot_nt(mix_s[1], oo[lanes, :])
        ggrad = ggrad * aux[:, 3:4]
        ggrad_o[:, lanes] = ggrad
        z = gate_z[:, lanes]
        sg_o[:, lanes] = ggrad * (z * jax.nn.sigmoid(z))
        return 0

    lax.fori_loop(0, di // gs, gating, 0)
    moves.done(ggrad_o, sg_o)
    spread_columns(small[...], rank + count, count, cw_s)
    moves.need(sd)

    def chunk(g, _):
        lanes = pl.ds(pl.multiple_of(g * 128, 128), 128)
        rates = [jnp.broadcast_to(rate_s[n : n + 1, lanes], (SUB, 128)) for n in range(count)]

        def step(i, carry):
            grads, total = carry
            j = steps_in - 1 - i
            at = pl.ds(pl.multiple_of(j * SUB, SUB), SUB)
            sd_here = sd[at, lanes]
            sgrad = sg_o[at, lanes]
            grads = tuple(
                jnp.exp2(sd_here * rates[n]) * (grads[n] + sgrad * cw_s[j * count + n])
                for n in range(count)
            )
            return (grads, total + sd_here)

        zero = jnp.zeros((SUB, 128), f32)
        grads, total = lax.fori_loop(0, steps_in, step, ((zero,) * count, zero), unroll=4)
        row = sublane_iota(128)
        last = []
        for n in range(count):
            joined = suffix_states(jnp.exp2(rates[n] * total), grads[n])
            y_o[n, :, lanes] = jnp.where(row == SUB - 1, 0.0, pltpu.roll(joined, SUB - 1, 0))
            last.append(joined[0:1, :])
        sum_s[pl.ds(g, 1), :] = jnp.sum(total, axis=0, keepdims=True)
        to_copies(state_o, jnp.concatenate(last, axis=0).astype(bf16), lanes)
        return 0

    sum_s[...] = jnp.zeros_like(sum_s)
    lax.fori_loop(0, di // 128, chunk, 0)
    total = sum_s[...]
    top = total.astype(bf16)
    to_copies(state_o, top, slice(di, di + 128))
    to_copies(state_o, (total - top.astype(f32)).astype(bf16), slice(di + 128, di + 256))


def slot_rows(stride, capacity, blocks):
    dims = (2 * capacity * blocks, stride * blocks)
    row = lax.broadcasted_iota(jnp.int32, dims, 0)
    column = lax.broadcasted_iota(jnp.int32, dims, 1)
    half = capacity * blocks
    slot = row % capacity + row // half * capacity
    start = row % half // capacity * stride
    wide = (start + slot == column).astype(bf16)
    at_last = start + 2 * capacity + slot // 2 == column
    even = (at_last & (slot % 2 == 0)).astype(bf16)
    odd = (at_last & (slot % 2 == 1)).astype(bf16)
    return wide, even, odd


def unpack_kernel(arrived, out, *, stride, capacity):
    blocks = 16
    third = arrived.shape[1] // 2
    slots = out.shape[0] // 2
    wide, even, odd = slot_rows(stride, capacity, blocks)
    size = capacity * blocks
    for group in range(slots // size):
        packed = arrived[group * stride * blocks : (group + 1) * stride * blocks, :]
        last = dot_nn(even, packed[:, :third]) + dot_nn(odd, packed[:, third:])
        rows = jnp.concatenate([dot_nn(wide, packed), last], axis=1).astype(bf16)
        out[group * size : (group + 1) * size, :] = rows[:size, :]
        out[slots + group * size : slots + (group + 1) * size, :] = rows[size:, :]


def expert_kernel(
    moves, mine, other, w_gate, w_up, w_down, in_o, grad_o, act_o, gate_o, up_o, ours_o, theirs_o
):
    slots = mine.shape[0] // 2
    in_o[:slots, :] = mine[:slots, :]
    in_o[slots:, :] = other[:slots, :]
    grad_o[:slots, :] = mine[slots:, :]
    grad_o[slots:, :] = other[slots:, :]
    moves.need(w_gate)
    gate_in = dot_nn(in_o[...], w_gate[...])
    moves.need(w_up)
    up_in = dot_nn(in_o[...], w_up[...])
    moves.done(in_o)
    sig = jax.nn.sigmoid(gate_in)
    silu = gate_in * sig
    act = (silu * up_in).astype(bf16)
    act_o[...] = act
    moves.need(w_down)
    outputs = dot_nn(act, w_down[...])
    ours_o[:slots, :] = outputs[:slots, :]
    theirs_o[:slots, :] = outputs[slots:, :].astype(bf16)
    act_grad = dot_nt(grad_o[...], w_down[...])
    moves.done(grad_o, act_o)
    gate_grad = (act_grad * up_in * sig * (1.0 + gate_in * (1.0 - sig))).astype(bf16)
    up_grad = (act_grad * silu).astype(bf16)
    gate_o[...] = gate_grad
    up_o[...] = up_grad
    total = dot_nt(gate_grad, w_gate[...]) + dot_nt(up_grad, w_up[...])
    ours_o[slots:, :] = total[:slots, :]
    theirs_o[slots:, :] = total[slots:, :].astype(bf16)


def pack_back_kernel(ours, theirs, out, *, stride, capacity):
    blocks = 16
    third = out.shape[1] // 2
    slots = ours.shape[0] // 2
    wide, even, odd = slot_rows(stride, capacity, blocks)
    size = capacity * blocks
    for group in range(slots // size):
        first = slice(group * size, (group + 1) * size)
        second = slice(slots + group * size, slots + (group + 1) * size)
        rows = jnp.concatenate([ours[first, :], ours[second, :]], axis=0) + jnp.concatenate(
            [theirs[first, :], theirs[second, :]], axis=0
        ).astype(f32)
        rows = rows.astype(bf16)
        narrow = rows[:, 2 * third :]
        last = jnp.concatenate([dot_tn(even, narrow), dot_tn(odd, narrow)], axis=1)
        out[group * stride * blocks : (group + 1) * stride * blocks, :] = (
            dot_tn(wide, rows[:, : 2 * third]) + last
        ).astype(bf16)


def aside_kernel(
    moves, core, side, zm, zo, aux, pre, gate_z, scanned, ggrad, combined, middle, meta,
    out_o, comb_o, skip_o, ngrad_o, *, width, span
):
    rows, di = pre.shape
    half = zm.shape[1]
    gs = group_of(di)
    pieces = width // 16
    result = (middle[...] + meta[:, 0:1] * meta[:, 1:2] * combined[...]).astype(bf16)
    out_o[...] = dot_tn(token_order(rows), result).astype(bf16)
    def gating(g, carry):
        mine, other = carry
        lanes = pl.ds(pl.multiple_of(g * gs, gs), gs)
        grad = ggrad[:, lanes]
        z = gate_z[:, lanes]
        sig = jax.nn.sigmoid(z)
        here = scanned[:, lanes]
        zgrad = grad * here * sig * (1.0 + z * (1.0 - sig))
        z_low = zgrad.astype(bf16)
        z_turned = zgrad.T.astype(bf16)
        gated_turned = (here * (z * sig) * aux[:, 3:4]).T.astype(bf16)
        for i in range(gs // 16):
            piece = g * (gs // 16) + i
            to = pl.multiple_of(piece // pieces * span + piece % pieces * 16, 16)
            comb_o[pl.ds(to, 16), :] = z_turned[i * 16 : (i + 1) * 16, :]
            owner = piece // pieces
            holder = owner // 2 * 2 + side[0]
            to = holder * span + (1 + owner % 2) * width + piece % pieces * 16
            comb_o[pl.ds(pl.multiple_of(to, 16), 16), :] = gated_turned[i * 16 : (i + 1) * 16, :]
        pre_here = pre[:, lanes]
        act = pre_here * jax.nn.sigmoid(pre_here)
        skip_o[:, lanes] = jnp.sum(grad * (z * sig) * act, axis=0, keepdims=True)
        return (mine + dot_nn(z_low, zm[lanes, :]), other + dot_nn(z_low, zo[lanes, :]))

    moves.need(zm, zo)
    zero = jnp.zeros((rows, half), f32)
    mine, other = lax.fori_loop(0, di // gs, gating, (zero, zero))
    ngrad_o[0] = mine
    ngrad_o[1] = other


def scan_kernel(
    moves, place, xd, par, sd, q, pre, steps, sig_step, small, x_in, tpre, entry, y_in, tsuf, arrived, near,
    sgrad, cgrad_o, xd_o, spar_o, router_o, bw_s, cw_s, bacc_s, cacc_s, st_s, dk_s, sgr_s, asc_s, plow_s,
    rate_s, after_s, *, rank, count
):
    rows, di = pre.shape
    negative_rates(par, rate_s)
    after_s[...] = jnp.zeros_like(after_s)
    groups = arrived.shape[0] // count
    members = near.shape[0] // count
    spread_columns(small[...], rank, count, bw_s)
    spread_columns(small[...], rank + count, count, cw_s)
    bacc_s[...] = jnp.zeros_like(bacc_s)
    cacc_s[...] = jnp.zeros_like(cacc_s)
    spar_o[...] = jnp.zeros_like(spar_o)
    moves.need(arrived, near)

    def after_here(i, _):
        block = pl.ds(pl.multiple_of((groups - 1 - i) * count, count), count)
        carry_step(step_sums(arrived, block, di), arrived[block, :di], rate_s, after_s)
        return 0

    def just_after(i, _):
        block = pl.ds(pl.multiple_of((members - 1 - i) * count, count), count)
        carry_step(step_sums(near, block, di), near[block, :di], rate_s, after_s)
        return 0

    lax.fori_loop(0, groups - 1 - place[0] // members, after_here, 0)
    lax.fori_loop(0, members - 1 - place[0] % members, just_after, 0)
    router_sum = jnp.zeros(router_o.shape, f32)
    for there in range(groups):
        router_sum += arrived[there * count : (there + 1) * count, di + 256 :].astype(f32)
    router_o[...] = router_sum
    steps_in = rows // SUB
    gs = group_of(di)
    moves.need(x_in, sd, q, sgrad, y_in)

    def scan(g, _):
        lanes = pl.ds(pl.multiple_of(g * 128, 128), 128)
        rates = [
            jnp.broadcast_to(rate_s[n : n + 1, lanes], (SUB, 128)) for n in range(count)
        ]
        before = tpre[:, lanes]
        behind = tsuf[:, lanes]
        first = tuple(
            x_in[n, :, lanes] + jnp.exp2(rates[n] * before) * entry[n : n + 1, lanes]
            for n in range(count)
        )

        def forward(j, states):
            at = pl.ds(pl.multiple_of(j * SUB, SUB), SUB)
            sd_here = sd[at, lanes]
            q_here = q[at, lanes]
            fresh = []
            for n in range(count):
                decay = jnp.exp2(sd_here * rates[n])
                dk_s[j * count + n] = decay
                st_s[j * count + n] = states[n]
                fresh.append(decay * states[n] + q_here * bw_s[j * count + n])
            return tuple(fresh)

        last = lax.fori_loop(0, steps_in, forward, first, unroll=4)
        for n in range(count):
            st_s[steps_in * count + n] = last[n]
        zero = jnp.zeros((SUB, 128), f32)
        arriving = tuple(
            y_in[n, :, lanes] + jnp.exp2(rates[n] * behind) * after_s[n : n + 1, lanes]
            for n in range(count)
        )

        def backward(i, carry):
            grads, rate_grads = carry
            j = steps_in - 1 - i
            at = pl.ds(pl.multiple_of(j * SUB, SUB), SUB)
            sd_here = sd[at, lanes]
            q_here = q[at, lanes]
            sg = sgrad[at, lanes]
            onto = zero
            along = zero
            fresh = []
            fresh_rates = []
            for n in range(count):
                k = j * count + n
                lam = grads[n] + sg * cw_s[k]
                cacc_s[k] += sg * st_s[k + count]
                bacc_s[k] += lam * q_here
                onto = onto + lam * bw_s[k]
                carried = lam * dk_s[k]
                logs = carried * st_s[k]
                along = along + logs * rates[n]
                fresh.append(carried)
                fresh_rates.append(rate_grads[n] + logs * sd_here)
            sgr_s[at, lanes] = along
            asc_s[at, lanes] = onto
            return (tuple(fresh), tuple(fresh_rates))

        _, rate_grads = lax.fori_loop(0, steps_in, backward, (arriving, (zero,) * count), unroll=2)
        for n in range(count):
            spar_o[8 + n : 9 + n, lanes] = LN2 * jnp.sum(
                rate_grads[n] * rates[n], axis=0, keepdims=True
            )
        return 0

    lax.fori_loop(0, di // 128, scan, 0)

    moves.need(pre, sig_step, xd, steps)
    lane8 = lax.broadcasted_iota(jnp.int32, (SUB, 128), 1)
    blocks = []
    for j in range(steps_in):
        block = jnp.zeros((SUB, 128), f32)
        for n in range(count):
            k = j * count + n
            block = jnp.where(
                lane8 == rank + n, jnp.sum(bacc_s[k], axis=1, keepdims=True), block
            )
            block = jnp.where(
                lane8 == rank + count + n, jnp.sum(cacc_s[k], axis=1, keepdims=True), block
            )
        blocks.append(block)
    coef_grad = jnp.concatenate(blocks, axis=0)
    lane = lax.broadcasted_iota(jnp.int32, (rows, 128), 1)
    step_low = jnp.where(
        lane >= 128 - rank, pltpu.roll(small[...], 128 - rank, 1), 0.0
    ).astype(bf16)

    def steps_back(g, total):
        lanes = pl.ds(pl.multiple_of(g * gs, gs), gs)
        pre_here = pre[:, lanes]
        act = pre_here * jax.nn.sigmoid(pre_here)
        pre_grad = (LN2 * sgr_s[:, lanes] + act * asc_s[:, lanes]) * sig_step[:, lanes]
        spar_o[KC + 1 : KC + 2, lanes] = jnp.sum(pre_grad, axis=0, keepdims=True)
        pre_low = pre_grad.astype(bf16)
        plow_s[:, lanes] = pre_low
        return total + dot_nn(pre_low, xd[lanes, :])

    rank_grad = lax.fori_loop(0, di // gs, steps_back, jnp.zeros((rows, 128), f32))
    small_low = jnp.where(lane < rank, pltpu.roll(rank_grad, rank, 1), coef_grad).astype(bf16)

    def act_back(g, _):
        lanes = pl.ds(pl.multiple_of(g * gs, gs), gs)
        pre_here = pre[:, lanes]
        sig = jax.nn.sigmoid(pre_here)
        act_low = (pre_here * sig).astype(bf16)
        total = (
            sgrad[:, lanes] * par[KC + 2 : KC + 3, lanes]
            + steps[:, lanes] * asc_s[:, lanes]
            + dot_nt(small_low, xd[lanes, :])
        )
        cgrad_o[:, lanes] = total * sig * (1.0 + pre_here * (1.0 - sig))
        xd_o[lanes, :] = (dot_tn(act_low, small_low) + dot_tn(plow_s[:, lanes], step_low)).astype(bf16)
        return 0

    lax.fori_loop(0, di // gs, act_back, 0)


def last_kernel(
    moves, core, cgrad, halo, aux, ext, par, wm, wo, ngrad_z, spar, skip, xd, hid, gain_two,
    router_sum, pay_o, ngrad_o, extra_o, low_s, far_s, *, width
):
    rows, di = cgrad.shape
    half = wo.shape[1] - 128
    gs = 128
    ahead_lane = spar.shape[0] + 4 * (hid.shape[1] // width)
    moves.need(xd)

    def conv(g, _):
        lanes = pl.ds(pl.multiple_of(g * gs, gs), gs)
        cg = cgrad[:, lanes]
        grad = par[KC - 1 : KC, lanes] * cg
        parts = [jnp.sum(cg * ext[(KC - 1) * SUB :, lanes], axis=0, keepdims=True)]
        zero = jnp.zeros((1, gs), f32)
        behind = [zero] * (KC - 1)
        for ahead in range(1, KC):
            tap = par[KC - 1 - ahead : KC - ahead, lanes]
            masked = cg * aux[:, ahead - 1 : ahead]
            shifted = ext[(KC - 1 - ahead) * SUB : (KC - 1 - ahead) * SUB + rows, lanes]
            parts.append(jnp.sum(masked * shifted, axis=0, keepdims=True))
            pieces = [masked[ahead * SUB :, :]]
            for i in range(ahead):
                pieces.append(from_after(masked[i * SUB : (i + 1) * SUB, :], zero))
                k = KC - 1 - ahead + i
                behind[k] = behind[k] + tap * masked[i * SUB : i * SUB + 1, :]
            grad = grad + tap * jnp.concatenate(pieces, axis=0)
        low_s[:, lanes] = grad.astype(bf16)
        pay_o[lanes, 0:128] = grad.T.astype(bf16)
        pay_o[lanes, 128:256] = xd[lanes, :]
        extra = jnp.concatenate(behind + [jnp.zeros((SUB - KC + 1, gs), f32)], axis=0)
        far_s[:SUB, lanes] = extra.astype(bf16)
        own = jnp.concatenate(
            parts[::-1]
            + [jnp.sum(cg, axis=0, keepdims=True), spar[KC + 1 : KC + 2, lanes], skip[:, lanes]]
            + [zero, spar[8:, lanes], jnp.zeros((ahead_lane - spar.shape[0], gs), f32), extra]
            + [jnp.zeros((128 - ahead_lane - SUB, gs), f32)],
            axis=0,
        )
        pay_o[lanes, 256:384] = own.T.astype(bf16)
        return 0

    lax.fori_loop(0, di // gs, conv, 0)
    far_s[SUB:, :] = jnp.zeros_like(far_s[SUB:, :])
    moves.need(wm, wo, ngrad_z, hid)
    low = core[0] == 0

    def onto_inputs(values):
        mine = dot_nn(values, wm[:, :half])
        other = dot_nn(values, wo[:, :half])
        return mine, other

    def joined(mine, other):
        return jnp.concatenate([jnp.where(low, mine, other), jnp.where(low, other, mine)], axis=1)

    mine, other = onto_inputs(low_s[...])
    ngrad = joined(mine + ngrad_z[0], other + ngrad_z[1])
    ngrad_o[...] = ngrad
    far = joined(*onto_inputs(far_s[...]))[:SUB, :]
    extra_o[...] = far
    first = hid[...].astype(f32)
    scale = lax.rsqrt(jnp.mean(first * first, axis=1, keepdims=True) + epsilon)
    gains = jnp.sum(ngrad * first * scale, axis=0, keepdims=True)
    first = halo[SUB:, :].astype(f32)
    scale = lax.rsqrt(jnp.mean(first * first, axis=1, keepdims=True) + epsilon)
    gains = gains + jnp.sum(far * first * scale, axis=0, keepdims=True)
    model = first.shape[1]
    each = model // width
    row = lax.broadcasted_iota(jnp.int32, (width, model), 0)
    column = lax.broadcasted_iota(jnp.int32, (width, model), 1)
    here = column // each == row
    extra = jnp.zeros((width, 128), f32)
    router_row = jnp.concatenate([router_sum[0:1, :], router_sum[1:2, :]], axis=1)
    router_top = router_row.astype(bf16).astype(f32)
    rows_sent = (gains, gain_two[...], router_top, router_row - router_top)
    for k, values in enumerate(rows_sent):
        spread = jnp.where(here, values, 0.0).astype(bf16)
        at = lax.broadcasted_iota(jnp.int32, (model, 128), 0)
        to = lax.broadcasted_iota(jnp.int32, (model, 128), 1)
        placed = (at % each + spar.shape[0] + k * each == to).astype(bf16)
        extra = extra + dot_nn(spread, placed)
    extra = extra.astype(bf16)
    for place in range(di // width):
        pay_o[place * width : (place + 1) * width, 256:384] += extra


def hidden_kernel(ngrad_in, beyond, hid, mgrad, gain, first_o):
    first = hid[...].astype(f32)
    rows = first.shape[0]
    ngrad = ngrad_in[...]
    row = lax.broadcasted_iota(jnp.int32, first.shape, 0)
    for i in range(KC - 1):
        at = rows - 1 - (KC - 2 - i) * SUB
        ngrad = ngrad + jnp.where(row == at, beyond[i : i + 1, :], 0.0)
    scale = lax.rsqrt(jnp.mean(first * first, axis=1, keepdims=True) + epsilon)
    scaled = gain[...].reshape(1, -1) * ngrad
    cube = scale * scale * scale
    grad = (
        mgrad[...] + scale * scaled - first * cube * jnp.mean(first * scaled, axis=1, keepdims=True)
    )
    order = token_order(rows)
    top = grad.astype(bf16)
    left = grad - top.astype(f32)
    mid = left.astype(bf16)
    low_part = (left - mid.astype(f32)).astype(bf16)
    first_o[...] = dot_tn(order, top) + dot_tn(order, mid) + dot_tn(order, low_part)


def ready_kernel(
    moves, side, comb, nrm_all, mix_half, z_o, mine_o, theirs_o, z_s, gated_s
):
    places = comb.shape[0]
    width = z_o.shape[0]
    for place in range(places):
        z_s[:, place * 128 : (place + 1) * 128] = comb[place, :width, :]
    for k in range(places // 2):
        place = 2 * k + side[0]
        gated_s[:, k * 128 : (k + 1) * 128] = comb[place, width : 3 * width, :]
    moves.need(mix_half)
    grads = dot_nn(gated_s[...], mix_half[...]).astype(bf16)
    first = side[0] == 0
    mine_o[...] = jnp.where(first, grads[:width, :], grads[width:, :])
    theirs_o[...] = jnp.where(first, grads[width:, :], grads[:width, :])
    moves.need(nrm_all)
    z_o[...] = dot_nn(z_s[...], nrm_all[...]).astype(bf16)


def grads_kernel(moves, got, nrm_all, out_o, left_s, *, base):
    places, width, _ = got.shape
    model = nrm_all.shape[1]
    each = model // width
    rest = jnp.zeros((width, 256), f32)
    routers = [jnp.zeros((width, 128), f32) for _ in range(places * each // 128)]
    lane = lax.broadcasted_iota(jnp.int32, (width, 128), 1)
    row = lax.broadcasted_iota(jnp.int32, (128, 128), 0)
    column = lax.broadcasted_iota(jnp.int32, (128, 128), 1)
    after = row - (base + 2 * each)
    late = column == 127 - (KC - 2 - after) * SUB
    placed = (late & (after >= 0) & (after < KC - 1)).astype(bf16)
    for place in range(places):
        at = gathered_place(place)
        inner = got[at, :, :128]
        if place + 1 < places:
            beyond = dot_nn(got[gathered_place(place + 1), :, 256:384], placed)
            inner = (inner.astype(f32) + beyond).astype(bf16)
        left_s[:, at * 128 : (at + 1) * 128] = inner
        there = got[at, :, 128:].astype(f32)
        rest = rest + there
        k = place * each // 128
        inside = place * each % 128
        mine = (lane >= inside) & (lane < inside + each)
        for part in range(2):
            turn = (inside - base - part * each) % 128
            routers[k] = routers[k] + jnp.where(mine, pltpu.roll(there[:, 128:], turn, 1), 0.0)
    out_o[width:, :256] = rest.astype(bf16)
    out_o[width:, 256:] = jnp.concatenate(routers, axis=1).astype(bf16)
    moves.need(nrm_all)
    out_o[:width, :model] = dot_nn(left_s[...], nrm_all[...]).astype(bf16)


def token_order(rows):
    steps_in = rows // SUB
    row = lax.broadcasted_iota(jnp.int32, (rows, rows), 0)
    column = lax.broadcasted_iota(jnp.int32, (rows, rows), 1)
    return ((row % SUB) * steps_in + row // SUB == column).astype(bf16)


def final_kernel(
    ours, theirs, ours_two, theirs_two, x_o, z_o, out_o, conv_o, bias_o, xp_o, dt_o, db_o, al_o, skip_o, router_o, one_o,
    two_o, mine_s, other_s, *, rank, count, experts
):
    width = out_o.shape[0]
    model = router_o.shape[1]
    each = model // width
    x_o[...] = ours[:width, :model].astype(f32) + theirs[:width, :model].astype(f32)
    z_o[...] = ours_two[:width, :].astype(f32) + theirs_two[:width, :].astype(f32)
    out_o[...] = ours_two[width:, :].astype(f32) + theirs_two[width:, :].astype(f32)
    rest = slice(width, 2 * width)
    xd = ours[rest, :128].astype(f32) + theirs[rest, :128].astype(f32)
    xp_o[...] = xd[:, : rank + 2 * count]
    gap = jnp.zeros((128 - width, 128), f32)
    turned = jnp.concatenate([xd, gap], axis=0).T
    dt_o[...] = turned[128 - rank :, :width]
    vectors = jnp.zeros((128, 128), f32)
    for part, held in ((ours, mine_s), (theirs, other_s)):
        block = jnp.concatenate([part[rest, 128:256].astype(f32), gap], axis=0).T
        vectors = vectors + block
        for k in range(experts * each // 128):
            lanes = slice(256 + k * 128, 384 + k * 128)
            piece = jnp.concatenate([part[rest, lanes].astype(f32), gap], axis=0)
            held[k * 128 : (k + 1) * 128, :] = piece.T
        held[experts * each :, :] = jnp.zeros_like(held[experts * each :, :])
        held[experts * each : (experts + 2) * each, :] = block[8 + count : 8 + count + 2 * each, :]
    conv_o[...] = vectors[:KC, :width]
    bias_o[...] = vectors[KC : KC + 1, :width].reshape(width)
    db_o[...] = vectors[KC + 1 : KC + 2, :width].reshape(width)
    skip_o[...] = vectors[KC + 2 : KC + 3, :width].reshape(width)
    al_o[...] = vectors[8 : 8 + count, :width]
    row = lax.broadcasted_iota(jnp.int32, (128, model), 0)
    column = lax.broadcasted_iota(jnp.int32, (128, model), 1)
    total = jnp.zeros((experts + 8, model), f32)
    for at in range(each):
        to = (row * each + at == column).astype(bf16)
        picked = pl.ds(at, experts + 8, stride=each)
        total = total + dot_nn(mine_s[picked, :].astype(bf16), to)
        total = total + dot_nn(other_s[picked, :].astype(bf16), to)
    router_o[...] = total[:experts, :]
    one_o[...] = total[experts : experts + 1, :].reshape(model)
    two_o[...] = total[experts + 1 : experts + 2, :].reshape(model)


def token_order(rows):
    steps_in = rows // SUB
    row = lax.broadcasted_iota(jnp.int32, (rows, rows), 0)
    column = lax.broadcasted_iota(jnp.int32, (rows, rows), 1)
    return ((row % SUB) * steps_in + row // SUB == column).astype(bf16)


def exchange(values):
    return lax.all_to_all(values, "wide", split_axis=0, concat_axis=0, tiled=True)


def exchange_near(values, members):
    groups = [[u * members + z for z in range(members)] for u in range(32 // members)]
    blocks = values.reshape(members, -1, values.shape[1])
    return lax.all_to_all(
        blocks, "wide", split_axis=0, concat_axis=0, tiled=True, axis_index_groups=groups
    ).reshape(values.shape)


def exchange_far(values, members):
    groups = [[u * members + z for u in range(32 // members)] for z in range(members)]
    blocks = values.reshape(32 // members, -1, values.shape[1])
    return lax.all_to_all(
        blocks, "wide", split_axis=0, concat_axis=0, tiled=True, axis_index_groups=groups
    ).reshape(values.shape)


def gathered_place(place):
    return (place // 8 * 4 + place % 4) * 2 + place // 4 % 2


def exchange_channels(values):
    order = sorted(range(32), key=gathered_place)
    return lax.all_to_all(
        values, "wide", split_axis=0, concat_axis=0, tiled=True, axis_index_groups=[order]
    )


def other_chip(values):
    return lax.ppermute(values, "wide", [(i, i ^ 4) for i in range(32)])


def pair_up(values, partner, place):
    first = (place // 4) % 2 == 0
    return jnp.concatenate(
        [jnp.where(first, values, partner), jnp.where(first, partner, values)], axis=0
    )


def gather_pairs(both):
    groups = [[(y * 2 + x) * 4 + z for y in range(4) for z in range(4)] for x in range(2)]
    return lax.all_gather(both, "wide", axis=0, tiled=True, axis_index_groups=groups)


def exchange_sides(values):
    groups = [
        [(side * 2 + core) * 32 + place for side in range(2) for place in range(32)]
        for core in range(2)
    ]
    return lax.all_to_all(
        values, ("dp", "wide"), split_axis=0, concat_axis=0, tiled=True, axis_index_groups=groups
    )


def other_core(values):
    return lax.ppermute(values, "dp", [(0, 1), (1, 0), (2, 3), (3, 2)])


def other_side(values):
    return lax.ppermute(values, "dp", [(0, 2), (2, 0), (1, 3), (3, 1)])


def body(
    hidden, cotangent, routes, seg_lengths, gain_mix, in_x, in_z, conv_w, conv_b, x_proj, dt_proj,
    dt_bias, a_log, skip_d, out_proj, gain_moe, router, w_gate, w_up, w_down,
):
    rows, model = hidden.shape
    places = lax.axis_size("wide")
    place = lax.axis_index("wide")
    core = (lax.axis_index("dp") % 2).astype(jnp.int32).reshape(1)
    place_arr = place.astype(jnp.int32).reshape(1)
    width = in_x.shape[1]
    di = width * places
    count = a_log.shape[0]
    rank = dt_proj.shape[0]
    experts = router.shape[1]
    capacity = max(CAP * rows // (4 * places), 2)
    stride = -(-2 * capacity // 16) * 16
    half = model // 2
    steps_in = rows // SUB
    shift = SUB.bit_length() - 1
    span = 3 * width
    members = 4
    side = (place // 4 % 2).astype(jnp.int32).reshape(1)

    pay_one, gate_share = call(
        partial(pack_kernel, places=places),
        [shape((di, half + 128), bf16), shape((width, model), bf16)],
        [],
        (
            core, in_x.T, x_proj, dt_proj, conv_w, conv_b, dt_bias, skip_d, a_log, in_z.T, out_proj,
        ),
        smem=1,
    )
    pay_one, hidden, cotangent, routes, seg_lengths = lax.optimization_barrier(
        (pay_one, hidden, cotangent, routes, seg_lengths)
    )
    gate_partner = other_chip(gate_share)
    pay_one, gate_partner = lax.optimization_barrier((pay_one, gate_partner))
    wm = exchange_channels(pay_one.reshape(places, width, half + 128)).reshape(di, half + 128)
    zm = gather_pairs(pair_up(gate_share, gate_partner, place))
    nrm, tail, hid, cot, route, aux = call(
        prepare_kernel,
        [
            shape((rows, model), bf16),
            shape((16, model), bf16),
            shape((rows, model), bf16),
            shape((rows, model), bf16),
            shape((rows, 1), jnp.int32),
            shape((rows, 128)),
        ],
        [],
        (place_arr * rows, seg_lengths, hidden, cotangent, routes.T, gain_mix),
        smem=2,
    )
    halo = lax.ppermute(tail, "wide", [(i, i + 1) for i in range(places - 1)])
    nrm_partner = other_chip(nrm)
    wm, halo = lax.optimization_barrier((wm, halo))
    wo = other_core(wm)
    ext, pre, steps, sig_step, small, x_in, tpre, tsuf, states, par, xd_weight, sd, q = call(
        partial(front_kernel, rank=rank, count=count),
        [
            shape((rows + (KC - 1) * SUB, di)),
            shape((rows, di)),
            shape((rows, di)),
            shape((rows, di)),
            shape((rows, 128)),
            shape((count, SUB, di)),
            shape((SUB, di)),
            shape((SUB, di)),
            shape((members * count, di + 256), bf16),
            shape((8 + count, di)),
            shape((di, 128), bf16),
            shape((rows, di)),
            shape((rows, di)),
        ],
        [
            pltpu.VMEM((steps_in * count, SUB, 128), f32),
            pltpu.VMEM((2, rows + 16, half), bf16),
            pltpu.VMEM((16, 128), f32),
        ],
        (core, nrm, halo, wm, wo, aux),
        smem=1,
        late=(3, 4),
        early=(0, 1, 2, 3, 9, 10, 11, 12),
    )

    near = exchange_near(states, members)
    zm, nrm_partner, near = lax.optimization_barrier((zm, nrm_partner, near))
    zo = other_core(zm)
    z_lanes = pl.ds(0, half)
    out_lanes = pl.ds(half, half)
    gate_z = call(
        gate_kernel,
        [shape((rows, di))],
        [pltpu.VMEM((2, rows, half), bf16)],
        (core, nrm, zm, zo),
        smem=1,
        late=(2, 3),
        lanes={2: z_lanes, 3: z_lanes},
    )[0]
    states = call(
        partial(forward_group_kernel, di=di, count=count),
        [shape((places // members * count, di + 256), bf16)],
        [pltpu.VMEM((count, di), f32)] * 2,
        (near, par),
    )[0]
    states = exchange_far(states, members)

    nrm_pair = pair_up(nrm, nrm_partner, place)
    states, gate_z, nrm_pair = lax.optimization_barrier((states, gate_z, nrm_pair))
    normed_all = gather_pairs(nrm_pair)
    scanned, send, middle, ntwo, chances, meta, hot, entry = call(
        partial(
            middle_kernel,
            rank=rank,
            count=count,
            experts=experts,
            stride=stride,
            capacity=capacity,
            shift=shift,
        ),
        [
            shape((rows, di)),
            shape((2 * experts * stride, 2 * model // 3), bf16),
            shape((rows, model)),
            shape((rows, model), bf16),
            shape((rows, experts)),
            shape((rows, 8)),
            shape((3, 2 * rows, experts * stride), bf16),
            shape((count, di)),
        ],
        [
            pltpu.VMEM((steps_in * count, SUB, 128), f32),
            pltpu.VMEM((steps_in * count, SUB, 128), f32),
            pltpu.VMEM((count, di), f32),
        ],
        (
            core, place_arr, zm, zo, par, aux, pre, sd, q, x_in, small, states, near, tpre, hid, cot,
            route, gain_moe, router.T, gate_z,
        ),
        smem=2,
        late=(11, 12, 9, 7, 8, 6, 19, 2, 3),
        early=(7, 0),
        lanes={2: out_lanes, 3: out_lanes},
    )
    arrived = exchange_sides(send.reshape(2 * experts, stride, -1)).reshape(send.shape)
    slots = 2 * places * capacity
    mine = call(
        partial(unpack_kernel, stride=stride, capacity=capacity),
        [shape((2 * slots, model), bf16)],
        [],
        (arrived,),
    )[0]
    expert_in, grad_rows, hidden_act, gate_grad, up_grad, ours, theirs = call(
        expert_kernel,
        [shape((2 * slots, model), bf16)] * 2
        + [shape((2 * slots, w_gate.shape[2]), bf16)] * 3
        + [shape((2 * slots, model)), shape((2 * slots, model), bf16)],
        [],
        (mine, other_core(mine), w_gate[0], w_up[0], w_down[0]),
        late=(2, 3, 4),
        early=(0, 1, 2, 3, 4, 5, 6),
    )
    back = call(
        partial(pack_back_kernel, stride=stride, capacity=capacity),
        [shape(send.shape, bf16)],
        [],
        (ours, other_core(theirs)),
    )[0]
    back = exchange_sides(back.reshape(2 * experts, stride, -1)).reshape(send.shape)
    grad_w_down = dot_tn(hidden_act, grad_rows)[None]
    grad_w_gate = dot_tn(expert_in, gate_grad)[None]
    grad_w_up = dot_tn(expert_in, up_grad)[None]
    back, grad_w_down, grad_w_gate, grad_w_up = lax.optimization_barrier(
        (back, grad_w_down, grad_w_gate, grad_w_up)
    )

    combined, mixlow, mgrad, ggrad, sgrad, gain_two, y_in, adjoints = call(
        partial(back_kernel, rank=rank, count=count, experts=experts),
        [
            shape((rows, model)),
            shape((rows, model), bf16),
            shape((rows, model)),
            shape((rows, di)),
            shape((rows, di)),
            shape((1, model)),
            shape((count, SUB, di)),
            shape((members * count, di + 256 + half), bf16),
        ],
        [
            pltpu.VMEM((steps_in * count, SUB, 128), f32),
            pltpu.VMEM((2, rows, half), bf16),
            pltpu.VMEM((count, di), f32),
            pltpu.VMEM((16, 128), f32),
        ],
        (
            core, back, zm, zo, par, aux, sd, small, gate_z, hot, middle, meta, chances, route,
            cot, gain_moe, router.T, ntwo,
        ),
        smem=1,
        late=(2, 3, 8, 6),
        early=(1, 2, 0, 3, 4),
        lanes={2: out_lanes, 3: out_lanes},
    )
    near_back = exchange_near(adjoints, members)
    adjoints = call(
        partial(backward_group_kernel, di=di, count=count),
        [shape((places // members * count, di + 256 + half), bf16)],
        [pltpu.VMEM((count, di), f32)] * 2,
        (near_back, par),
    )[0]
    adjoints = exchange_far(adjoints, members)
    out, comb, skip_part, ngrad_z = call(
        partial(aside_kernel, width=width, span=span),
        [
            shape((rows, model), bf16),
            shape((places * span, 128), bf16),
            shape((1, di)),
            shape((2, rows, half)),
        ],
        [],
        (
            core, side, zm, zo, aux, pre, gate_z, scanned, ggrad, combined, middle, meta,
        ),
        smem=2,
        late=(2, 3),
        lanes={2: z_lanes, 3: z_lanes},
    )
    adjoints, comb = lax.optimization_barrier((adjoints, comb))
    mixlow, normed_all = lax.optimization_barrier((mixlow, normed_all))
    mix_half = gather_pairs(mixlow)
    comb_got = exchange_channels(comb.reshape(places, span, 128))

    cgrad, xd, spar, router_sum = call(
        partial(scan_kernel, rank=rank, count=count),
        [shape((rows, di)), shape((di, 128), bf16), shape((8 + count, di)), shape((count, half))],
        [pltpu.VMEM((steps_in * count, SUB, 128), f32)] * 4
        + [pltpu.VMEM(((steps_in + 1) * count, SUB, 128), f32)]
        + [pltpu.VMEM((steps_in * count, SUB, 128), f32)]
        + [pltpu.VMEM((rows, di), f32)] * 2
        + [pltpu.VMEM((rows, di), bf16)]
        + [pltpu.VMEM((count, di), f32)] * 2,
        (
            place_arr, xd_weight, par, sd, q, pre, steps, sig_step, small, x_in, tpre, entry, y_in,
            tsuf, adjoints, near_back, sgrad,
        ),
        smem=1,
        late=(14, 15, 9, 3, 4, 16, 12, 5, 7, 1, 6),
    )
    pay, ngrad, beyond = call(
        partial(last_kernel, width=width),
        [shape((di, 384), bf16), shape((rows, model)), shape((SUB, model))],
        [pltpu.VMEM((rows, di), bf16), pltpu.VMEM((16, di), bf16)],
        (
            core, cgrad, halo, aux, ext, par, wm, wo, ngrad_z, spar, skip_part, xd, hid, gain_two,
            router_sum,
        ),
        smem=1,
        late=(11, 6, 7, 8, 12),
    )
    got_pay = exchange_channels(pay.reshape(places, width, 384))
    beyond = lax.ppermute(beyond, "wide", [(i + 1, i) for i in range(places - 1)])
    z_ready, out_ready, out_theirs = call(
        ready_kernel,
        [shape((width, model), bf16)] * 3,
        [
            pltpu.VMEM((width, places * rows), bf16),
            pltpu.VMEM((2 * width, places // 2 * rows), bf16),
        ],
        (side, comb_got, normed_all, mix_half),
        smem=1,
        late=(3, 2),
    )
    beyond, z_ready = lax.optimization_barrier((beyond, z_ready))
    first_grad = call(
        hidden_kernel, [shape((rows, model))], [], (ngrad, beyond, hid, mgrad, gain_mix)
    )[0]
    out_other = other_chip(out_theirs)
    got_pay, out_other, first_grad = lax.optimization_barrier((got_pay, out_other, first_grad))
    out_ready = (out_ready.astype(f32) + out_other.astype(f32)).astype(bf16)
    ready = jnp.concatenate([z_ready, out_ready], axis=0)
    ready = (ready.astype(f32) + other_core(ready).astype(f32)).astype(bf16)
    ready_side = other_side(ready)
    per_place = model // width
    mats = call(
        partial(grads_kernel, base=8 + count + 2 * per_place),
        [shape((2 * width, 256 + places * per_place), bf16)],
        [pltpu.VMEM((width, places * rows), bf16)],
        (got_pay, normed_all),
        late=(1,),
    )[0]
    mats = (mats.astype(f32) + other_core(mats).astype(f32)).astype(bf16)
    grad_x, grad_z, grad_out, grad_conv, grad_bias, grad_xp, grad_dt, grad_db, grad_al, grad_sk, grad_router, gain_one, gain_two = call(
        partial(final_kernel, rank=rank, count=count, experts=experts),
        [
            shape((width, model)),
            shape((width, model)),
            shape((width, model)),
            shape((KC, width)),
            shape((width,)),
            shape((width, rank + 2 * count)),
            shape((rank, width)),
            shape((width,)),
            shape((count, width)),
            shape((width,)),
            shape((experts, model)),
            shape((model,)),
            shape((model,)),
        ],
        [pltpu.VMEM(((experts + 8) * per_place, 128), f32)] * 2,
        (mats, other_side(mats), ready, ready_side),
    )
    return (
        out,
        first_grad,
        gain_one,
        grad_x.T,
        grad_z.T,
        grad_conv,
        grad_bias,
        grad_xp,
        grad_dt,
        grad_db,
        grad_al,
        grad_sk,
        grad_out,
        gain_two,
        grad_router.T,
        grad_w_gate,
        grad_w_up,
        grad_w_down,
    )


def solution(mesh):
    rows = P(("dp", "wide"), None)
    expert_columns = P("wide", None, "dp")
    expert_rows = P("wide", "dp", None)
    placed = (
        rows, rows, rows, P("dp", None), P(), P(None, "wide"), P(None, "wide"), P(None, "wide"),
        P("wide"), P("wide", None), P(None, "wide"), P("wide"), P(None, "wide"), P("wide"),
        P("wide", None), P(), P(), expert_columns, expert_columns, expert_rows,
    )
    given = (
        rows, rows, P(), P(None, "wide"), P(None, "wide"), P(None, "wide"), P("wide"),
        P("wide", None), P(None, "wide"), P("wide"), P(None, "wide"), P("wide"), P("wide", None),
        P(), P(), expert_columns, expert_columns, expert_rows,
    )
    return jax.shard_map(body, mesh=mesh, in_specs=placed, out_specs=given, check_vma=False)
```

```python
from functools import partial

import jax
import jax.numpy as jnp
from jax import lax
from jax.experimental import pallas as pl
from jax.experimental.pallas import tpu as pltpu
from jax.sharding import PartitionSpec as P

f32 = jnp.float32
bf16 = jnp.bfloat16
KC = 4
SUB = 8
CAP = 5
STOP = 1e6
LOG2E = 1.4426950408889634
LN2 = 0.6931471805599453
epsilon = 1e-05
VMEM_LIMIT = 56 * 1024 * 1024


def dot_nn(left, right):
    return lax.dot_general(left, right, (((1,), (0,)), ((), ())), preferred_element_type=f32)


def dot_nt(left, right):
    return lax.dot_general(left, right, (((1,), (1,)), ((), ())), preferred_element_type=f32)


def dot_tn(left, right):
    return lax.dot_general(left, right, (((0,), (0,)), ((), ())), preferred_element_type=f32)


class Moves:
    def __init__(self):
        self.arriving = {}
        self.leaving = {}
        self.started = []

    def need(self, *refs):
        for ref in refs:
            copy = self.arriving.pop(id(ref), None)
            if copy is not None:
                copy.wait()

    def done(self, *refs):
        for ref in refs:
            copy = self.leaving.pop(id(ref), None)
            if copy is not None:
                copy.start()
                self.started.append(copy)


def call(
    kernel, out_shapes, scratch, args, smem=0, late=(), early=(), lanes=None, limit=VMEM_LIMIT
):
    lanes = lanes or {}
    vmem = pl.BlockSpec(memory_space=pltpu.VMEM)
    hbm = pl.BlockSpec(memory_space=pl.ANY)
    specs = [pl.BlockSpec(memory_space=pltpu.SMEM)] * smem
    specs += [hbm if i in late else vmem for i in range(smem, len(args))]
    buffers = []
    for i in late:
        dims = (args[i].shape[0], lanes[i].size) if i in lanes else args[i].shape
        buffers.append(pltpu.VMEM(dims, args[i].dtype))
    buffers += [pltpu.VMEM(out_shapes[i].shape, out_shapes[i].dtype) for i in early]
    moving = len(buffers)
    extra = buffers + [pltpu.SemaphoreType.DMA((moving,))] if moving else []

    def staged(*refs):
        refs = list(refs)
        own = refs[len(refs) - moving - 1 : -1]
        semaphores = refs[-1]
        refs = refs[: len(refs) - moving - 1]
        moves = Moves()
        for k, i in enumerate(late):
            source = refs[i].at[:, lanes[i]] if i in lanes else refs[i]
            copy = pltpu.make_async_copy(source, own[k], semaphores.at[k])
            copy.start()
            refs[i] = own[k]
            moves.arriving[id(own[k])] = copy
        for k, i in enumerate(early, len(late)):
            at = len(args) + i
            moves.leaving[id(own[k])] = pltpu.make_async_copy(own[k], refs[at], semaphores.at[k])
            refs[at] = own[k]
        kernel(moves, *refs)
        moves.need(*own)
        moves.done(*own)
        for copy in moves.started:
            copy.wait()

    return pl.pallas_call(
        staged if moving else kernel,
        out_shape=out_shapes,
        in_specs=specs,
        out_specs=[hbm if i in early else vmem for i in range(len(out_shapes))],
        scratch_shapes=list(scratch) + extra,
        compiler_params=pltpu.CompilerParams(vmem_limit_bytes=limit),
    )(*args)


def shape(dims, dtype=f32):
    return jax.ShapeDtypeStruct(dims, dtype)


def group_of(di):
    return 256 if di % 256 == 0 else 128


def sublane_iota(width):
    return lax.broadcasted_iota(jnp.int32, (SUB, width), 0)


def from_before(block, first):
    row = sublane_iota(block.shape[1])
    return jnp.where(row == 0, jnp.broadcast_to(first, block.shape), pltpu.roll(block, 1, 0))


def from_after(block, last):
    row = sublane_iota(block.shape[1])
    return jnp.where(
        row == SUB - 1, jnp.broadcast_to(last, block.shape), pltpu.roll(block, SUB - 1, 0)
    )


def spread_columns(small, first, count, out):
    steps = small.shape[0] // SUB
    for j in range(steps):
        block = small[j * SUB : (j + 1) * SUB, :]
        for n in range(count):
            out[j * count + n] = jnp.broadcast_to(block[:, first + n : first + n + 1], (SUB, 128))


def prefix_states(decay, state):
    row = sublane_iota(state.shape[1])
    for shift in (1, 2, 4):
        inside = row >= shift
        state = state + decay * jnp.where(inside, pltpu.roll(state, shift, 0), 0.0)
        decay = decay * jnp.where(inside, pltpu.roll(decay, shift, 0), 1.0)
    return state


def suffix_states(decay, state):
    row = sublane_iota(state.shape[1])
    for shift in (1, 2, 4):
        inside = row < SUB - shift
        state = state + decay * jnp.where(inside, pltpu.roll(state, SUB - shift, 0), 0.0)
        decay = decay * jnp.where(inside, pltpu.roll(decay, SUB - shift, 0), 1.0)
    return state


def prefix_sum(values):
    row = sublane_iota(values.shape[1])
    for shift in (1, 2, 4):
        values = values + jnp.where(row >= shift, pltpu.roll(values, shift, 0), 0.0)
    return values


def suffix_sum(values):
    row = sublane_iota(values.shape[1])
    for shift in (1, 2, 4):
        values = values + jnp.where(row < SUB - shift, pltpu.roll(values, SUB - shift, 0), 0.0)
    return values


def one_hot(dims, offset):
    row = lax.broadcasted_iota(jnp.int32, dims, 0)
    column = lax.broadcasted_iota(jnp.int32, dims, 1)
    return (row + offset == column).astype(bf16)


def pack_gate_kernel(core, in_z, out_proj, gate_o):
    half = in_z.shape[1] // 2
    start = pl.multiple_of(core[0] * half, 128)
    gate_o[:, :half] = in_z[:, pl.ds(start, half)]
    gate_o[:, half:] = out_proj[:, pl.ds(start, half)]


def pack_kernel(
    core, in_x, x_proj, dt_proj, conv_w, conv_b, dt_bias, skip_d, a_log, out, *, places
):
    width, model = in_x.shape
    half = model // 2
    here = core[0]
    mine = in_x[:, pl.ds(pl.multiple_of(here * half, 128), half)]
    narrow = x_proj.shape[1]
    steps = dot_nn(x_proj[...], one_hot((narrow, 128), 0)) + dot_tn(
        dt_proj[...], one_hot((dt_proj.shape[0], 128), 128 - dt_proj.shape[0])
    )
    values = jnp.concatenate(
        [
            conv_w[...],
            conv_b[...].reshape(1, width),
            dt_bias[...].reshape(1, width),
            skip_d[...].reshape(1, width),
            jnp.zeros((1, width), f32),
            a_log[...],
        ],
        axis=0,
    )
    top = values.astype(bf16)
    left = values - top.astype(f32)
    mid = left.astype(bf16)
    low = (left - mid.astype(f32)).astype(bf16)
    count = values.shape[0]
    extra = dot_tn(top, one_hot((count, 128), 0))
    extra = extra + dot_tn(mid, one_hot((count, 128), count))
    extra = extra + dot_tn(low, one_hot((count, 128), 2 * count))
    rest = jnp.where(here == 0, steps, extra).astype(bf16)
    for place in range(places):
        out[place * width : (place + 1) * width, :half] = mine
        out[place * width : (place + 1) * width, half:] = rest


def prepare_kernel(
    base, lengths, hidden, cot, route, gain, nrm_o, tail_o, hid_o, cot_o, route_o, aux_o
):
    rows = hidden.shape[0]
    steps_in = rows // SUB
    row = lax.broadcasted_iota(jnp.int32, (rows, rows), 0)
    column = lax.broadcasted_iota(jnp.int32, (rows, rows), 1)
    in_order = (row % SUB) * steps_in + row // SUB == column
    order = in_order.astype(bf16)
    hid = dot_nn(order, hidden[...])
    hid_o[...] = hid.astype(bf16)
    cot_o[...] = dot_nn(order, cot[...]).astype(bf16)
    ours = jnp.where(in_order, jnp.broadcast_to(route[...], (rows, rows)), 0)
    route_o[...] = jnp.sum(ours, axis=1, keepdims=True)
    scale = lax.rsqrt(jnp.mean(hid * hid, axis=1, keepdims=True) + epsilon)
    normed = (hid * scale * gain[...].reshape(1, -1)).astype(bf16)
    nrm_o[...] = normed
    tail_row = lax.broadcasted_iota(jnp.int32, (16, rows), 0)
    tail_column = lax.broadcasted_iota(jnp.int32, (16, rows), 1)
    picked = (tail_column == rows - 1 - (KC - 2 - tail_row) * SUB) & (tail_row < KC - 1)
    tail = dot_nn(picked.astype(bf16), normed)
    tail_row = tail_row - SUB
    picked = (tail_column == rows - 1 - (KC - 2 - tail_row) * SUB) & (tail_row < KC - 1)
    picked = picked & (tail_row >= 0)
    tail_o[...] = (tail + dot_nn(picked.astype(bf16), hid.astype(bf16))).astype(bf16)

    def layout(position, lane):
        back = position - (lane + 1)
        segment = jnp.zeros_like(position)
        segment_back = jnp.zeros_like(position)
        reset = position == 0
        end = jnp.int32(0)
        for j in range(lengths.shape[1] - 1):
            end = end + lengths[0, j]
            segment = segment + (position >= end).astype(jnp.int32)
            segment_back = segment_back + (back >= end).astype(jnp.int32)
            reset = reset | (position == end)
        same = (back >= 0) & (segment == segment_back)
        live = position < end
        picked = jnp.where(lane == KC - 1, live.astype(f32), reset.astype(f32))
        return jnp.where(lane < KC - 1, same.astype(f32), picked)

    at = lax.broadcasted_iota(jnp.int32, (rows, 128), 0)
    lane = lax.broadcasted_iota(jnp.int32, (rows, 128), 1)
    aux_o[...] = layout(base[0] + (at % SUB) * steps_in + at // SUB, lane)


def front_kernel(
    moves, core, nrm_in, halo_in, wm, wo, aux, ext_o, pre_o, steps_o, sig_o, small_o, x_o, tpre_o, tsuf_o,
    state_o, par_o, xd_o, sd_s, q_s, bw_s, nrm_s, sum_s, *, rank, count
):
    rows, di = pre_o.shape
    half = wo.shape[1] - 128
    steps_in = rows // SUB
    gs = group_of(di)
    low = core[0] == 0
    nrm_s[0, :rows] = jnp.where(low, nrm_in[:, :half], nrm_in[:, half:])
    nrm_s[1, :rows] = jnp.where(low, nrm_in[:, half:], nrm_in[:, :half])
    nrm_s[0, rows:] = jnp.where(low, halo_in[:, :half], halo_in[:, half:])
    nrm_s[1, rows:] = jnp.where(low, halo_in[:, half:], halo_in[:, :half])
    small_o[...] = jnp.zeros_like(small_o)
    moves.need(wm, wo)
    par = par_o
    total_rows = par_o.shape[0]

    def unpack(g, _):
        lanes = pl.ds(pl.multiple_of(g * 128, 128), 128)
        mine = wm[lanes, half:]
        other = wo[lanes, half:]
        xd_o[lanes, :] = jnp.where(low, mine, other)
        turned = jnp.where(low, other, mine).astype(f32).T
        par_o[:, lanes] = (
            turned[:total_rows, :]
            + turned[total_rows : 2 * total_rows, :]
            + turned[2 * total_rows : 3 * total_rows, :]
        )
        return 0

    lax.fori_loop(0, di // 128, unpack, 0)

    def project(g, _):
        lanes = pl.ds(pl.multiple_of(g * gs, gs), gs)
        inner = dot_nt(nrm_s[0], wm[lanes, :half]) + dot_nt(nrm_s[1], wo[lanes, :half])
        for back in range(1, KC):
            block = inner[rows - back * SUB : rows - (back - 1) * SUB, :]
            halo = inner[rows + KC - 1 - back : rows + KC - back, :]
            ext_o[(KC - 1 - back) * SUB : (KC - back) * SUB, lanes] = from_before(block, halo)
        ext_o[(KC - 1) * SUB :, lanes] = inner[:rows, :]
        total = par[KC : KC + 1, lanes] + par[KC - 1 : KC, lanes] * inner[:rows, :]
        for back in range(1, KC):
            shifted = ext_o[(KC - 1 - back) * SUB : (KC - 1 - back) * SUB + rows, lanes]
            total = total + par[KC - 1 - back : KC - back, lanes] * shifted * aux[:, back - 1 : back]
        pre_o[:, lanes] = total
        act = total * jax.nn.sigmoid(total)
        q_s[:, lanes] = act
        small_o[...] += dot_nn(act.astype(bf16), xd_o[lanes, :])
        return 0

    lax.fori_loop(0, di // gs, project, 0)
    moves.done(ext_o, pre_o, par_o, xd_o)
    small = small_o[...]
    lane = lax.broadcasted_iota(jnp.int32, small.shape, 1)
    step_low = jnp.where(lane >= 128 - rank, pltpu.roll(small, 128 - rank, 1), 0.0).astype(bf16)
    spread_columns(small, rank, count, bw_s)

    def stepping(g, _):
        lanes = pl.ds(pl.multiple_of(g * gs, gs), gs)
        step_pre = dot_nt(step_low, xd_o[lanes, :]) + par[KC + 1 : KC + 2, lanes]
        small_exp = jnp.exp(-jnp.abs(step_pre))
        steps = jnp.maximum(step_pre, 0.0) + jnp.log1p(small_exp)
        steps_o[:, lanes] = steps
        sig_o[:, lanes] = jax.nn.sigmoid(step_pre)
        q_s[:, lanes] = q_s[:, lanes] * steps
        sd_s[:, lanes] = jnp.where(aux[:, 4:5] > 0.5, STOP, steps)
        return 0

    lax.fori_loop(0, di // gs, stepping, 0)
    moves.done(steps_o, sig_o, sd_s, q_s)

    def chunk(g, _):
        lanes = pl.ds(pl.multiple_of(g * 128, 128), 128)
        rates = [
            jnp.broadcast_to(-LOG2E * jnp.exp(par[8 + n : 9 + n, lanes]), (SUB, 128))
            for n in range(count)
        ]

        def step(j, carry):
            states, total = carry
            at = pl.ds(pl.multiple_of(j * SUB, SUB), SUB)
            sd = sd_s[at, lanes]
            q = q_s[at, lanes]
            states = tuple(
                jnp.exp2(sd * rates[n]) * states[n] + q * bw_s[j * count + n] for n in range(count)
            )
            return (states, total + sd)

        zero = jnp.zeros((SUB, 128), f32)
        states, total = lax.fori_loop(0, steps_in, step, ((zero,) * count, zero), unroll=8)
        row = sublane_iota(128)
        ahead = prefix_sum(total)
        behind = suffix_sum(total)
        tpre_o[:, lanes] = jnp.where(row == 0, 0.0, pltpu.roll(ahead, 1, 0))
        tsuf_o[:, lanes] = jnp.where(row == SUB - 1, 0.0, pltpu.roll(behind, SUB - 1, 0))
        last = []
        for n in range(count):
            joined = prefix_states(jnp.exp2(rates[n] * total), states[n])
            x_o[n, :, lanes] = jnp.where(row == 0, 0.0, pltpu.roll(joined, 1, 0))
            last.append(joined[SUB - 1 : SUB, :])
        sum_s[pl.ds(g, 1), :] = ahead[SUB - 1 : SUB, :]
        to_copies(state_o, jnp.concatenate(last, axis=0).astype(bf16), lanes)
        return 0

    sum_s[...] = jnp.zeros_like(sum_s)
    lax.fori_loop(0, di // 128, chunk, 0)
    sums = sum_s[...]
    top = sums.astype(bf16)
    left = (sums - top.astype(f32)).astype(bf16)
    to_copies(state_o, top, slice(di, di + 128))
    to_copies(state_o, left, slice(di + 128, di + 256))


def to_copies(out, values, lanes):
    count = values.shape[0]
    for place in range(out.shape[0] // count):
        out[place * count : (place + 1) * count, lanes] = values


def negative_rates(par, out):
    out[...] = -LOG2E * jnp.exp(par[8:, :])


def group_kernel(arrived, out, state_s, sum_s, *, di, count, reverse):
    members = arrived.shape[0] // count
    rest = arrived.shape[1] - di - 256
    copies = out.shape[0] // count
    state_s[...] = jnp.zeros_like(state_s)
    total = jnp.zeros((count, 128), f32)
    for place in range(members - 1, -1, -1) if reverse else range(members):
        block = slice(place * count, (place + 1) * count)
        sums = arrived[block, di : di + 128].astype(f32)
        sums = sums + arrived[block, di + 128 : di + 256].astype(f32)
        total = total + sums
        carry_step(sums, arrived[block, :di], sum_s, state_s)
    joined = state_s[...].astype(bf16)
    top = total.astype(bf16)
    left = (total - top.astype(f32)).astype(bf16)
    for copy in range(copies):
        block = slice(copy * count, (copy + 1) * count)
        out[block, :di] = joined
        out[block, di : di + 128] = top
        out[block, di + 128 : di + 256] = left
    if rest:
        extra = jnp.zeros((count, rest), f32)
        for place in range(members):
            extra = extra + arrived[place * count : (place + 1) * count, di + 256 :].astype(f32)
        gap = jnp.zeros((count - 2, rest), f32)
        for copy in range(copies):
            rows = jnp.concatenate([extra[2 * copy : 2 * copy + 2, :], gap], axis=0)
            out[copy * count : (copy + 1) * count, di + 256 :] = rows.astype(bf16)


def forward_group_kernel(arrived, par, out, state_s, rate_s, *, di, count):
    negative_rates(par, rate_s)
    group_kernel(arrived, out, state_s, rate_s, di=di, count=count, reverse=False)


def backward_group_kernel(arrived, par, out, state_s, rate_s, *, di, count):
    negative_rates(par, rate_s)
    group_kernel(arrived, out, state_s, rate_s, di=di, count=count, reverse=True)


def step_sums(arrived, block, di):
    return arrived[block, di : di + 128].astype(f32) + arrived[block, di + 128 : di + 256].astype(
        f32
    )


def carry_step(decay_sums, arrived, rate_s, state_s):
    for g in range(state_s.shape[1] // 128):
        lanes = slice(g * 128, (g + 1) * 128)
        decay = jnp.exp2(rate_s[:, lanes] * decay_sums[g : g + 1, :])
        state_s[:, lanes] = decay * state_s[:, lanes] + arrived[:, lanes].astype(f32)


def gate_kernel(moves, core, nrm, zm, zo, gate_z_o, nrm_s):
    rows, di = gate_z_o.shape
    half = zm.shape[1]
    gs = group_of(di)
    low = core[0] == 0
    nrm_s[0] = jnp.where(low, nrm[:, :half], nrm[:, half:])
    nrm_s[1] = jnp.where(low, nrm[:, half:], nrm[:, :half])
    moves.need(zm, zo)

    def project(g, _):
        lanes = pl.ds(pl.multiple_of(g * gs, gs), gs)
        gate_z_o[:, lanes] = dot_nt(nrm_s[0], zm[lanes, :]) + dot_nt(nrm_s[1], zo[lanes, :])
        return 0

    lax.fori_loop(0, di // gs, project, 0)


def middle_kernel(
    moves, core, place, om, oo, par, aux, pre, sd, q, x_in, small, arrived, near, tpre, hid, cot,
    route, gain, router, gate_z, scan_o, send_o, middle_o, ntwo_o, chance_o, meta_o, hot_o,
    entry_o, bw_s, cw_s, rate_s, *, rank, count, experts, stride, capacity, shift
):
    rows, di = pre.shape
    half = om.shape[1]
    steps_in = rows // SUB
    gs = group_of(di)
    low = core[0] == 0
    spread_columns(small[...], rank, count, bw_s)
    spread_columns(small[...], rank + count, count, cw_s)
    negative_rates(par, rate_s)
    moves.need(arrived, near)
    entry_o[...] = jnp.zeros_like(entry_o)
    members = near.shape[0] // count

    def before_here(there, _):
        block = pl.ds(pl.multiple_of(there * count, count), count)
        carry_step(step_sums(arrived, block, di), arrived[block, :di], rate_s, entry_o)
        return 0

    def just_before(there, _):
        block = pl.ds(pl.multiple_of(there * count, count), count)
        carry_step(step_sums(near, block, di), near[block, :di], rate_s, entry_o)
        return 0

    lax.fori_loop(0, place[0] // members, before_here, 0)
    lax.fori_loop(0, place[0] % members, just_before, 0)
    moves.done(entry_o)
    moves.need(x_in, sd, q)

    def scan(g, _):
        lanes = pl.ds(pl.multiple_of(g * 128, 128), 128)
        rates = [jnp.broadcast_to(rate_s[n : n + 1, lanes], (SUB, 128)) for n in range(count)]
        before = tpre[:, lanes]
        first = tuple(
            x_in[n, :, lanes] + jnp.exp2(rates[n] * before) * entry_o[n : n + 1, lanes]
            for n in range(count)
        )
        def step(j, states):
            at = pl.ds(pl.multiple_of(j * SUB, SUB), SUB)
            sd_here = sd[at, lanes]
            q_here = q[at, lanes]
            total = jnp.zeros((SUB, 128), f32)
            fresh = []
            for n in range(count):
                state = jnp.exp2(sd_here * rates[n]) * states[n] + q_here * bw_s[j * count + n]
                total = total + state * cw_s[j * count + n]
                fresh.append(state)
            scan_o[at, lanes] = total
            return tuple(fresh)

        lax.fori_loop(0, steps_in, step, first, unroll=8)
        return 0

    lax.fori_loop(0, di // 128, scan, 0)

    def gating(g, carry):
        mine, other = carry
        lanes = pl.ds(pl.multiple_of(g * gs, gs), gs)
        z = gate_z[:, lanes]
        pre_here = pre[:, lanes]
        scanned = scan_o[:, lanes] + par[KC + 2 : KC + 3, lanes] * (
            pre_here * jax.nn.sigmoid(pre_here)
        )
        scan_o[:, lanes] = scanned
        gated = (scanned * (z * jax.nn.sigmoid(z)) * aux[:, 3:4]).astype(bf16)
        return (mine + dot_nn(gated, om[lanes, :]), other + dot_nn(gated, oo[lanes, :]))

    zero = jnp.zeros((rows, half), f32)
    moves.need(pre, gate_z, om, oo)
    mine, other = lax.fori_loop(0, di // gs, gating, (zero, zero))
    moves.done(scan_o)
    mixed = jnp.concatenate([jnp.where(low, mine, other), jnp.where(low, other, mine)], axis=1)
    middle = hid[...].astype(f32) + mixed
    middle_o[...] = middle
    scale = lax.rsqrt(jnp.mean(middle * middle, axis=1, keepdims=True) + epsilon)
    ntwo = (middle * scale * gain[...].reshape(1, -1)).astype(bf16)
    ntwo_o[...] = ntwo
    logits = dot_nt(ntwo, router[...])
    top = jnp.max(logits, axis=1, keepdims=True)
    raised = jnp.exp(logits - top)
    chances = raised / jnp.sum(raised, axis=1, keepdims=True)
    chance_o[...] = chances
    lane = lax.broadcasted_iota(jnp.int32, (rows, experts), 1)
    chosen = route[...] == lane
    chosen_f = chosen.astype(f32)
    gate = jnp.sum(chances * chosen_f, axis=1, keepdims=True)
    taken = chosen_f * aux[:, 3:4]
    here = lax.broadcasted_iota(jnp.int32, (rows, rows), 0)
    there = lax.broadcasted_iota(jnp.int32, (rows, rows), 1)
    own_id = (here & (SUB - 1)) * steps_in + (here >> shift)
    other_id = (there & (SUB - 1)) * steps_in + (there >> shift)
    earlier = (other_id < own_id).astype(bf16)
    ranks = jnp.sum(dot_nn(earlier, taken.astype(bf16)) * chosen_f, axis=1, keepdims=True)
    kept = aux[:, 3:4] * (ranks < capacity).astype(f32)
    weight = gate * kept
    up = (cot[...].astype(f32) * weight).astype(bf16)
    values = jnp.concatenate([ntwo, up], axis=0)
    rank_low = ranks.astype(jnp.int32)
    slot = jnp.concatenate([rank_low, rank_low + capacity], axis=0)
    block = route[...] * stride
    block = jnp.concatenate([block, block], axis=0)
    kept_on = jnp.concatenate([kept, kept], axis=0) > 0.5
    place = lax.broadcasted_iota(jnp.int32, (2 * rows, experts * stride), 1)
    wide_hot = ((block + slot == place) & kept_on).astype(bf16)
    at_last = (block + 2 * capacity + slot // 2 == place) & kept_on
    even_hot = (at_last & (slot % 2 == 0)).astype(bf16)
    odd_hot = (at_last & (slot % 2 == 1)).astype(bf16)
    hot_o[0] = wide_hot
    hot_o[1] = even_hot
    hot_o[2] = odd_hot
    moves.done(hot_o, middle_o, ntwo_o)
    third = ntwo.shape[1] // 3
    narrow = values[:, 2 * third :]
    last = jnp.concatenate([dot_tn(even_hot, narrow), dot_tn(odd_hot, narrow)], axis=1)
    packed = (dot_tn(wide_hot, values[:, : 2 * third]) + last).astype(bf16)
    send_o[: experts * stride, :] = packed
    send_o[experts * stride :, :] = packed
    lane8 = lax.broadcasted_iota(jnp.int32, (rows, 8), 1)
    meta_o[...] = jnp.where(
        lane8 == 0, gate, jnp.where(lane8 == 1, kept, jnp.where(lane8 == 2, scale, 0.0))
    )


def back_kernel(
    moves, core, back, om, oo, par, aux, sd, small, gate_z, hot, middle, meta, chances, route, cot, gain,
    router, ntwo, combined_o, mixlow_o, mgrad_o, ggrad_o, sg_o, gain_o, y_o, state_o, cw_s, mix_s,
    rate_s, sum_s, *, rank, count, experts
):
    rows, di = sd.shape
    half = om.shape[1]
    steps_in = rows // SUB
    gs = group_of(di)
    negative_rates(par, rate_s)
    slots = back.shape[0] // 2
    third = back.shape[1] // 2
    rows_back = (back[:slots, :].astype(f32) + back[slots:, :].astype(f32)).astype(bf16)
    last = dot_nn(hot[1], rows_back[:, :third]) + dot_nn(hot[2], rows_back[:, third:])
    both = jnp.concatenate([dot_nn(hot[0], rows_back), last], axis=1)
    combined = both[:rows, :]
    dispatch = both[rows:, :]
    combined_o[...] = combined
    gate = meta[:, 0:1]
    kept = meta[:, 1:2]
    scale = meta[:, 2:3]
    mid = middle[...]
    up = cot[...].astype(f32)
    gate_total = kept * jnp.sum(up * combined, axis=1, keepdims=True)
    lane = lax.broadcasted_iota(jnp.int32, (rows, experts), 1)
    chosen_f = (route[...] == lane).astype(f32)
    logit_grad = (gate * (chosen_f - chances[...]) * gate_total).astype(bf16)
    router_rows = dot_tn(logit_grad, ntwo[...])
    members = state_o.shape[0] // count
    for member in range(members):
        rows_here = []
        for group in range(experts // members):
            row = router_rows[group * members + member : group * members + member + 1, :]
            rows_here += [row[:, :half], row[:, half:]]
        block = slice(member * count, (member + 1) * count)
        state_o[block, di + 256 :] = jnp.concatenate(rows_here, axis=0).astype(bf16)
    ngrad = dot_nn(logit_grad, router[...]) + dispatch
    gain_o[...] = jnp.sum(ngrad * mid * scale, axis=0, keepdims=True)
    scaled = gain[...].reshape(1, -1) * ngrad
    cube = scale * scale * scale
    mgrad = up + scale * scaled - mid * cube * jnp.mean(mid * scaled, axis=1, keepdims=True)
    mgrad_o[...] = mgrad
    low = core[0] == 0
    mixlow = mgrad.astype(bf16)
    mixlow_o[...] = mixlow
    mix_s[0] = jnp.where(low, mixlow[:, :half], mixlow[:, half:])
    mix_s[1] = jnp.where(low, mixlow[:, half:], mixlow[:, :half])
    moves.done(mixlow_o, mgrad_o, combined_o)
    moves.need(om, oo, gate_z)

    def gating(g, _):
        lanes = pl.ds(pl.multiple_of(g * gs, gs), gs)
        ggrad = dot_nt(mix_s[0], om[lanes, :]) + dot_nt(mix_s[1], oo[lanes, :])
        ggrad = ggrad * aux[:, 3:4]
        ggrad_o[:, lanes] = ggrad
        z = gate_z[:, lanes]
        sg_o[:, lanes] = ggrad * (z * jax.nn.sigmoid(z))
        return 0

    lax.fori_loop(0, di // gs, gating, 0)
    moves.done(ggrad_o, sg_o)
    spread_columns(small[...], rank + count, count, cw_s)
    moves.need(sd)

    def chunk(g, _):
        lanes = pl.ds(pl.multiple_of(g * 128, 128), 128)
        rates = [jnp.broadcast_to(rate_s[n : n + 1, lanes], (SUB, 128)) for n in range(count)]

        def step(i, carry):
            grads, total = carry
            j = steps_in - 1 - i
            at = pl.ds(pl.multiple_of(j * SUB, SUB), SUB)
            sd_here = sd[at, lanes]
            sgrad = sg_o[at, lanes]
            grads = tuple(
                jnp.exp2(sd_here * rates[n]) * (grads[n] + sgrad * cw_s[j * count + n])
                for n in range(count)
            )
            return (grads, total + sd_here)

        zero = jnp.zeros((SUB, 128), f32)
        grads, total = lax.fori_loop(0, steps_in, step, ((zero,) * count, zero), unroll=8)
        row = sublane_iota(128)
        last = []
        for n in range(count):
            joined = suffix_states(jnp.exp2(rates[n] * total), grads[n])
            y_o[n, :, lanes] = jnp.where(row == SUB - 1, 0.0, pltpu.roll(joined, SUB - 1, 0))
            last.append(joined[0:1, :])
        sum_s[pl.ds(g, 1), :] = jnp.sum(total, axis=0, keepdims=True)
        to_copies(state_o, jnp.concatenate(last, axis=0).astype(bf16), lanes)
        return 0

    sum_s[...] = jnp.zeros_like(sum_s)
    lax.fori_loop(0, di // 128, chunk, 0)
    total = sum_s[...]
    top = total.astype(bf16)
    to_copies(state_o, top, slice(di, di + 128))
    to_copies(state_o, (total - top.astype(f32)).astype(bf16), slice(di + 128, di + 256))


def slot_rows(stride, capacity, blocks):
    dims = (2 * capacity * blocks, stride * blocks)
    row = lax.broadcasted_iota(jnp.int32, dims, 0)
    column = lax.broadcasted_iota(jnp.int32, dims, 1)
    half = capacity * blocks
    slot = row % capacity + row // half * capacity
    start = row % half // capacity * stride
    wide = (start + slot == column).astype(bf16)
    at_last = start + 2 * capacity + slot // 2 == column
    even = (at_last & (slot % 2 == 0)).astype(bf16)
    odd = (at_last & (slot % 2 == 1)).astype(bf16)
    return wide, even, odd


def unpack(packed, hots):
    wide, even, odd = hots
    third = packed.shape[1] // 2
    last = dot_nn(even, packed[:, :third]) + dot_nn(odd, packed[:, third:])
    return jnp.concatenate([dot_nn(wide, packed), last], axis=1).astype(bf16)


def pack(rows, hots):
    wide, even, odd = hots
    third = rows.shape[1] // 3
    narrow = rows[:, 2 * third :]
    last = jnp.concatenate([dot_tn(even, narrow), dot_tn(odd, narrow)], axis=1)
    return dot_tn(wide, rows[:, : 2 * third]) + last


def expert_kernel(
    moves, mine, other, w_gate, w_up, w_down, in_o, grad_o, act_o, gate_o, up_o, ours_o, theirs_o,
    *, stride, capacity
):
    blocks = 16
    hots = slot_rows(stride, capacity, blocks)
    size = capacity * blocks
    groups = mine.shape[0] // (stride * blocks)
    for part, arrived in enumerate((mine, other)):
        for group in range(groups):
            rows = unpack(arrived[group * stride * blocks : (group + 1) * stride * blocks, :], hots)
            at = (part * groups + group) * size
            in_o[at : at + size, :] = rows[:size, :]
            grad_o[at : at + size, :] = rows[size:, :]
    moves.need(w_gate)
    gate_in = dot_nn(in_o[...], w_gate[...])
    moves.need(w_up)
    up_in = dot_nn(in_o[...], w_up[...])
    moves.done(in_o)
    sig = jax.nn.sigmoid(gate_in)
    silu = gate_in * sig
    act = (silu * up_in).astype(bf16)
    act_o[...] = act
    moves.need(w_down)
    outputs = dot_nn(act, w_down[...])
    act_grad = dot_nt(grad_o[...], w_down[...])
    moves.done(grad_o, act_o)
    gate_grad = (act_grad * up_in * sig * (1.0 + gate_in * (1.0 - sig))).astype(bf16)
    up_grad = (act_grad * silu).astype(bf16)
    gate_o[...] = gate_grad
    up_o[...] = up_grad
    moves.done(gate_o, up_o)
    total = dot_nt(gate_grad, w_gate[...]) + dot_nt(up_grad, w_up[...])
    for part, out in ((1, theirs_o), (0, ours_o)):
        for group in range(groups):
            at = (part * groups + group) * size
            rows = jnp.concatenate([outputs[at : at + size, :], total[at : at + size, :]], axis=0)
            packed = pack(rows.astype(bf16), hots)
            out[group * stride * blocks : (group + 1) * stride * blocks, :] = packed.astype(out.dtype)
        moves.done(out)


def aside_kernel(
    moves, core, side, zm, zo, aux, pre, gate_z, scanned, ggrad, combined, middle, meta,
    out_o, comb_o, skip_o, ngrad_o, *, width, span
):
    rows, di = pre.shape
    half = zm.shape[1]
    gs = group_of(di)
    pieces = width // 16
    result = (middle[...] + meta[:, 0:1] * meta[:, 1:2] * combined[...]).astype(bf16)
    out_o[...] = dot_tn(token_order(rows), result).astype(bf16)
    def gating(g, carry):
        mine, other = carry
        lanes = pl.ds(pl.multiple_of(g * gs, gs), gs)
        grad = ggrad[:, lanes]
        z = gate_z[:, lanes]
        sig = jax.nn.sigmoid(z)
        here = scanned[:, lanes]
        zgrad = grad * here * sig * (1.0 + z * (1.0 - sig))
        z_low = zgrad.astype(bf16)
        z_turned = zgrad.T.astype(bf16)
        gated_turned = (here * (z * sig) * aux[:, 3:4]).T.astype(bf16)
        for i in range(gs // 16):
            piece = g * (gs // 16) + i
            to = pl.multiple_of(piece // pieces * span + piece % pieces * 16, 16)
            comb_o[pl.ds(to, 16), :] = z_turned[i * 16 : (i + 1) * 16, :]
            owner = piece // pieces
            holder = owner // 2 * 2 + side[0]
            to = holder * span + (1 + owner % 2) * width + piece % pieces * 16
            comb_o[pl.ds(pl.multiple_of(to, 16), 16), :] = gated_turned[i * 16 : (i + 1) * 16, :]
        pre_here = pre[:, lanes]
        act = pre_here * jax.nn.sigmoid(pre_here)
        skip_o[:, lanes] = jnp.sum(grad * (z * sig) * act, axis=0, keepdims=True)
        return (mine + dot_nn(z_low, zm[lanes, :]), other + dot_nn(z_low, zo[lanes, :]))

    moves.need(zm, zo)
    zero = jnp.zeros((rows, half), f32)
    mine, other = lax.fori_loop(0, di // gs, gating, (zero, zero))
    ngrad_o[0] = mine
    ngrad_o[1] = other


def scan_kernel(
    moves, place, xd, par, sd, q, pre, steps, sig_step, small, x_in, tpre, entry, y_in, tsuf, arrived, near,
    sgrad, cgrad_o, xd_o, spar_o, router_o, bw_s, cw_s, bacc_s, cacc_s, st_s, dk_s, sgr_s, asc_s, plow_s,
    rate_s, after_s, *, rank, count
):
    rows, di = pre.shape
    negative_rates(par, rate_s)
    after_s[...] = jnp.zeros_like(after_s)
    groups = arrived.shape[0] // count
    members = near.shape[0] // count
    spread_columns(small[...], rank, count, bw_s)
    spread_columns(small[...], rank + count, count, cw_s)
    bacc_s[...] = jnp.zeros_like(bacc_s)
    cacc_s[...] = jnp.zeros_like(cacc_s)
    spar_o[...] = jnp.zeros_like(spar_o)
    moves.need(arrived, near)

    def after_here(i, _):
        block = pl.ds(pl.multiple_of((groups - 1 - i) * count, count), count)
        carry_step(step_sums(arrived, block, di), arrived[block, :di], rate_s, after_s)
        return 0

    def just_after(i, _):
        block = pl.ds(pl.multiple_of((members - 1 - i) * count, count), count)
        carry_step(step_sums(near, block, di), near[block, :di], rate_s, after_s)
        return 0

    lax.fori_loop(0, groups - 1 - place[0] // members, after_here, 0)
    lax.fori_loop(0, members - 1 - place[0] % members, just_after, 0)
    router_sum = jnp.zeros(router_o.shape, f32)
    for there in range(groups):
        router_sum += arrived[there * count : (there + 1) * count, di + 256 :].astype(f32)
    router_o[...] = router_sum
    steps_in = rows // SUB
    gs = group_of(di)
    moves.need(x_in, sd, q, sgrad, y_in)

    def scan(g, _):
        lanes = pl.ds(pl.multiple_of(g * 128, 128), 128)
        rates = [
            jnp.broadcast_to(rate_s[n : n + 1, lanes], (SUB, 128)) for n in range(count)
        ]
        before = tpre[:, lanes]
        behind = tsuf[:, lanes]
        first = tuple(
            x_in[n, :, lanes] + jnp.exp2(rates[n] * before) * entry[n : n + 1, lanes]
            for n in range(count)
        )

        def forward(j, states):
            at = pl.ds(pl.multiple_of(j * SUB, SUB), SUB)
            sd_here = sd[at, lanes]
            q_here = q[at, lanes]
            fresh = []
            for n in range(count):
                decay = jnp.exp2(sd_here * rates[n])
                dk_s[j * count + n] = decay
                st_s[j * count + n] = states[n]
                fresh.append(decay * states[n] + q_here * bw_s[j * count + n])
            return tuple(fresh)

        last = lax.fori_loop(0, steps_in, forward, first, unroll=8)
        for n in range(count):
            st_s[steps_in * count + n] = last[n]
        zero = jnp.zeros((SUB, 128), f32)
        arriving = tuple(
            y_in[n, :, lanes] + jnp.exp2(rates[n] * behind) * after_s[n : n + 1, lanes]
            for n in range(count)
        )

        def backward(i, carry):
            grads, rate_grads = carry
            j = steps_in - 1 - i
            at = pl.ds(pl.multiple_of(j * SUB, SUB), SUB)
            sd_here = sd[at, lanes]
            q_here = q[at, lanes]
            sg = sgrad[at, lanes]
            onto = zero
            along = zero
            fresh = []
            fresh_rates = []
            for n in range(count):
                k = j * count + n
                lam = grads[n] + sg * cw_s[k]
                cacc_s[k] += sg * st_s[k + count]
                bacc_s[k] += lam * q_here
                onto = onto + lam * bw_s[k]
                carried = lam * dk_s[k]
                logs = carried * st_s[k]
                along = along + logs * rates[n]
                fresh.append(carried)
                fresh_rates.append(rate_grads[n] + logs * sd_here)
            sgr_s[at, lanes] = along
            asc_s[at, lanes] = onto
            return (tuple(fresh), tuple(fresh_rates))

        _, rate_grads = lax.fori_loop(0, steps_in, backward, (arriving, (zero,) * count), unroll=2)
        for n in range(count):
            spar_o[8 + n : 9 + n, lanes] = LN2 * jnp.sum(
                rate_grads[n] * rates[n], axis=0, keepdims=True
            )
        return 0

    lax.fori_loop(0, di // 128, scan, 0)

    moves.need(pre, sig_step, xd, steps)
    lane8 = lax.broadcasted_iota(jnp.int32, (SUB, 128), 1)
    blocks = []
    for j in range(steps_in):
        block = jnp.zeros((SUB, 128), f32)
        for n in range(count):
            k = j * count + n
            block = jnp.where(
                lane8 == rank + n, jnp.sum(bacc_s[k], axis=1, keepdims=True), block
            )
            block = jnp.where(
                lane8 == rank + count + n, jnp.sum(cacc_s[k], axis=1, keepdims=True), block
            )
        blocks.append(block)
    coef_grad = jnp.concatenate(blocks, axis=0)
    lane = lax.broadcasted_iota(jnp.int32, (rows, 128), 1)
    step_low = jnp.where(
        lane >= 128 - rank, pltpu.roll(small[...], 128 - rank, 1), 0.0
    ).astype(bf16)

    def steps_back(g, total):
        lanes = pl.ds(pl.multiple_of(g * gs, gs), gs)
        pre_here = pre[:, lanes]
        act = pre_here * jax.nn.sigmoid(pre_here)
        pre_grad = (LN2 * sgr_s[:, lanes] + act * asc_s[:, lanes]) * sig_step[:, lanes]
        spar_o[KC + 1 : KC + 2, lanes] = jnp.sum(pre_grad, axis=0, keepdims=True)
        pre_low = pre_grad.astype(bf16)
        plow_s[:, lanes] = pre_low
        return total + dot_nn(pre_low, xd[lanes, :])

    rank_grad = lax.fori_loop(0, di // gs, steps_back, jnp.zeros((rows, 128), f32))
    small_low = jnp.where(lane < rank, pltpu.roll(rank_grad, rank, 1), coef_grad).astype(bf16)

    def act_back(g, _):
        lanes = pl.ds(pl.multiple_of(g * gs, gs), gs)
        pre_here = pre[:, lanes]
        sig = jax.nn.sigmoid(pre_here)
        act_low = (pre_here * sig).astype(bf16)
        total = (
            sgrad[:, lanes] * par[KC + 2 : KC + 3, lanes]
            + steps[:, lanes] * asc_s[:, lanes]
            + dot_nt(small_low, xd[lanes, :])
        )
        cgrad_o[:, lanes] = total * sig * (1.0 + pre_here * (1.0 - sig))
        xd_o[lanes, :] = (dot_tn(act_low, small_low) + dot_tn(plow_s[:, lanes], step_low)).astype(bf16)
        return 0

    lax.fori_loop(0, di // gs, act_back, 0)


def last_kernel(
    moves, core, cgrad, halo, aux, ext, par, wm, wo, ngrad_z, spar, skip, xd, hid, gain_two,
    router_sum, pay_o, ngrad_o, extra_o, low_s, far_s, *, width
):
    rows, di = cgrad.shape
    gs = 128
    moves.need(ext)
    ahead_lane = spar.shape[0] + 4 * (hid.shape[1] // width)
    moves.need(xd)

    def conv(g, _):
        lanes = pl.ds(pl.multiple_of(g * gs, gs), gs)
        cg = cgrad[:, lanes]
        grad = par[KC - 1 : KC, lanes] * cg
        parts = [jnp.sum(cg * ext[(KC - 1) * SUB :, lanes], axis=0, keepdims=True)]
        zero = jnp.zeros((1, gs), f32)
        behind = [zero] * (KC - 1)
        for ahead in range(1, KC):
            tap = par[KC - 1 - ahead : KC - ahead, lanes]
            masked = cg * aux[:, ahead - 1 : ahead]
            shifted = ext[(KC - 1 - ahead) * SUB : (KC - 1 - ahead) * SUB + rows, lanes]
            parts.append(jnp.sum(masked * shifted, axis=0, keepdims=True))
            pieces = [masked[ahead * SUB :, :]]
            for i in range(ahead):
                pieces.append(from_after(masked[i * SUB : (i + 1) * SUB, :], zero))
                k = KC - 1 - ahead + i
                behind[k] = behind[k] + tap * masked[i * SUB : i * SUB + 1, :]
            grad = grad + tap * jnp.concatenate(pieces, axis=0)
        low_s[:, lanes] = grad.astype(bf16)
        pay_o[lanes, 0:128] = grad.T.astype(bf16)
        pay_o[lanes, 128:256] = xd[lanes, :]
        extra = jnp.concatenate(behind + [jnp.zeros((SUB - KC + 1, gs), f32)], axis=0)
        far_s[:SUB, lanes] = extra.astype(bf16)
        own = jnp.concatenate(
            parts[::-1]
            + [jnp.sum(cg, axis=0, keepdims=True), spar[KC + 1 : KC + 2, lanes], skip[:, lanes]]
            + [zero, spar[8:, lanes], jnp.zeros((ahead_lane - spar.shape[0], gs), f32), extra]
            + [jnp.zeros((128 - ahead_lane - SUB, gs), f32)],
            axis=0,
        )
        pay_o[lanes, 256:384] = own.T.astype(bf16)
        return 0

    lax.fori_loop(0, di // gs, conv, 0)
    far_s[SUB:, :] = jnp.zeros_like(far_s[SUB:, :])
    moves.need(wm, wo, ngrad_z, hid)
    low = core[0] == 0

    def onto_inputs(values):
        return dot_nn(values, wm[...]), dot_nn(values, wo[...])

    def joined(mine, other):
        return jnp.concatenate([jnp.where(low, mine, other), jnp.where(low, other, mine)], axis=1)

    mine, other = onto_inputs(low_s[...])
    ngrad = joined(mine + ngrad_z[0], other + ngrad_z[1])
    ngrad_o[...] = ngrad
    far = joined(*onto_inputs(far_s[...]))[:SUB, :]
    extra_o[...] = far
    first = hid[...].astype(f32)
    scale = lax.rsqrt(jnp.mean(first * first, axis=1, keepdims=True) + epsilon)
    gains = jnp.sum(ngrad * first * scale, axis=0, keepdims=True)
    first = halo[SUB:, :].astype(f32)
    scale = lax.rsqrt(jnp.mean(first * first, axis=1, keepdims=True) + epsilon)
    gains = gains + jnp.sum(far * first * scale, axis=0, keepdims=True)
    model = first.shape[1]
    each = model // width
    row = lax.broadcasted_iota(jnp.int32, (width, model), 0)
    column = lax.broadcasted_iota(jnp.int32, (width, model), 1)
    here = column // each == row
    extra = jnp.zeros((width, 128), f32)
    router_row = jnp.concatenate([router_sum[0:1, :], router_sum[1:2, :]], axis=1)
    router_top = router_row.astype(bf16).astype(f32)
    rows_sent = (gains, gain_two[...], router_top, router_row - router_top)
    for k, values in enumerate(rows_sent):
        spread = jnp.where(here, values, 0.0).astype(bf16)
        at = lax.broadcasted_iota(jnp.int32, (model, 128), 0)
        to = lax.broadcasted_iota(jnp.int32, (model, 128), 1)
        placed = (at % each + spar.shape[0] + k * each == to).astype(bf16)
        extra = extra + dot_nn(spread, placed)
    extra = extra.astype(bf16)
    for place in range(di // width):
        pay_o[place * width : (place + 1) * width, 256:384] += extra


def tail_kernel(
    moves, place, core, xd, par, sd, q, pre, steps, sig_step, small, x_in, tpre, entry, y_in, tsuf,
    arrived, near, sgrad, halo, aux, ext, wm, wo, ngrad_z, skip, hid, gain_two,
    pay_o, ngrad_o, extra_o, low_s, far_s, cgrad_s, xd_s, spar_s, router_s, *scratch,
    rank, count, width
):
    scan_kernel(
        moves, place, xd, par, sd, q, pre, steps, sig_step, small, x_in, tpre, entry, y_in, tsuf,
        arrived, near, sgrad, cgrad_s, xd_s, spar_s, router_s, *scratch, rank=rank, count=count
    )
    last_kernel(
        moves, core, cgrad_s, halo, aux, ext, par, wm, wo, ngrad_z, spar_s, skip, xd_s, hid,
        gain_two, router_s, pay_o, ngrad_o, extra_o, low_s, far_s, width=width
    )


def hidden_kernel(ngrad_in, beyond, hid, mgrad, gain, first_o):
    first = hid[...].astype(f32)
    rows = first.shape[0]
    ngrad = ngrad_in[...]
    row = lax.broadcasted_iota(jnp.int32, first.shape, 0)
    for i in range(KC - 1):
        at = rows - 1 - (KC - 2 - i) * SUB
        ngrad = ngrad + jnp.where(row == at, beyond[i : i + 1, :], 0.0)
    scale = lax.rsqrt(jnp.mean(first * first, axis=1, keepdims=True) + epsilon)
    scaled = gain[...].reshape(1, -1) * ngrad
    cube = scale * scale * scale
    grad = (
        mgrad[...] + scale * scaled - first * cube * jnp.mean(first * scaled, axis=1, keepdims=True)
    )
    order = token_order(rows)
    top = grad.astype(bf16)
    left = grad - top.astype(f32)
    mid = left.astype(bf16)
    low_part = (left - mid.astype(f32)).astype(bf16)
    first_o[...] = dot_tn(order, top) + dot_tn(order, mid) + dot_tn(order, low_part)


def ready_kernel(
    moves, side, comb, nrm_all, mix_half, z_o, mine_o, theirs_o, z_s, gated_s
):
    places = comb.shape[0]
    width = z_o.shape[0]
    for place in range(places):
        z_s[:, place * 128 : (place + 1) * 128] = comb[place, :width, :]
    for k in range(places // 2):
        place = 2 * k + side[0]
        gated_s[:, k * 128 : (k + 1) * 128] = comb[place, width : 3 * width, :]
    moves.need(mix_half)
    grads = dot_nn(gated_s[...], mix_half[...]).astype(bf16)
    first = side[0] == 0
    mine_o[...] = jnp.where(first, grads[:width, :], grads[width:, :])
    theirs_o[...] = jnp.where(first, grads[width:, :], grads[:width, :])
    moves.need(nrm_all)
    z_o[...] = dot_nn(z_s[...], nrm_all[...]).astype(bf16)


def grads_kernel(got, nrm_all, out_o, left_s, *, base):
    places, width, _ = got.shape
    model = nrm_all.shape[1]
    each = model // width
    rest = jnp.zeros((width, 256), f32)
    routers = [jnp.zeros((width, 128), f32) for _ in range(places * each // 128)]
    lane = lax.broadcasted_iota(jnp.int32, (width, 128), 1)
    row = lax.broadcasted_iota(jnp.int32, (128, 128), 0)
    column = lax.broadcasted_iota(jnp.int32, (128, 128), 1)
    after = row - (base + 2 * each)
    late = column == 127 - (KC - 2 - after) * SUB
    placed = (late & (after >= 0) & (after < KC - 1)).astype(bf16)
    for place in range(places):
        at = gathered_place(place)
        inner = got[at, :, :128]
        if place + 1 < places:
            beyond = dot_nn(got[gathered_place(place + 1), :, 256:384], placed)
            inner = (inner.astype(f32) + beyond).astype(bf16)
        left_s[:, at * 128 : (at + 1) * 128] = inner
        there = got[at, :, 128:].astype(f32)
        rest = rest + there
        k = place * each // 128
        inside = place * each % 128
        mine = (lane >= inside) & (lane < inside + each)
        for part in range(2):
            turn = (inside - base - part * each) % 128
            routers[k] = routers[k] + jnp.where(mine, pltpu.roll(there[:, 128:], turn, 1), 0.0)
    out_o[width:, :256] = rest.astype(bf16)
    out_o[width:, 256:] = jnp.concatenate(routers, axis=1).astype(bf16)
    out_o[:width, :model] = dot_nn(left_s[...], nrm_all[...]).astype(bf16)


def token_order(rows):
    steps_in = rows // SUB
    row = lax.broadcasted_iota(jnp.int32, (rows, rows), 0)
    column = lax.broadcasted_iota(jnp.int32, (rows, rows), 1)
    return ((row % SUB) * steps_in + row // SUB == column).astype(bf16)


def final_kernel(
    ours, theirs, ours_two, theirs_two, x_o, z_o, out_o, conv_o, bias_o, xp_o, dt_o, db_o, al_o, skip_o, router_o, one_o,
    two_o, mine_s, other_s, *, rank, count, experts
):
    width = out_o.shape[0]
    model = router_o.shape[1]
    each = model // width
    x_o[...] = ours[:width, :model].astype(f32) + theirs[:width, :model].astype(f32)
    z_o[...] = ours_two[:width, :].astype(f32) + theirs_two[:width, :].astype(f32)
    out_o[...] = ours_two[width:, :].astype(f32) + theirs_two[width:, :].astype(f32)
    rest = slice(width, 2 * width)
    xd = ours[rest, :128].astype(f32) + theirs[rest, :128].astype(f32)
    xp_o[...] = xd[:, : rank + 2 * count]
    gap = jnp.zeros((128 - width, 128), f32)
    turned = jnp.concatenate([xd, gap], axis=0).T
    dt_o[...] = turned[128 - rank :, :width]
    vectors = jnp.zeros((128, 128), f32)
    for part, held in ((ours, mine_s), (theirs, other_s)):
        block = jnp.concatenate([part[rest, 128:256].astype(f32), gap], axis=0).T
        vectors = vectors + block
        for k in range(experts * each // 128):
            lanes = slice(256 + k * 128, 384 + k * 128)
            piece = jnp.concatenate([part[rest, lanes].astype(f32), gap], axis=0)
            held[k * 128 : (k + 1) * 128, :] = piece.T
        held[experts * each :, :] = jnp.zeros_like(held[experts * each :, :])
        held[experts * each : (experts + 2) * each, :] = block[8 + count : 8 + count + 2 * each, :]
    conv_o[...] = vectors[:KC, :width]
    bias_o[...] = vectors[KC : KC + 1, :width].reshape(width)
    db_o[...] = vectors[KC + 1 : KC + 2, :width].reshape(width)
    skip_o[...] = vectors[KC + 2 : KC + 3, :width].reshape(width)
    al_o[...] = vectors[8 : 8 + count, :width]
    row = lax.broadcasted_iota(jnp.int32, (128, model), 0)
    column = lax.broadcasted_iota(jnp.int32, (128, model), 1)
    total = jnp.zeros((experts + 8, model), f32)
    for at in range(each):
        to = (row * each + at == column).astype(bf16)
        picked = pl.ds(at, experts + 8, stride=each)
        total = total + dot_nn(mine_s[picked, :].astype(bf16), to)
        total = total + dot_nn(other_s[picked, :].astype(bf16), to)
    router_o[...] = total[:experts, :]
    one_o[...] = total[experts : experts + 1, :].reshape(model)
    two_o[...] = total[experts + 1 : experts + 2, :].reshape(model)


def token_order(rows):
    steps_in = rows // SUB
    row = lax.broadcasted_iota(jnp.int32, (rows, rows), 0)
    column = lax.broadcasted_iota(jnp.int32, (rows, rows), 1)
    return ((row % SUB) * steps_in + row // SUB == column).astype(bf16)


def exchange(values):
    return lax.all_to_all(values, "wide", split_axis=0, concat_axis=0, tiled=True)


def exchange_near(values, members):
    groups = [[u * members + z for z in range(members)] for u in range(32 // members)]
    blocks = values.reshape(members, -1, values.shape[1])
    return lax.all_to_all(
        blocks, "wide", split_axis=0, concat_axis=0, tiled=True, axis_index_groups=groups
    ).reshape(values.shape)


def exchange_far(values, members):
    groups = [[u * members + z for u in range(32 // members)] for z in range(members)]
    blocks = values.reshape(32 // members, -1, values.shape[1])
    return lax.all_to_all(
        blocks, "wide", split_axis=0, concat_axis=0, tiled=True, axis_index_groups=groups
    ).reshape(values.shape)


def gathered_place(place):
    return (place // 8 * 4 + place % 4) * 2 + place // 4 % 2


def exchange_channels(values):
    order = sorted(range(32), key=gathered_place)
    return lax.all_to_all(
        values, "wide", split_axis=0, concat_axis=0, tiled=True, axis_index_groups=[order]
    )


def other_chip(values):
    return lax.ppermute(values, "wide", [(i, i ^ 4) for i in range(32)])


def pair_up(values, partner, place):
    first = (place // 4) % 2 == 0
    return jnp.concatenate(
        [jnp.where(first, values, partner), jnp.where(first, partner, values)], axis=0
    )


def gather_pairs(both):
    groups = [[(y * 2 + x) * 4 + z for y in range(4) for z in range(4)] for x in range(2)]
    return lax.all_gather(both, "wide", axis=0, tiled=True, axis_index_groups=groups)


def exchange_sides(values):
    groups = [
        [(side * 2 + core) * 32 + place for side in range(2) for place in range(32)]
        for core in range(2)
    ]
    return lax.all_to_all(
        values, ("dp", "wide"), split_axis=0, concat_axis=0, tiled=True, axis_index_groups=groups
    )


def other_core(values):
    return lax.ppermute(values, "dp", [(0, 1), (1, 0), (2, 3), (3, 2)])


def other_side(values):
    return lax.ppermute(values, "dp", [(0, 2), (2, 0), (1, 3), (3, 1)])


def body(
    hidden, cotangent, routes, seg_lengths, gain_mix, in_x, in_z, conv_w, conv_b, x_proj, dt_proj,
    dt_bias, a_log, skip_d, out_proj, gain_moe, router, w_gate, w_up, w_down,
):
    rows, model = hidden.shape
    places = lax.axis_size("wide")
    place = lax.axis_index("wide")
    core = (lax.axis_index("dp") % 2).astype(jnp.int32).reshape(1)
    place_arr = place.astype(jnp.int32).reshape(1)
    width = in_x.shape[1]
    di = width * places
    count = a_log.shape[0]
    rank = dt_proj.shape[0]
    experts = router.shape[1]
    capacity = max(CAP * rows // (4 * places), 2)
    stride = -(-2 * capacity // 16) * 16
    half = model // 2
    steps_in = rows // SUB
    shift = SUB.bit_length() - 1
    span = 3 * width
    members = 4
    side = (place // 4 % 2).astype(jnp.int32).reshape(1)

    gate_share = call(
        pack_gate_kernel, [shape((width, model), bf16)], [], (core, in_z.T, out_proj), smem=1
    )[0]
    gate_share, x_proj = lax.optimization_barrier((gate_share, x_proj))
    pay_one = call(
        partial(pack_kernel, places=places),
        [shape((di, half + 128), bf16)],
        [],
        (core, in_x.T, x_proj, dt_proj, conv_w, conv_b, dt_bias, skip_d, a_log),
        smem=1,
    )[0]
    pay_one, hidden, cotangent, routes, seg_lengths = lax.optimization_barrier(
        (pay_one, hidden, cotangent, routes, seg_lengths)
    )
    gate_partner = other_chip(gate_share)
    pay_one, gate_partner = lax.optimization_barrier((pay_one, gate_partner))
    wm = exchange_channels(pay_one.reshape(places, width, half + 128)).reshape(di, half + 128)
    zm = gather_pairs(pair_up(gate_share, gate_partner, place))
    nrm, tail, hid, cot, route, aux = call(
        prepare_kernel,
        [
            shape((rows, model), bf16),
            shape((16, model), bf16),
            shape((rows, model), bf16),
            shape((rows, model), bf16),
            shape((rows, 1), jnp.int32),
            shape((rows, 128)),
        ],
        [],
        (place_arr * rows, seg_lengths, hidden, cotangent, routes.T, gain_mix),
        smem=2,
    )
    halo = lax.ppermute(tail, "wide", [(i, i + 1) for i in range(places - 1)])
    nrm_partner = other_chip(nrm)
    wm, halo = lax.optimization_barrier((wm, halo))
    wo = other_core(wm)
    ext, pre, steps, sig_step, small, x_in, tpre, tsuf, states, par, xd_weight, sd, q = call(
        partial(front_kernel, rank=rank, count=count),
        [
            shape((rows + (KC - 1) * SUB, di)),
            shape((rows, di)),
            shape((rows, di)),
            shape((rows, di)),
            shape((rows, 128)),
            shape((count, SUB, di)),
            shape((SUB, di)),
            shape((SUB, di)),
            shape((members * count, di + 256), bf16),
            shape((8 + count, di)),
            shape((di, 128), bf16),
            shape((rows, di)),
            shape((rows, di)),
        ],
        [
            pltpu.VMEM((steps_in * count, SUB, 128), f32),
            pltpu.VMEM((2, rows + 16, half), bf16),
            pltpu.VMEM((16, 128), f32),
        ],
        (core, nrm, halo, wm, wo, aux),
        smem=1,
        late=(3, 4),
        early=(0, 1, 2, 3, 9, 10, 11, 12),
    )

    near = exchange_near(states, members)
    zm, nrm_partner, near = lax.optimization_barrier((zm, nrm_partner, near))
    zo = other_core(zm)
    z_lanes = pl.ds(0, half)
    out_lanes = pl.ds(half, half)
    gate_z = call(
        gate_kernel,
        [shape((rows, di))],
        [pltpu.VMEM((2, rows, half), bf16)],
        (core, nrm, zm, zo),
        smem=1,
        late=(2, 3),
        lanes={2: z_lanes, 3: z_lanes},
    )[0]
    states = call(
        partial(forward_group_kernel, di=di, count=count),
        [shape((places // members * count, di + 256), bf16)],
        [pltpu.VMEM((count, di), f32)] * 2,
        (near, par),
        limit=12 * 1024 * 1024,
    )[0]
    states = exchange_far(states, members)

    nrm_pair = pair_up(nrm, nrm_partner, place)
    states, gate_z, nrm_pair = lax.optimization_barrier((states, gate_z, nrm_pair))
    normed_all = gather_pairs(nrm_pair)
    scanned, send, middle, ntwo, chances, meta, hot, entry = call(
        partial(
            middle_kernel,
            rank=rank,
            count=count,
            experts=experts,
            stride=stride,
            capacity=capacity,
            shift=shift,
        ),
        [
            shape((rows, di)),
            shape((2 * experts * stride, 2 * model // 3), bf16),
            shape((rows, model)),
            shape((rows, model), bf16),
            shape((rows, experts)),
            shape((rows, 8)),
            shape((3, 2 * rows, experts * stride), bf16),
            shape((count, di)),
        ],
        [
            pltpu.VMEM((steps_in * count, SUB, 128), f32),
            pltpu.VMEM((steps_in * count, SUB, 128), f32),
            pltpu.VMEM((count, di), f32),
        ],
        (
            core, place_arr, zm, zo, par, aux, pre, sd, q, x_in, small, states, near, tpre, hid, cot,
            route, gain_moe, router.T, gate_z,
        ),
        smem=2,
        late=(11, 12, 9, 7, 8, 6, 19, 2, 3),
        early=(7, 0, 6, 2, 3),
        lanes={2: out_lanes, 3: out_lanes},
    )
    arrived = exchange_sides(send.reshape(2 * experts, stride, -1)).reshape(send.shape)
    slots = 2 * places * capacity
    theirs_in = other_core(arrived)
    expert_in, grad_rows, hidden_act, gate_grad, up_grad, ours, theirs = call(
        partial(expert_kernel, stride=stride, capacity=capacity),
        [shape((2 * slots, model), bf16)] * 2
        + [shape((2 * slots, w_gate.shape[2]), bf16)] * 3
        + [shape(send.shape, bf16)] * 2,
        [],
        (arrived, theirs_in, w_gate[0], w_up[0], w_down[0]),
        late=(2, 3, 4),
        early=(0, 1, 2, 3, 4, 5, 6),
    )
    back = (ours.astype(f32) + other_core(theirs).astype(f32)).astype(bf16)
    back = exchange_sides(back.reshape(2 * experts, stride, -1)).reshape(send.shape)
    grad_w_down = dot_tn(hidden_act, grad_rows)[None]
    grad_w_gate = dot_tn(expert_in, gate_grad)[None]
    grad_w_up = dot_tn(expert_in, up_grad)[None]
    back, grad_w_down, grad_w_gate, grad_w_up = lax.optimization_barrier(
        (back, grad_w_down, grad_w_gate, grad_w_up)
    )

    combined, mixlow, mgrad, ggrad, sgrad, gain_two, y_in, adjoints = call(
        partial(back_kernel, rank=rank, count=count, experts=experts),
        [
            shape((rows, model)),
            shape((rows, model), bf16),
            shape((rows, model)),
            shape((rows, di)),
            shape((rows, di)),
            shape((1, model)),
            shape((count, SUB, di)),
            shape((members * count, di + 256 + half), bf16),
        ],
        [
            pltpu.VMEM((steps_in * count, SUB, 128), f32),
            pltpu.VMEM((2, rows, half), bf16),
            pltpu.VMEM((count, di), f32),
            pltpu.VMEM((16, 128), f32),
        ],
        (
            core, back, zm, zo, par, aux, sd, small, gate_z, hot, middle, meta, chances, route,
            cot, gain_moe, router.T, ntwo,
        ),
        smem=1,
        late=(2, 3, 8, 6),
        early=(1, 2, 0, 3, 4),
        lanes={2: out_lanes, 3: out_lanes},
    )
    near_back = exchange_near(adjoints, members)
    adjoints = call(
        partial(backward_group_kernel, di=di, count=count),
        [shape((places // members * count, di + 256 + half), bf16)],
        [pltpu.VMEM((count, di), f32)] * 2,
        (near_back, par),
        limit=12 * 1024 * 1024,
    )[0]
    adjoints = exchange_far(adjoints, members)
    out, comb, skip_part, ngrad_z = call(
        partial(aside_kernel, width=width, span=span),
        [
            shape((rows, model), bf16),
            shape((places * span, 128), bf16),
            shape((1, di)),
            shape((2, rows, half)),
        ],
        [],
        (
            core, side, zm, zo, aux, pre, gate_z, scanned, ggrad, combined, middle, meta,
        ),
        smem=2,
        late=(2, 3),
        lanes={2: z_lanes, 3: z_lanes},
    )
    adjoints, comb = lax.optimization_barrier((adjoints, comb))
    mixlow, normed_all = lax.optimization_barrier((mixlow, normed_all))
    mix_half = gather_pairs(mixlow)
    comb_got = exchange_channels(comb.reshape(places, span, 128))

    pay, ngrad, beyond = call(
        partial(tail_kernel, rank=rank, count=count, width=width),
        [shape((di, 384), bf16), shape((rows, model)), shape((SUB, model))],
        [
            pltpu.VMEM((rows, di), bf16),
            pltpu.VMEM((16, di), bf16),
            pltpu.VMEM((rows, di), f32),
            pltpu.VMEM((di, 128), bf16),
            pltpu.VMEM((8 + count, di), f32),
            pltpu.VMEM((count, half), f32),
        ]
        + [pltpu.VMEM((steps_in * count, SUB, 128), f32)] * 4
        + [pltpu.VMEM(((steps_in + 1) * count, SUB, 128), f32)]
        + [pltpu.VMEM((steps_in * count, SUB, 128), f32)]
        + [pltpu.VMEM((rows, di), f32)] * 2
        + [pltpu.VMEM((rows, di), bf16)]
        + [pltpu.VMEM((count, di), f32)] * 2,
        (
            place_arr, core, xd_weight, par, sd, q, pre, steps, sig_step, small, x_in, tpre, entry,
            y_in, tsuf, adjoints, near_back, sgrad, halo, aux, ext, wm, wo, ngrad_z, skip_part, hid,
            gain_two,
        ),
        smem=2,
        late=(15, 16, 10, 4, 5, 17, 13, 6, 8, 2, 7, 20, 21, 22, 23, 25),
        lanes={21: z_lanes, 22: z_lanes},
    )
    got_pay = exchange_channels(pay.reshape(places, width, 384))
    beyond = lax.ppermute(beyond, "wide", [(i + 1, i) for i in range(places - 1)])
    z_ready, out_ready, out_theirs = call(
        ready_kernel,
        [shape((width, model), bf16)] * 3,
        [
            pltpu.VMEM((width, places * rows), bf16),
            pltpu.VMEM((2 * width, places // 2 * rows), bf16),
        ],
        (side, comb_got, normed_all, mix_half),
        smem=1,
        late=(3,),
        limit=24 * 1024 * 1024,
    )
    out_other = other_chip(out_theirs)
    got_pay, out_other, beyond = lax.optimization_barrier((got_pay, out_other, beyond))
    first_grad = call(
        hidden_kernel, [shape((rows, model))], [], (ngrad, beyond, hid, mgrad, gain_mix), limit=12 * 1024 * 1024
    )[0]
    out_ready = (out_ready.astype(f32) + out_other.astype(f32)).astype(bf16)
    ready = jnp.concatenate([z_ready, out_ready], axis=0)
    ready = (ready.astype(f32) + other_core(ready).astype(f32)).astype(bf16)
    ready_side = other_side(ready)
    per_place = model // width
    mats = call(
        partial(grads_kernel, base=8 + count + 2 * per_place),
        [shape((2 * width, 256 + places * per_place), bf16)],
        [pltpu.VMEM((width, places * rows), bf16)],
        (got_pay, normed_all),
        limit=24 * 1024 * 1024,
    )[0]
    mats = (mats.astype(f32) + other_core(mats).astype(f32)).astype(bf16)
    grad_x, grad_z, grad_out, grad_conv, grad_bias, grad_xp, grad_dt, grad_db, grad_al, grad_sk, grad_router, gain_one, gain_two = call(
        partial(final_kernel, rank=rank, count=count, experts=experts),
        [
            shape((width, model)),
            shape((width, model)),
            shape((width, model)),
            shape((KC, width)),
            shape((width,)),
            shape((width, rank + 2 * count)),
            shape((rank, width)),
            shape((width,)),
            shape((count, width)),
            shape((width,)),
            shape((experts, model)),
            shape((model,)),
            shape((model,)),
        ],
        [pltpu.VMEM(((experts + 8) * per_place, 128), f32)] * 2,
        (mats, other_side(mats), ready, ready_side),
        limit=12 * 1024 * 1024,
    )
    return (
        out,
        first_grad,
        gain_one,
        grad_x.T,
        grad_z.T,
        grad_conv,
        grad_bias,
        grad_xp,
        grad_dt,
        grad_db,
        grad_al,
        grad_sk,
        grad_out,
        gain_two,
        grad_router.T,
        grad_w_gate,
        grad_w_up,
        grad_w_down,
    )


def solution(mesh):
    rows = P(("dp", "wide"), None)
    expert_columns = P("wide", None, "dp")
    expert_rows = P("wide", "dp", None)
    placed = (
        rows, rows, rows, P("dp", None), P(), P(None, "wide"), P(None, "wide"), P(None, "wide"),
        P("wide"), P("wide", None), P(None, "wide"), P("wide"), P(None, "wide"), P("wide"),
        P("wide", None), P(), P(), expert_columns, expert_columns, expert_rows,
    )
    given = (
        rows, rows, P(), P(None, "wide"), P(None, "wide"), P(None, "wide"), P("wide"),
        P("wide", None), P(None, "wide"), P("wide"), P(None, "wide"), P("wide"), P("wide", None),
        P(), P(), expert_columns, expert_columns, expert_rows,
    )
    return jax.shard_map(body, mesh=mesh, in_specs=placed, out_specs=given, check_vma=False)
```

```python
from functools import partial

import jax
import jax.numpy as jnp
from jax import lax
from jax.experimental import pallas as pl
from jax.experimental.pallas import tpu as pltpu
from jax.sharding import PartitionSpec as P

f32 = jnp.float32
bf16 = jnp.bfloat16
KC = 4
SUB = 8
CAP = 5
STOP = 1e6
LOG2E = 1.4426950408889634
LN2 = 0.6931471805599453
epsilon = 1e-05
VMEM_LIMIT = 56 * 1024 * 1024


def dot_nn(left, right):
    return lax.dot_general(left, right, (((1,), (0,)), ((), ())), preferred_element_type=f32)


def dot_nt(left, right):
    return lax.dot_general(left, right, (((1,), (1,)), ((), ())), preferred_element_type=f32)


def dot_tn(left, right):
    return lax.dot_general(left, right, (((0,), (0,)), ((), ())), preferred_element_type=f32)


class Moves:
    def __init__(self):
        self.arriving = {}
        self.leaving = {}
        self.started = []

    def need(self, *refs):
        for ref in refs:
            copy = self.arriving.pop(id(ref), None)
            if copy is not None:
                copy.wait()

    def done(self, *refs):
        for ref in refs:
            copy = self.leaving.pop(id(ref), None)
            if copy is not None:
                copy.start()
                self.started.append(copy)


def call(
    kernel, out_shapes, scratch, args, smem=0, late=(), early=(), lanes=None, limit=VMEM_LIMIT
):
    lanes = lanes or {}
    vmem = pl.BlockSpec(memory_space=pltpu.VMEM)
    hbm = pl.BlockSpec(memory_space=pl.ANY)
    specs = [pl.BlockSpec(memory_space=pltpu.SMEM)] * smem
    specs += [hbm if i in late else vmem for i in range(smem, len(args))]
    buffers = []
    for i in late:
        dims = (args[i].shape[0], lanes[i].size) if i in lanes else args[i].shape
        buffers.append(pltpu.VMEM(dims, args[i].dtype))
    buffers += [pltpu.VMEM(out_shapes[i].shape, out_shapes[i].dtype) for i in early]
    moving = len(buffers)
    extra = buffers + [pltpu.SemaphoreType.DMA((moving,))] if moving else []

    def staged(*refs):
        refs = list(refs)
        own = refs[len(refs) - moving - 1 : -1]
        semaphores = refs[-1]
        refs = refs[: len(refs) - moving - 1]
        moves = Moves()
        for k, i in enumerate(late):
            source = refs[i].at[:, lanes[i]] if i in lanes else refs[i]
            copy = pltpu.make_async_copy(source, own[k], semaphores.at[k])
            copy.start()
            refs[i] = own[k]
            moves.arriving[id(own[k])] = copy
        for k, i in enumerate(early, len(late)):
            at = len(args) + i
            moves.leaving[id(own[k])] = pltpu.make_async_copy(own[k], refs[at], semaphores.at[k])
            refs[at] = own[k]
        kernel(moves, *refs)
        moves.need(*own)
        moves.done(*own)
        for copy in moves.started:
            copy.wait()

    return pl.pallas_call(
        staged if moving else kernel,
        out_shape=out_shapes,
        in_specs=specs,
        out_specs=[hbm if i in early else vmem for i in range(len(out_shapes))],
        scratch_shapes=list(scratch) + extra,
        compiler_params=pltpu.CompilerParams(vmem_limit_bytes=limit),
    )(*args)


def shape(dims, dtype=f32):
    return jax.ShapeDtypeStruct(dims, dtype)


def group_of(di):
    return 256 if di % 256 == 0 else 128


def sublane_iota(width):
    return lax.broadcasted_iota(jnp.int32, (SUB, width), 0)


def from_before(block, first):
    row = sublane_iota(block.shape[1])
    return jnp.where(row == 0, jnp.broadcast_to(first, block.shape), pltpu.roll(block, 1, 0))


def from_after(block, last):
    row = sublane_iota(block.shape[1])
    return jnp.where(
        row == SUB - 1, jnp.broadcast_to(last, block.shape), pltpu.roll(block, SUB - 1, 0)
    )


def spread_columns(small, first, count, out):
    steps = small.shape[0] // SUB
    for j in range(steps):
        block = small[j * SUB : (j + 1) * SUB, :]
        for n in range(count):
            out[j * count + n] = jnp.broadcast_to(block[:, first + n : first + n + 1], (SUB, 128))


def prefix_states(decay, state):
    row = sublane_iota(state.shape[1])
    for shift in (1, 2, 4):
        inside = row >= shift
        state = state + decay * jnp.where(inside, pltpu.roll(state, shift, 0), 0.0)
        decay = decay * jnp.where(inside, pltpu.roll(decay, shift, 0), 1.0)
    return state


def suffix_states(decay, state):
    row = sublane_iota(state.shape[1])
    for shift in (1, 2, 4):
        inside = row < SUB - shift
        state = state + decay * jnp.where(inside, pltpu.roll(state, SUB - shift, 0), 0.0)
        decay = decay * jnp.where(inside, pltpu.roll(decay, SUB - shift, 0), 1.0)
    return state


def prefix_sum(values):
    row = sublane_iota(values.shape[1])
    for shift in (1, 2, 4):
        values = values + jnp.where(row >= shift, pltpu.roll(values, shift, 0), 0.0)
    return values


def suffix_sum(values):
    row = sublane_iota(values.shape[1])
    for shift in (1, 2, 4):
        values = values + jnp.where(row < SUB - shift, pltpu.roll(values, SUB - shift, 0), 0.0)
    return values


def one_hot(dims, offset):
    row = lax.broadcasted_iota(jnp.int32, dims, 0)
    column = lax.broadcasted_iota(jnp.int32, dims, 1)
    return (row + offset == column).astype(bf16)


def pack_gate_kernel(core, in_z, out_proj, gate_o):
    half = in_z.shape[1] // 2
    start = pl.multiple_of(core[0] * half, 128)
    gate_o[:, :half] = in_z[:, pl.ds(start, half)]
    gate_o[:, half:] = out_proj[:, pl.ds(start, half)]


def pack_kernel(
    core, in_x, x_proj, dt_proj, conv_w, conv_b, dt_bias, skip_d, a_log, out, *, places
):
    width, model = in_x.shape
    half = model // 2
    here = core[0]
    mine = in_x[:, pl.ds(pl.multiple_of(here * half, 128), half)]
    narrow = x_proj.shape[1]
    steps = dot_nn(x_proj[...], one_hot((narrow, 128), 0)) + dot_tn(
        dt_proj[...], one_hot((dt_proj.shape[0], 128), 128 - dt_proj.shape[0])
    )
    values = jnp.concatenate(
        [
            conv_w[...],
            conv_b[...].reshape(1, width),
            dt_bias[...].reshape(1, width),
            skip_d[...].reshape(1, width),
            jnp.zeros((1, width), f32),
            a_log[...],
        ],
        axis=0,
    )
    top = values.astype(bf16)
    left = values - top.astype(f32)
    mid = left.astype(bf16)
    low = (left - mid.astype(f32)).astype(bf16)
    count = values.shape[0]
    extra = dot_tn(top, one_hot((count, 128), 0))
    extra = extra + dot_tn(mid, one_hot((count, 128), count))
    extra = extra + dot_tn(low, one_hot((count, 128), 2 * count))
    rest = jnp.where(here == 0, steps, extra).astype(bf16)
    for place in range(places):
        out[place * width : (place + 1) * width, :half] = mine
        out[place * width : (place + 1) * width, half:] = rest


def prepare_kernel(
    base, lengths, hidden, cot, route, gain, nrm_o, tail_o, hid_o, cot_o, route_o, aux_o
):
    rows = hidden.shape[0]
    steps_in = rows // SUB
    row = lax.broadcasted_iota(jnp.int32, (rows, rows), 0)
    column = lax.broadcasted_iota(jnp.int32, (rows, rows), 1)
    in_order = (row % SUB) * steps_in + row // SUB == column
    order = in_order.astype(bf16)
    hid = dot_nn(order, hidden[...])
    hid_o[...] = hid.astype(bf16)
    cot_o[...] = dot_nn(order, cot[...]).astype(bf16)
    ours = jnp.where(in_order, jnp.broadcast_to(route[...], (rows, rows)), 0)
    route_o[...] = jnp.sum(ours, axis=1, keepdims=True)
    scale = lax.rsqrt(jnp.mean(hid * hid, axis=1, keepdims=True) + epsilon)
    normed = (hid * scale * gain[...].reshape(1, -1)).astype(bf16)
    nrm_o[...] = normed
    tail_row = lax.broadcasted_iota(jnp.int32, (16, rows), 0)
    tail_column = lax.broadcasted_iota(jnp.int32, (16, rows), 1)
    picked = (tail_column == rows - 1 - (KC - 2 - tail_row) * SUB) & (tail_row < KC - 1)
    tail = dot_nn(picked.astype(bf16), normed)
    tail_row = tail_row - SUB
    picked = (tail_column == rows - 1 - (KC - 2 - tail_row) * SUB) & (tail_row < KC - 1)
    picked = picked & (tail_row >= 0)
    tail_o[...] = (tail + dot_nn(picked.astype(bf16), hid.astype(bf16))).astype(bf16)

    def layout(position, lane):
        back = position - (lane + 1)
        segment = jnp.zeros_like(position)
        segment_back = jnp.zeros_like(position)
        reset = position == 0
        end = jnp.int32(0)
        for j in range(lengths.shape[1] - 1):
            end = end + lengths[0, j]
            segment = segment + (position >= end).astype(jnp.int32)
            segment_back = segment_back + (back >= end).astype(jnp.int32)
            reset = reset | (position == end)
        same = (back >= 0) & (segment == segment_back)
        live = position < end
        picked = jnp.where(lane == KC - 1, live.astype(f32), reset.astype(f32))
        return jnp.where(lane < KC - 1, same.astype(f32), picked)

    at = lax.broadcasted_iota(jnp.int32, (rows, 128), 0)
    lane = lax.broadcasted_iota(jnp.int32, (rows, 128), 1)
    aux_o[...] = layout(base[0] + (at % SUB) * steps_in + at // SUB, lane)


def front_kernel(
    moves, core, nrm_in, halo_in, wm, wo, aux, ext_o, pre_o, steps_o, sig_o, small_o, x_o, tpre_o, tsuf_o,
    state_o, par_o, xd_o, sd_s, q_s, bw_s, nrm_s, sum_s, *, rank, count
):
    rows, di = pre_o.shape
    half = wo.shape[1] - 128
    steps_in = rows // SUB
    gs = group_of(di)
    low = core[0] == 0
    nrm_s[0, :rows] = jnp.where(low, nrm_in[:, :half], nrm_in[:, half:])
    nrm_s[1, :rows] = jnp.where(low, nrm_in[:, half:], nrm_in[:, :half])
    nrm_s[0, rows:] = jnp.where(low, halo_in[:, :half], halo_in[:, half:])
    nrm_s[1, rows:] = jnp.where(low, halo_in[:, half:], halo_in[:, :half])
    small_o[...] = jnp.zeros_like(small_o)
    moves.need(wm, wo)
    par = par_o
    total_rows = par_o.shape[0]

    def unpack(g, _):
        lanes = pl.ds(pl.multiple_of(g * 128, 128), 128)
        mine = wm[lanes, half:]
        other = wo[lanes, half:]
        xd_o[lanes, :] = jnp.where(low, mine, other)
        turned = jnp.where(low, other, mine).astype(f32).T
        par_o[:, lanes] = (
            turned[:total_rows, :]
            + turned[total_rows : 2 * total_rows, :]
            + turned[2 * total_rows : 3 * total_rows, :]
        )
        return 0

    lax.fori_loop(0, di // 128, unpack, 0)

    def project(g, _):
        lanes = pl.ds(pl.multiple_of(g * gs, gs), gs)
        inner = dot_nt(nrm_s[0], wm[lanes, :half]) + dot_nt(nrm_s[1], wo[lanes, :half])
        for back in range(1, KC):
            block = inner[rows - back * SUB : rows - (back - 1) * SUB, :]
            halo = inner[rows + KC - 1 - back : rows + KC - back, :]
            ext_o[(KC - 1 - back) * SUB : (KC - back) * SUB, lanes] = from_before(block, halo)
        ext_o[(KC - 1) * SUB :, lanes] = inner[:rows, :]
        total = par[KC : KC + 1, lanes] + par[KC - 1 : KC, lanes] * inner[:rows, :]
        for back in range(1, KC):
            shifted = ext_o[(KC - 1 - back) * SUB : (KC - 1 - back) * SUB + rows, lanes]
            total = total + par[KC - 1 - back : KC - back, lanes] * shifted * aux[:, back - 1 : back]
        pre_o[:, lanes] = total
        act = total * jax.nn.sigmoid(total)
        q_s[:, lanes] = act
        small_o[...] += dot_nn(act.astype(bf16), xd_o[lanes, :])
        return 0

    lax.fori_loop(0, di // gs, project, 0)
    moves.done(ext_o, pre_o, par_o, xd_o)
    small = small_o[...]
    lane = lax.broadcasted_iota(jnp.int32, small.shape, 1)
    step_low = jnp.where(lane >= 128 - rank, pltpu.roll(small, 128 - rank, 1), 0.0).astype(bf16)
    spread_columns(small, rank, count, bw_s)

    def stepping(g, _):
        lanes = pl.ds(pl.multiple_of(g * gs, gs), gs)
        step_pre = dot_nt(step_low, xd_o[lanes, :]) + par[KC + 1 : KC + 2, lanes]
        small_exp = jnp.exp(-jnp.abs(step_pre))
        steps = jnp.maximum(step_pre, 0.0) + jnp.log1p(small_exp)
        steps_o[:, lanes] = steps
        sig_o[:, lanes] = jax.nn.sigmoid(step_pre)
        q_s[:, lanes] = q_s[:, lanes] * steps
        sd_s[:, lanes] = jnp.where(aux[:, 4:5] > 0.5, STOP, steps)
        return 0

    lax.fori_loop(0, di // gs, stepping, 0)
    moves.done(steps_o, sig_o, sd_s, q_s)

    def chunk(g, _):
        lanes = pl.ds(pl.multiple_of(g * 128, 128), 128)
        rates = [
            jnp.broadcast_to(-LOG2E * jnp.exp(par[8 + n : 9 + n, lanes]), (SUB, 128))
            for n in range(count)
        ]

        def step(j, carry):
            states, total = carry
            at = pl.ds(pl.multiple_of(j * SUB, SUB), SUB)
            sd = sd_s[at, lanes]
            q = q_s[at, lanes]
            states = tuple(
                jnp.exp2(sd * rates[n]) * states[n] + q * bw_s[j * count + n] for n in range(count)
            )
            return (states, total + sd)

        zero = jnp.zeros((SUB, 128), f32)
        states, total = lax.fori_loop(0, steps_in, step, ((zero,) * count, zero), unroll=8)
        row = sublane_iota(128)
        ahead = prefix_sum(total)
        behind = suffix_sum(total)
        tpre_o[:, lanes] = jnp.where(row == 0, 0.0, pltpu.roll(ahead, 1, 0))
        tsuf_o[:, lanes] = jnp.where(row == SUB - 1, 0.0, pltpu.roll(behind, SUB - 1, 0))
        last = []
        for n in range(count):
            joined = prefix_states(jnp.exp2(rates[n] * total), states[n])
            x_o[n, :, lanes] = jnp.where(row == 0, 0.0, pltpu.roll(joined, 1, 0))
            last.append(joined[SUB - 1 : SUB, :])
        sum_s[pl.ds(g, 1), :] = ahead[SUB - 1 : SUB, :]
        to_copies(state_o, jnp.concatenate(last, axis=0).astype(bf16), lanes)
        return 0

    sum_s[...] = jnp.zeros_like(sum_s)
    lax.fori_loop(0, di // 128, chunk, 0)
    sums = sum_s[...]
    top = sums.astype(bf16)
    left = (sums - top.astype(f32)).astype(bf16)
    to_copies(state_o, top, slice(di, di + 128))
    to_copies(state_o, left, slice(di + 128, di + 256))


def to_copies(out, values, lanes):
    count = values.shape[0]
    for place in range(out.shape[0] // count):
        out[place * count : (place + 1) * count, lanes] = values


def negative_rates(par, out):
    out[...] = -LOG2E * jnp.exp(par[8:, :])


def group_kernel(arrived, out, state_s, sum_s, *, di, count, reverse):
    members = arrived.shape[0] // count
    rest = arrived.shape[1] - di - 256
    copies = out.shape[0] // count
    state_s[...] = jnp.zeros_like(state_s)
    total = jnp.zeros((count, 128), f32)
    for place in range(members - 1, -1, -1) if reverse else range(members):
        block = slice(place * count, (place + 1) * count)
        sums = arrived[block, di : di + 128].astype(f32)
        sums = sums + arrived[block, di + 128 : di + 256].astype(f32)
        total = total + sums
        carry_step(sums, arrived[block, :di], sum_s, state_s)
    joined = state_s[...].astype(bf16)
    top = total.astype(bf16)
    left = (total - top.astype(f32)).astype(bf16)
    for copy in range(copies):
        block = slice(copy * count, (copy + 1) * count)
        out[block, :di] = joined
        out[block, di : di + 128] = top
        out[block, di + 128 : di + 256] = left
    if rest:
        extra = jnp.zeros((count, rest), f32)
        for place in range(members):
            extra = extra + arrived[place * count : (place + 1) * count, di + 256 :].astype(f32)
        gap = jnp.zeros((count - 2, rest), f32)
        for copy in range(copies):
            rows = jnp.concatenate([extra[2 * copy : 2 * copy + 2, :], gap], axis=0)
            out[copy * count : (copy + 1) * count, di + 256 :] = rows.astype(bf16)


def forward_group_kernel(arrived, par, out, state_s, rate_s, *, di, count):
    negative_rates(par, rate_s)
    group_kernel(arrived, out, state_s, rate_s, di=di, count=count, reverse=False)


def backward_group_kernel(arrived, par, out, state_s, rate_s, *, di, count):
    negative_rates(par, rate_s)
    group_kernel(arrived, out, state_s, rate_s, di=di, count=count, reverse=True)


def step_sums(arrived, block, di):
    return arrived[block, di : di + 128].astype(f32) + arrived[block, di + 128 : di + 256].astype(
        f32
    )


def carry_step(decay_sums, arrived, rate_s, state_s):
    for g in range(state_s.shape[1] // 128):
        lanes = slice(g * 128, (g + 1) * 128)
        decay = jnp.exp2(rate_s[:, lanes] * decay_sums[g : g + 1, :])
        state_s[:, lanes] = decay * state_s[:, lanes] + arrived[:, lanes].astype(f32)


def gate_kernel(moves, core, nrm, zm, zo, gate_z_o, nrm_s):
    rows, di = gate_z_o.shape
    half = zm.shape[1]
    gs = group_of(di)
    low = core[0] == 0
    nrm_s[0] = jnp.where(low, nrm[:, :half], nrm[:, half:])
    nrm_s[1] = jnp.where(low, nrm[:, half:], nrm[:, :half])
    moves.need(zm, zo)

    def project(g, _):
        lanes = pl.ds(pl.multiple_of(g * gs, gs), gs)
        gate_z_o[:, lanes] = dot_nt(nrm_s[0], zm[lanes, :]) + dot_nt(nrm_s[1], zo[lanes, :])
        return 0

    lax.fori_loop(0, di // gs, project, 0)


def middle_kernel(
    moves, core, place, om, oo, par, aux, pre, sd, q, x_in, small, arrived, near, tpre, hid, cot,
    route, gain, router, gate_z, scan_o, send_o, middle_o, ntwo_o, chance_o, meta_o, hot_o,
    entry_o, bw_s, cw_s, rate_s, *, rank, count, experts, stride, capacity, shift
):
    rows, di = pre.shape
    half = om.shape[1]
    steps_in = rows // SUB
    gs = group_of(di)
    low = core[0] == 0
    spread_columns(small[...], rank, count, bw_s)
    spread_columns(small[...], rank + count, count, cw_s)
    negative_rates(par, rate_s)
    moves.need(arrived, near)
    entry_o[...] = jnp.zeros_like(entry_o)
    members = near.shape[0] // count

    def before_here(there, _):
        block = pl.ds(pl.multiple_of(there * count, count), count)
        carry_step(step_sums(arrived, block, di), arrived[block, :di], rate_s, entry_o)
        return 0

    def just_before(there, _):
        block = pl.ds(pl.multiple_of(there * count, count), count)
        carry_step(step_sums(near, block, di), near[block, :di], rate_s, entry_o)
        return 0

    lax.fori_loop(0, place[0] // members, before_here, 0)
    lax.fori_loop(0, place[0] % members, just_before, 0)
    moves.done(entry_o)
    moves.need(x_in, sd, q)

    def scan(g, _):
        lanes = pl.ds(pl.multiple_of(g * 128, 128), 128)
        rates = [jnp.broadcast_to(rate_s[n : n + 1, lanes], (SUB, 128)) for n in range(count)]
        before = tpre[:, lanes]
        first = tuple(
            x_in[n, :, lanes] + jnp.exp2(rates[n] * before) * entry_o[n : n + 1, lanes]
            for n in range(count)
        )
        def step(j, states):
            at = pl.ds(pl.multiple_of(j * SUB, SUB), SUB)
            sd_here = sd[at, lanes]
            q_here = q[at, lanes]
            total = jnp.zeros((SUB, 128), f32)
            fresh = []
            for n in range(count):
                state = jnp.exp2(sd_here * rates[n]) * states[n] + q_here * bw_s[j * count + n]
                total = total + state * cw_s[j * count + n]
                fresh.append(state)
            scan_o[at, lanes] = total
            return tuple(fresh)

        lax.fori_loop(0, steps_in, step, first, unroll=8)
        return 0

    lax.fori_loop(0, di // 128, scan, 0)

    def gating(g, carry):
        mine, other = carry
        lanes = pl.ds(pl.multiple_of(g * gs, gs), gs)
        z = gate_z[:, lanes]
        pre_here = pre[:, lanes]
        scanned = scan_o[:, lanes] + par[KC + 2 : KC + 3, lanes] * (
            pre_here * jax.nn.sigmoid(pre_here)
        )
        scan_o[:, lanes] = scanned
        gated = (scanned * (z * jax.nn.sigmoid(z)) * aux[:, 3:4]).astype(bf16)
        return (mine + dot_nn(gated, om[lanes, :]), other + dot_nn(gated, oo[lanes, :]))

    zero = jnp.zeros((rows, half), f32)
    moves.need(pre, gate_z, om, oo)
    mine, other = lax.fori_loop(0, di // gs, gating, (zero, zero))
    moves.done(scan_o)
    mixed = jnp.concatenate([jnp.where(low, mine, other), jnp.where(low, other, mine)], axis=1)
    middle = hid[...].astype(f32) + mixed
    middle_o[...] = middle
    scale = lax.rsqrt(jnp.mean(middle * middle, axis=1, keepdims=True) + epsilon)
    ntwo = (middle * scale * gain[...].reshape(1, -1)).astype(bf16)
    ntwo_o[...] = ntwo
    logits = dot_nt(ntwo, router[...])
    top = jnp.max(logits, axis=1, keepdims=True)
    raised = jnp.exp(logits - top)
    chances = raised / jnp.sum(raised, axis=1, keepdims=True)
    chance_o[...] = chances
    lane = lax.broadcasted_iota(jnp.int32, (rows, experts), 1)
    chosen = route[...] == lane
    chosen_f = chosen.astype(f32)
    gate = jnp.sum(chances * chosen_f, axis=1, keepdims=True)
    taken = chosen_f * aux[:, 3:4]
    here = lax.broadcasted_iota(jnp.int32, (rows, rows), 0)
    there = lax.broadcasted_iota(jnp.int32, (rows, rows), 1)
    own_id = (here & (SUB - 1)) * steps_in + (here >> shift)
    other_id = (there & (SUB - 1)) * steps_in + (there >> shift)
    earlier = (other_id < own_id).astype(bf16)
    ranks = jnp.sum(dot_nn(earlier, taken.astype(bf16)) * chosen_f, axis=1, keepdims=True)
    kept = aux[:, 3:4] * (ranks < capacity).astype(f32)
    weight = gate * kept
    up = (cot[...].astype(f32) * weight).astype(bf16)
    values = jnp.concatenate([ntwo, up], axis=0)
    rank_low = ranks.astype(jnp.int32)
    slot = jnp.concatenate([rank_low, rank_low + capacity], axis=0)
    block = route[...] * stride
    block = jnp.concatenate([block, block], axis=0)
    kept_on = jnp.concatenate([kept, kept], axis=0) > 0.5
    place = lax.broadcasted_iota(jnp.int32, (2 * rows, experts * stride), 1)
    wide_hot = ((block + slot == place) & kept_on).astype(bf16)
    at_last = (block + 2 * capacity + slot // 2 == place) & kept_on
    even_hot = (at_last & (slot % 2 == 0)).astype(bf16)
    odd_hot = (at_last & (slot % 2 == 1)).astype(bf16)
    hot_o[0] = wide_hot
    hot_o[1] = even_hot
    hot_o[2] = odd_hot
    moves.done(hot_o, middle_o, ntwo_o)
    third = ntwo.shape[1] // 3
    narrow = values[:, 2 * third :]
    last = jnp.concatenate([dot_tn(even_hot, narrow), dot_tn(odd_hot, narrow)], axis=1)
    packed = (dot_tn(wide_hot, values[:, : 2 * third]) + last).astype(bf16)
    send_o[: experts * stride, :] = packed
    send_o[experts * stride :, :] = packed
    lane8 = lax.broadcasted_iota(jnp.int32, (rows, 8), 1)
    meta_o[...] = jnp.where(
        lane8 == 0, gate, jnp.where(lane8 == 1, kept, jnp.where(lane8 == 2, scale, 0.0))
    )


def back_kernel(
    moves, core, back, om, oo, par, aux, sd, small, gate_z, hot, middle, meta, chances, route, cot, gain,
    router, ntwo, combined_o, mixlow_o, mgrad_o, ggrad_o, sg_o, gain_o, y_o, state_o, cw_s, mix_s,
    rate_s, sum_s, *, rank, count, experts
):
    rows, di = sd.shape
    half = om.shape[1]
    steps_in = rows // SUB
    gs = group_of(di)
    negative_rates(par, rate_s)
    slots = back.shape[0] // 2
    third = back.shape[1] // 2
    rows_back = (back[:slots, :].astype(f32) + back[slots:, :].astype(f32)).astype(bf16)
    last = dot_nn(hot[1], rows_back[:, :third]) + dot_nn(hot[2], rows_back[:, third:])
    both = jnp.concatenate([dot_nn(hot[0], rows_back), last], axis=1)
    combined = both[:rows, :]
    dispatch = both[rows:, :]
    combined_o[...] = combined
    gate = meta[:, 0:1]
    kept = meta[:, 1:2]
    scale = meta[:, 2:3]
    mid = middle[...]
    up = cot[...].astype(f32)
    gate_total = kept * jnp.sum(up * combined, axis=1, keepdims=True)
    lane = lax.broadcasted_iota(jnp.int32, (rows, experts), 1)
    chosen_f = (route[...] == lane).astype(f32)
    logit_grad = (gate * (chosen_f - chances[...]) * gate_total).astype(bf16)
    router_rows = dot_tn(logit_grad, ntwo[...])
    members = state_o.shape[0] // count
    for member in range(members):
        rows_here = []
        for group in range(experts // members):
            row = router_rows[group * members + member : group * members + member + 1, :]
            rows_here += [row[:, :half], row[:, half:]]
        block = slice(member * count, (member + 1) * count)
        state_o[block, di + 256 :] = jnp.concatenate(rows_here, axis=0).astype(bf16)
    ngrad = dot_nn(logit_grad, router[...]) + dispatch
    gain_o[...] = jnp.sum(ngrad * mid * scale, axis=0, keepdims=True)
    scaled = gain[...].reshape(1, -1) * ngrad
    cube = scale * scale * scale
    mgrad = up + scale * scaled - mid * cube * jnp.mean(mid * scaled, axis=1, keepdims=True)
    mgrad_o[...] = mgrad
    low = core[0] == 0
    mixlow = mgrad.astype(bf16)
    mixlow_o[...] = mixlow
    mix_s[0] = jnp.where(low, mixlow[:, :half], mixlow[:, half:])
    mix_s[1] = jnp.where(low, mixlow[:, half:], mixlow[:, :half])
    moves.done(mixlow_o, mgrad_o, combined_o)
    moves.need(om, oo, gate_z)

    def gating(g, _):
        lanes = pl.ds(pl.multiple_of(g * gs, gs), gs)
        ggrad = dot_nt(mix_s[0], om[lanes, :]) + dot_nt(mix_s[1], oo[lanes, :])
        ggrad = ggrad * aux[:, 3:4]
        ggrad_o[:, lanes] = ggrad
        z = gate_z[:, lanes]
        sg_o[:, lanes] = ggrad * (z * jax.nn.sigmoid(z))
        return 0

    lax.fori_loop(0, di // gs, gating, 0)
    moves.done(ggrad_o, sg_o)
    spread_columns(small[...], rank + count, count, cw_s)
    moves.need(sd)

    def chunk(g, _):
        lanes = pl.ds(pl.multiple_of(g * 128, 128), 128)
        rates = [jnp.broadcast_to(rate_s[n : n + 1, lanes], (SUB, 128)) for n in range(count)]

        def step(i, carry):
            grads, total = carry
            j = steps_in - 1 - i
            at = pl.ds(pl.multiple_of(j * SUB, SUB), SUB)
            sd_here = sd[at, lanes]
            sgrad = sg_o[at, lanes]
            grads = tuple(
                jnp.exp2(sd_here * rates[n]) * (grads[n] + sgrad * cw_s[j * count + n])
                for n in range(count)
            )
            return (grads, total + sd_here)

        zero = jnp.zeros((SUB, 128), f32)
        grads, total = lax.fori_loop(0, steps_in, step, ((zero,) * count, zero), unroll=8)
        row = sublane_iota(128)
        last = []
        for n in range(count):
            joined = suffix_states(jnp.exp2(rates[n] * total), grads[n])
            y_o[n, :, lanes] = jnp.where(row == SUB - 1, 0.0, pltpu.roll(joined, SUB - 1, 0))
            last.append(joined[0:1, :])
        sum_s[pl.ds(g, 1), :] = jnp.sum(total, axis=0, keepdims=True)
        to_copies(state_o, jnp.concatenate(last, axis=0).astype(bf16), lanes)
        return 0

    sum_s[...] = jnp.zeros_like(sum_s)
    lax.fori_loop(0, di // 128, chunk, 0)
    total = sum_s[...]
    top = total.astype(bf16)
    to_copies(state_o, top, slice(di, di + 128))
    to_copies(state_o, (total - top.astype(f32)).astype(bf16), slice(di + 128, di + 256))


def slot_rows(stride, capacity, blocks):
    dims = (2 * capacity * blocks, stride * blocks)
    row = lax.broadcasted_iota(jnp.int32, dims, 0)
    column = lax.broadcasted_iota(jnp.int32, dims, 1)
    half = capacity * blocks
    slot = row % capacity + row // half * capacity
    start = row % half // capacity * stride
    wide = (start + slot == column).astype(bf16)
    at_last = start + 2 * capacity + slot // 2 == column
    even = (at_last & (slot % 2 == 0)).astype(bf16)
    odd = (at_last & (slot % 2 == 1)).astype(bf16)
    return wide, even, odd


def unpack(packed, hots):
    wide, even, odd = hots
    third = packed.shape[1] // 2
    last = dot_nn(even, packed[:, :third]) + dot_nn(odd, packed[:, third:])
    return jnp.concatenate([dot_nn(wide, packed), last], axis=1).astype(bf16)


def pack(rows, hots):
    wide, even, odd = hots
    third = rows.shape[1] // 3
    narrow = rows[:, 2 * third :]
    last = jnp.concatenate([dot_tn(even, narrow), dot_tn(odd, narrow)], axis=1)
    return dot_tn(wide, rows[:, : 2 * third]) + last


def expert_kernel(
    moves, arrived, w_gate, w_up, w_down, w_gate_two, w_up_two, w_down_two, kept_o, sent_o, back_o,
    *, stride, capacity
):
    blocks = 16
    hots = slot_rows(stride, capacity, blocks)
    size = capacity * blocks
    groups = arrived.shape[0] // (stride * blocks)
    slots = kept_o.shape[0] // 5
    for group in range(groups):
        rows = unpack(arrived[group * stride * blocks : (group + 1) * stride * blocks, :], hots)
        at = group * size
        kept_o[at : at + size, :] = rows[:size, :]
        kept_o[slots + at : slots + at + size, :] = rows[size:, :]
    sent_o[: 2 * slots, :] = kept_o[: 2 * slots, :]
    inputs = kept_o[:slots, :]
    grads = kept_o[slots : 2 * slots, :]
    outputs = 0.0
    total = 0.0
    weights = ((sent_o, w_gate_two, w_up_two, w_down_two), (kept_o, w_gate, w_up, w_down))
    for out, gate_weight, up_weight, down_weight in weights[::-1]:
        moves.need(gate_weight)
        gate_in = dot_nn(inputs, gate_weight[...])
        moves.need(up_weight)
        up_in = dot_nn(inputs, up_weight[...])
        sig = jax.nn.sigmoid(gate_in)
        silu = gate_in * sig
        act = (silu * up_in).astype(bf16)
        out[2 * slots : 3 * slots, :] = act
        moves.need(down_weight)
        outputs = outputs + dot_nn(act, down_weight[...])
        act_grad = dot_nt(grads, down_weight[...])
        gate_grad = (act_grad * up_in * sig * (1.0 + gate_in * (1.0 - sig))).astype(bf16)
        up_grad = (act_grad * silu).astype(bf16)
        out[3 * slots : 4 * slots, :] = gate_grad
        out[4 * slots :, :] = up_grad
        moves.done(out)
        total = total + dot_nt(gate_grad, gate_weight[...]) + dot_nt(up_grad, up_weight[...])
    for group in range(groups):
        at = group * size
        rows = jnp.concatenate([outputs[at : at + size, :], total[at : at + size, :]], axis=0)
        packed = pack(rows.astype(bf16), hots).astype(bf16)
        back_o[group * stride * blocks : (group + 1) * stride * blocks, :] = packed


def aside_kernel(
    moves, core, side, zm, zo, aux, pre, gate_z, scanned, ggrad, combined, middle, meta,
    out_o, comb_o, skip_o, ngrad_o, *, width, span
):
    rows, di = pre.shape
    half = zm.shape[1]
    gs = group_of(di)
    pieces = width // 16
    result = (middle[...] + meta[:, 0:1] * meta[:, 1:2] * combined[...]).astype(bf16)
    out_o[...] = dot_tn(token_order(rows), result).astype(bf16)
    def gating(g, carry):
        mine, other = carry
        lanes = pl.ds(pl.multiple_of(g * gs, gs), gs)
        grad = ggrad[:, lanes]
        z = gate_z[:, lanes]
        sig = jax.nn.sigmoid(z)
        here = scanned[:, lanes]
        zgrad = grad * here * sig * (1.0 + z * (1.0 - sig))
        z_low = zgrad.astype(bf16)
        z_turned = zgrad.T.astype(bf16)
        gated_turned = (here * (z * sig) * aux[:, 3:4]).T.astype(bf16)
        for i in range(gs // 16):
            piece = g * (gs // 16) + i
            to = pl.multiple_of(piece // pieces * span + piece % pieces * 16, 16)
            comb_o[pl.ds(to, 16), :] = z_turned[i * 16 : (i + 1) * 16, :]
            owner = piece // pieces
            holder = owner // 2 * 2 + side[0]
            to = holder * span + (1 + owner % 2) * width + piece % pieces * 16
            comb_o[pl.ds(pl.multiple_of(to, 16), 16), :] = gated_turned[i * 16 : (i + 1) * 16, :]
        pre_here = pre[:, lanes]
        act = pre_here * jax.nn.sigmoid(pre_here)
        skip_o[:, lanes] = jnp.sum(grad * (z * sig) * act, axis=0, keepdims=True)
        return (mine + dot_nn(z_low, zm[lanes, :]), other + dot_nn(z_low, zo[lanes, :]))

    moves.need(zm, zo)
    zero = jnp.zeros((rows, half), f32)
    mine, other = lax.fori_loop(0, di // gs, gating, (zero, zero))
    ngrad_o[0] = mine
    ngrad_o[1] = other


def scan_kernel(
    moves, place, xd, par, sd, q, pre, steps, sig_step, small, x_in, tpre, entry, y_in, tsuf, arrived, near,
    sgrad, cgrad_o, xd_o, spar_o, router_o, bw_s, cw_s, bacc_s, cacc_s, st_s, dk_s, sgr_s, asc_s, plow_s,
    rate_s, after_s, *, rank, count
):
    rows, di = pre.shape
    negative_rates(par, rate_s)
    after_s[...] = jnp.zeros_like(after_s)
    groups = arrived.shape[0] // count
    members = near.shape[0] // count
    spread_columns(small[...], rank, count, bw_s)
    spread_columns(small[...], rank + count, count, cw_s)
    bacc_s[...] = jnp.zeros_like(bacc_s)
    cacc_s[...] = jnp.zeros_like(cacc_s)
    spar_o[...] = jnp.zeros_like(spar_o)
    moves.need(arrived, near)

    def after_here(i, _):
        block = pl.ds(pl.multiple_of((groups - 1 - i) * count, count), count)
        carry_step(step_sums(arrived, block, di), arrived[block, :di], rate_s, after_s)
        return 0

    def just_after(i, _):
        block = pl.ds(pl.multiple_of((members - 1 - i) * count, count), count)
        carry_step(step_sums(near, block, di), near[block, :di], rate_s, after_s)
        return 0

    lax.fori_loop(0, groups - 1 - place[0] // members, after_here, 0)
    lax.fori_loop(0, members - 1 - place[0] % members, just_after, 0)
    router_sum = jnp.zeros(router_o.shape, f32)
    for there in range(groups):
        router_sum += arrived[there * count : (there + 1) * count, di + 256 :].astype(f32)
    router_o[...] = router_sum
    steps_in = rows // SUB
    gs = group_of(di)
    moves.need(x_in, sd, q, sgrad, y_in)

    def scan(g, _):
        lanes = pl.ds(pl.multiple_of(g * 128, 128), 128)
        rates = [
            jnp.broadcast_to(rate_s[n : n + 1, lanes], (SUB, 128)) for n in range(count)
        ]
        before = tpre[:, lanes]
        behind = tsuf[:, lanes]
        first = tuple(
            x_in[n, :, lanes] + jnp.exp2(rates[n] * before) * entry[n : n + 1, lanes]
            for n in range(count)
        )

        def forward(j, states):
            at = pl.ds(pl.multiple_of(j * SUB, SUB), SUB)
            sd_here = sd[at, lanes]
            q_here = q[at, lanes]
            fresh = []
            for n in range(count):
                decay = jnp.exp2(sd_here * rates[n])
                dk_s[j * count + n] = decay
                st_s[j * count + n] = states[n]
                fresh.append(decay * states[n] + q_here * bw_s[j * count + n])
            return tuple(fresh)

        last = lax.fori_loop(0, steps_in, forward, first, unroll=8)
        for n in range(count):
            st_s[steps_in * count + n] = last[n]
        zero = jnp.zeros((SUB, 128), f32)
        arriving = tuple(
            y_in[n, :, lanes] + jnp.exp2(rates[n] * behind) * after_s[n : n + 1, lanes]
            for n in range(count)
        )

        def backward(i, carry):
            grads, rate_grads = carry
            j = steps_in - 1 - i
            at = pl.ds(pl.multiple_of(j * SUB, SUB), SUB)
            sd_here = sd[at, lanes]
            q_here = q[at, lanes]
            sg = sgrad[at, lanes]
            onto = zero
            along = zero
            fresh = []
            fresh_rates = []
            for n in range(count):
                k = j * count + n
                lam = grads[n] + sg * cw_s[k]
                cacc_s[k] += sg * st_s[k + count]
                bacc_s[k] += lam * q_here
                onto = onto + lam * bw_s[k]
                carried = lam * dk_s[k]
                logs = carried * st_s[k]
                along = along + logs * rates[n]
                fresh.append(carried)
                fresh_rates.append(rate_grads[n] + logs * sd_here)
            sgr_s[at, lanes] = along
            asc_s[at, lanes] = onto
            return (tuple(fresh), tuple(fresh_rates))

        _, rate_grads = lax.fori_loop(0, steps_in, backward, (arriving, (zero,) * count), unroll=2)
        for n in range(count):
            spar_o[8 + n : 9 + n, lanes] = LN2 * jnp.sum(
                rate_grads[n] * rates[n], axis=0, keepdims=True
            )
        return 0

    lax.fori_loop(0, di // 128, scan, 0)

    moves.need(pre, sig_step, xd, steps)
    lane8 = lax.broadcasted_iota(jnp.int32, (SUB, 128), 1)
    blocks = []
    for j in range(steps_in):
        block = jnp.zeros((SUB, 128), f32)
        for n in range(count):
            k = j * count + n
            block = jnp.where(
                lane8 == rank + n, jnp.sum(bacc_s[k], axis=1, keepdims=True), block
            )
            block = jnp.where(
                lane8 == rank + count + n, jnp.sum(cacc_s[k], axis=1, keepdims=True), block
            )
        blocks.append(block)
    coef_grad = jnp.concatenate(blocks, axis=0)
    lane = lax.broadcasted_iota(jnp.int32, (rows, 128), 1)
    step_low = jnp.where(
        lane >= 128 - rank, pltpu.roll(small[...], 128 - rank, 1), 0.0
    ).astype(bf16)

    def steps_back(g, total):
        lanes = pl.ds(pl.multiple_of(g * gs, gs), gs)
        pre_here = pre[:, lanes]
        act = pre_here * jax.nn.sigmoid(pre_here)
        pre_grad = (LN2 * sgr_s[:, lanes] + act * asc_s[:, lanes]) * sig_step[:, lanes]
        spar_o[KC + 1 : KC + 2, lanes] = jnp.sum(pre_grad, axis=0, keepdims=True)
        pre_low = pre_grad.astype(bf16)
        plow_s[:, lanes] = pre_low
        return total + dot_nn(pre_low, xd[lanes, :])

    rank_grad = lax.fori_loop(0, di // gs, steps_back, jnp.zeros((rows, 128), f32))
    small_low = jnp.where(lane < rank, pltpu.roll(rank_grad, rank, 1), coef_grad).astype(bf16)

    def act_back(g, _):
        lanes = pl.ds(pl.multiple_of(g * gs, gs), gs)
        pre_here = pre[:, lanes]
        sig = jax.nn.sigmoid(pre_here)
        act_low = (pre_here * sig).astype(bf16)
        total = (
            sgrad[:, lanes] * par[KC + 2 : KC + 3, lanes]
            + steps[:, lanes] * asc_s[:, lanes]
            + dot_nt(small_low, xd[lanes, :])
        )
        cgrad_o[:, lanes] = total * sig * (1.0 + pre_here * (1.0 - sig))
        xd_o[lanes, :] = (dot_tn(act_low, small_low) + dot_tn(plow_s[:, lanes], step_low)).astype(bf16)
        return 0

    lax.fori_loop(0, di // gs, act_back, 0)


def last_kernel(
    moves, core, cgrad, halo, aux, ext, par, wm, wo, ngrad_z, spar, skip, xd, hid, gain_two,
    router_sum, pay_o, ngrad_o, extra_o, low_s, far_s, *, width
):
    rows, di = cgrad.shape
    gs = 128
    moves.need(ext)
    ahead_lane = spar.shape[0] + 4 * (hid.shape[1] // width)
    moves.need(xd)

    def conv(g, _):
        lanes = pl.ds(pl.multiple_of(g * gs, gs), gs)
        cg = cgrad[:, lanes]
        grad = par[KC - 1 : KC, lanes] * cg
        parts = [jnp.sum(cg * ext[(KC - 1) * SUB :, lanes], axis=0, keepdims=True)]
        zero = jnp.zeros((1, gs), f32)
        behind = [zero] * (KC - 1)
        for ahead in range(1, KC):
            tap = par[KC - 1 - ahead : KC - ahead, lanes]
            masked = cg * aux[:, ahead - 1 : ahead]
            shifted = ext[(KC - 1 - ahead) * SUB : (KC - 1 - ahead) * SUB + rows, lanes]
            parts.append(jnp.sum(masked * shifted, axis=0, keepdims=True))
            pieces = [masked[ahead * SUB :, :]]
            for i in range(ahead):
                pieces.append(from_after(masked[i * SUB : (i + 1) * SUB, :], zero))
                k = KC - 1 - ahead + i
                behind[k] = behind[k] + tap * masked[i * SUB : i * SUB + 1, :]
            grad = grad + tap * jnp.concatenate(pieces, axis=0)
        low_s[:, lanes] = grad.astype(bf16)
        pay_o[lanes, 0:128] = grad.T.astype(bf16)
        pay_o[lanes, 128:256] = xd[lanes, :]
        extra = jnp.concatenate(behind + [jnp.zeros((SUB - KC + 1, gs), f32)], axis=0)
        far_s[:SUB, lanes] = extra.astype(bf16)
        own = jnp.concatenate(
            parts[::-1]
            + [jnp.sum(cg, axis=0, keepdims=True), spar[KC + 1 : KC + 2, lanes], skip[:, lanes]]
            + [zero, spar[8:, lanes], jnp.zeros((ahead_lane - spar.shape[0], gs), f32), extra]
            + [jnp.zeros((128 - ahead_lane - SUB, gs), f32)],
            axis=0,
        )
        pay_o[lanes, 256:384] = own.T.astype(bf16)
        return 0

    lax.fori_loop(0, di // gs, conv, 0)
    far_s[SUB:, :] = jnp.zeros_like(far_s[SUB:, :])
    moves.need(wm, wo, ngrad_z, hid)
    low = core[0] == 0

    def onto_inputs(values):
        return dot_nn(values, wm[...]), dot_nn(values, wo[...])

    def joined(mine, other):
        return jnp.concatenate([jnp.where(low, mine, other), jnp.where(low, other, mine)], axis=1)

    mine, other = onto_inputs(low_s[...])
    ngrad = joined(mine + ngrad_z[0], other + ngrad_z[1])
    ngrad_o[...] = ngrad
    far = joined(*onto_inputs(far_s[...]))[:SUB, :]
    extra_o[...] = far
    first = hid[...].astype(f32)
    scale = lax.rsqrt(jnp.mean(first * first, axis=1, keepdims=True) + epsilon)
    gains = jnp.sum(ngrad * first * scale, axis=0, keepdims=True)
    first = halo[SUB:, :].astype(f32)
    scale = lax.rsqrt(jnp.mean(first * first, axis=1, keepdims=True) + epsilon)
    gains = gains + jnp.sum(far * first * scale, axis=0, keepdims=True)
    model = first.shape[1]
    each = model // width
    row = lax.broadcasted_iota(jnp.int32, (width, model), 0)
    column = lax.broadcasted_iota(jnp.int32, (width, model), 1)
    here = column // each == row
    extra = jnp.zeros((width, 128), f32)
    router_row = jnp.concatenate([router_sum[0:1, :], router_sum[1:2, :]], axis=1)
    router_top = router_row.astype(bf16).astype(f32)
    rows_sent = (gains, gain_two[...], router_top, router_row - router_top)
    for k, values in enumerate(rows_sent):
        spread = jnp.where(here, values, 0.0).astype(bf16)
        at = lax.broadcasted_iota(jnp.int32, (model, 128), 0)
        to = lax.broadcasted_iota(jnp.int32, (model, 128), 1)
        placed = (at % each + spar.shape[0] + k * each == to).astype(bf16)
        extra = extra + dot_nn(spread, placed)
    extra = extra.astype(bf16)
    for place in range(di // width):
        pay_o[place * width : (place + 1) * width, 256:384] += extra


def tail_kernel(
    moves, place, core, xd, par, sd, q, pre, steps, sig_step, small, x_in, tpre, entry, y_in, tsuf,
    arrived, near, sgrad, halo, aux, ext, wm, wo, ngrad_z, skip, hid, gain_two,
    pay_o, ngrad_o, extra_o, low_s, far_s, cgrad_s, xd_s, spar_s, router_s, *scratch,
    rank, count, width
):
    scan_kernel(
        moves, place, xd, par, sd, q, pre, steps, sig_step, small, x_in, tpre, entry, y_in, tsuf,
        arrived, near, sgrad, cgrad_s, xd_s, spar_s, router_s, *scratch, rank=rank, count=count
    )
    last_kernel(
        moves, core, cgrad_s, halo, aux, ext, par, wm, wo, ngrad_z, spar_s, skip, xd_s, hid,
        gain_two, router_s, pay_o, ngrad_o, extra_o, low_s, far_s, width=width
    )


def hidden_kernel(ngrad_in, beyond, hid, mgrad, gain, first_o):
    first = hid[...].astype(f32)
    rows = first.shape[0]
    ngrad = ngrad_in[...]
    row = lax.broadcasted_iota(jnp.int32, first.shape, 0)
    for i in range(KC - 1):
        at = rows - 1 - (KC - 2 - i) * SUB
        ngrad = ngrad + jnp.where(row == at, beyond[i : i + 1, :], 0.0)
    scale = lax.rsqrt(jnp.mean(first * first, axis=1, keepdims=True) + epsilon)
    scaled = gain[...].reshape(1, -1) * ngrad
    cube = scale * scale * scale
    grad = (
        mgrad[...] + scale * scaled - first * cube * jnp.mean(first * scaled, axis=1, keepdims=True)
    )
    order = token_order(rows)
    top = grad.astype(bf16)
    left = grad - top.astype(f32)
    mid = left.astype(bf16)
    low_part = (left - mid.astype(f32)).astype(bf16)
    first_o[...] = dot_tn(order, top) + dot_tn(order, mid) + dot_tn(order, low_part)


def ready_kernel(
    moves, side, comb, nrm_all, mix_half, z_o, mine_o, theirs_o, z_s, gated_s
):
    places = comb.shape[0]
    width = z_o.shape[0]
    for place in range(places):
        z_s[:, place * 128 : (place + 1) * 128] = comb[place, :width, :]
    for k in range(places // 2):
        place = 2 * k + side[0]
        gated_s[:, k * 128 : (k + 1) * 128] = comb[place, width : 3 * width, :]
    moves.need(mix_half)
    grads = dot_nn(gated_s[...], mix_half[...]).astype(bf16)
    first = side[0] == 0
    mine_o[...] = jnp.where(first, grads[:width, :], grads[width:, :])
    theirs_o[...] = jnp.where(first, grads[width:, :], grads[:width, :])
    moves.need(nrm_all)
    z_o[...] = dot_nn(z_s[...], nrm_all[...]).astype(bf16)


def grads_kernel(got, nrm_all, out_o, left_s, *, base):
    places, width, _ = got.shape
    model = nrm_all.shape[1]
    each = model // width
    rest = jnp.zeros((width, 256), f32)
    routers = [jnp.zeros((width, 128), f32) for _ in range(places * each // 128)]
    lane = lax.broadcasted_iota(jnp.int32, (width, 128), 1)
    row = lax.broadcasted_iota(jnp.int32, (128, 128), 0)
    column = lax.broadcasted_iota(jnp.int32, (128, 128), 1)
    after = row - (base + 2 * each)
    late = column == 127 - (KC - 2 - after) * SUB
    placed = (late & (after >= 0) & (after < KC - 1)).astype(bf16)
    for place in range(places):
        at = gathered_place(place)
        inner = got[at, :, :128]
        if place + 1 < places:
            beyond = dot_nn(got[gathered_place(place + 1), :, 256:384], placed)
            inner = (inner.astype(f32) + beyond).astype(bf16)
        left_s[:, at * 128 : (at + 1) * 128] = inner
        there = got[at, :, 128:].astype(f32)
        rest = rest + there
        k = place * each // 128
        inside = place * each % 128
        mine = (lane >= inside) & (lane < inside + each)
        for part in range(2):
            turn = (inside - base - part * each) % 128
            routers[k] = routers[k] + jnp.where(mine, pltpu.roll(there[:, 128:], turn, 1), 0.0)
    out_o[width:, :256] = rest.astype(bf16)
    out_o[width:, 256:] = jnp.concatenate(routers, axis=1).astype(bf16)
    out_o[:width, :model] = dot_nn(left_s[...], nrm_all[...]).astype(bf16)


def token_order(rows):
    steps_in = rows // SUB
    row = lax.broadcasted_iota(jnp.int32, (rows, rows), 0)
    column = lax.broadcasted_iota(jnp.int32, (rows, rows), 1)
    return ((row % SUB) * steps_in + row // SUB == column).astype(bf16)


def final_kernel(
    ours, theirs, ours_two, theirs_two, x_o, z_o, out_o, conv_o, bias_o, xp_o, dt_o, db_o, al_o, skip_o, router_o, one_o,
    two_o, mine_s, other_s, *, rank, count, experts
):
    width = out_o.shape[0]
    model = router_o.shape[1]
    each = model // width
    x_o[...] = ours[:width, :model].astype(f32) + theirs[:width, :model].astype(f32)
    z_o[...] = ours_two[:width, :].astype(f32) + theirs_two[:width, :].astype(f32)
    out_o[...] = ours_two[width:, :].astype(f32) + theirs_two[width:, :].astype(f32)
    rest = slice(width, 2 * width)
    xd = ours[rest, :128].astype(f32) + theirs[rest, :128].astype(f32)
    xp_o[...] = xd[:, : rank + 2 * count]
    gap = jnp.zeros((128 - width, 128), f32)
    turned = jnp.concatenate([xd, gap], axis=0).T
    dt_o[...] = turned[128 - rank :, :width]
    vectors = jnp.zeros((128, 128), f32)
    for part, held in ((ours, mine_s), (theirs, other_s)):
        block = jnp.concatenate([part[rest, 128:256].astype(f32), gap], axis=0).T
        vectors = vectors + block
        for k in range(experts * each // 128):
            lanes = slice(256 + k * 128, 384 + k * 128)
            piece = jnp.concatenate([part[rest, lanes].astype(f32), gap], axis=0)
            held[k * 128 : (k + 1) * 128, :] = piece.T
        held[experts * each :, :] = jnp.zeros_like(held[experts * each :, :])
        held[experts * each : (experts + 2) * each, :] = block[8 + count : 8 + count + 2 * each, :]
    conv_o[...] = vectors[:KC, :width]
    bias_o[...] = vectors[KC : KC + 1, :width].reshape(width)
    db_o[...] = vectors[KC + 1 : KC + 2, :width].reshape(width)
    skip_o[...] = vectors[KC + 2 : KC + 3, :width].reshape(width)
    al_o[...] = vectors[8 : 8 + count, :width]
    row = lax.broadcasted_iota(jnp.int32, (128, model), 0)
    column = lax.broadcasted_iota(jnp.int32, (128, model), 1)
    total = jnp.zeros((experts + 8, model), f32)
    for at in range(each):
        to = (row * each + at == column).astype(bf16)
        picked = pl.ds(at, experts + 8, stride=each)
        total = total + dot_nn(mine_s[picked, :].astype(bf16), to)
        total = total + dot_nn(other_s[picked, :].astype(bf16), to)
    router_o[...] = total[:experts, :]
    one_o[...] = total[experts : experts + 1, :].reshape(model)
    two_o[...] = total[experts + 1 : experts + 2, :].reshape(model)


def token_order(rows):
    steps_in = rows // SUB
    row = lax.broadcasted_iota(jnp.int32, (rows, rows), 0)
    column = lax.broadcasted_iota(jnp.int32, (rows, rows), 1)
    return ((row % SUB) * steps_in + row // SUB == column).astype(bf16)


def exchange(values):
    return lax.all_to_all(values, "wide", split_axis=0, concat_axis=0, tiled=True)


def exchange_near(values, members):
    groups = [[u * members + z for z in range(members)] for u in range(32 // members)]
    blocks = values.reshape(members, -1, values.shape[1])
    return lax.all_to_all(
        blocks, "wide", split_axis=0, concat_axis=0, tiled=True, axis_index_groups=groups
    ).reshape(values.shape)


def exchange_far(values, members):
    groups = [[u * members + z for u in range(32 // members)] for z in range(members)]
    blocks = values.reshape(32 // members, -1, values.shape[1])
    return lax.all_to_all(
        blocks, "wide", split_axis=0, concat_axis=0, tiled=True, axis_index_groups=groups
    ).reshape(values.shape)


def gathered_place(place):
    return (place // 8 * 4 + place % 4) * 2 + place // 4 % 2


def exchange_channels(values):
    order = sorted(range(32), key=gathered_place)
    return lax.all_to_all(
        values, "wide", split_axis=0, concat_axis=0, tiled=True, axis_index_groups=[order]
    )


def other_chip(values):
    return lax.ppermute(values, "wide", [(i, i ^ 4) for i in range(32)])


def pair_up(values, partner, place):
    first = (place // 4) % 2 == 0
    return jnp.concatenate(
        [jnp.where(first, values, partner), jnp.where(first, partner, values)], axis=0
    )


def gather_pairs(both):
    groups = [[(y * 2 + x) * 4 + z for y in range(4) for z in range(4)] for x in range(2)]
    return lax.all_gather(both, "wide", axis=0, tiled=True, axis_index_groups=groups)


def exchange_sides(values):
    groups = [
        [(side * 2 + core) * 32 + place for side in range(2) for place in range(32)]
        for core in range(2)
    ]
    return lax.all_to_all(
        values, ("dp", "wide"), split_axis=0, concat_axis=0, tiled=True, axis_index_groups=groups
    )


def other_core(values):
    return lax.ppermute(values, "dp", [(0, 1), (1, 0), (2, 3), (3, 2)])


def other_side(values):
    return lax.ppermute(values, "dp", [(0, 2), (2, 0), (1, 3), (3, 1)])


def body(
    hidden, cotangent, routes, seg_lengths, gain_mix, in_x, in_z, conv_w, conv_b, x_proj, dt_proj,
    dt_bias, a_log, skip_d, out_proj, gain_moe, router, w_gate, w_up, w_down,
):
    rows, model = hidden.shape
    places = lax.axis_size("wide")
    place = lax.axis_index("wide")
    core = (lax.axis_index("dp") % 2).astype(jnp.int32).reshape(1)
    place_arr = place.astype(jnp.int32).reshape(1)
    width = in_x.shape[1]
    di = width * places
    count = a_log.shape[0]
    rank = dt_proj.shape[0]
    experts = router.shape[1]
    capacity = max(CAP * rows // (4 * places), 2)
    stride = -(-2 * capacity // 16) * 16
    half = model // 2
    steps_in = rows // SUB
    shift = SUB.bit_length() - 1
    span = 3 * width
    members = 4
    side = (place // 4 % 2).astype(jnp.int32).reshape(1)

    gate_share = call(
        pack_gate_kernel, [shape((width, model), bf16)], [], (core, in_z.T, out_proj), smem=1
    )[0]
    gate_share, x_proj = lax.optimization_barrier((gate_share, x_proj))
    pay_one = call(
        partial(pack_kernel, places=places),
        [shape((di, half + 128), bf16)],
        [],
        (core, in_x.T, x_proj, dt_proj, conv_w, conv_b, dt_bias, skip_d, a_log),
        smem=1,
    )[0]
    w_gate_two, w_up_two, w_down_two = (other_core(w[0]) for w in (w_gate, w_up, w_down))
    pay_one, hidden, cotangent, routes, seg_lengths = lax.optimization_barrier(
        (pay_one, hidden, cotangent, routes, seg_lengths)
    )
    gate_partner = other_chip(gate_share)
    pay_one, gate_partner = lax.optimization_barrier((pay_one, gate_partner))
    wm = exchange_channels(pay_one.reshape(places, width, half + 128)).reshape(di, half + 128)
    zm = gather_pairs(pair_up(gate_share, gate_partner, place))
    nrm, tail, hid, cot, route, aux = call(
        prepare_kernel,
        [
            shape((rows, model), bf16),
            shape((16, model), bf16),
            shape((rows, model), bf16),
            shape((rows, model), bf16),
            shape((rows, 1), jnp.int32),
            shape((rows, 128)),
        ],
        [],
        (place_arr * rows, seg_lengths, hidden, cotangent, routes.T, gain_mix),
        smem=2,
    )
    halo = lax.ppermute(tail, "wide", [(i, i + 1) for i in range(places - 1)])
    nrm_partner = other_chip(nrm)
    wm, halo = lax.optimization_barrier((wm, halo))
    wo = other_core(wm)
    ext, pre, steps, sig_step, small, x_in, tpre, tsuf, states, par, xd_weight, sd, q = call(
        partial(front_kernel, rank=rank, count=count),
        [
            shape((rows + (KC - 1) * SUB, di)),
            shape((rows, di)),
            shape((rows, di)),
            shape((rows, di)),
            shape((rows, 128)),
            shape((count, SUB, di)),
            shape((SUB, di)),
            shape((SUB, di)),
            shape((members * count, di + 256), bf16),
            shape((8 + count, di)),
            shape((di, 128), bf16),
            shape((rows, di)),
            shape((rows, di)),
        ],
        [
            pltpu.VMEM((steps_in * count, SUB, 128), f32),
            pltpu.VMEM((2, rows + 16, half), bf16),
            pltpu.VMEM((16, 128), f32),
        ],
        (core, nrm, halo, wm, wo, aux),
        smem=1,
        late=(3, 4),
        early=(0, 1, 2, 3, 9, 10, 11, 12),
    )

    near = exchange_near(states, members)
    zm, nrm_partner, near = lax.optimization_barrier((zm, nrm_partner, near))
    zo = other_core(zm)
    z_lanes = pl.ds(0, half)
    out_lanes = pl.ds(half, half)
    gate_z = call(
        gate_kernel,
        [shape((rows, di))],
        [pltpu.VMEM((2, rows, half), bf16)],
        (core, nrm, zm, zo),
        smem=1,
        late=(2, 3),
        lanes={2: z_lanes, 3: z_lanes},
    )[0]
    states = call(
        partial(forward_group_kernel, di=di, count=count),
        [shape((places // members * count, di + 256), bf16)],
        [pltpu.VMEM((count, di), f32)] * 2,
        (near, par),
        limit=12 * 1024 * 1024,
    )[0]
    states = exchange_far(states, members)

    nrm_pair = pair_up(nrm, nrm_partner, place)
    states, gate_z, nrm_pair = lax.optimization_barrier((states, gate_z, nrm_pair))
    normed_all = gather_pairs(nrm_pair)
    scanned, send, middle, ntwo, chances, meta, hot, entry = call(
        partial(
            middle_kernel,
            rank=rank,
            count=count,
            experts=experts,
            stride=stride,
            capacity=capacity,
            shift=shift,
        ),
        [
            shape((rows, di)),
            shape((2 * experts * stride, 2 * model // 3), bf16),
            shape((rows, model)),
            shape((rows, model), bf16),
            shape((rows, experts)),
            shape((rows, 8)),
            shape((3, 2 * rows, experts * stride), bf16),
            shape((count, di)),
        ],
        [
            pltpu.VMEM((steps_in * count, SUB, 128), f32),
            pltpu.VMEM((steps_in * count, SUB, 128), f32),
            pltpu.VMEM((count, di), f32),
        ],
        (
            core, place_arr, zm, zo, par, aux, pre, sd, q, x_in, small, states, near, tpre, hid, cot,
            route, gain_moe, router.T, gate_z,
        ),
        smem=2,
        late=(11, 12, 9, 7, 8, 6, 19, 2, 3),
        early=(7, 0, 6, 2, 3),
        lanes={2: out_lanes, 3: out_lanes},
    )
    arrived = exchange_sides(send.reshape(2 * experts, stride, -1)).reshape(send.shape)
    slots = 2 * places * capacity
    kept, sent, back = call(
        partial(expert_kernel, stride=stride, capacity=capacity),
        [shape((5 * slots, model), bf16)] * 2 + [shape(send.shape, bf16)],
        [],
        (arrived, w_gate[0], w_up[0], w_down[0], w_gate_two, w_up_two, w_down_two),
        late=(1, 2, 3, 4, 5, 6),
        early=(0, 1, 2),
    )
    back = exchange_sides(back.reshape(2 * experts, stride, -1)).reshape(send.shape)
    given = other_core(sent)

    def both_cores(left, right):
        total = 0.0
        for part in (kept, given):
            rows_left = part[left * slots : (left + 1) * slots]
            total = total + dot_tn(rows_left, part[right * slots : (right + 1) * slots])
        return total[None]

    grad_w_down = both_cores(2, 1)
    grad_w_gate = both_cores(0, 3)
    grad_w_up = both_cores(0, 4)
    back, grad_w_down, grad_w_gate, grad_w_up = lax.optimization_barrier(
        (back, grad_w_down, grad_w_gate, grad_w_up)
    )

    combined, mixlow, mgrad, ggrad, sgrad, gain_two, y_in, adjoints = call(
        partial(back_kernel, rank=rank, count=count, experts=experts),
        [
            shape((rows, model)),
            shape((rows, model), bf16),
            shape((rows, model)),
            shape((rows, di)),
            shape((rows, di)),
            shape((1, model)),
            shape((count, SUB, di)),
            shape((members * count, di + 256 + half), bf16),
        ],
        [
            pltpu.VMEM((steps_in * count, SUB, 128), f32),
            pltpu.VMEM((2, rows, half), bf16),
            pltpu.VMEM((count, di), f32),
            pltpu.VMEM((16, 128), f32),
        ],
        (
            core, back, zm, zo, par, aux, sd, small, gate_z, hot, middle, meta, chances, route,
            cot, gain_moe, router.T, ntwo,
        ),
        smem=1,
        late=(2, 3, 8, 6),
        early=(1, 2, 0, 3, 4),
        lanes={2: out_lanes, 3: out_lanes},
    )
    near_back = exchange_near(adjoints, members)
    adjoints = call(
        partial(backward_group_kernel, di=di, count=count),
        [shape((places // members * count, di + 256 + half), bf16)],
        [pltpu.VMEM((count, di), f32)] * 2,
        (near_back, par),
        limit=12 * 1024 * 1024,
    )[0]
    adjoints = exchange_far(adjoints, members)
    out, comb, skip_part, ngrad_z = call(
        partial(aside_kernel, width=width, span=span),
        [
            shape((rows, model), bf16),
            shape((places * span, 128), bf16),
            shape((1, di)),
            shape((2, rows, half)),
        ],
        [],
        (
            core, side, zm, zo, aux, pre, gate_z, scanned, ggrad, combined, middle, meta,
        ),
        smem=2,
        late=(2, 3),
        lanes={2: z_lanes, 3: z_lanes},
    )
    adjoints, comb = lax.optimization_barrier((adjoints, comb))
    mixlow, normed_all = lax.optimization_barrier((mixlow, normed_all))
    mix_half = gather_pairs(mixlow)
    comb_got = exchange_channels(comb.reshape(places, span, 128))

    pay, ngrad, beyond = call(
        partial(tail_kernel, rank=rank, count=count, width=width),
        [shape((di, 384), bf16), shape((rows, model)), shape((SUB, model))],
        [
            pltpu.VMEM((rows, di), bf16),
            pltpu.VMEM((16, di), bf16),
            pltpu.VMEM((rows, di), f32),
            pltpu.VMEM((di, 128), bf16),
            pltpu.VMEM((8 + count, di), f32),
            pltpu.VMEM((count, half), f32),
        ]
        + [pltpu.VMEM((steps_in * count, SUB, 128), f32)] * 4
        + [pltpu.VMEM(((steps_in + 1) * count, SUB, 128), f32)]
        + [pltpu.VMEM((steps_in * count, SUB, 128), f32)]
        + [pltpu.VMEM((rows, di), f32)] * 2
        + [pltpu.VMEM((rows, di), bf16)]
        + [pltpu.VMEM((count, di), f32)] * 2,
        (
            place_arr, core, xd_weight, par, sd, q, pre, steps, sig_step, small, x_in, tpre, entry,
            y_in, tsuf, adjoints, near_back, sgrad, halo, aux, ext, wm, wo, ngrad_z, skip_part, hid,
            gain_two,
        ),
        smem=2,
        late=(15, 16, 10, 4, 5, 17, 13, 6, 8, 2, 7, 20, 21, 22, 23, 25),
        lanes={21: z_lanes, 22: z_lanes},
    )
    got_pay = exchange_channels(pay.reshape(places, width, 384))
    beyond = lax.ppermute(beyond, "wide", [(i + 1, i) for i in range(places - 1)])
    z_ready, out_ready, out_theirs = call(
        ready_kernel,
        [shape((width, model), bf16)] * 3,
        [
            pltpu.VMEM((width, places * rows), bf16),
            pltpu.VMEM((2 * width, places // 2 * rows), bf16),
        ],
        (side, comb_got, normed_all, mix_half),
        smem=1,
        late=(3,),
        limit=24 * 1024 * 1024,
    )
    out_other = other_chip(out_theirs)
    got_pay, out_other, beyond = lax.optimization_barrier((got_pay, out_other, beyond))
    first_grad = call(
        hidden_kernel, [shape((rows, model))], [], (ngrad, beyond, hid, mgrad, gain_mix), limit=12 * 1024 * 1024
    )[0]
    out_ready = (out_ready.astype(f32) + out_other.astype(f32)).astype(bf16)
    ready = jnp.concatenate([z_ready, out_ready], axis=0)
    ready = (ready.astype(f32) + other_core(ready).astype(f32)).astype(bf16)
    ready_side = other_side(ready)
    per_place = model // width
    mats = call(
        partial(grads_kernel, base=8 + count + 2 * per_place),
        [shape((2 * width, 256 + places * per_place), bf16)],
        [pltpu.VMEM((width, places * rows), bf16)],
        (got_pay, normed_all),
        limit=24 * 1024 * 1024,
    )[0]
    mats = (mats.astype(f32) + other_core(mats).astype(f32)).astype(bf16)
    grad_x, grad_z, grad_out, grad_conv, grad_bias, grad_xp, grad_dt, grad_db, grad_al, grad_sk, grad_router, gain_one, gain_two = call(
        partial(final_kernel, rank=rank, count=count, experts=experts),
        [
            shape((width, model)),
            shape((width, model)),
            shape((width, model)),
            shape((KC, width)),
            shape((width,)),
            shape((width, rank + 2 * count)),
            shape((rank, width)),
            shape((width,)),
            shape((count, width)),
            shape((width,)),
            shape((experts, model)),
            shape((model,)),
            shape((model,)),
        ],
        [pltpu.VMEM(((experts + 8) * per_place, 128), f32)] * 2,
        (mats, other_side(mats), ready, ready_side),
        limit=12 * 1024 * 1024,
    )
    return (
        out,
        first_grad,
        gain_one,
        grad_x.T,
        grad_z.T,
        grad_conv,
        grad_bias,
        grad_xp,
        grad_dt,
        grad_db,
        grad_al,
        grad_sk,
        grad_out,
        gain_two,
        grad_router.T,
        grad_w_gate,
        grad_w_up,
        grad_w_down,
    )


def solution(mesh):
    rows = P(("dp", "wide"), None)
    expert_columns = P("wide", None, "dp")
    expert_rows = P("wide", "dp", None)
    placed = (
        rows, rows, rows, P("dp", None), P(), P(None, "wide"), P(None, "wide"), P(None, "wide"),
        P("wide"), P("wide", None), P(None, "wide"), P("wide"), P(None, "wide"), P("wide"),
        P("wide", None), P(), P(), expert_columns, expert_columns, expert_rows,
    )
    given = (
        rows, rows, P(), P(None, "wide"), P(None, "wide"), P(None, "wide"), P("wide"),
        P("wide", None), P(None, "wide"), P("wide"), P(None, "wide"), P("wide"), P("wide", None),
        P(), P(), expert_columns, expert_columns, expert_rows,
    )
    return jax.shard_map(body, mesh=mesh, in_specs=placed, out_specs=given, check_vma=False)
```

```python
from functools import partial

import jax
import jax.numpy as jnp
from jax import lax
from jax.experimental import pallas as pl
from jax.experimental.pallas import tpu as pltpu
from jax.sharding import PartitionSpec as P

f32 = jnp.float32
bf16 = jnp.bfloat16
KC = 4
SUB = 8
CAP = 5
STOP = 1e6
LOG2E = 1.4426950408889634
LN2 = 0.6931471805599453
epsilon = 1e-05
VMEM_LIMIT = 56 * 1024 * 1024


def dot_nn(left, right):
    return lax.dot_general(left, right, (((1,), (0,)), ((), ())), preferred_element_type=f32)


def dot_nt(left, right):
    return lax.dot_general(left, right, (((1,), (1,)), ((), ())), preferred_element_type=f32)


def dot_tn(left, right):
    return lax.dot_general(left, right, (((0,), (0,)), ((), ())), preferred_element_type=f32)


class Moves:
    def __init__(self):
        self.arriving = {}
        self.leaving = {}
        self.started = []

    def need(self, *refs):
        for ref in refs:
            copy = self.arriving.pop(id(ref), None)
            if copy is not None:
                copy.wait()

    def done(self, *refs):
        for ref in refs:
            copy = self.leaving.pop(id(ref), None)
            if copy is not None:
                copy.start()
                self.started.append(copy)


def call(
    kernel, out_shapes, scratch, args, smem=0, late=(), early=(), lanes=None, limit=VMEM_LIMIT
):
    lanes = lanes or {}
    vmem = pl.BlockSpec(memory_space=pltpu.VMEM)
    hbm = pl.BlockSpec(memory_space=pl.ANY)
    specs = [pl.BlockSpec(memory_space=pltpu.SMEM)] * smem
    specs += [hbm if i in late else vmem for i in range(smem, len(args))]
    buffers = []
    for i in late:
        dims = (args[i].shape[0], lanes[i].size) if i in lanes else args[i].shape
        buffers.append(pltpu.VMEM(dims, args[i].dtype))
    buffers += [pltpu.VMEM(out_shapes[i].shape, out_shapes[i].dtype) for i in early]
    moving = len(buffers)
    extra = buffers + [pltpu.SemaphoreType.DMA((moving,))] if moving else []

    def staged(*refs):
        refs = list(refs)
        own = refs[len(refs) - moving - 1 : -1]
        semaphores = refs[-1]
        refs = refs[: len(refs) - moving - 1]
        moves = Moves()
        for k, i in enumerate(late):
            source = refs[i].at[:, lanes[i]] if i in lanes else refs[i]
            copy = pltpu.make_async_copy(source, own[k], semaphores.at[k])
            copy.start()
            refs[i] = own[k]
            moves.arriving[id(own[k])] = copy
        for k, i in enumerate(early, len(late)):
            at = len(args) + i
            moves.leaving[id(own[k])] = pltpu.make_async_copy(own[k], refs[at], semaphores.at[k])
            refs[at] = own[k]
        kernel(moves, *refs)
        moves.need(*own)
        moves.done(*own)
        for copy in moves.started:
            copy.wait()

    return pl.pallas_call(
        staged if moving else kernel,
        out_shape=out_shapes,
        in_specs=specs,
        out_specs=[hbm if i in early else vmem for i in range(len(out_shapes))],
        scratch_shapes=list(scratch) + extra,
        compiler_params=pltpu.CompilerParams(vmem_limit_bytes=limit),
    )(*args)


def shape(dims, dtype=f32):
    return jax.ShapeDtypeStruct(dims, dtype)


def group_of(di):
    return 256 if di % 256 == 0 else 128


def sublane_iota(width):
    return lax.broadcasted_iota(jnp.int32, (SUB, width), 0)


def from_before(block, first):
    row = sublane_iota(block.shape[1])
    return jnp.where(row == 0, jnp.broadcast_to(first, block.shape), pltpu.roll(block, 1, 0))


def from_after(block, last):
    row = sublane_iota(block.shape[1])
    return jnp.where(
        row == SUB - 1, jnp.broadcast_to(last, block.shape), pltpu.roll(block, SUB - 1, 0)
    )


def spread_columns(small, first, count, out):
    steps = small.shape[0] // SUB
    for j in range(steps):
        block = small[j * SUB : (j + 1) * SUB, :]
        for n in range(count):
            out[j * count + n] = jnp.broadcast_to(block[:, first + n : first + n + 1], (SUB, 128))


def prefix_states(decay, state):
    row = sublane_iota(state.shape[1])
    for shift in (1, 2, 4):
        inside = row >= shift
        state = state + decay * jnp.where(inside, pltpu.roll(state, shift, 0), 0.0)
        decay = decay * jnp.where(inside, pltpu.roll(decay, shift, 0), 1.0)
    return state


def suffix_states(decay, state):
    row = sublane_iota(state.shape[1])
    for shift in (1, 2, 4):
        inside = row < SUB - shift
        state = state + decay * jnp.where(inside, pltpu.roll(state, SUB - shift, 0), 0.0)
        decay = decay * jnp.where(inside, pltpu.roll(decay, SUB - shift, 0), 1.0)
    return state


def prefix_sum(values):
    row = sublane_iota(values.shape[1])
    for shift in (1, 2, 4):
        values = values + jnp.where(row >= shift, pltpu.roll(values, shift, 0), 0.0)
    return values


def suffix_sum(values):
    row = sublane_iota(values.shape[1])
    for shift in (1, 2, 4):
        values = values + jnp.where(row < SUB - shift, pltpu.roll(values, SUB - shift, 0), 0.0)
    return values


def one_hot(dims, offset):
    row = lax.broadcasted_iota(jnp.int32, dims, 0)
    column = lax.broadcasted_iota(jnp.int32, dims, 1)
    return (row + offset == column).astype(bf16)


def pack_gate_kernel(core, in_z, out_proj, gate_o):
    half = in_z.shape[1] // 2
    start = pl.multiple_of(core[0] * half, 128)
    gate_o[:, :half] = in_z[:, pl.ds(start, half)]
    gate_o[:, half:] = out_proj[:, pl.ds(start, half)]


def pack_kernel(
    core, in_x, x_proj, dt_proj, conv_w, conv_b, dt_bias, skip_d, a_log, out, *, places
):
    width, model = in_x.shape
    half = model // 2
    here = core[0]
    mine = in_x[:, pl.ds(pl.multiple_of(here * half, 128), half)]
    narrow = x_proj.shape[1]
    steps = dot_nn(x_proj[...], one_hot((narrow, 128), 0)) + dot_tn(
        dt_proj[...], one_hot((dt_proj.shape[0], 128), 128 - dt_proj.shape[0])
    )
    values = jnp.concatenate(
        [
            conv_w[...],
            conv_b[...].reshape(1, width),
            dt_bias[...].reshape(1, width),
            skip_d[...].reshape(1, width),
            jnp.zeros((1, width), f32),
            a_log[...],
        ],
        axis=0,
    )
    top = values.astype(bf16)
    left = values - top.astype(f32)
    mid = left.astype(bf16)
    low = (left - mid.astype(f32)).astype(bf16)
    count = values.shape[0]
    extra = dot_tn(top, one_hot((count, 128), 0))
    extra = extra + dot_tn(mid, one_hot((count, 128), count))
    extra = extra + dot_tn(low, one_hot((count, 128), 2 * count))
    rest = jnp.where(here == 0, steps, extra).astype(bf16)
    for place in range(places):
        out[place * width : (place + 1) * width, :half] = mine
        out[place * width : (place + 1) * width, half:] = rest


def prepare_kernel(
    base, lengths, hidden, cot, route, gain, nrm_o, tail_o, hid_o, cot_o, route_o, aux_o
):
    rows = hidden.shape[0]
    steps_in = rows // SUB
    row = lax.broadcasted_iota(jnp.int32, (rows, rows), 0)
    column = lax.broadcasted_iota(jnp.int32, (rows, rows), 1)
    in_order = (row % SUB) * steps_in + row // SUB == column
    order = in_order.astype(bf16)
    hid = dot_nn(order, hidden[...])
    hid_o[...] = hid.astype(bf16)
    cot_o[...] = dot_nn(order, cot[...]).astype(bf16)
    ours = jnp.where(in_order, jnp.broadcast_to(route[...], (rows, rows)), 0)
    route_o[...] = jnp.sum(ours, axis=1, keepdims=True)
    scale = lax.rsqrt(jnp.mean(hid * hid, axis=1, keepdims=True) + epsilon)
    normed = (hid * scale * gain[...].reshape(1, -1)).astype(bf16)
    nrm_o[...] = normed
    tail_row = lax.broadcasted_iota(jnp.int32, (16, rows), 0)
    tail_column = lax.broadcasted_iota(jnp.int32, (16, rows), 1)
    picked = (tail_column == rows - 1 - (KC - 2 - tail_row) * SUB) & (tail_row < KC - 1)
    tail = dot_nn(picked.astype(bf16), normed)
    tail_row = tail_row - SUB
    picked = (tail_column == rows - 1 - (KC - 2 - tail_row) * SUB) & (tail_row < KC - 1)
    picked = picked & (tail_row >= 0)
    tail_o[...] = (tail + dot_nn(picked.astype(bf16), hid.astype(bf16))).astype(bf16)

    def layout(position, lane):
        back = position - (lane + 1)
        segment = jnp.zeros_like(position)
        segment_back = jnp.zeros_like(position)
        reset = position == 0
        end = jnp.int32(0)
        for j in range(lengths.shape[1] - 1):
            end = end + lengths[0, j]
            segment = segment + (position >= end).astype(jnp.int32)
            segment_back = segment_back + (back >= end).astype(jnp.int32)
            reset = reset | (position == end)
        same = (back >= 0) & (segment == segment_back)
        live = position < end
        picked = jnp.where(lane == KC - 1, live.astype(f32), reset.astype(f32))
        return jnp.where(lane < KC - 1, same.astype(f32), picked)

    at = lax.broadcasted_iota(jnp.int32, (rows, 128), 0)
    lane = lax.broadcasted_iota(jnp.int32, (rows, 128), 1)
    aux_o[...] = layout(base[0] + (at % SUB) * steps_in + at // SUB, lane)


def front_kernel(
    moves, core, nrm_in, halo_in, wm, wo, rest_m, rest_o, aux, ext_o, pre_o, steps_o, sig_o, small_o, x_o, tpre_o, tsuf_o,
    state_o, par_o, xd_o, sd_s, q_s, bw_s, nrm_s, sum_s, *, rank, count
):
    rows, di = pre_o.shape
    half = wo.shape[1]
    steps_in = rows // SUB
    gs = group_of(di)
    low = core[0] == 0
    nrm_s[0, :rows] = jnp.where(low, nrm_in[:, :half], nrm_in[:, half:])
    nrm_s[1, :rows] = jnp.where(low, nrm_in[:, half:], nrm_in[:, :half])
    nrm_s[0, rows:] = jnp.where(low, halo_in[:, :half], halo_in[:, half:])
    nrm_s[1, rows:] = jnp.where(low, halo_in[:, half:], halo_in[:, :half])
    small_o[...] = jnp.zeros_like(small_o)
    moves.need(rest_m, rest_o)
    par = par_o
    total_rows = par_o.shape[0]

    def unpack(g, _):
        lanes = pl.ds(pl.multiple_of(g * 128, 128), 128)
        mine = rest_m[lanes, :]
        other = rest_o[lanes, :]
        xd_o[lanes, :] = jnp.where(low, mine, other)
        turned = jnp.where(low, other, mine).astype(f32).T
        par_o[:, lanes] = (
            turned[:total_rows, :]
            + turned[total_rows : 2 * total_rows, :]
            + turned[2 * total_rows : 3 * total_rows, :]
        )
        return 0

    lax.fori_loop(0, di // 128, unpack, 0)
    moves.need(wm, wo)

    def project(g, _):
        lanes = pl.ds(pl.multiple_of(g * gs, gs), gs)
        inner = dot_nt(nrm_s[0], wm[lanes, :half]) + dot_nt(nrm_s[1], wo[lanes, :half])
        for back in range(1, KC):
            block = inner[rows - back * SUB : rows - (back - 1) * SUB, :]
            halo = inner[rows + KC - 1 - back : rows + KC - back, :]
            ext_o[(KC - 1 - back) * SUB : (KC - back) * SUB, lanes] = from_before(block, halo)
        ext_o[(KC - 1) * SUB :, lanes] = inner[:rows, :]
        total = par[KC : KC + 1, lanes] + par[KC - 1 : KC, lanes] * inner[:rows, :]
        for back in range(1, KC):
            shifted = ext_o[(KC - 1 - back) * SUB : (KC - 1 - back) * SUB + rows, lanes]
            total = total + par[KC - 1 - back : KC - back, lanes] * shifted * aux[:, back - 1 : back]
        pre_o[:, lanes] = total
        act = total * jax.nn.sigmoid(total)
        q_s[:, lanes] = act
        small_o[...] += dot_nn(act.astype(bf16), xd_o[lanes, :])
        return 0

    lax.fori_loop(0, di // gs, project, 0)
    moves.done(ext_o, pre_o, par_o, xd_o)
    small = small_o[...]
    lane = lax.broadcasted_iota(jnp.int32, small.shape, 1)
    step_low = jnp.where(lane >= 128 - rank, pltpu.roll(small, 128 - rank, 1), 0.0).astype(bf16)
    spread_columns(small, rank, count, bw_s)

    def stepping(g, _):
        lanes = pl.ds(pl.multiple_of(g * gs, gs), gs)
        step_pre = dot_nt(step_low, xd_o[lanes, :]) + par[KC + 1 : KC + 2, lanes]
        small_exp = jnp.exp(-jnp.abs(step_pre))
        steps = jnp.maximum(step_pre, 0.0) + jnp.log1p(small_exp)
        steps_o[:, lanes] = steps
        sig_o[:, lanes] = jax.nn.sigmoid(step_pre)
        q_s[:, lanes] = q_s[:, lanes] * steps
        sd_s[:, lanes] = jnp.where(aux[:, 4:5] > 0.5, STOP, steps)
        return 0

    lax.fori_loop(0, di // gs, stepping, 0)
    moves.done(steps_o, sig_o, sd_s, q_s)

    def chunk(g, _):
        lanes = pl.ds(pl.multiple_of(g * 128, 128), 128)
        rates = [
            jnp.broadcast_to(-LOG2E * jnp.exp(par[8 + n : 9 + n, lanes]), (SUB, 128))
            for n in range(count)
        ]

        def step(j, carry):
            states, total = carry
            at = pl.ds(pl.multiple_of(j * SUB, SUB), SUB)
            sd = sd_s[at, lanes]
            q = q_s[at, lanes]
            states = tuple(
                jnp.exp2(sd * rates[n]) * states[n] + q * bw_s[j * count + n] for n in range(count)
            )
            return (states, total + sd)

        zero = jnp.zeros((SUB, 128), f32)
        states, total = lax.fori_loop(0, steps_in, step, ((zero,) * count, zero), unroll=16)
        row = sublane_iota(128)
        ahead = prefix_sum(total)
        behind = suffix_sum(total)
        tpre_o[:, lanes] = jnp.where(row == 0, 0.0, pltpu.roll(ahead, 1, 0))
        tsuf_o[:, lanes] = jnp.where(row == SUB - 1, 0.0, pltpu.roll(behind, SUB - 1, 0))
        last = []
        for n in range(count):
            joined = prefix_states(jnp.exp2(rates[n] * total), states[n])
            x_o[n, :, lanes] = jnp.where(row == 0, 0.0, pltpu.roll(joined, 1, 0))
            last.append(joined[SUB - 1 : SUB, :])
        sum_s[pl.ds(g, 1), :] = ahead[SUB - 1 : SUB, :]
        to_copies(state_o, jnp.concatenate(last, axis=0).astype(bf16), lanes)
        return 0

    sum_s[...] = jnp.zeros_like(sum_s)
    lax.fori_loop(0, di // 128, chunk, 0)
    sums = sum_s[...]
    top = sums.astype(bf16)
    left = (sums - top.astype(f32)).astype(bf16)
    to_copies(state_o, top, slice(di, di + 128))
    to_copies(state_o, left, slice(di + 128, di + 256))


def to_copies(out, values, lanes):
    count = values.shape[0]
    for place in range(out.shape[0] // count):
        out[place * count : (place + 1) * count, lanes] = values


def negative_rates(par, out):
    out[...] = -LOG2E * jnp.exp(par[8:, :])


def group_kernel(arrived, out, state_s, sum_s, *, di, count, reverse):
    members = arrived.shape[0] // count
    rest = arrived.shape[1] - di - 256
    copies = out.shape[0] // count
    state_s[...] = jnp.zeros_like(state_s)
    total = jnp.zeros((count, 128), f32)
    for place in range(members - 1, -1, -1) if reverse else range(members):
        block = slice(place * count, (place + 1) * count)
        sums = arrived[block, di : di + 128].astype(f32)
        sums = sums + arrived[block, di + 128 : di + 256].astype(f32)
        total = total + sums
        carry_step(sums, arrived[block, :di], sum_s, state_s)
    joined = state_s[...].astype(bf16)
    top = total.astype(bf16)
    left = (total - top.astype(f32)).astype(bf16)
    for copy in range(copies):
        block = slice(copy * count, (copy + 1) * count)
        out[block, :di] = joined
        out[block, di : di + 128] = top
        out[block, di + 128 : di + 256] = left
    if rest:
        extra = jnp.zeros((count, rest), f32)
        for place in range(members):
            extra = extra + arrived[place * count : (place + 1) * count, di + 256 :].astype(f32)
        gap = jnp.zeros((count - 2, rest), f32)
        for copy in range(copies):
            rows = jnp.concatenate([extra[2 * copy : 2 * copy + 2, :], gap], axis=0)
            out[copy * count : (copy + 1) * count, di + 256 :] = rows.astype(bf16)


def forward_group_kernel(arrived, par, out, state_s, rate_s, *, di, count):
    negative_rates(par, rate_s)
    group_kernel(arrived, out, state_s, rate_s, di=di, count=count, reverse=False)


def backward_group_kernel(arrived, par, out, state_s, rate_s, *, di, count):
    negative_rates(par, rate_s)
    group_kernel(arrived, out, state_s, rate_s, di=di, count=count, reverse=True)


def step_sums(arrived, block, di):
    return arrived[block, di : di + 128].astype(f32) + arrived[block, di + 128 : di + 256].astype(
        f32
    )


def carry_step(decay_sums, arrived, rate_s, state_s):
    for g in range(state_s.shape[1] // 128):
        lanes = slice(g * 128, (g + 1) * 128)
        decay = jnp.exp2(rate_s[:, lanes] * decay_sums[g : g + 1, :])
        state_s[:, lanes] = decay * state_s[:, lanes] + arrived[:, lanes].astype(f32)


def gate_kernel(moves, core, nrm, zm, zo, gate_z_o, nrm_s):
    rows, di = gate_z_o.shape
    half = zm.shape[1]
    gs = group_of(di)
    low = core[0] == 0
    nrm_s[0] = jnp.where(low, nrm[:, :half], nrm[:, half:])
    nrm_s[1] = jnp.where(low, nrm[:, half:], nrm[:, :half])
    moves.need(zm, zo)

    def project(g, _):
        lanes = pl.ds(pl.multiple_of(g * gs, gs), gs)
        gate_z_o[:, lanes] = dot_nt(nrm_s[0], zm[lanes, :]) + dot_nt(nrm_s[1], zo[lanes, :])
        return 0

    lax.fori_loop(0, di // gs, project, 0)


def middle_kernel(
    moves, core, place, om, oo, par, aux, pre, sd, q, x_in, small, arrived, near, tpre, hid, cot,
    route, gain, router, gate_z, scan_o, send_o, middle_o, ntwo_o, chance_o, meta_o, hot_o,
    entry_o, bw_s, cw_s, rate_s, *, rank, count, experts, stride, capacity, shift
):
    rows, di = pre.shape
    half = om.shape[1]
    steps_in = rows // SUB
    gs = group_of(di)
    low = core[0] == 0
    spread_columns(small[...], rank, count, bw_s)
    spread_columns(small[...], rank + count, count, cw_s)
    negative_rates(par, rate_s)
    moves.need(arrived, near)
    entry_o[...] = jnp.zeros_like(entry_o)
    members = near.shape[0] // count

    def before_here(there, _):
        block = pl.ds(pl.multiple_of(there * count, count), count)
        carry_step(step_sums(arrived, block, di), arrived[block, :di], rate_s, entry_o)
        return 0

    def just_before(there, _):
        block = pl.ds(pl.multiple_of(there * count, count), count)
        carry_step(step_sums(near, block, di), near[block, :di], rate_s, entry_o)
        return 0

    lax.fori_loop(0, place[0] // members, before_here, 0)
    lax.fori_loop(0, place[0] % members, just_before, 0)
    moves.done(entry_o)
    moves.need(x_in, sd, q)

    def scan(g, _):
        lanes = pl.ds(pl.multiple_of(g * 128, 128), 128)
        rates = [jnp.broadcast_to(rate_s[n : n + 1, lanes], (SUB, 128)) for n in range(count)]
        before = tpre[:, lanes]
        first = tuple(
            x_in[n, :, lanes] + jnp.exp2(rates[n] * before) * entry_o[n : n + 1, lanes]
            for n in range(count)
        )
        def step(j, states):
            at = pl.ds(pl.multiple_of(j * SUB, SUB), SUB)
            sd_here = sd[at, lanes]
            q_here = q[at, lanes]
            total = jnp.zeros((SUB, 128), f32)
            fresh = []
            for n in range(count):
                state = jnp.exp2(sd_here * rates[n]) * states[n] + q_here * bw_s[j * count + n]
                total = total + state * cw_s[j * count + n]
                fresh.append(state)
            scan_o[at, lanes] = total
            return tuple(fresh)

        lax.fori_loop(0, steps_in, step, first, unroll=16)
        return 0

    lax.fori_loop(0, di // 128, scan, 0)

    def gating(g, carry):
        mine, other = carry
        lanes = pl.ds(pl.multiple_of(g * gs, gs), gs)
        z = gate_z[:, lanes]
        pre_here = pre[:, lanes]
        scanned = scan_o[:, lanes] + par[KC + 2 : KC + 3, lanes] * (
            pre_here * jax.nn.sigmoid(pre_here)
        )
        scan_o[:, lanes] = scanned
        gated = (scanned * (z * jax.nn.sigmoid(z)) * aux[:, 3:4]).astype(bf16)
        return (mine + dot_nn(gated, om[lanes, :]), other + dot_nn(gated, oo[lanes, :]))

    zero = jnp.zeros((rows, half), f32)
    moves.need(pre, gate_z, om, oo)
    mine, other = lax.fori_loop(0, di // gs, gating, (zero, zero))
    moves.done(scan_o)
    mixed = jnp.concatenate([jnp.where(low, mine, other), jnp.where(low, other, mine)], axis=1)
    middle = hid[...].astype(f32) + mixed
    middle_o[...] = middle
    scale = lax.rsqrt(jnp.mean(middle * middle, axis=1, keepdims=True) + epsilon)
    ntwo = (middle * scale * gain[...].reshape(1, -1)).astype(bf16)
    ntwo_o[...] = ntwo
    logits = dot_nt(ntwo, router[...])
    top = jnp.max(logits, axis=1, keepdims=True)
    raised = jnp.exp(logits - top)
    chances = raised / jnp.sum(raised, axis=1, keepdims=True)
    chance_o[...] = chances
    lane = lax.broadcasted_iota(jnp.int32, (rows, experts), 1)
    chosen = route[...] == lane
    chosen_f = chosen.astype(f32)
    gate = jnp.sum(chances * chosen_f, axis=1, keepdims=True)
    taken = chosen_f * aux[:, 3:4]
    here = lax.broadcasted_iota(jnp.int32, (rows, rows), 0)
    there = lax.broadcasted_iota(jnp.int32, (rows, rows), 1)
    own_id = (here & (SUB - 1)) * steps_in + (here >> shift)
    other_id = (there & (SUB - 1)) * steps_in + (there >> shift)
    earlier = (other_id < own_id).astype(bf16)
    ranks = jnp.sum(dot_nn(earlier, taken.astype(bf16)) * chosen_f, axis=1, keepdims=True)
    kept = aux[:, 3:4] * (ranks < capacity).astype(f32)
    weight = gate * kept
    up = (cot[...].astype(f32) * weight).astype(bf16)
    values = jnp.concatenate([ntwo, up], axis=0)
    rank_low = ranks.astype(jnp.int32)
    slot = jnp.concatenate([rank_low, rank_low + capacity], axis=0)
    block = route[...] * stride
    block = jnp.concatenate([block, block], axis=0)
    kept_on = jnp.concatenate([kept, kept], axis=0) > 0.5
    place = lax.broadcasted_iota(jnp.int32, (2 * rows, experts * stride), 1)
    wide_hot = ((block + slot == place) & kept_on).astype(bf16)
    at_last = (block + 2 * capacity + slot // 2 == place) & kept_on
    even_hot = (at_last & (slot % 2 == 0)).astype(bf16)
    odd_hot = (at_last & (slot % 2 == 1)).astype(bf16)
    hot_o[0] = wide_hot
    hot_o[1] = even_hot
    hot_o[2] = odd_hot
    moves.done(hot_o, middle_o, ntwo_o)
    third = ntwo.shape[1] // 3
    narrow = values[:, 2 * third :]
    last = jnp.concatenate([dot_tn(even_hot, narrow), dot_tn(odd_hot, narrow)], axis=1)
    packed = (dot_tn(wide_hot, values[:, : 2 * third]) + last).astype(bf16)
    send_o[: experts * stride, :] = packed
    send_o[experts * stride :, :] = packed
    lane8 = lax.broadcasted_iota(jnp.int32, (rows, 8), 1)
    meta_o[...] = jnp.where(
        lane8 == 0, gate, jnp.where(lane8 == 1, kept, jnp.where(lane8 == 2, scale, 0.0))
    )


def back_kernel(
    moves, core, back, om, oo, par, aux, sd, small, gate_z, hot, middle, meta, chances, route, cot, gain,
    router, ntwo, combined_o, mixlow_o, mgrad_o, ggrad_o, sg_o, gain_o, y_o, state_o, cw_s, mix_s,
    rate_s, sum_s, *, rank, count, experts
):
    rows, di = sd.shape
    half = om.shape[1]
    steps_in = rows // SUB
    gs = group_of(di)
    negative_rates(par, rate_s)
    slots = back.shape[0] // 2
    third = back.shape[1] // 2
    rows_back = (back[:slots, :].astype(f32) + back[slots:, :].astype(f32)).astype(bf16)
    last = dot_nn(hot[1], rows_back[:, :third]) + dot_nn(hot[2], rows_back[:, third:])
    both = jnp.concatenate([dot_nn(hot[0], rows_back), last], axis=1)
    combined = both[:rows, :]
    dispatch = both[rows:, :]
    combined_o[...] = combined
    gate = meta[:, 0:1]
    kept = meta[:, 1:2]
    scale = meta[:, 2:3]
    mid = middle[...]
    up = cot[...].astype(f32)
    gate_total = kept * jnp.sum(up * combined, axis=1, keepdims=True)
    lane = lax.broadcasted_iota(jnp.int32, (rows, experts), 1)
    chosen_f = (route[...] == lane).astype(f32)
    logit_grad = (gate * (chosen_f - chances[...]) * gate_total).astype(bf16)
    router_rows = dot_tn(logit_grad, ntwo[...])
    members = state_o.shape[0] // count
    for member in range(members):
        rows_here = []
        for group in range(experts // members):
            row = router_rows[group * members + member : group * members + member + 1, :]
            rows_here += [row[:, :half], row[:, half:]]
        block = slice(member * count, (member + 1) * count)
        state_o[block, di + 256 :] = jnp.concatenate(rows_here, axis=0).astype(bf16)
    ngrad = dot_nn(logit_grad, router[...]) + dispatch
    gain_o[...] = jnp.sum(ngrad * mid * scale, axis=0, keepdims=True)
    scaled = gain[...].reshape(1, -1) * ngrad
    cube = scale * scale * scale
    mgrad = up + scale * scaled - mid * cube * jnp.mean(mid * scaled, axis=1, keepdims=True)
    mgrad_o[...] = mgrad
    low = core[0] == 0
    mixlow = mgrad.astype(bf16)
    mixlow_o[...] = mixlow
    mix_s[0] = jnp.where(low, mixlow[:, :half], mixlow[:, half:])
    mix_s[1] = jnp.where(low, mixlow[:, half:], mixlow[:, :half])
    moves.done(mixlow_o, mgrad_o, combined_o)
    moves.need(om, oo, gate_z)

    def gating(g, _):
        lanes = pl.ds(pl.multiple_of(g * gs, gs), gs)
        ggrad = dot_nt(mix_s[0], om[lanes, :]) + dot_nt(mix_s[1], oo[lanes, :])
        ggrad = ggrad * aux[:, 3:4]
        ggrad_o[:, lanes] = ggrad
        z = gate_z[:, lanes]
        sg_o[:, lanes] = ggrad * (z * jax.nn.sigmoid(z))
        return 0

    lax.fori_loop(0, di // gs, gating, 0)
    moves.done(ggrad_o, sg_o)
    spread_columns(small[...], rank + count, count, cw_s)
    moves.need(sd)

    def chunk(g, _):
        lanes = pl.ds(pl.multiple_of(g * 128, 128), 128)
        rates = [jnp.broadcast_to(rate_s[n : n + 1, lanes], (SUB, 128)) for n in range(count)]

        def step(i, carry):
            grads, total = carry
            j = steps_in - 1 - i
            at = pl.ds(pl.multiple_of(j * SUB, SUB), SUB)
            sd_here = sd[at, lanes]
            sgrad = sg_o[at, lanes]
            grads = tuple(
                jnp.exp2(sd_here * rates[n]) * (grads[n] + sgrad * cw_s[j * count + n])
                for n in range(count)
            )
            return (grads, total + sd_here)

        zero = jnp.zeros((SUB, 128), f32)
        grads, total = lax.fori_loop(0, steps_in, step, ((zero,) * count, zero), unroll=16)
        row = sublane_iota(128)
        last = []
        for n in range(count):
            joined = suffix_states(jnp.exp2(rates[n] * total), grads[n])
            y_o[n, :, lanes] = jnp.where(row == SUB - 1, 0.0, pltpu.roll(joined, SUB - 1, 0))
            last.append(joined[0:1, :])
        sum_s[pl.ds(g, 1), :] = jnp.sum(total, axis=0, keepdims=True)
        to_copies(state_o, jnp.concatenate(last, axis=0).astype(bf16), lanes)
        return 0

    sum_s[...] = jnp.zeros_like(sum_s)
    lax.fori_loop(0, di // 128, chunk, 0)
    total = sum_s[...]
    top = total.astype(bf16)
    to_copies(state_o, top, slice(di, di + 128))
    to_copies(state_o, (total - top.astype(f32)).astype(bf16), slice(di + 128, di + 256))


def slot_rows(stride, capacity, blocks):
    dims = (2 * capacity * blocks, stride * blocks)
    row = lax.broadcasted_iota(jnp.int32, dims, 0)
    column = lax.broadcasted_iota(jnp.int32, dims, 1)
    half = capacity * blocks
    slot = row % capacity + row // half * capacity
    start = row % half // capacity * stride
    wide = (start + slot == column).astype(bf16)
    at_last = start + 2 * capacity + slot // 2 == column
    even = (at_last & (slot % 2 == 0)).astype(bf16)
    odd = (at_last & (slot % 2 == 1)).astype(bf16)
    return wide, even, odd


def unpack(packed, hots):
    wide, even, odd = hots
    third = packed.shape[1] // 2
    last = dot_nn(even, packed[:, :third]) + dot_nn(odd, packed[:, third:])
    return jnp.concatenate([dot_nn(wide, packed), last], axis=1).astype(bf16)


def pack(rows, hots):
    wide, even, odd = hots
    third = rows.shape[1] // 3
    narrow = rows[:, 2 * third :]
    last = jnp.concatenate([dot_tn(even, narrow), dot_tn(odd, narrow)], axis=1)
    return dot_tn(wide, rows[:, : 2 * third]) + last


def expert_kernel(
    moves, arrived, w_gate, w_up, w_down, w_gate_two, w_up_two, w_down_two, kept_o, sent_o, back_o,
    *, stride, capacity
):
    blocks = 16
    hots = slot_rows(stride, capacity, blocks)
    size = capacity * blocks
    groups = arrived.shape[0] // (stride * blocks)
    slots = kept_o.shape[0] // 5
    for group in range(groups):
        rows = unpack(arrived[group * stride * blocks : (group + 1) * stride * blocks, :], hots)
        at = group * size
        kept_o[at : at + size, :] = rows[:size, :]
        kept_o[slots + at : slots + at + size, :] = rows[size:, :]
    sent_o[: 2 * slots, :] = kept_o[: 2 * slots, :]
    inputs = kept_o[:slots, :]
    grads = kept_o[slots : 2 * slots, :]
    outputs = 0.0
    total = 0.0
    weights = ((sent_o, w_gate_two, w_up_two, w_down_two), (kept_o, w_gate, w_up, w_down))
    for out, gate_weight, up_weight, down_weight in weights[::-1]:
        moves.need(gate_weight)
        gate_in = dot_nn(inputs, gate_weight[...])
        moves.need(up_weight)
        up_in = dot_nn(inputs, up_weight[...])
        sig = jax.nn.sigmoid(gate_in)
        silu = gate_in * sig
        act = (silu * up_in).astype(bf16)
        out[2 * slots : 3 * slots, :] = act
        moves.need(down_weight)
        outputs = outputs + dot_nn(act, down_weight[...])
        act_grad = dot_nt(grads, down_weight[...])
        gate_grad = (act_grad * up_in * sig * (1.0 + gate_in * (1.0 - sig))).astype(bf16)
        up_grad = (act_grad * silu).astype(bf16)
        out[3 * slots : 4 * slots, :] = gate_grad
        out[4 * slots :, :] = up_grad
        moves.done(out)
        total = total + dot_nt(gate_grad, gate_weight[...]) + dot_nt(up_grad, up_weight[...])
    for group in range(groups):
        at = group * size
        rows = jnp.concatenate([outputs[at : at + size, :], total[at : at + size, :]], axis=0)
        packed = pack(rows.astype(bf16), hots).astype(bf16)
        back_o[group * stride * blocks : (group + 1) * stride * blocks, :] = packed


def aside_kernel(
    moves, core, side, zm, zo, aux, pre, gate_z, scanned, ggrad, combined, middle, meta,
    out_o, comb_o, skip_o, ngrad_o, *, width, span
):
    rows, di = pre.shape
    half = zm.shape[1]
    gs = group_of(di)
    pieces = width // 16
    result = (middle[...] + meta[:, 0:1] * meta[:, 1:2] * combined[...]).astype(bf16)
    out_o[...] = dot_tn(token_order(rows), result).astype(bf16)
    def gating(g, carry):
        mine, other = carry
        lanes = pl.ds(pl.multiple_of(g * gs, gs), gs)
        grad = ggrad[:, lanes]
        z = gate_z[:, lanes]
        sig = jax.nn.sigmoid(z)
        here = scanned[:, lanes]
        zgrad = grad * here * sig * (1.0 + z * (1.0 - sig))
        z_low = zgrad.astype(bf16)
        z_turned = zgrad.T.astype(bf16)
        gated_turned = (here * (z * sig) * aux[:, 3:4]).T.astype(bf16)
        for i in range(gs // 16):
            piece = g * (gs // 16) + i
            to = pl.multiple_of(piece // pieces * span + piece % pieces * 16, 16)
            comb_o[pl.ds(to, 16), :] = z_turned[i * 16 : (i + 1) * 16, :]
            owner = piece // pieces
            holder = owner // 2 * 2 + side[0]
            to = holder * span + (1 + owner % 2) * width + piece % pieces * 16
            comb_o[pl.ds(pl.multiple_of(to, 16), 16), :] = gated_turned[i * 16 : (i + 1) * 16, :]
        pre_here = pre[:, lanes]
        act = pre_here * jax.nn.sigmoid(pre_here)
        skip_o[:, lanes] = jnp.sum(grad * (z * sig) * act, axis=0, keepdims=True)
        return (mine + dot_nn(z_low, zm[lanes, :]), other + dot_nn(z_low, zo[lanes, :]))

    moves.need(zm, zo)
    zero = jnp.zeros((rows, half), f32)
    mine, other = lax.fori_loop(0, di // gs, gating, (zero, zero))
    ngrad_o[0] = mine
    ngrad_o[1] = other


def scan_kernel(
    moves, place, xd, par, sd, q, pre, steps, sig_step, small, x_in, tpre, entry, y_in, tsuf, arrived, near,
    sgrad, cgrad_o, xd_o, spar_o, router_o, bw_s, cw_s, bacc_s, cacc_s, st_s, dk_s, sgr_s, asc_s, plow_s,
    rate_s, after_s, *, rank, count
):
    rows, di = pre.shape
    negative_rates(par, rate_s)
    after_s[...] = jnp.zeros_like(after_s)
    groups = arrived.shape[0] // count
    members = near.shape[0] // count
    spread_columns(small[...], rank, count, bw_s)
    spread_columns(small[...], rank + count, count, cw_s)
    bacc_s[...] = jnp.zeros_like(bacc_s)
    cacc_s[...] = jnp.zeros_like(cacc_s)
    spar_o[...] = jnp.zeros_like(spar_o)
    moves.need(arrived, near)

    def after_here(i, _):
        block = pl.ds(pl.multiple_of((groups - 1 - i) * count, count), count)
        carry_step(step_sums(arrived, block, di), arrived[block, :di], rate_s, after_s)
        return 0

    def just_after(i, _):
        block = pl.ds(pl.multiple_of((members - 1 - i) * count, count), count)
        carry_step(step_sums(near, block, di), near[block, :di], rate_s, after_s)
        return 0

    lax.fori_loop(0, groups - 1 - place[0] // members, after_here, 0)
    lax.fori_loop(0, members - 1 - place[0] % members, just_after, 0)
    router_sum = jnp.zeros(router_o.shape, f32)
    for there in range(groups):
        router_sum += arrived[there * count : (there + 1) * count, di + 256 :].astype(f32)
    router_o[...] = router_sum
    steps_in = rows // SUB
    gs = group_of(di)
    moves.need(x_in, sd, q, sgrad, y_in)

    def scan(g, _):
        lanes = pl.ds(pl.multiple_of(g * 128, 128), 128)
        rates = [
            jnp.broadcast_to(rate_s[n : n + 1, lanes], (SUB, 128)) for n in range(count)
        ]
        before = tpre[:, lanes]
        behind = tsuf[:, lanes]
        first = tuple(
            x_in[n, :, lanes] + jnp.exp2(rates[n] * before) * entry[n : n + 1, lanes]
            for n in range(count)
        )

        def forward(j, states):
            at = pl.ds(pl.multiple_of(j * SUB, SUB), SUB)
            sd_here = sd[at, lanes]
            q_here = q[at, lanes]
            fresh = []
            for n in range(count):
                decay = jnp.exp2(sd_here * rates[n])
                dk_s[j * count + n] = decay
                st_s[j * count + n] = states[n]
                fresh.append(decay * states[n] + q_here * bw_s[j * count + n])
            return tuple(fresh)

        last = lax.fori_loop(0, steps_in, forward, first, unroll=16)
        for n in range(count):
            st_s[steps_in * count + n] = last[n]
        zero = jnp.zeros((SUB, 128), f32)
        arriving = tuple(
            y_in[n, :, lanes] + jnp.exp2(rates[n] * behind) * after_s[n : n + 1, lanes]
            for n in range(count)
        )

        def backward(i, carry):
            grads, rate_grads = carry
            j = steps_in - 1 - i
            at = pl.ds(pl.multiple_of(j * SUB, SUB), SUB)
            sd_here = sd[at, lanes]
            q_here = q[at, lanes]
            sg = sgrad[at, lanes]
            onto = zero
            along = zero
            fresh = []
            fresh_rates = []
            for n in range(count):
                k = j * count + n
                lam = grads[n] + sg * cw_s[k]
                cacc_s[k] += sg * st_s[k + count]
                bacc_s[k] += lam * q_here
                onto = onto + lam * bw_s[k]
                carried = lam * dk_s[k]
                logs = carried * st_s[k]
                along = along + logs * rates[n]
                fresh.append(carried)
                fresh_rates.append(rate_grads[n] + logs * sd_here)
            sgr_s[at, lanes] = along
            asc_s[at, lanes] = onto
            return (tuple(fresh), tuple(fresh_rates))

        _, rate_grads = lax.fori_loop(0, steps_in, backward, (arriving, (zero,) * count), unroll=2)
        for n in range(count):
            spar_o[8 + n : 9 + n, lanes] = LN2 * jnp.sum(
                rate_grads[n] * rates[n], axis=0, keepdims=True
            )
        return 0

    lax.fori_loop(0, di // 128, scan, 0)

    moves.need(pre, sig_step, xd, steps)
    lane8 = lax.broadcasted_iota(jnp.int32, (SUB, 128), 1)
    blocks = []
    for j in range(steps_in):
        block = jnp.zeros((SUB, 128), f32)
        for n in range(count):
            k = j * count + n
            block = jnp.where(
                lane8 == rank + n, jnp.sum(bacc_s[k], axis=1, keepdims=True), block
            )
            block = jnp.where(
                lane8 == rank + count + n, jnp.sum(cacc_s[k], axis=1, keepdims=True), block
            )
        blocks.append(block)
    coef_grad = jnp.concatenate(blocks, axis=0)
    lane = lax.broadcasted_iota(jnp.int32, (rows, 128), 1)
    step_low = jnp.where(
        lane >= 128 - rank, pltpu.roll(small[...], 128 - rank, 1), 0.0
    ).astype(bf16)

    def steps_back(g, total):
        lanes = pl.ds(pl.multiple_of(g * gs, gs), gs)
        pre_here = pre[:, lanes]
        act = pre_here * jax.nn.sigmoid(pre_here)
        pre_grad = (LN2 * sgr_s[:, lanes] + act * asc_s[:, lanes]) * sig_step[:, lanes]
        spar_o[KC + 1 : KC + 2, lanes] = jnp.sum(pre_grad, axis=0, keepdims=True)
        pre_low = pre_grad.astype(bf16)
        plow_s[:, lanes] = pre_low
        return total + dot_nn(pre_low, xd[lanes, :])

    rank_grad = lax.fori_loop(0, di // gs, steps_back, jnp.zeros((rows, 128), f32))
    small_low = jnp.where(lane < rank, pltpu.roll(rank_grad, rank, 1), coef_grad).astype(bf16)

    def act_back(g, _):
        lanes = pl.ds(pl.multiple_of(g * gs, gs), gs)
        pre_here = pre[:, lanes]
        sig = jax.nn.sigmoid(pre_here)
        act_low = (pre_here * sig).astype(bf16)
        total = (
            sgrad[:, lanes] * par[KC + 2 : KC + 3, lanes]
            + steps[:, lanes] * asc_s[:, lanes]
            + dot_nt(small_low, xd[lanes, :])
        )
        cgrad_o[:, lanes] = total * sig * (1.0 + pre_here * (1.0 - sig))
        xd_o[lanes, :] = (dot_tn(act_low, small_low) + dot_tn(plow_s[:, lanes], step_low)).astype(bf16)
        return 0

    lax.fori_loop(0, di // gs, act_back, 0)


def last_kernel(
    moves, core, cgrad, halo, aux, ext, par, wm, wo, ngrad_z, spar, skip, xd, hid, gain_two,
    router_sum, pay_o, ngrad_o, extra_o, low_s, far_s, *, width
):
    rows, di = cgrad.shape
    gs = 128
    moves.need(ext)
    ahead_lane = spar.shape[0] + 4 * (hid.shape[1] // width)
    moves.need(xd)

    def conv(g, _):
        lanes = pl.ds(pl.multiple_of(g * gs, gs), gs)
        cg = cgrad[:, lanes]
        grad = par[KC - 1 : KC, lanes] * cg
        parts = [jnp.sum(cg * ext[(KC - 1) * SUB :, lanes], axis=0, keepdims=True)]
        zero = jnp.zeros((1, gs), f32)
        behind = [zero] * (KC - 1)
        for ahead in range(1, KC):
            tap = par[KC - 1 - ahead : KC - ahead, lanes]
            masked = cg * aux[:, ahead - 1 : ahead]
            shifted = ext[(KC - 1 - ahead) * SUB : (KC - 1 - ahead) * SUB + rows, lanes]
            parts.append(jnp.sum(masked * shifted, axis=0, keepdims=True))
            pieces = [masked[ahead * SUB :, :]]
            for i in range(ahead):
                pieces.append(from_after(masked[i * SUB : (i + 1) * SUB, :], zero))
                k = KC - 1 - ahead + i
                behind[k] = behind[k] + tap * masked[i * SUB : i * SUB + 1, :]
            grad = grad + tap * jnp.concatenate(pieces, axis=0)
        low_s[:, lanes] = grad.astype(bf16)
        pay_o[lanes, 0:128] = grad.T.astype(bf16)
        pay_o[lanes, 128:256] = xd[lanes, :]
        extra = jnp.concatenate(behind + [jnp.zeros((SUB - KC + 1, gs), f32)], axis=0)
        far_s[:SUB, lanes] = extra.astype(bf16)
        own = jnp.concatenate(
            parts[::-1]
            + [jnp.sum(cg, axis=0, keepdims=True), spar[KC + 1 : KC + 2, lanes], skip[:, lanes]]
            + [zero, spar[8:, lanes], jnp.zeros((ahead_lane - spar.shape[0], gs), f32), extra]
            + [jnp.zeros((128 - ahead_lane - SUB, gs), f32)],
            axis=0,
        )
        pay_o[lanes, 256:384] = own.T.astype(bf16)
        return 0

    lax.fori_loop(0, di // gs, conv, 0)
    far_s[SUB:, :] = jnp.zeros_like(far_s[SUB:, :])
    moves.need(wm, wo, ngrad_z, hid)
    low = core[0] == 0

    def onto_inputs(values):
        return dot_nn(values, wm[...]), dot_nn(values, wo[...])

    def joined(mine, other):
        return jnp.concatenate([jnp.where(low, mine, other), jnp.where(low, other, mine)], axis=1)

    mine, other = onto_inputs(low_s[...])
    ngrad = joined(mine + ngrad_z[0], other + ngrad_z[1])
    ngrad_o[...] = ngrad
    far = joined(*onto_inputs(far_s[...]))[:SUB, :]
    extra_o[...] = far
    first = hid[...].astype(f32)
    scale = lax.rsqrt(jnp.mean(first * first, axis=1, keepdims=True) + epsilon)
    gains = jnp.sum(ngrad * first * scale, axis=0, keepdims=True)
    first = halo[SUB:, :].astype(f32)
    scale = lax.rsqrt(jnp.mean(first * first, axis=1, keepdims=True) + epsilon)
    gains = gains + jnp.sum(far * first * scale, axis=0, keepdims=True)
    model = first.shape[1]
    each = model // width
    row = lax.broadcasted_iota(jnp.int32, (width, model), 0)
    column = lax.broadcasted_iota(jnp.int32, (width, model), 1)
    here = column // each == row
    extra = jnp.zeros((width, 128), f32)
    router_row = jnp.concatenate([router_sum[0:1, :], router_sum[1:2, :]], axis=1)
    router_top = router_row.astype(bf16).astype(f32)
    rows_sent = (gains, gain_two[...], router_top, router_row - router_top)
    for k, values in enumerate(rows_sent):
        spread = jnp.where(here, values, 0.0).astype(bf16)
        at = lax.broadcasted_iota(jnp.int32, (model, 128), 0)
        to = lax.broadcasted_iota(jnp.int32, (model, 128), 1)
        placed = (at % each + spar.shape[0] + k * each == to).astype(bf16)
        extra = extra + dot_nn(spread, placed)
    extra = extra.astype(bf16)
    for place in range(di // width):
        pay_o[place * width : (place + 1) * width, 256:384] += extra


def tail_kernel(
    moves, place, core, xd, par, sd, q, pre, steps, sig_step, small, x_in, tpre, entry, y_in, tsuf,
    arrived, near, sgrad, halo, aux, ext, wm, wo, ngrad_z, skip, hid, gain_two,
    pay_o, ngrad_o, extra_o, low_s, far_s, cgrad_s, xd_s, spar_s, router_s, *scratch,
    rank, count, width
):
    scan_kernel(
        moves, place, xd, par, sd, q, pre, steps, sig_step, small, x_in, tpre, entry, y_in, tsuf,
        arrived, near, sgrad, cgrad_s, xd_s, spar_s, router_s, *scratch, rank=rank, count=count
    )
    last_kernel(
        moves, core, cgrad_s, halo, aux, ext, par, wm, wo, ngrad_z, spar_s, skip, xd_s, hid,
        gain_two, router_s, pay_o, ngrad_o, extra_o, low_s, far_s, width=width
    )


def hidden_kernel(ngrad_in, beyond, hid, mgrad, gain, first_o):
    first = hid[...].astype(f32)
    rows = first.shape[0]
    ngrad = ngrad_in[...]
    row = lax.broadcasted_iota(jnp.int32, first.shape, 0)
    for i in range(KC - 1):
        at = rows - 1 - (KC - 2 - i) * SUB
        ngrad = ngrad + jnp.where(row == at, beyond[i : i + 1, :], 0.0)
    scale = lax.rsqrt(jnp.mean(first * first, axis=1, keepdims=True) + epsilon)
    scaled = gain[...].reshape(1, -1) * ngrad
    cube = scale * scale * scale
    grad = (
        mgrad[...] + scale * scaled - first * cube * jnp.mean(first * scaled, axis=1, keepdims=True)
    )
    order = token_order(rows)
    top = grad.astype(bf16)
    left = grad - top.astype(f32)
    mid = left.astype(bf16)
    low_part = (left - mid.astype(f32)).astype(bf16)
    first_o[...] = dot_tn(order, top) + dot_tn(order, mid) + dot_tn(order, low_part)


def ready_kernel(
    moves, side, comb, nrm_all, mix_half, z_o, mine_o, theirs_o, z_s, gated_s
):
    places = comb.shape[0]
    width = z_o.shape[0]
    for place in range(places):
        z_s[:, place * 128 : (place + 1) * 128] = comb[place, :width, :]
    for k in range(places // 2):
        place = 2 * k + side[0]
        gated_s[:, k * 128 : (k + 1) * 128] = comb[place, width : 3 * width, :]
    moves.need(mix_half)
    grads = dot_nn(gated_s[...], mix_half[...]).astype(bf16)
    first = side[0] == 0
    mine_o[...] = jnp.where(first, grads[:width, :], grads[width:, :])
    theirs_o[...] = jnp.where(first, grads[width:, :], grads[:width, :])
    moves.need(nrm_all)
    z_o[...] = dot_nn(z_s[...], nrm_all[...]).astype(bf16)


def grads_kernel(got, nrm_all, out_o, left_s, *, base):
    places, width, _ = got.shape
    model = nrm_all.shape[1]
    each = model // width
    rest = jnp.zeros((width, 256), f32)
    routers = [jnp.zeros((width, 128), f32) for _ in range(places * each // 128)]
    lane = lax.broadcasted_iota(jnp.int32, (width, 128), 1)
    row = lax.broadcasted_iota(jnp.int32, (128, 128), 0)
    column = lax.broadcasted_iota(jnp.int32, (128, 128), 1)
    after = row - (base + 2 * each)
    late = column == 127 - (KC - 2 - after) * SUB
    placed = (late & (after >= 0) & (after < KC - 1)).astype(bf16)
    for place in range(places):
        at = gathered_place(place)
        inner = got[at, :, :128]
        if place + 1 < places:
            beyond = dot_nn(got[gathered_place(place + 1), :, 256:384], placed)
            inner = (inner.astype(f32) + beyond).astype(bf16)
        left_s[:, at * 128 : (at + 1) * 128] = inner
        there = got[at, :, 128:].astype(f32)
        rest = rest + there
        k = place * each // 128
        inside = place * each % 128
        mine = (lane >= inside) & (lane < inside + each)
        for part in range(2):
            turn = (inside - base - part * each) % 128
            routers[k] = routers[k] + jnp.where(mine, pltpu.roll(there[:, 128:], turn, 1), 0.0)
    out_o[width:, :256] = rest.astype(bf16)
    out_o[width:, 256:] = jnp.concatenate(routers, axis=1).astype(bf16)
    out_o[:width, :model] = dot_nn(left_s[...], nrm_all[...]).astype(bf16)


def token_order(rows):
    steps_in = rows // SUB
    row = lax.broadcasted_iota(jnp.int32, (rows, rows), 0)
    column = lax.broadcasted_iota(jnp.int32, (rows, rows), 1)
    return ((row % SUB) * steps_in + row // SUB == column).astype(bf16)


def final_kernel(
    ours, theirs, ours_two, theirs_two, x_o, z_o, out_o, conv_o, bias_o, xp_o, dt_o, db_o, al_o, skip_o, router_o, one_o,
    two_o, mine_s, other_s, *, rank, count, experts
):
    width = out_o.shape[0]
    model = router_o.shape[1]
    each = model // width
    x_o[...] = ours[:width, :model].astype(f32) + theirs[:width, :model].astype(f32)
    z_o[...] = ours_two[:width, :].astype(f32) + theirs_two[:width, :].astype(f32)
    out_o[...] = ours_two[width:, :].astype(f32) + theirs_two[width:, :].astype(f32)
    rest = slice(width, 2 * width)
    xd = ours[rest, :128].astype(f32) + theirs[rest, :128].astype(f32)
    xp_o[...] = xd[:, : rank + 2 * count]
    gap = jnp.zeros((128 - width, 128), f32)
    turned = jnp.concatenate([xd, gap], axis=0).T
    dt_o[...] = turned[128 - rank :, :width]
    vectors = jnp.zeros((128, 128), f32)
    for part, held in ((ours, mine_s), (theirs, other_s)):
        block = jnp.concatenate([part[rest, 128:256].astype(f32), gap], axis=0).T
        vectors = vectors + block
        for k in range(experts * each // 128):
            lanes = slice(256 + k * 128, 384 + k * 128)
            piece = jnp.concatenate([part[rest, lanes].astype(f32), gap], axis=0)
            held[k * 128 : (k + 1) * 128, :] = piece.T
        held[experts * each :, :] = jnp.zeros_like(held[experts * each :, :])
        held[experts * each : (experts + 2) * each, :] = block[8 + count : 8 + count + 2 * each, :]
    conv_o[...] = vectors[:KC, :width]
    bias_o[...] = vectors[KC : KC + 1, :width].reshape(width)
    db_o[...] = vectors[KC + 1 : KC + 2, :width].reshape(width)
    skip_o[...] = vectors[KC + 2 : KC + 3, :width].reshape(width)
    al_o[...] = vectors[8 : 8 + count, :width]
    row = lax.broadcasted_iota(jnp.int32, (128, model), 0)
    column = lax.broadcasted_iota(jnp.int32, (128, model), 1)
    total = jnp.zeros((experts + 8, model), f32)
    for at in range(each):
        to = (row * each + at == column).astype(bf16)
        picked = pl.ds(at, experts + 8, stride=each)
        total = total + dot_nn(mine_s[picked, :].astype(bf16), to)
        total = total + dot_nn(other_s[picked, :].astype(bf16), to)
    router_o[...] = total[:experts, :]
    one_o[...] = total[experts : experts + 1, :].reshape(model)
    two_o[...] = total[experts + 1 : experts + 2, :].reshape(model)


def token_order(rows):
    steps_in = rows // SUB
    row = lax.broadcasted_iota(jnp.int32, (rows, rows), 0)
    column = lax.broadcasted_iota(jnp.int32, (rows, rows), 1)
    return ((row % SUB) * steps_in + row // SUB == column).astype(bf16)


def exchange(values):
    return lax.all_to_all(values, "wide", split_axis=0, concat_axis=0, tiled=True)


def exchange_near(values, members):
    groups = [[u * members + z for z in range(members)] for u in range(32 // members)]
    blocks = values.reshape(members, -1, values.shape[1])
    return lax.all_to_all(
        blocks, "wide", split_axis=0, concat_axis=0, tiled=True, axis_index_groups=groups
    ).reshape(values.shape)


def exchange_far(values, members):
    groups = [[u * members + z for u in range(32 // members)] for z in range(members)]
    blocks = values.reshape(32 // members, -1, values.shape[1])
    return lax.all_to_all(
        blocks, "wide", split_axis=0, concat_axis=0, tiled=True, axis_index_groups=groups
    ).reshape(values.shape)


def gathered_place(place):
    return (place // 8 * 4 + place % 4) * 2 + place // 4 % 2


def exchange_channels(values):
    order = sorted(range(32), key=gathered_place)
    return lax.all_to_all(
        values, "wide", split_axis=0, concat_axis=0, tiled=True, axis_index_groups=[order]
    )


def other_chip(values):
    return lax.ppermute(values, "wide", [(i, i ^ 4) for i in range(32)])


def pair_up(values, partner, place):
    first = (place // 4) % 2 == 0
    return jnp.concatenate(
        [jnp.where(first, values, partner), jnp.where(first, partner, values)], axis=0
    )


def gather_pairs(both):
    groups = [[(y * 2 + x) * 4 + z for y in range(4) for z in range(4)] for x in range(2)]
    return lax.all_gather(both, "wide", axis=0, tiled=True, axis_index_groups=groups)


def exchange_sides(values):
    groups = [
        [(side * 2 + core) * 32 + place for side in range(2) for place in range(32)]
        for core in range(2)
    ]
    return lax.all_to_all(
        values, ("dp", "wide"), split_axis=0, concat_axis=0, tiled=True, axis_index_groups=groups
    )


def other_core(values):
    return lax.ppermute(values, "dp", [(0, 1), (1, 0), (2, 3), (3, 2)])


def other_side(values):
    return lax.ppermute(values, "dp", [(0, 2), (2, 0), (1, 3), (3, 1)])


def body(
    hidden, cotangent, routes, seg_lengths, gain_mix, in_x, in_z, conv_w, conv_b, x_proj, dt_proj,
    dt_bias, a_log, skip_d, out_proj, gain_moe, router, w_gate, w_up, w_down,
):
    rows, model = hidden.shape
    places = lax.axis_size("wide")
    place = lax.axis_index("wide")
    core = (lax.axis_index("dp") % 2).astype(jnp.int32).reshape(1)
    place_arr = place.astype(jnp.int32).reshape(1)
    width = in_x.shape[1]
    di = width * places
    count = a_log.shape[0]
    rank = dt_proj.shape[0]
    experts = router.shape[1]
    capacity = max(CAP * rows // (4 * places), 2)
    stride = -(-2 * capacity // 16) * 16
    half = model // 2
    steps_in = rows // SUB
    shift = SUB.bit_length() - 1
    span = 3 * width
    members = 4
    side = (place // 4 % 2).astype(jnp.int32).reshape(1)

    gate_share = call(
        pack_gate_kernel, [shape((width, model), bf16)], [], (core, in_z.T, out_proj), smem=1
    )[0]
    gate_share, x_proj = lax.optimization_barrier((gate_share, x_proj))
    pay_one = call(
        partial(pack_kernel, places=places),
        [shape((di, half + 128), bf16)],
        [],
        (core, in_x.T, x_proj, dt_proj, conv_w, conv_b, dt_bias, skip_d, a_log),
        smem=1,
    )[0]
    w_gate_two, w_up_two, w_down_two = (other_core(w[0]) for w in (w_gate, w_up, w_down))
    pay_one, hidden, cotangent, routes, seg_lengths = lax.optimization_barrier(
        (pay_one, hidden, cotangent, routes, seg_lengths)
    )
    gate_partner = other_chip(gate_share)
    pay_one, gate_partner = lax.optimization_barrier((pay_one, gate_partner))
    wm = exchange_channels(pay_one.reshape(places, width, half + 128)).reshape(di, half + 128)
    zm = gather_pairs(pair_up(gate_share, gate_partner, place))
    nrm, tail, hid, cot, route, aux = call(
        prepare_kernel,
        [
            shape((rows, model), bf16),
            shape((16, model), bf16),
            shape((rows, model), bf16),
            shape((rows, model), bf16),
            shape((rows, 1), jnp.int32),
            shape((rows, 128)),
        ],
        [],
        (place_arr * rows, seg_lengths, hidden, cotangent, routes.T, gain_mix),
        smem=2,
    )
    halo = lax.ppermute(tail, "wide", [(i, i + 1) for i in range(places - 1)])
    nrm_partner = other_chip(nrm)
    wm, halo = lax.optimization_barrier((wm, halo))
    wo = other_core(wm)
    ext, pre, steps, sig_step, small, x_in, tpre, tsuf, states, par, xd_weight, sd, q = call(
        partial(front_kernel, rank=rank, count=count),
        [
            shape((rows + (KC - 1) * SUB, di)),
            shape((rows, di)),
            shape((rows, di)),
            shape((rows, di)),
            shape((rows, 128)),
            shape((count, SUB, di)),
            shape((SUB, di)),
            shape((SUB, di)),
            shape((members * count, di + 256), bf16),
            shape((8 + count, di)),
            shape((di, 128), bf16),
            shape((rows, di)),
            shape((rows, di)),
        ],
        [
            pltpu.VMEM((steps_in * count, SUB, 128), f32),
            pltpu.VMEM((2, rows + 16, half), bf16),
            pltpu.VMEM((16, 128), f32),
        ],
        (core, nrm, halo, wm, wo, wm, wo, aux),
        smem=1,
        late=(5, 6, 3, 4),
        early=(0, 1, 2, 3, 9, 10, 11, 12),
        lanes={3: pl.ds(0, half), 4: pl.ds(0, half), 5: pl.ds(half, 128), 6: pl.ds(half, 128)},
    )

    near = exchange_near(states, members)
    zm, nrm_partner, near = lax.optimization_barrier((zm, nrm_partner, near))
    zo = other_core(zm)
    z_lanes = pl.ds(0, half)
    out_lanes = pl.ds(half, half)
    gate_z = call(
        gate_kernel,
        [shape((rows, di))],
        [pltpu.VMEM((2, rows, half), bf16)],
        (core, nrm, zm, zo),
        smem=1,
        late=(2, 3),
        lanes={2: z_lanes, 3: z_lanes},
    )[0]
    states = call(
        partial(forward_group_kernel, di=di, count=count),
        [shape((places // members * count, di + 256), bf16)],
        [pltpu.VMEM((count, di), f32)] * 2,
        (near, par),
        limit=12 * 1024 * 1024,
    )[0]
    states = exchange_far(states, members)

    nrm_pair = pair_up(nrm, nrm_partner, place)
    states, gate_z, nrm_pair = lax.optimization_barrier((states, gate_z, nrm_pair))
    normed_all = gather_pairs(nrm_pair)
    scanned, send, middle, ntwo, chances, meta, hot, entry = call(
        partial(
            middle_kernel,
            rank=rank,
            count=count,
            experts=experts,
            stride=stride,
            capacity=capacity,
            shift=shift,
        ),
        [
            shape((rows, di)),
            shape((2 * experts * stride, 2 * model // 3), bf16),
            shape((rows, model)),
            shape((rows, model), bf16),
            shape((rows, experts)),
            shape((rows, 8)),
            shape((3, 2 * rows, experts * stride), bf16),
            shape((count, di)),
        ],
        [
            pltpu.VMEM((steps_in * count, SUB, 128), f32),
            pltpu.VMEM((steps_in * count, SUB, 128), f32),
            pltpu.VMEM((count, di), f32),
        ],
        (
            core, place_arr, zm, zo, par, aux, pre, sd, q, x_in, small, states, near, tpre, hid, cot,
            route, gain_moe, router.T, gate_z,
        ),
        smem=2,
        late=(11, 12, 9, 7, 8, 6, 19, 2, 3),
        early=(7, 0, 6, 2, 3),
        lanes={2: out_lanes, 3: out_lanes},
    )
    arrived = exchange_sides(send.reshape(2 * experts, stride, -1)).reshape(send.shape)
    slots = 2 * places * capacity
    kept, sent, back = call(
        partial(expert_kernel, stride=stride, capacity=capacity),
        [shape((5 * slots, model), bf16)] * 2 + [shape(send.shape, bf16)],
        [],
        (arrived, w_gate[0], w_up[0], w_down[0], w_gate_two, w_up_two, w_down_two),
        late=(1, 2, 3, 4, 5, 6),
        early=(0, 1, 2),
        limit=44 * 1024 * 1024,
    )
    back = exchange_sides(back.reshape(2 * experts, stride, -1)).reshape(send.shape)
    given = other_core(sent)

    def both_cores(left, right):
        total = 0.0
        for part in (kept, given):
            rows_left = part[left * slots : (left + 1) * slots]
            total = total + dot_tn(rows_left, part[right * slots : (right + 1) * slots])
        return total[None]

    grad_w_down = both_cores(2, 1)
    grad_w_gate = both_cores(0, 3)
    grad_w_up = both_cores(0, 4)
    back, grad_w_down, grad_w_gate, grad_w_up = lax.optimization_barrier(
        (back, grad_w_down, grad_w_gate, grad_w_up)
    )

    combined, mixlow, mgrad, ggrad, sgrad, gain_two, y_in, adjoints = call(
        partial(back_kernel, rank=rank, count=count, experts=experts),
        [
            shape((rows, model)),
            shape((rows, model), bf16),
            shape((rows, model)),
            shape((rows, di)),
            shape((rows, di)),
            shape((1, model)),
            shape((count, SUB, di)),
            shape((members * count, di + 256 + half), bf16),
        ],
        [
            pltpu.VMEM((steps_in * count, SUB, 128), f32),
            pltpu.VMEM((2, rows, half), bf16),
            pltpu.VMEM((count, di), f32),
            pltpu.VMEM((16, 128), f32),
        ],
        (
            core, back, zm, zo, par, aux, sd, small, gate_z, hot, middle, meta, chances, route,
            cot, gain_moe, router.T, ntwo,
        ),
        smem=1,
        late=(2, 3, 8, 6),
        early=(1, 2, 0, 3, 4),
        lanes={2: out_lanes, 3: out_lanes},
    )
    near_back = exchange_near(adjoints, members)
    adjoints = call(
        partial(backward_group_kernel, di=di, count=count),
        [shape((places // members * count, di + 256 + half), bf16)],
        [pltpu.VMEM((count, di), f32)] * 2,
        (near_back, par),
        limit=12 * 1024 * 1024,
    )[0]
    adjoints = exchange_far(adjoints, members)
    out, comb, skip_part, ngrad_z = call(
        partial(aside_kernel, width=width, span=span),
        [
            shape((rows, model), bf16),
            shape((places * span, 128), bf16),
            shape((1, di)),
            shape((2, rows, half)),
        ],
        [],
        (
            core, side, zm, zo, aux, pre, gate_z, scanned, ggrad, combined, middle, meta,
        ),
        smem=2,
        late=(2, 3),
        lanes={2: z_lanes, 3: z_lanes},
    )
    adjoints, comb = lax.optimization_barrier((adjoints, comb))
    mixlow, normed_all = lax.optimization_barrier((mixlow, normed_all))
    mix_half = gather_pairs(mixlow)
    comb_got = exchange_channels(comb.reshape(places, span, 128))

    pay, ngrad, beyond = call(
        partial(tail_kernel, rank=rank, count=count, width=width),
        [shape((di, 384), bf16), shape((rows, model)), shape((SUB, model))],
        [
            pltpu.VMEM((rows, di), bf16),
            pltpu.VMEM((16, di), bf16),
            pltpu.VMEM((rows, di), f32),
            pltpu.VMEM((di, 128), bf16),
            pltpu.VMEM((8 + count, di), f32),
            pltpu.VMEM((count, half), f32),
        ]
        + [pltpu.VMEM((steps_in * count, SUB, 128), f32)] * 4
        + [pltpu.VMEM(((steps_in + 1) * count, SUB, 128), f32)]
        + [pltpu.VMEM((steps_in * count, SUB, 128), f32)]
        + [pltpu.VMEM((rows, di), f32)] * 2
        + [pltpu.VMEM((rows, di), bf16)]
        + [pltpu.VMEM((count, di), f32)] * 2,
        (
            place_arr, core, xd_weight, par, sd, q, pre, steps, sig_step, small, x_in, tpre, entry,
            y_in, tsuf, adjoints, near_back, sgrad, halo, aux, ext, wm, wo, ngrad_z, skip_part, hid,
            gain_two,
        ),
        smem=2,
        late=(15, 16, 10, 4, 5, 17, 13, 6, 8, 2, 7, 20, 21, 22, 23, 25),
        lanes={21: z_lanes, 22: z_lanes},
    )
    got_pay = exchange_channels(pay.reshape(places, width, 384))
    beyond = lax.ppermute(beyond, "wide", [(i + 1, i) for i in range(places - 1)])
    z_ready, out_ready, out_theirs = call(
        ready_kernel,
        [shape((width, model), bf16)] * 3,
        [
            pltpu.VMEM((width, places * rows), bf16),
            pltpu.VMEM((2 * width, places // 2 * rows), bf16),
        ],
        (side, comb_got, normed_all, mix_half),
        smem=1,
        late=(3,),
        limit=24 * 1024 * 1024,
    )
    out_other = other_chip(out_theirs)
    got_pay, out_other, beyond = lax.optimization_barrier((got_pay, out_other, beyond))
    first_grad = call(
        hidden_kernel, [shape((rows, model))], [], (ngrad, beyond, hid, mgrad, gain_mix), limit=12 * 1024 * 1024
    )[0]
    out_ready = (out_ready.astype(f32) + out_other.astype(f32)).astype(bf16)
    ready = jnp.concatenate([z_ready, out_ready], axis=0)
    ready = (ready.astype(f32) + other_core(ready).astype(f32)).astype(bf16)
    ready_side = other_side(ready)
    per_place = model // width
    mats = call(
        partial(grads_kernel, base=8 + count + 2 * per_place),
        [shape((2 * width, 256 + places * per_place), bf16)],
        [pltpu.VMEM((width, places * rows), bf16)],
        (got_pay, normed_all),
        limit=24 * 1024 * 1024,
    )[0]
    mats = (mats.astype(f32) + other_core(mats).astype(f32)).astype(bf16)
    grad_x, grad_z, grad_out, grad_conv, grad_bias, grad_xp, grad_dt, grad_db, grad_al, grad_sk, grad_router, gain_one, gain_two = call(
        partial(final_kernel, rank=rank, count=count, experts=experts),
        [
            shape((width, model)),
            shape((width, model)),
            shape((width, model)),
            shape((KC, width)),
            shape((width,)),
            shape((width, rank + 2 * count)),
            shape((rank, width)),
            shape((width,)),
            shape((count, width)),
            shape((width,)),
            shape((experts, model)),
            shape((model,)),
            shape((model,)),
        ],
        [pltpu.VMEM(((experts + 8) * per_place, 128), f32)] * 2,
        (mats, other_side(mats), ready, ready_side),
        limit=12 * 1024 * 1024,
    )
    return (
        out,
        first_grad,
        gain_one,
        grad_x.T,
        grad_z.T,
        grad_conv,
        grad_bias,
        grad_xp,
        grad_dt,
        grad_db,
        grad_al,
        grad_sk,
        grad_out,
        gain_two,
        grad_router.T,
        grad_w_gate,
        grad_w_up,
        grad_w_down,
    )


def solution(mesh):
    rows = P(("dp", "wide"), None)
    expert_columns = P("wide", None, "dp")
    expert_rows = P("wide", "dp", None)
    placed = (
        rows, rows, rows, P("dp", None), P(), P(None, "wide"), P(None, "wide"), P(None, "wide"),
        P("wide"), P("wide", None), P(None, "wide"), P("wide"), P(None, "wide"), P("wide"),
        P("wide", None), P(), P(), expert_columns, expert_columns, expert_rows,
    )
    given = (
        rows, rows, P(), P(None, "wide"), P(None, "wide"), P(None, "wide"), P("wide"),
        P("wide", None), P(None, "wide"), P("wide"), P(None, "wide"), P("wide"), P("wide", None),
        P(), P(), expert_columns, expert_columns, expert_rows,
    )
    return jax.shard_map(body, mesh=mesh, in_specs=placed, out_specs=given, check_vma=False)
```

```python
from functools import partial

import jax
import jax.numpy as jnp
from jax import lax
from jax.experimental import pallas as pl
from jax.experimental.pallas import tpu as pltpu
from jax.sharding import PartitionSpec as P

f32 = jnp.float32
bf16 = jnp.bfloat16
KC = 4
SUB = 8
CAP = 5
STOP = 1e6
LOG2E = 1.4426950408889634
LN2 = 0.6931471805599453
epsilon = 1e-05
VMEM_LIMIT = 56 * 1024 * 1024


def dot_nn(left, right):
    return lax.dot_general(left, right, (((1,), (0,)), ((), ())), preferred_element_type=f32)


def dot_nt(left, right):
    return lax.dot_general(left, right, (((1,), (1,)), ((), ())), preferred_element_type=f32)


def dot_tn(left, right):
    return lax.dot_general(left, right, (((0,), (0,)), ((), ())), preferred_element_type=f32)


class Moves:
    def __init__(self):
        self.arriving = {}
        self.leaving = {}
        self.started = []

    def need(self, *refs):
        for ref in refs:
            copy = self.arriving.pop(id(ref), None)
            if copy is not None:
                copy.wait()

    def done(self, *refs):
        for ref in refs:
            copy = self.leaving.pop(id(ref), None)
            if copy is not None:
                copy.start()
                self.started.append(copy)


def call(
    kernel, out_shapes, scratch, args, smem=0, late=(), early=(), lanes=None, limit=VMEM_LIMIT
):
    lanes = lanes or {}
    vmem = pl.BlockSpec(memory_space=pltpu.VMEM)
    hbm = pl.BlockSpec(memory_space=pl.ANY)
    specs = [pl.BlockSpec(memory_space=pltpu.SMEM)] * smem
    specs += [hbm if i in late else vmem for i in range(smem, len(args))]
    buffers = []
    for i in late:
        dims = (args[i].shape[0], lanes[i].size) if i in lanes else args[i].shape
        buffers.append(pltpu.VMEM(dims, args[i].dtype))
    buffers += [pltpu.VMEM(out_shapes[i].shape, out_shapes[i].dtype) for i in early]
    moving = len(buffers)
    extra = buffers + [pltpu.SemaphoreType.DMA((moving,))] if moving else []

    def staged(*refs):
        refs = list(refs)
        own = refs[len(refs) - moving - 1 : -1]
        semaphores = refs[-1]
        refs = refs[: len(refs) - moving - 1]
        moves = Moves()
        for k, i in enumerate(late):
            source = refs[i].at[:, lanes[i]] if i in lanes else refs[i]
            copy = pltpu.make_async_copy(source, own[k], semaphores.at[k])
            copy.start()
            refs[i] = own[k]
            moves.arriving[id(own[k])] = copy
        for k, i in enumerate(early, len(late)):
            at = len(args) + i
            moves.leaving[id(own[k])] = pltpu.make_async_copy(own[k], refs[at], semaphores.at[k])
            refs[at] = own[k]
        kernel(moves, *refs)
        moves.need(*own)
        moves.done(*own)
        for copy in moves.started:
            copy.wait()

    return pl.pallas_call(
        staged if moving else kernel,
        out_shape=out_shapes,
        in_specs=specs,
        out_specs=[hbm if i in early else vmem for i in range(len(out_shapes))],
        scratch_shapes=list(scratch) + extra,
        compiler_params=pltpu.CompilerParams(vmem_limit_bytes=limit),
    )(*args)


def shape(dims, dtype=f32):
    return jax.ShapeDtypeStruct(dims, dtype)


def group_of(di):
    return 256 if di % 256 == 0 else 128


def sublane_iota(width):
    return lax.broadcasted_iota(jnp.int32, (SUB, width), 0)


def from_before(block, first):
    row = sublane_iota(block.shape[1])
    return jnp.where(row == 0, jnp.broadcast_to(first, block.shape), pltpu.roll(block, 1, 0))


def from_after(block, last):
    row = sublane_iota(block.shape[1])
    return jnp.where(
        row == SUB - 1, jnp.broadcast_to(last, block.shape), pltpu.roll(block, SUB - 1, 0)
    )


def spread_columns(small, first, count, out):
    steps = small.shape[0] // SUB
    for j in range(steps):
        block = small[j * SUB : (j + 1) * SUB, :]
        for n in range(count):
            out[j * count + n] = jnp.broadcast_to(block[:, first + n : first + n + 1], (SUB, 128))


def prefix_states(decay, state):
    row = sublane_iota(state.shape[1])
    for shift in (1, 2, 4):
        inside = row >= shift
        state = state + decay * jnp.where(inside, pltpu.roll(state, shift, 0), 0.0)
        decay = decay * jnp.where(inside, pltpu.roll(decay, shift, 0), 1.0)
    return state


def suffix_states(decay, state):
    row = sublane_iota(state.shape[1])
    for shift in (1, 2, 4):
        inside = row < SUB - shift
        state = state + decay * jnp.where(inside, pltpu.roll(state, SUB - shift, 0), 0.0)
        decay = decay * jnp.where(inside, pltpu.roll(decay, SUB - shift, 0), 1.0)
    return state


def prefix_sum(values):
    row = sublane_iota(values.shape[1])
    for shift in (1, 2, 4):
        values = values + jnp.where(row >= shift, pltpu.roll(values, shift, 0), 0.0)
    return values


def suffix_sum(values):
    row = sublane_iota(values.shape[1])
    for shift in (1, 2, 4):
        values = values + jnp.where(row < SUB - shift, pltpu.roll(values, SUB - shift, 0), 0.0)
    return values


def one_hot(dims, offset):
    row = lax.broadcasted_iota(jnp.int32, dims, 0)
    column = lax.broadcasted_iota(jnp.int32, dims, 1)
    return (row + offset == column).astype(bf16)


def pack_gate_kernel(core, in_z, out_proj, gate_o):
    half = in_z.shape[1] // 2
    start = pl.multiple_of(core[0] * half, 128)
    gate_o[:, :half] = in_z[:, pl.ds(start, half)]
    gate_o[:, half:] = out_proj[:, pl.ds(start, half)]


def pack_kernel(
    core, in_x, x_proj, dt_proj, conv_w, conv_b, dt_bias, skip_d, a_log, out, *, places
):
    width, model = in_x.shape
    half = model // 2
    here = core[0]
    mine = in_x[:, pl.ds(pl.multiple_of(here * half, 128), half)]
    narrow = x_proj.shape[1]
    steps = dot_nn(x_proj[...], one_hot((narrow, 128), 0)) + dot_tn(
        dt_proj[...], one_hot((dt_proj.shape[0], 128), 128 - dt_proj.shape[0])
    )
    values = jnp.concatenate(
        [
            conv_w[...],
            conv_b[...].reshape(1, width),
            dt_bias[...].reshape(1, width),
            skip_d[...].reshape(1, width),
            jnp.zeros((1, width), f32),
            a_log[...],
        ],
        axis=0,
    )
    top = values.astype(bf16)
    left = values - top.astype(f32)
    mid = left.astype(bf16)
    low = (left - mid.astype(f32)).astype(bf16)
    count = values.shape[0]
    extra = dot_tn(top, one_hot((count, 128), 0))
    extra = extra + dot_tn(mid, one_hot((count, 128), count))
    extra = extra + dot_tn(low, one_hot((count, 128), 2 * count))
    rest = jnp.where(here == 0, steps, extra).astype(bf16)
    for place in range(places):
        out[place * width : (place + 1) * width, :half] = mine
        out[place * width : (place + 1) * width, half:] = rest


def prepare_kernel(
    base, lengths, hidden, cot, route, gain, nrm_o, tail_o, hid_o, cot_o, route_o, aux_o
):
    rows = hidden.shape[0]
    steps_in = rows // SUB
    row = lax.broadcasted_iota(jnp.int32, (rows, rows), 0)
    column = lax.broadcasted_iota(jnp.int32, (rows, rows), 1)
    in_order = (row % SUB) * steps_in + row // SUB == column
    order = in_order.astype(bf16)
    hid = dot_nn(order, hidden[...])
    hid_o[...] = hid.astype(bf16)
    cot_o[...] = dot_nn(order, cot[...]).astype(bf16)
    ours = jnp.where(in_order, jnp.broadcast_to(route[...], (rows, rows)), 0)
    route_o[...] = jnp.sum(ours, axis=1, keepdims=True)
    scale = lax.rsqrt(jnp.mean(hid * hid, axis=1, keepdims=True) + epsilon)
    normed = (hid * scale * gain[...].reshape(1, -1)).astype(bf16)
    nrm_o[...] = normed
    tail_row = lax.broadcasted_iota(jnp.int32, (16, rows), 0)
    tail_column = lax.broadcasted_iota(jnp.int32, (16, rows), 1)
    picked = (tail_column == rows - 1 - (KC - 2 - tail_row) * SUB) & (tail_row < KC - 1)
    tail = dot_nn(picked.astype(bf16), normed)
    tail_row = tail_row - SUB
    picked = (tail_column == rows - 1 - (KC - 2 - tail_row) * SUB) & (tail_row < KC - 1)
    picked = picked & (tail_row >= 0)
    tail_o[...] = (tail + dot_nn(picked.astype(bf16), hid.astype(bf16))).astype(bf16)

    def layout(position, lane):
        back = position - (lane + 1)
        segment = jnp.zeros_like(position)
        segment_back = jnp.zeros_like(position)
        reset = position == 0
        end = jnp.int32(0)
        for j in range(lengths.shape[1] - 1):
            end = end + lengths[0, j]
            segment = segment + (position >= end).astype(jnp.int32)
            segment_back = segment_back + (back >= end).astype(jnp.int32)
            reset = reset | (position == end)
        same = (back >= 0) & (segment == segment_back)
        live = position < end
        picked = jnp.where(lane == KC - 1, live.astype(f32), reset.astype(f32))
        return jnp.where(lane < KC - 1, same.astype(f32), picked)

    at = lax.broadcasted_iota(jnp.int32, (rows, 128), 0)
    lane = lax.broadcasted_iota(jnp.int32, (rows, 128), 1)
    aux_o[...] = layout(base[0] + (at % SUB) * steps_in + at // SUB, lane)


def front_kernel(
    moves, core, nrm_in, halo_in, wm, wo, rest_m, rest_o, aux, ext_o, pre_o, steps_o, sig_o, small_o, x_o, tpre_o, tsuf_o,
    state_o, par_o, xd_o, sd_s, q_s, bw_s, nrm_s, sum_s, *, rank, count
):
    rows, di = pre_o.shape
    half = wo.shape[1]
    steps_in = rows // SUB
    gs = group_of(di)
    low = core[0] == 0
    nrm_s[0, :rows] = jnp.where(low, nrm_in[:, :half], nrm_in[:, half:])
    nrm_s[1, :rows] = jnp.where(low, nrm_in[:, half:], nrm_in[:, :half])
    nrm_s[0, rows:] = jnp.where(low, halo_in[:, :half], halo_in[:, half:])
    nrm_s[1, rows:] = jnp.where(low, halo_in[:, half:], halo_in[:, :half])
    small_o[...] = jnp.zeros_like(small_o)
    moves.need(rest_m, rest_o)
    par = par_o
    total_rows = par_o.shape[0]

    def unpack(g, _):
        lanes = pl.ds(pl.multiple_of(g * 128, 128), 128)
        mine = rest_m[lanes, :]
        other = rest_o[lanes, :]
        xd_o[lanes, :] = jnp.where(low, mine, other)
        turned = jnp.where(low, other, mine).astype(f32).T
        par_o[:, lanes] = (
            turned[:total_rows, :]
            + turned[total_rows : 2 * total_rows, :]
            + turned[2 * total_rows : 3 * total_rows, :]
        )
        return 0

    lax.fori_loop(0, di // 128, unpack, 0)
    moves.need(wm, wo)

    def project(g, _):
        lanes = pl.ds(pl.multiple_of(g * gs, gs), gs)
        inner = dot_nt(nrm_s[0], wm[lanes, :half]) + dot_nt(nrm_s[1], wo[lanes, :half])
        for back in range(1, KC):
            block = inner[rows - back * SUB : rows - (back - 1) * SUB, :]
            halo = inner[rows + KC - 1 - back : rows + KC - back, :]
            ext_o[(KC - 1 - back) * SUB : (KC - back) * SUB, lanes] = from_before(block, halo)
        ext_o[(KC - 1) * SUB :, lanes] = inner[:rows, :]
        total = par[KC : KC + 1, lanes] + par[KC - 1 : KC, lanes] * inner[:rows, :]
        for back in range(1, KC):
            shifted = ext_o[(KC - 1 - back) * SUB : (KC - 1 - back) * SUB + rows, lanes]
            total = total + par[KC - 1 - back : KC - back, lanes] * shifted * aux[:, back - 1 : back]
        pre_o[:, lanes] = total
        act = total * jax.nn.sigmoid(total)
        q_s[:, lanes] = act
        small_o[...] += dot_nn(act.astype(bf16), xd_o[lanes, :])
        return 0

    lax.fori_loop(0, di // gs, project, 0)
    moves.done(ext_o, pre_o, par_o, xd_o)
    small = small_o[...]
    lane = lax.broadcasted_iota(jnp.int32, small.shape, 1)
    step_low = jnp.where(lane >= 128 - rank, pltpu.roll(small, 128 - rank, 1), 0.0).astype(bf16)
    spread_columns(small, rank, count, bw_s)

    def stepping(g, _):
        lanes = pl.ds(pl.multiple_of(g * gs, gs), gs)
        step_pre = dot_nt(step_low, xd_o[lanes, :]) + par[KC + 1 : KC + 2, lanes]
        small_exp = jnp.exp(-jnp.abs(step_pre))
        steps = jnp.maximum(step_pre, 0.0) + jnp.log1p(small_exp)
        steps_o[:, lanes] = steps
        sig_o[:, lanes] = jax.nn.sigmoid(step_pre)
        q_s[:, lanes] = q_s[:, lanes] * steps
        sd_s[:, lanes] = jnp.where(aux[:, 4:5] > 0.5, STOP, steps)
        return 0

    lax.fori_loop(0, di // gs, stepping, 0)
    moves.done(steps_o, sig_o, sd_s, q_s)

    def chunk(g, _):
        lanes = pl.ds(pl.multiple_of(g * 128, 128), 128)
        rates = [
            jnp.broadcast_to(-LOG2E * jnp.exp(par[8 + n : 9 + n, lanes]), (SUB, 128))
            for n in range(count)
        ]

        def step(j, carry):
            states, total = carry
            at = pl.ds(pl.multiple_of(j * SUB, SUB), SUB)
            sd = sd_s[at, lanes]
            q = q_s[at, lanes]
            states = tuple(
                jnp.exp2(sd * rates[n]) * states[n] + q * bw_s[j * count + n] for n in range(count)
            )
            return (states, total + sd)

        zero = jnp.zeros((SUB, 128), f32)
        states, total = lax.fori_loop(0, steps_in, step, ((zero,) * count, zero), unroll=16)
        row = sublane_iota(128)
        ahead = prefix_sum(total)
        behind = suffix_sum(total)
        tpre_o[:, lanes] = jnp.where(row == 0, 0.0, pltpu.roll(ahead, 1, 0))
        tsuf_o[:, lanes] = jnp.where(row == SUB - 1, 0.0, pltpu.roll(behind, SUB - 1, 0))
        last = []
        for n in range(count):
            joined = prefix_states(jnp.exp2(rates[n] * total), states[n])
            x_o[n, :, lanes] = jnp.where(row == 0, 0.0, pltpu.roll(joined, 1, 0))
            last.append(joined[SUB - 1 : SUB, :])
        sum_s[pl.ds(g, 1), :] = ahead[SUB - 1 : SUB, :]
        to_copies(state_o, jnp.concatenate(last, axis=0).astype(bf16), lanes)
        return 0

    sum_s[...] = jnp.zeros_like(sum_s)
    lax.fori_loop(0, di // 128, chunk, 0)
    sums = sum_s[...]
    top = sums.astype(bf16)
    left = (sums - top.astype(f32)).astype(bf16)
    to_copies(state_o, top, slice(di, di + 128))
    to_copies(state_o, left, slice(di + 128, di + 256))


def to_copies(out, values, lanes):
    count = values.shape[0]
    for place in range(out.shape[0] // count):
        out[place * count : (place + 1) * count, lanes] = values


def negative_rates(par, out):
    out[...] = -LOG2E * jnp.exp(par[8:, :])


def group_kernel(arrived, out, state_s, sum_s, *, di, count, reverse):
    members = arrived.shape[0] // count
    rest = arrived.shape[1] - di - 256
    copies = out.shape[0] // count
    state_s[...] = jnp.zeros_like(state_s)
    total = jnp.zeros((count, 128), f32)
    for place in range(members - 1, -1, -1) if reverse else range(members):
        block = slice(place * count, (place + 1) * count)
        sums = arrived[block, di : di + 128].astype(f32)
        sums = sums + arrived[block, di + 128 : di + 256].astype(f32)
        total = total + sums
        carry_step(sums, arrived[block, :di], sum_s, state_s)
    joined = state_s[...].astype(bf16)
    top = total.astype(bf16)
    left = (total - top.astype(f32)).astype(bf16)
    for copy in range(copies):
        block = slice(copy * count, (copy + 1) * count)
        out[block, :di] = joined
        out[block, di : di + 128] = top
        out[block, di + 128 : di + 256] = left
    if rest:
        extra = jnp.zeros((count, rest), f32)
        for place in range(members):
            extra = extra + arrived[place * count : (place + 1) * count, di + 256 :].astype(f32)
        gap = jnp.zeros((count - 2, rest), f32)
        for copy in range(copies):
            rows = jnp.concatenate([extra[2 * copy : 2 * copy + 2, :], gap], axis=0)
            out[copy * count : (copy + 1) * count, di + 256 :] = rows.astype(bf16)


def forward_group_kernel(arrived, par, out, state_s, rate_s, *, di, count):
    negative_rates(par, rate_s)
    group_kernel(arrived, out, state_s, rate_s, di=di, count=count, reverse=False)


def backward_group_kernel(arrived, par, out, state_s, rate_s, *, di, count):
    negative_rates(par, rate_s)
    group_kernel(arrived, out, state_s, rate_s, di=di, count=count, reverse=True)


def step_sums(arrived, block, di):
    return arrived[block, di : di + 128].astype(f32) + arrived[block, di + 128 : di + 256].astype(
        f32
    )


def carry_step(decay_sums, arrived, rate_s, state_s):
    for g in range(state_s.shape[1] // 128):
        lanes = slice(g * 128, (g + 1) * 128)
        decay = jnp.exp2(rate_s[:, lanes] * decay_sums[g : g + 1, :])
        state_s[:, lanes] = decay * state_s[:, lanes] + arrived[:, lanes].astype(f32)


def gate_kernel(moves, core, nrm, zm, zo, gate_z_o, nrm_s):
    rows, di = gate_z_o.shape
    half = zm.shape[1]
    gs = group_of(di)
    low = core[0] == 0
    nrm_s[0] = jnp.where(low, nrm[:, :half], nrm[:, half:])
    nrm_s[1] = jnp.where(low, nrm[:, half:], nrm[:, :half])
    moves.need(zm, zo)

    def project(g, _):
        lanes = pl.ds(pl.multiple_of(g * gs, gs), gs)
        gate_z_o[:, lanes] = dot_nt(nrm_s[0], zm[lanes, :]) + dot_nt(nrm_s[1], zo[lanes, :])
        return 0

    lax.fori_loop(0, di // gs, project, 0)


def middle_kernel(
    moves, core, place, om, oo, par, aux, pre, sd, q, x_in, small, arrived, near, tpre, hid, cot,
    route, gain, router, gate_z, scan_o, send_o, middle_o, ntwo_o, chance_o, meta_o, hot_o,
    entry_o, bw_s, cw_s, rate_s, *, rank, count, experts, stride, capacity, shift
):
    rows, di = pre.shape
    half = om.shape[1]
    steps_in = rows // SUB
    gs = group_of(di)
    low = core[0] == 0
    spread_columns(small[...], rank, count, bw_s)
    spread_columns(small[...], rank + count, count, cw_s)
    negative_rates(par, rate_s)
    moves.need(arrived, near)
    entry_o[...] = jnp.zeros_like(entry_o)
    members = near.shape[0] // count

    def before_here(there, _):
        block = pl.ds(pl.multiple_of(there * count, count), count)
        carry_step(step_sums(arrived, block, di), arrived[block, :di], rate_s, entry_o)
        return 0

    def just_before(there, _):
        block = pl.ds(pl.multiple_of(there * count, count), count)
        carry_step(step_sums(near, block, di), near[block, :di], rate_s, entry_o)
        return 0

    lax.fori_loop(0, place[0] // members, before_here, 0)
    lax.fori_loop(0, place[0] % members, just_before, 0)
    moves.done(entry_o)
    moves.need(x_in, sd, q)

    def scan(g, _):
        lanes = pl.ds(pl.multiple_of(g * 128, 128), 128)
        rates = [jnp.broadcast_to(rate_s[n : n + 1, lanes], (SUB, 128)) for n in range(count)]
        before = tpre[:, lanes]
        first = tuple(
            x_in[n, :, lanes] + jnp.exp2(rates[n] * before) * entry_o[n : n + 1, lanes]
            for n in range(count)
        )
        def step(j, states):
            at = pl.ds(pl.multiple_of(j * SUB, SUB), SUB)
            sd_here = sd[at, lanes]
            q_here = q[at, lanes]
            total = jnp.zeros((SUB, 128), f32)
            fresh = []
            for n in range(count):
                state = jnp.exp2(sd_here * rates[n]) * states[n] + q_here * bw_s[j * count + n]
                total = total + state * cw_s[j * count + n]
                fresh.append(state)
            scan_o[at, lanes] = total
            return tuple(fresh)

        lax.fori_loop(0, steps_in, step, first, unroll=16)
        return 0

    lax.fori_loop(0, di // 128, scan, 0)

    def gating(g, carry):
        mine, other = carry
        lanes = pl.ds(pl.multiple_of(g * gs, gs), gs)
        z = gate_z[:, lanes]
        pre_here = pre[:, lanes]
        scanned = scan_o[:, lanes] + par[KC + 2 : KC + 3, lanes] * (
            pre_here * jax.nn.sigmoid(pre_here)
        )
        scan_o[:, lanes] = scanned
        gated = (scanned * (z * jax.nn.sigmoid(z)) * aux[:, 3:4]).astype(bf16)
        return (mine + dot_nn(gated, om[lanes, :]), other + dot_nn(gated, oo[lanes, :]))

    zero = jnp.zeros((rows, half), f32)
    moves.need(pre, gate_z, om, oo)
    mine, other = lax.fori_loop(0, di // gs, gating, (zero, zero))
    moves.done(scan_o)
    mixed = jnp.concatenate([jnp.where(low, mine, other), jnp.where(low, other, mine)], axis=1)
    middle = hid[...].astype(f32) + mixed
    middle_o[...] = middle
    scale = lax.rsqrt(jnp.mean(middle * middle, axis=1, keepdims=True) + epsilon)
    ntwo = (middle * scale * gain[...].reshape(1, -1)).astype(bf16)
    ntwo_o[...] = ntwo
    logits = dot_nt(ntwo, router[...])
    top = jnp.max(logits, axis=1, keepdims=True)
    raised = jnp.exp(logits - top)
    chances = raised / jnp.sum(raised, axis=1, keepdims=True)
    chance_o[...] = chances
    lane = lax.broadcasted_iota(jnp.int32, (rows, experts), 1)
    chosen = route[...] == lane
    chosen_f = chosen.astype(f32)
    gate = jnp.sum(chances * chosen_f, axis=1, keepdims=True)
    taken = chosen_f * aux[:, 3:4]
    here = lax.broadcasted_iota(jnp.int32, (rows, rows), 0)
    there = lax.broadcasted_iota(jnp.int32, (rows, rows), 1)
    own_id = (here & (SUB - 1)) * steps_in + (here >> shift)
    other_id = (there & (SUB - 1)) * steps_in + (there >> shift)
    earlier = (other_id < own_id).astype(bf16)
    ranks = jnp.sum(dot_nn(earlier, taken.astype(bf16)) * chosen_f, axis=1, keepdims=True)
    kept = aux[:, 3:4] * (ranks < capacity).astype(f32)
    weight = gate * kept
    up = (cot[...].astype(f32) * weight).astype(bf16)
    values = jnp.concatenate([ntwo, up], axis=0)
    rank_low = ranks.astype(jnp.int32)
    slot = jnp.concatenate([rank_low, rank_low + capacity], axis=0)
    block = route[...] * stride
    block = jnp.concatenate([block, block], axis=0)
    kept_on = jnp.concatenate([kept, kept], axis=0) > 0.5
    place = lax.broadcasted_iota(jnp.int32, (2 * rows, experts * stride), 1)
    wide_hot = ((block + slot == place) & kept_on).astype(bf16)
    at_last = (block + 2 * capacity + slot // 2 == place) & kept_on
    even_hot = (at_last & (slot % 2 == 0)).astype(bf16)
    odd_hot = (at_last & (slot % 2 == 1)).astype(bf16)
    hot_o[0] = wide_hot
    hot_o[1] = even_hot
    hot_o[2] = odd_hot
    moves.done(hot_o, middle_o, ntwo_o)
    third = ntwo.shape[1] // 3
    narrow = values[:, 2 * third :]
    last = jnp.concatenate([dot_tn(even_hot, narrow), dot_tn(odd_hot, narrow)], axis=1)
    packed = (dot_tn(wide_hot, values[:, : 2 * third]) + last).astype(bf16)
    send_o[: experts * stride, :] = packed
    send_o[experts * stride :, :] = packed
    lane8 = lax.broadcasted_iota(jnp.int32, (rows, 8), 1)
    meta_o[...] = jnp.where(
        lane8 == 0, gate, jnp.where(lane8 == 1, kept, jnp.where(lane8 == 2, scale, 0.0))
    )


def back_kernel(
    moves, core, back, om, oo, par, aux, sd, small, gate_z, hot, middle, meta, chances, route, cot, gain,
    router, ntwo, combined_o, mixlow_o, mgrad_o, ggrad_o, sg_o, gain_o, y_o, state_o, cw_s, mix_s,
    rate_s, sum_s, *, rank, count, experts
):
    rows, di = sd.shape
    half = om.shape[1]
    steps_in = rows // SUB
    gs = group_of(di)
    negative_rates(par, rate_s)
    slots = back.shape[0] // 2
    third = back.shape[1] // 2
    rows_back = (back[:slots, :].astype(f32) + back[slots:, :].astype(f32)).astype(bf16)
    last = dot_nn(hot[1], rows_back[:, :third]) + dot_nn(hot[2], rows_back[:, third:])
    both = jnp.concatenate([dot_nn(hot[0], rows_back), last], axis=1)
    combined = both[:rows, :]
    dispatch = both[rows:, :]
    combined_o[...] = combined
    gate = meta[:, 0:1]
    kept = meta[:, 1:2]
    scale = meta[:, 2:3]
    mid = middle[...]
    up = cot[...].astype(f32)
    gate_total = kept * jnp.sum(up * combined, axis=1, keepdims=True)
    lane = lax.broadcasted_iota(jnp.int32, (rows, experts), 1)
    chosen_f = (route[...] == lane).astype(f32)
    logit_grad = (gate * (chosen_f - chances[...]) * gate_total).astype(bf16)
    router_rows = dot_tn(logit_grad, ntwo[...])
    members = state_o.shape[0] // count
    for member in range(members):
        rows_here = []
        for group in range(experts // members):
            row = router_rows[group * members + member : group * members + member + 1, :]
            rows_here += [row[:, :half], row[:, half:]]
        block = slice(member * count, (member + 1) * count)
        state_o[block, di + 256 :] = jnp.concatenate(rows_here, axis=0).astype(bf16)
    ngrad = dot_nn(logit_grad, router[...]) + dispatch
    gain_o[...] = jnp.sum(ngrad * mid * scale, axis=0, keepdims=True)
    scaled = gain[...].reshape(1, -1) * ngrad
    cube = scale * scale * scale
    mgrad = up + scale * scaled - mid * cube * jnp.mean(mid * scaled, axis=1, keepdims=True)
    mgrad_o[...] = mgrad
    low = core[0] == 0
    mixlow = mgrad.astype(bf16)
    mixlow_o[...] = mixlow
    mix_s[0] = jnp.where(low, mixlow[:, :half], mixlow[:, half:])
    mix_s[1] = jnp.where(low, mixlow[:, half:], mixlow[:, :half])
    moves.done(mixlow_o, mgrad_o, combined_o)
    moves.need(om, oo, gate_z)

    def gating(g, _):
        lanes = pl.ds(pl.multiple_of(g * gs, gs), gs)
        ggrad = dot_nt(mix_s[0], om[lanes, :]) + dot_nt(mix_s[1], oo[lanes, :])
        ggrad = ggrad * aux[:, 3:4]
        ggrad_o[:, lanes] = ggrad
        z = gate_z[:, lanes]
        sg_o[:, lanes] = ggrad * (z * jax.nn.sigmoid(z))
        return 0

    lax.fori_loop(0, di // gs, gating, 0)
    moves.done(ggrad_o, sg_o)
    spread_columns(small[...], rank + count, count, cw_s)
    moves.need(sd)

    def chunk(g, _):
        lanes = pl.ds(pl.multiple_of(g * 128, 128), 128)
        rates = [jnp.broadcast_to(rate_s[n : n + 1, lanes], (SUB, 128)) for n in range(count)]

        def step(i, carry):
            grads, total = carry
            j = steps_in - 1 - i
            at = pl.ds(pl.multiple_of(j * SUB, SUB), SUB)
            sd_here = sd[at, lanes]
            sgrad = sg_o[at, lanes]
            grads = tuple(
                jnp.exp2(sd_here * rates[n]) * (grads[n] + sgrad * cw_s[j * count + n])
                for n in range(count)
            )
            return (grads, total + sd_here)

        zero = jnp.zeros((SUB, 128), f32)
        grads, total = lax.fori_loop(0, steps_in, step, ((zero,) * count, zero), unroll=16)
        row = sublane_iota(128)
        last = []
        for n in range(count):
            joined = suffix_states(jnp.exp2(rates[n] * total), grads[n])
            y_o[n, :, lanes] = jnp.where(row == SUB - 1, 0.0, pltpu.roll(joined, SUB - 1, 0))
            last.append(joined[0:1, :])
        sum_s[pl.ds(g, 1), :] = jnp.sum(total, axis=0, keepdims=True)
        to_copies(state_o, jnp.concatenate(last, axis=0).astype(bf16), lanes)
        return 0

    sum_s[...] = jnp.zeros_like(sum_s)
    lax.fori_loop(0, di // 128, chunk, 0)
    total = sum_s[...]
    top = total.astype(bf16)
    to_copies(state_o, top, slice(di, di + 128))
    to_copies(state_o, (total - top.astype(f32)).astype(bf16), slice(di + 128, di + 256))


def slot_rows(stride, capacity, blocks):
    dims = (2 * capacity * blocks, stride * blocks)
    row = lax.broadcasted_iota(jnp.int32, dims, 0)
    column = lax.broadcasted_iota(jnp.int32, dims, 1)
    half = capacity * blocks
    slot = row % capacity + row // half * capacity
    start = row % half // capacity * stride
    wide = (start + slot == column).astype(bf16)
    at_last = start + 2 * capacity + slot // 2 == column
    even = (at_last & (slot % 2 == 0)).astype(bf16)
    odd = (at_last & (slot % 2 == 1)).astype(bf16)
    return wide, even, odd


def unpack(packed, hots):
    wide, even, odd = hots
    third = packed.shape[1] // 2
    last = dot_nn(even, packed[:, :third]) + dot_nn(odd, packed[:, third:])
    return jnp.concatenate([dot_nn(wide, packed), last], axis=1).astype(bf16)


def pack(rows, hots):
    wide, even, odd = hots
    third = rows.shape[1] // 3
    narrow = rows[:, 2 * third :]
    last = jnp.concatenate([dot_tn(even, narrow), dot_tn(odd, narrow)], axis=1)
    return dot_tn(wide, rows[:, : 2 * third]) + last


def expert_kernel(
    moves, arrived, w_gate, w_up, w_down, w_gate_two, w_up_two, w_down_two, kept_o, sent_o, back_o,
    *, stride, capacity
):
    blocks = 16
    hots = slot_rows(stride, capacity, blocks)
    size = capacity * blocks
    groups = arrived.shape[0] // (stride * blocks)
    slots = kept_o.shape[0] // 5
    for group in range(groups):
        rows = unpack(arrived[group * stride * blocks : (group + 1) * stride * blocks, :], hots)
        at = group * size
        kept_o[at : at + size, :] = rows[:size, :]
        kept_o[slots + at : slots + at + size, :] = rows[size:, :]
    sent_o[: 2 * slots, :] = kept_o[: 2 * slots, :]
    inputs = kept_o[:slots, :]
    grads = kept_o[slots : 2 * slots, :]
    outputs = 0.0
    total = 0.0
    weights = ((sent_o, w_gate_two, w_up_two, w_down_two), (kept_o, w_gate, w_up, w_down))
    for out, gate_weight, up_weight, down_weight in weights[::-1]:
        moves.need(gate_weight)
        gate_in = dot_nn(inputs, gate_weight[...])
        moves.need(up_weight)
        up_in = dot_nn(inputs, up_weight[...])
        sig = jax.nn.sigmoid(gate_in)
        silu = gate_in * sig
        act = (silu * up_in).astype(bf16)
        out[2 * slots : 3 * slots, :] = act
        moves.need(down_weight)
        outputs = outputs + dot_nn(act, down_weight[...])
        act_grad = dot_nt(grads, down_weight[...])
        gate_grad = (act_grad * up_in * sig * (1.0 + gate_in * (1.0 - sig))).astype(bf16)
        up_grad = (act_grad * silu).astype(bf16)
        out[3 * slots : 4 * slots, :] = gate_grad
        out[4 * slots :, :] = up_grad
        moves.done(out)
        total = total + dot_nt(gate_grad, gate_weight[...]) + dot_nt(up_grad, up_weight[...])
    for group in range(groups):
        at = group * size
        rows = jnp.concatenate([outputs[at : at + size, :], total[at : at + size, :]], axis=0)
        packed = pack(rows.astype(bf16), hots).astype(bf16)
        back_o[group * stride * blocks : (group + 1) * stride * blocks, :] = packed


def aside_kernel(
    moves, core, side, zm, zo, aux, pre, gate_z, scanned, ggrad, combined, middle, meta,
    out_o, comb_o, skip_o, ngrad_o, *, width, span
):
    rows, di = pre.shape
    half = zm.shape[1]
    gs = group_of(di)
    pieces = width // 16
    result = (middle[...] + meta[:, 0:1] * meta[:, 1:2] * combined[...]).astype(bf16)
    out_o[...] = dot_tn(token_order(rows), result).astype(bf16)
    def gating(g, carry):
        mine, other = carry
        lanes = pl.ds(pl.multiple_of(g * gs, gs), gs)
        grad = ggrad[:, lanes]
        z = gate_z[:, lanes]
        sig = jax.nn.sigmoid(z)
        here = scanned[:, lanes]
        zgrad = grad * here * sig * (1.0 + z * (1.0 - sig))
        z_low = zgrad.astype(bf16)
        z_turned = zgrad.T.astype(bf16)
        gated_turned = (here * (z * sig) * aux[:, 3:4]).T.astype(bf16)
        for i in range(gs // 16):
            piece = g * (gs // 16) + i
            to = pl.multiple_of(piece // pieces * span + piece % pieces * 16, 16)
            comb_o[pl.ds(to, 16), :] = z_turned[i * 16 : (i + 1) * 16, :]
            owner = piece // pieces
            holder = owner // 2 * 2 + side[0]
            to = holder * span + (1 + owner % 2) * width + piece % pieces * 16
            comb_o[pl.ds(pl.multiple_of(to, 16), 16), :] = gated_turned[i * 16 : (i + 1) * 16, :]
        pre_here = pre[:, lanes]
        act = pre_here * jax.nn.sigmoid(pre_here)
        skip_o[:, lanes] = jnp.sum(grad * (z * sig) * act, axis=0, keepdims=True)
        return (mine + dot_nn(z_low, zm[lanes, :]), other + dot_nn(z_low, zo[lanes, :]))

    moves.need(zm, zo)
    zero = jnp.zeros((rows, half), f32)
    mine, other = lax.fori_loop(0, di // gs, gating, (zero, zero))
    ngrad_o[0] = mine
    ngrad_o[1] = other


def scan_kernel(
    moves, place, xd, par, sd, q, pre, steps, sig_step, small, x_in, tpre, entry, y_in, tsuf, arrived, near,
    sgrad, cgrad_o, xd_o, spar_o, router_o, bw_s, cw_s, bacc_s, cacc_s, st_s, dk_s, sgr_s, asc_s, plow_s,
    rate_s, after_s, *, rank, count
):
    rows, di = pre.shape
    negative_rates(par, rate_s)
    after_s[...] = jnp.zeros_like(after_s)
    groups = arrived.shape[0] // count
    members = near.shape[0] // count
    spread_columns(small[...], rank, count, bw_s)
    spread_columns(small[...], rank + count, count, cw_s)
    bacc_s[...] = jnp.zeros_like(bacc_s)
    cacc_s[...] = jnp.zeros_like(cacc_s)
    spar_o[...] = jnp.zeros_like(spar_o)
    moves.need(arrived, near)

    def after_here(i, _):
        block = pl.ds(pl.multiple_of((groups - 1 - i) * count, count), count)
        carry_step(step_sums(arrived, block, di), arrived[block, :di], rate_s, after_s)
        return 0

    def just_after(i, _):
        block = pl.ds(pl.multiple_of((members - 1 - i) * count, count), count)
        carry_step(step_sums(near, block, di), near[block, :di], rate_s, after_s)
        return 0

    lax.fori_loop(0, groups - 1 - place[0] // members, after_here, 0)
    lax.fori_loop(0, members - 1 - place[0] % members, just_after, 0)
    router_sum = jnp.zeros(router_o.shape, f32)
    for there in range(groups):
        router_sum += arrived[there * count : (there + 1) * count, di + 256 :].astype(f32)
    router_o[...] = router_sum
    steps_in = rows // SUB
    gs = group_of(di)
    moves.need(x_in, sd, q, sgrad, y_in)

    def scan(g, _):
        lanes = pl.ds(pl.multiple_of(g * 128, 128), 128)
        rates = [
            jnp.broadcast_to(rate_s[n : n + 1, lanes], (SUB, 128)) for n in range(count)
        ]
        before = tpre[:, lanes]
        behind = tsuf[:, lanes]
        first = tuple(
            x_in[n, :, lanes] + jnp.exp2(rates[n] * before) * entry[n : n + 1, lanes]
            for n in range(count)
        )

        def forward(j, states):
            at = pl.ds(pl.multiple_of(j * SUB, SUB), SUB)
            sd_here = sd[at, lanes]
            q_here = q[at, lanes]
            fresh = []
            for n in range(count):
                decay = jnp.exp2(sd_here * rates[n])
                dk_s[j * count + n] = decay
                st_s[j * count + n] = states[n]
                fresh.append(decay * states[n] + q_here * bw_s[j * count + n])
            return tuple(fresh)

        last = lax.fori_loop(0, steps_in, forward, first, unroll=16)
        for n in range(count):
            st_s[steps_in * count + n] = last[n]
        zero = jnp.zeros((SUB, 128), f32)
        arriving = tuple(
            y_in[n, :, lanes] + jnp.exp2(rates[n] * behind) * after_s[n : n + 1, lanes]
            for n in range(count)
        )

        def backward(i, carry):
            grads, rate_grads = carry
            j = steps_in - 1 - i
            at = pl.ds(pl.multiple_of(j * SUB, SUB), SUB)
            sd_here = sd[at, lanes]
            q_here = q[at, lanes]
            sg = sgrad[at, lanes]
            onto = zero
            along = zero
            fresh = []
            fresh_rates = []
            for n in range(count):
                k = j * count + n
                lam = grads[n] + sg * cw_s[k]
                cacc_s[k] += sg * st_s[k + count]
                bacc_s[k] += lam * q_here
                onto = onto + lam * bw_s[k]
                carried = lam * dk_s[k]
                logs = carried * st_s[k]
                along = along + logs * rates[n]
                fresh.append(carried)
                fresh_rates.append(rate_grads[n] + logs * sd_here)
            sgr_s[at, lanes] = along
            asc_s[at, lanes] = onto
            return (tuple(fresh), tuple(fresh_rates))

        _, rate_grads = lax.fori_loop(0, steps_in, backward, (arriving, (zero,) * count), unroll=2)
        for n in range(count):
            spar_o[8 + n : 9 + n, lanes] = LN2 * jnp.sum(
                rate_grads[n] * rates[n], axis=0, keepdims=True
            )
        return 0

    lax.fori_loop(0, di // 128, scan, 0)

    moves.need(pre, sig_step, xd, steps)
    lane8 = lax.broadcasted_iota(jnp.int32, (SUB, 128), 1)
    blocks = []
    for j in range(steps_in):
        block = jnp.zeros((SUB, 128), f32)
        for n in range(count):
            k = j * count + n
            block = jnp.where(
                lane8 == rank + n, jnp.sum(bacc_s[k], axis=1, keepdims=True), block
            )
            block = jnp.where(
                lane8 == rank + count + n, jnp.sum(cacc_s[k], axis=1, keepdims=True), block
            )
        blocks.append(block)
    coef_grad = jnp.concatenate(blocks, axis=0)
    lane = lax.broadcasted_iota(jnp.int32, (rows, 128), 1)
    step_low = jnp.where(
        lane >= 128 - rank, pltpu.roll(small[...], 128 - rank, 1), 0.0
    ).astype(bf16)

    def steps_back(g, total):
        lanes = pl.ds(pl.multiple_of(g * gs, gs), gs)
        pre_here = pre[:, lanes]
        act = pre_here * jax.nn.sigmoid(pre_here)
        pre_grad = (LN2 * sgr_s[:, lanes] + act * asc_s[:, lanes]) * sig_step[:, lanes]
        spar_o[KC + 1 : KC + 2, lanes] = jnp.sum(pre_grad, axis=0, keepdims=True)
        pre_low = pre_grad.astype(bf16)
        plow_s[:, lanes] = pre_low
        return total + dot_nn(pre_low, xd[lanes, :])

    rank_grad = lax.fori_loop(0, di // gs, steps_back, jnp.zeros((rows, 128), f32))
    small_low = jnp.where(lane < rank, pltpu.roll(rank_grad, rank, 1), coef_grad).astype(bf16)

    def act_back(g, _):
        lanes = pl.ds(pl.multiple_of(g * gs, gs), gs)
        pre_here = pre[:, lanes]
        sig = jax.nn.sigmoid(pre_here)
        act_low = (pre_here * sig).astype(bf16)
        total = (
            sgrad[:, lanes] * par[KC + 2 : KC + 3, lanes]
            + steps[:, lanes] * asc_s[:, lanes]
            + dot_nt(small_low, xd[lanes, :])
        )
        cgrad_o[:, lanes] = total * sig * (1.0 + pre_here * (1.0 - sig))
        xd_o[lanes, :] = (dot_tn(act_low, small_low) + dot_tn(plow_s[:, lanes], step_low)).astype(bf16)
        return 0

    lax.fori_loop(0, di // gs, act_back, 0)


def last_kernel(
    moves, core, cgrad, halo, aux, ext, par, wm, wo, ngrad_z, spar, skip, xd, hid, gain_two,
    router_sum, pay_o, ngrad_o, extra_o, low_s, far_s, *, width
):
    rows, di = cgrad.shape
    gs = 128
    moves.need(ext)
    ahead_lane = spar.shape[0] + 4 * (hid.shape[1] // width)
    moves.need(xd)

    def conv(g, _):
        lanes = pl.ds(pl.multiple_of(g * gs, gs), gs)
        cg = cgrad[:, lanes]
        grad = par[KC - 1 : KC, lanes] * cg
        parts = [jnp.sum(cg * ext[(KC - 1) * SUB :, lanes], axis=0, keepdims=True)]
        zero = jnp.zeros((1, gs), f32)
        behind = [zero] * (KC - 1)
        for ahead in range(1, KC):
            tap = par[KC - 1 - ahead : KC - ahead, lanes]
            masked = cg * aux[:, ahead - 1 : ahead]
            shifted = ext[(KC - 1 - ahead) * SUB : (KC - 1 - ahead) * SUB + rows, lanes]
            parts.append(jnp.sum(masked * shifted, axis=0, keepdims=True))
            pieces = [masked[ahead * SUB :, :]]
            for i in range(ahead):
                pieces.append(from_after(masked[i * SUB : (i + 1) * SUB, :], zero))
                k = KC - 1 - ahead + i
                behind[k] = behind[k] + tap * masked[i * SUB : i * SUB + 1, :]
            grad = grad + tap * jnp.concatenate(pieces, axis=0)
        low_s[:, lanes] = grad.astype(bf16)
        pay_o[lanes, 0:128] = grad.T.astype(bf16)
        pay_o[lanes, 128:256] = xd[lanes, :]
        extra = jnp.concatenate(behind + [jnp.zeros((SUB - KC + 1, gs), f32)], axis=0)
        far_s[:SUB, lanes] = extra.astype(bf16)
        own = jnp.concatenate(
            parts[::-1]
            + [jnp.sum(cg, axis=0, keepdims=True), spar[KC + 1 : KC + 2, lanes], skip[:, lanes]]
            + [zero, spar[8:, lanes], jnp.zeros((ahead_lane - spar.shape[0], gs), f32), extra]
            + [jnp.zeros((128 - ahead_lane - SUB, gs), f32)],
            axis=0,
        )
        pay_o[lanes, 256:384] = own.T.astype(bf16)
        return 0

    lax.fori_loop(0, di // gs, conv, 0)
    far_s[SUB:, :] = jnp.zeros_like(far_s[SUB:, :])
    moves.need(wm, wo, ngrad_z, hid)
    low = core[0] == 0

    def onto_inputs(values):
        return dot_nn(values, wm[...]), dot_nn(values, wo[...])

    def joined(mine, other):
        return jnp.concatenate([jnp.where(low, mine, other), jnp.where(low, other, mine)], axis=1)

    mine, other = onto_inputs(low_s[...])
    ngrad = joined(mine + ngrad_z[0], other + ngrad_z[1])
    ngrad_o[...] = ngrad
    far = joined(*onto_inputs(far_s[...]))[:SUB, :]
    extra_o[...] = far
    first = hid[...].astype(f32)
    scale = lax.rsqrt(jnp.mean(first * first, axis=1, keepdims=True) + epsilon)
    gains = jnp.sum(ngrad * first * scale, axis=0, keepdims=True)
    first = halo[SUB:, :].astype(f32)
    scale = lax.rsqrt(jnp.mean(first * first, axis=1, keepdims=True) + epsilon)
    gains = gains + jnp.sum(far * first * scale, axis=0, keepdims=True)
    model = first.shape[1]
    each = model // width
    row = lax.broadcasted_iota(jnp.int32, (width, model), 0)
    column = lax.broadcasted_iota(jnp.int32, (width, model), 1)
    here = column // each == row
    extra = jnp.zeros((width, 128), f32)
    router_row = jnp.concatenate([router_sum[0:1, :], router_sum[1:2, :]], axis=1)
    router_top = router_row.astype(bf16).astype(f32)
    rows_sent = (gains, gain_two[...], router_top, router_row - router_top)
    for k, values in enumerate(rows_sent):
        spread = jnp.where(here, values, 0.0).astype(bf16)
        at = lax.broadcasted_iota(jnp.int32, (model, 128), 0)
        to = lax.broadcasted_iota(jnp.int32, (model, 128), 1)
        placed = (at % each + spar.shape[0] + k * each == to).astype(bf16)
        extra = extra + dot_nn(spread, placed)
    extra = extra.astype(bf16)
    for place in range(di // width):
        pay_o[place * width : (place + 1) * width, 256:384] += extra


def tail_kernel(
    moves, place, core, xd, par, sd, q, pre, steps, sig_step, small, x_in, tpre, entry, y_in, tsuf,
    arrived, near, sgrad, halo, aux, ext, wm, wo, ngrad_z, skip, hid, gain_two,
    pay_o, ngrad_o, extra_o, low_s, far_s, cgrad_s, xd_s, spar_s, router_s, *scratch,
    rank, count, width
):
    scan_kernel(
        moves, place, xd, par, sd, q, pre, steps, sig_step, small, x_in, tpre, entry, y_in, tsuf,
        arrived, near, sgrad, cgrad_s, xd_s, spar_s, router_s, *scratch, rank=rank, count=count
    )
    last_kernel(
        moves, core, cgrad_s, halo, aux, ext, par, wm, wo, ngrad_z, spar_s, skip, xd_s, hid,
        gain_two, router_s, pay_o, ngrad_o, extra_o, low_s, far_s, width=width
    )


def hidden_kernel(ngrad_in, beyond, hid, mgrad, gain, first_o):
    first = hid[...].astype(f32)
    rows = first.shape[0]
    ngrad = ngrad_in[...]
    row = lax.broadcasted_iota(jnp.int32, first.shape, 0)
    for i in range(KC - 1):
        at = rows - 1 - (KC - 2 - i) * SUB
        ngrad = ngrad + jnp.where(row == at, beyond[i : i + 1, :], 0.0)
    scale = lax.rsqrt(jnp.mean(first * first, axis=1, keepdims=True) + epsilon)
    scaled = gain[...].reshape(1, -1) * ngrad
    cube = scale * scale * scale
    grad = (
        mgrad[...] + scale * scaled - first * cube * jnp.mean(first * scaled, axis=1, keepdims=True)
    )
    order = token_order(rows)
    top = grad.astype(bf16)
    left = grad - top.astype(f32)
    mid = left.astype(bf16)
    low_part = (left - mid.astype(f32)).astype(bf16)
    first_o[...] = dot_tn(order, top) + dot_tn(order, mid) + dot_tn(order, low_part)


def ready_kernel(moves, side, comb, mix_half, mine_o, theirs_o, gated_s):
    places = comb.shape[0]
    width = mine_o.shape[0]
    for k in range(places // 2):
        place = 2 * k + side[0]
        gated_s[:, k * 128 : (k + 1) * 128] = comb[place, width : 3 * width, :]
    moves.need(mix_half)
    grads = dot_nn(gated_s[...], mix_half[...]).astype(bf16)
    first = side[0] == 0
    mine_o[...] = jnp.where(first, grads[:width, :], grads[width:, :])
    theirs_o[...] = jnp.where(first, grads[width:, :], grads[:width, :])


def grads_kernel(got, comb, nrm_all, out_one, out_two, out_o, left_s, *, base):
    places, width, _ = got.shape
    model = nrm_all.shape[1]
    each = model // width
    rest = jnp.zeros((width, 256), f32)
    routers = [jnp.zeros((width, 128), f32) for _ in range(places * each // 128)]
    lane = lax.broadcasted_iota(jnp.int32, (width, 128), 1)
    row = lax.broadcasted_iota(jnp.int32, (128, 128), 0)
    column = lax.broadcasted_iota(jnp.int32, (128, 128), 1)
    after = row - (base + 2 * each)
    late = column == 127 - (KC - 2 - after) * SUB
    placed = (late & (after >= 0) & (after < KC - 1)).astype(bf16)
    for place in range(places):
        at = gathered_place(place)
        inner = got[at, :, :128]
        if place + 1 < places:
            beyond = dot_nn(got[gathered_place(place + 1), :, 256:384], placed)
            inner = (inner.astype(f32) + beyond).astype(bf16)
        left_s[:width, at * 128 : (at + 1) * 128] = inner
        left_s[width:, at * 128 : (at + 1) * 128] = comb[at, :width, :]
        there = got[at, :, 128:].astype(f32)
        rest = rest + there
        k = place * each // 128
        inside = place * each % 128
        mine = (lane >= inside) & (lane < inside + each)
        for part in range(2):
            turn = (inside - base - part * each) % 128
            routers[k] = routers[k] + jnp.where(mine, pltpu.roll(there[:, 128:], turn, 1), 0.0)
    out_o[3 * width :, :model] = (out_one[...].astype(f32) + out_two[...].astype(f32)).astype(bf16)
    out_o[2 * width : 3 * width, :256] = rest.astype(bf16)
    out_o[2 * width : 3 * width, 256:] = jnp.concatenate(routers, axis=1).astype(bf16)
    out_o[: 2 * width, :model] = dot_nn(left_s[...], nrm_all[...]).astype(bf16)


def token_order(rows):
    steps_in = rows // SUB
    row = lax.broadcasted_iota(jnp.int32, (rows, rows), 0)
    column = lax.broadcasted_iota(jnp.int32, (rows, rows), 1)
    return ((row % SUB) * steps_in + row // SUB == column).astype(bf16)


def final_kernel(
    ours, theirs, x_o, z_o, out_o, conv_o, bias_o, xp_o, dt_o, db_o, al_o, skip_o, router_o, one_o,
    two_o, mine_s, other_s, *, rank, count, experts
):
    width = out_o.shape[0]
    model = router_o.shape[1]
    each = model // width
    x_o[...] = ours[:width, :model].astype(f32) + theirs[:width, :model].astype(f32)
    middle = slice(width, 2 * width)
    z_o[...] = ours[middle, :model].astype(f32) + theirs[middle, :model].astype(f32)
    last = slice(3 * width, 4 * width)
    out_o[...] = ours[last, :model].astype(f32) + theirs[last, :model].astype(f32)
    rest = slice(2 * width, 3 * width)
    xd = ours[rest, :128].astype(f32) + theirs[rest, :128].astype(f32)
    xp_o[...] = xd[:, : rank + 2 * count]
    gap = jnp.zeros((128 - width, 128), f32)
    turned = jnp.concatenate([xd, gap], axis=0).T
    dt_o[...] = turned[128 - rank :, :width]
    vectors = jnp.zeros((128, 128), f32)
    for part, held in ((ours, mine_s), (theirs, other_s)):
        block = jnp.concatenate([part[rest, 128:256].astype(f32), gap], axis=0).T
        vectors = vectors + block
        for k in range(experts * each // 128):
            lanes = slice(256 + k * 128, 384 + k * 128)
            piece = jnp.concatenate([part[rest, lanes].astype(f32), gap], axis=0)
            held[k * 128 : (k + 1) * 128, :] = piece.T
        held[experts * each :, :] = jnp.zeros_like(held[experts * each :, :])
        held[experts * each : (experts + 2) * each, :] = block[8 + count : 8 + count + 2 * each, :]
    conv_o[...] = vectors[:KC, :width]
    bias_o[...] = vectors[KC : KC + 1, :width].reshape(width)
    db_o[...] = vectors[KC + 1 : KC + 2, :width].reshape(width)
    skip_o[...] = vectors[KC + 2 : KC + 3, :width].reshape(width)
    al_o[...] = vectors[8 : 8 + count, :width]
    row = lax.broadcasted_iota(jnp.int32, (128, model), 0)
    column = lax.broadcasted_iota(jnp.int32, (128, model), 1)
    total = jnp.zeros((experts + 8, model), f32)
    for at in range(each):
        to = (row * each + at == column).astype(bf16)
        picked = pl.ds(at, experts + 8, stride=each)
        total = total + dot_nn(mine_s[picked, :].astype(bf16), to)
        total = total + dot_nn(other_s[picked, :].astype(bf16), to)
    router_o[...] = total[:experts, :]
    one_o[...] = total[experts : experts + 1, :].reshape(model)
    two_o[...] = total[experts + 1 : experts + 2, :].reshape(model)


def token_order(rows):
    steps_in = rows // SUB
    row = lax.broadcasted_iota(jnp.int32, (rows, rows), 0)
    column = lax.broadcasted_iota(jnp.int32, (rows, rows), 1)
    return ((row % SUB) * steps_in + row // SUB == column).astype(bf16)


def exchange(values):
    return lax.all_to_all(values, "wide", split_axis=0, concat_axis=0, tiled=True)


def exchange_near(values, members):
    groups = [[u * members + z for z in range(members)] for u in range(32 // members)]
    blocks = values.reshape(members, -1, values.shape[1])
    return lax.all_to_all(
        blocks, "wide", split_axis=0, concat_axis=0, tiled=True, axis_index_groups=groups
    ).reshape(values.shape)


def exchange_far(values, members):
    groups = [[u * members + z for u in range(32 // members)] for z in range(members)]
    blocks = values.reshape(32 // members, -1, values.shape[1])
    return lax.all_to_all(
        blocks, "wide", split_axis=0, concat_axis=0, tiled=True, axis_index_groups=groups
    ).reshape(values.shape)


def gathered_place(place):
    return (place // 8 * 4 + place % 4) * 2 + place // 4 % 2


def exchange_channels(values):
    order = sorted(range(32), key=gathered_place)
    return lax.all_to_all(
        values, "wide", split_axis=0, concat_axis=0, tiled=True, axis_index_groups=[order]
    )


def other_chip(values):
    return lax.ppermute(values, "wide", [(i, i ^ 4) for i in range(32)])


def pair_up(values, partner, place):
    first = (place // 4) % 2 == 0
    return jnp.concatenate(
        [jnp.where(first, values, partner), jnp.where(first, partner, values)], axis=0
    )


def gather_pairs(both):
    groups = [[(y * 2 + x) * 4 + z for y in range(4) for z in range(4)] for x in range(2)]
    return lax.all_gather(both, "wide", axis=0, tiled=True, axis_index_groups=groups)


def exchange_sides(values):
    groups = [
        [(side * 2 + core) * 32 + place for side in range(2) for place in range(32)]
        for core in range(2)
    ]
    return lax.all_to_all(
        values, ("dp", "wide"), split_axis=0, concat_axis=0, tiled=True, axis_index_groups=groups
    )


def other_core(values):
    return lax.ppermute(values, "dp", [(0, 1), (1, 0), (2, 3), (3, 2)])


def other_side(values):
    return lax.ppermute(values, "dp", [(0, 2), (2, 0), (1, 3), (3, 1)])


def body(
    hidden, cotangent, routes, seg_lengths, gain_mix, in_x, in_z, conv_w, conv_b, x_proj, dt_proj,
    dt_bias, a_log, skip_d, out_proj, gain_moe, router, w_gate, w_up, w_down,
):
    rows, model = hidden.shape
    places = lax.axis_size("wide")
    place = lax.axis_index("wide")
    core = (lax.axis_index("dp") % 2).astype(jnp.int32).reshape(1)
    place_arr = place.astype(jnp.int32).reshape(1)
    width = in_x.shape[1]
    di = width * places
    count = a_log.shape[0]
    rank = dt_proj.shape[0]
    experts = router.shape[1]
    capacity = max(CAP * rows // (4 * places), 2)
    stride = -(-2 * capacity // 16) * 16
    half = model // 2
    steps_in = rows // SUB
    shift = SUB.bit_length() - 1
    span = 3 * width
    members = 4
    side = (place // 4 % 2).astype(jnp.int32).reshape(1)

    gate_share = call(
        pack_gate_kernel, [shape((width, model), bf16)], [], (core, in_z.T, out_proj), smem=1
    )[0]
    gate_share, x_proj = lax.optimization_barrier((gate_share, x_proj))
    pay_one = call(
        partial(pack_kernel, places=places),
        [shape((di, half + 128), bf16)],
        [],
        (core, in_x.T, x_proj, dt_proj, conv_w, conv_b, dt_bias, skip_d, a_log),
        smem=1,
    )[0]
    w_gate_two, w_up_two, w_down_two = (other_core(w[0]) for w in (w_gate, w_up, w_down))
    pay_one, hidden, cotangent, routes, seg_lengths = lax.optimization_barrier(
        (pay_one, hidden, cotangent, routes, seg_lengths)
    )
    gate_partner = other_chip(gate_share)
    pay_one, gate_partner = lax.optimization_barrier((pay_one, gate_partner))
    wm = exchange_channels(pay_one.reshape(places, width, half + 128)).reshape(di, half + 128)
    zm = gather_pairs(pair_up(gate_share, gate_partner, place))
    nrm, tail, hid, cot, route, aux = call(
        prepare_kernel,
        [
            shape((rows, model), bf16),
            shape((16, model), bf16),
            shape((rows, model), bf16),
            shape((rows, model), bf16),
            shape((rows, 1), jnp.int32),
            shape((rows, 128)),
        ],
        [],
        (place_arr * rows, seg_lengths, hidden, cotangent, routes.T, gain_mix),
        smem=2,
    )
    halo = lax.ppermute(tail, "wide", [(i, i + 1) for i in range(places - 1)])
    nrm_partner = other_chip(nrm)
    wm, halo = lax.optimization_barrier((wm, halo))
    wo = other_core(wm)
    ext, pre, steps, sig_step, small, x_in, tpre, tsuf, states, par, xd_weight, sd, q = call(
        partial(front_kernel, rank=rank, count=count),
        [
            shape((rows + (KC - 1) * SUB, di)),
            shape((rows, di)),
            shape((rows, di)),
            shape((rows, di)),
            shape((rows, 128)),
            shape((count, SUB, di)),
            shape((SUB, di)),
            shape((SUB, di)),
            shape((members * count, di + 256), bf16),
            shape((8 + count, di)),
            shape((di, 128), bf16),
            shape((rows, di)),
            shape((rows, di)),
        ],
        [
            pltpu.VMEM((steps_in * count, SUB, 128), f32),
            pltpu.VMEM((2, rows + 16, half), bf16),
            pltpu.VMEM((16, 128), f32),
        ],
        (core, nrm, halo, wm, wo, wm, wo, aux),
        smem=1,
        late=(5, 6, 3, 4),
        early=(0, 1, 2, 3, 9, 10, 11, 12),
        lanes={3: pl.ds(0, half), 4: pl.ds(0, half), 5: pl.ds(half, 128), 6: pl.ds(half, 128)},
    )

    near = exchange_near(states, members)
    zm, nrm_partner, near = lax.optimization_barrier((zm, nrm_partner, near))
    zo = other_core(zm)
    z_lanes = pl.ds(0, half)
    out_lanes = pl.ds(half, half)
    gate_z = call(
        gate_kernel,
        [shape((rows, di))],
        [pltpu.VMEM((2, rows, half), bf16)],
        (core, nrm, zm, zo),
        smem=1,
        late=(2, 3),
        lanes={2: z_lanes, 3: z_lanes},
    )[0]
    states = call(
        partial(forward_group_kernel, di=di, count=count),
        [shape((places // members * count, di + 256), bf16)],
        [pltpu.VMEM((count, di), f32)] * 2,
        (near, par),
        limit=12 * 1024 * 1024,
    )[0]
    states = exchange_far(states, members)

    nrm_pair = pair_up(nrm, nrm_partner, place)
    states, gate_z, nrm_pair = lax.optimization_barrier((states, gate_z, nrm_pair))
    normed_all = gather_pairs(nrm_pair)
    scanned, send, middle, ntwo, chances, meta, hot, entry = call(
        partial(
            middle_kernel,
            rank=rank,
            count=count,
            experts=experts,
            stride=stride,
            capacity=capacity,
            shift=shift,
        ),
        [
            shape((rows, di)),
            shape((2 * experts * stride, 2 * model // 3), bf16),
            shape((rows, model)),
            shape((rows, model), bf16),
            shape((rows, experts)),
            shape((rows, 8)),
            shape((3, 2 * rows, experts * stride), bf16),
            shape((count, di)),
        ],
        [
            pltpu.VMEM((steps_in * count, SUB, 128), f32),
            pltpu.VMEM((steps_in * count, SUB, 128), f32),
            pltpu.VMEM((count, di), f32),
        ],
        (
            core, place_arr, zm, zo, par, aux, pre, sd, q, x_in, small, states, near, tpre, hid, cot,
            route, gain_moe, router.T, gate_z,
        ),
        smem=2,
        late=(11, 12, 9, 7, 8, 6, 19, 2, 3),
        early=(7, 0, 6, 2, 3),
        lanes={2: out_lanes, 3: out_lanes},
    )
    arrived = exchange_sides(send.reshape(2 * experts, stride, -1)).reshape(send.shape)
    slots = 2 * places * capacity
    kept, sent, back = call(
        partial(expert_kernel, stride=stride, capacity=capacity),
        [shape((5 * slots, model), bf16)] * 2 + [shape(send.shape, bf16)],
        [],
        (arrived, w_gate[0], w_up[0], w_down[0], w_gate_two, w_up_two, w_down_two),
        late=(1, 2, 3, 4, 5, 6),
        early=(0, 1, 2),
        limit=44 * 1024 * 1024,
    )
    back = exchange_sides(back.reshape(2 * experts, stride, -1)).reshape(send.shape)
    given = other_core(sent)

    def both_cores(left, right):
        total = 0.0
        for part in (kept, given):
            rows_left = part[left * slots : (left + 1) * slots]
            total = total + dot_tn(rows_left, part[right * slots : (right + 1) * slots])
        return total[None]

    grad_w_down = both_cores(2, 1)
    grad_w_gate = both_cores(0, 3)
    grad_w_up = both_cores(0, 4)
    back, grad_w_down, grad_w_gate, grad_w_up = lax.optimization_barrier(
        (back, grad_w_down, grad_w_gate, grad_w_up)
    )

    combined, mixlow, mgrad, ggrad, sgrad, gain_two, y_in, adjoints = call(
        partial(back_kernel, rank=rank, count=count, experts=experts),
        [
            shape((rows, model)),
            shape((rows, model), bf16),
            shape((rows, model)),
            shape((rows, di)),
            shape((rows, di)),
            shape((1, model)),
            shape((count, SUB, di)),
            shape((members * count, di + 256 + half), bf16),
        ],
        [
            pltpu.VMEM((steps_in * count, SUB, 128), f32),
            pltpu.VMEM((2, rows, half), bf16),
            pltpu.VMEM((count, di), f32),
            pltpu.VMEM((16, 128), f32),
        ],
        (
            core, back, zm, zo, par, aux, sd, small, gate_z, hot, middle, meta, chances, route,
            cot, gain_moe, router.T, ntwo,
        ),
        smem=1,
        late=(2, 3, 8, 6),
        early=(1, 2, 0, 3, 4),
        lanes={2: out_lanes, 3: out_lanes},
    )
    near_back = exchange_near(adjoints, members)
    adjoints = call(
        partial(backward_group_kernel, di=di, count=count),
        [shape((places // members * count, di + 256 + half), bf16)],
        [pltpu.VMEM((count, di), f32)] * 2,
        (near_back, par),
        limit=12 * 1024 * 1024,
    )[0]
    adjoints = exchange_far(adjoints, members)
    out, comb, skip_part, ngrad_z = call(
        partial(aside_kernel, width=width, span=span),
        [
            shape((rows, model), bf16),
            shape((places * span, 128), bf16),
            shape((1, di)),
            shape((2, rows, half)),
        ],
        [],
        (
            core, side, zm, zo, aux, pre, gate_z, scanned, ggrad, combined, middle, meta,
        ),
        smem=2,
        late=(2, 3),
        lanes={2: z_lanes, 3: z_lanes},
    )
    adjoints, comb = lax.optimization_barrier((adjoints, comb))
    mixlow, normed_all = lax.optimization_barrier((mixlow, normed_all))
    mix_half = gather_pairs(mixlow)
    comb_got = exchange_channels(comb.reshape(places, span, 128))

    pay, ngrad, beyond = call(
        partial(tail_kernel, rank=rank, count=count, width=width),
        [shape((di, 384), bf16), shape((rows, model)), shape((SUB, model))],
        [
            pltpu.VMEM((rows, di), bf16),
            pltpu.VMEM((16, di), bf16),
            pltpu.VMEM((rows, di), f32),
            pltpu.VMEM((di, 128), bf16),
            pltpu.VMEM((8 + count, di), f32),
            pltpu.VMEM((count, half), f32),
        ]
        + [pltpu.VMEM((steps_in * count, SUB, 128), f32)] * 4
        + [pltpu.VMEM(((steps_in + 1) * count, SUB, 128), f32)]
        + [pltpu.VMEM((steps_in * count, SUB, 128), f32)]
        + [pltpu.VMEM((rows, di), f32)] * 2
        + [pltpu.VMEM((rows, di), bf16)]
        + [pltpu.VMEM((count, di), f32)] * 2,
        (
            place_arr, core, xd_weight, par, sd, q, pre, steps, sig_step, small, x_in, tpre, entry,
            y_in, tsuf, adjoints, near_back, sgrad, halo, aux, ext, wm, wo, ngrad_z, skip_part, hid,
            gain_two,
        ),
        smem=2,
        late=(15, 16, 10, 4, 5, 17, 13, 6, 8, 2, 7, 20, 21, 22, 23, 25),
        lanes={21: z_lanes, 22: z_lanes},
    )
    got_pay = exchange_channels(pay.reshape(places, width, 384))
    beyond = lax.ppermute(beyond, "wide", [(i + 1, i) for i in range(places - 1)])
    out_ready, out_theirs = call(
        ready_kernel,
        [shape((width, model), bf16)] * 2,
        [pltpu.VMEM((2 * width, places // 2 * rows), bf16)],
        (side, comb_got, mix_half),
        smem=1,
        late=(2,),
        limit=24 * 1024 * 1024,
    )
    out_other = other_chip(out_theirs)
    got_pay, out_other, beyond = lax.optimization_barrier((got_pay, out_other, beyond))
    first_grad = call(
        hidden_kernel, [shape((rows, model))], [], (ngrad, beyond, hid, mgrad, gain_mix), limit=12 * 1024 * 1024
    )[0]
    per_place = model // width
    mats = call(
        partial(grads_kernel, base=8 + count + 2 * per_place),
        [shape((4 * width, 256 + places * per_place), bf16)],
        [pltpu.VMEM((2 * width, places * rows), bf16)],
        (got_pay, comb_got, normed_all, out_ready, out_other),
        limit=24 * 1024 * 1024,
    )[0]
    mats = (mats.astype(f32) + other_core(mats).astype(f32)).astype(bf16)
    grad_x, grad_z, grad_out, grad_conv, grad_bias, grad_xp, grad_dt, grad_db, grad_al, grad_sk, grad_router, gain_one, gain_two = call(
        partial(final_kernel, rank=rank, count=count, experts=experts),
        [
            shape((width, model)),
            shape((width, model)),
            shape((width, model)),
            shape((KC, width)),
            shape((width,)),
            shape((width, rank + 2 * count)),
            shape((rank, width)),
            shape((width,)),
            shape((count, width)),
            shape((width,)),
            shape((experts, model)),
            shape((model,)),
            shape((model,)),
        ],
        [pltpu.VMEM(((experts + 8) * per_place, 128), f32)] * 2,
        (mats, other_side(mats)),
        limit=12 * 1024 * 1024,
    )
    return (
        out,
        first_grad,
        gain_one,
        grad_x.T,
        grad_z.T,
        grad_conv,
        grad_bias,
        grad_xp,
        grad_dt,
        grad_db,
        grad_al,
        grad_sk,
        grad_out,
        gain_two,
        grad_router.T,
        grad_w_gate,
        grad_w_up,
        grad_w_down,
    )


def solution(mesh):
    rows = P(("dp", "wide"), None)
    expert_columns = P("wide", None, "dp")
    expert_rows = P("wide", "dp", None)
    placed = (
        rows, rows, rows, P("dp", None), P(), P(None, "wide"), P(None, "wide"), P(None, "wide"),
        P("wide"), P("wide", None), P(None, "wide"), P("wide"), P(None, "wide"), P("wide"),
        P("wide", None), P(), P(), expert_columns, expert_columns, expert_rows,
    )
    given = (
        rows, rows, P(), P(None, "wide"), P(None, "wide"), P(None, "wide"), P("wide"),
        P("wide", None), P(None, "wide"), P("wide"), P(None, "wide"), P("wide"), P("wide", None),
        P(), P(), expert_columns, expert_columns, expert_rows,
    )
    return jax.shard_map(body, mesh=mesh, in_specs=placed, out_specs=given, check_vma=False)
```
